32 devices in a mesh: ctx: 8 (over y, x, core), head: 4 (over z).
Axes of the slice: x: 2, y: 2, z: 4, core: 2. Of those that a mesh axis runs over, the one named last changes fastest.
Arguments:
- queries: bfloat16 [16, 2048, 128], P('head', 'ctx'), may hold values from -110 to 110
- keys: bfloat16 [2, 2048, 128], P(None, 'ctx'), may hold values from -4 to 4
- values: bfloat16 [2, 2048, 128], P(None, 'ctx'), may hold values from -6 to 6
- d_out: bfloat16 [16, 2048, 128], P('head', 'ctx'), may hold values from -6 to 6
- doc_lengths: int32 [4], replicated, may hold values from 1 to 1024, 2048 in all
Outputs:
- d_queries: bfloat16 [16, 2048, 128], P('head', 'ctx')
- d_keys: bfloat16 [2, 2048, 128], P(None, ('ctx', 'head'))
- d_values: bfloat16 [2, 2048, 128], P(None, ('ctx', 'head'))
The draws below stay inside these ranges and needn't reach their ends.
Inputs may be any that keep to these rules, and one draw needn't show every extreme that they name: `doc_lengths`: documents lie end to end in order and their lengths sum to 2048; one of them has exactly 1024 tokens.
All inputs are finite; a program needn't handle non-finite values.
Results may differ from the reference program's by a relative error of at most 0.025.
Values may be sent and summed in bfloat16 or wider, within the bound.
No kernel may reach another device: no remote copies, remote signals or barrier semaphores. Data moves between devices by JAX's collectives and lax.ppermute only.
A program may use at most 64 MiB of HBM per device.

```python
import math
import jax
import jax.numpy as jnp
import numpy as np
from jax import lax

HD = 128
GROUP = 8
TOK_DEV = 256
QHEADS = 16
KVH = 2
TOKENS = 2048
REACH = 4
DOC_MOST = 1024
DOCS = 4


def paired_draw(key):
    query_seed = jax.random.fold_in(key, 101)
    key_seed = jax.random.fold_in(key, 202)
    key_vals = jnp.clip(jax.random.normal(key_seed, (KVH, TOKENS, HD), jnp.float32), -4.0, 4.0)
    query_vals = jnp.clip(jax.random.normal(query_seed, (QHEADS, TOKENS, HD), jnp.float32), -4.0, 4.0)
    return (query_vals, key_vals)


def draw_queries(key, part):
    return paired_draw(key)[0].astype(jnp.bfloat16)


def draw_keys(key, part):
    return paired_draw(key)[1].astype(jnp.bfloat16)


def block_scale(rng, extent, cuts, least, high):
    gain = 1.0
    for axis_at, parts in cuts:
        heights = jax.random.uniform(jax.random.fold_in(jax.random.fold_in(rng, 6), axis_at), (parts,), jnp.float32, least / len(cuts), high / len(cuts))
        gain = gain * jnp.repeat(jnp.exp(heights), extent[axis_at] // parts).reshape((-1,) + (1,) * (len(extent) - 1 - axis_at))
    return gain


def profile(amount, total, reach, lean):
    loads = [(1 << 20) // math.isqrt(standing ** lean) + 1 for standing in range(2, amount + 1)]
    surplus, counts = total - reach - (amount - 1), [1] * (amount - 1)
    while surplus > 0:
        movable = [i for i in range(amount - 1) if counts[i] < reach]
        mass, budget = sum([loads[i] for i in movable]), surplus
        for i in movable:
            addition = min(reach - counts[i], max(1, budget * loads[i] // mass), surplus)
            counts[i] = counts[i] + addition
            surplus = surplus - addition
    return np.array([reach] + counts)


def uneven(own_key, number_of, total, most, lean):
    if number_of == 2:
        one = jax.random.randint(own_key, (), max(1, total - most), min(most, total - 1) + 1)
        return jnp.stack([one, total - one])
    tallies = jnp.asarray(profile(number_of, total, most, lean), jnp.int32)
    twos = (number_of - 1) // 2
    source_of, receiver = tallies[1:1 + 2 * twos:2], tallies[2:2 + 2 * twos:2]
    room = jnp.minimum(source_of - 1, most - receiver)
    shifted = jax.random.randint(jax.random.fold_in(own_key, 1), (twos,), 0, 1 << 20) % (room + 1)
    tallies = tallies.at[1:1 + 2 * twos:2].set(source_of - shifted).at[2:2 + 2 * twos:2].set(receiver + shifted)
    return tallies[jax.random.permutation(jax.random.fold_in(own_key, 2), number_of)]


def gaussian(rng, extent, spread, most, split=(), kind=jnp.bfloat16):
    factor_of = block_scale(rng, extent, split, -0.22, 0.18) if split else 1.0
    array = jax.random.normal(rng, extent, jnp.float32) * spread * factor_of
    return jnp.minimum(jnp.maximum(array, -most), most).astype(kind)


def setup_inputs(seed: int = 0) -> dict:
    streams_of = jax.random.split(jax.random.key(seed), 6)
    queries = draw_queries(jax.random.fold_in(streams_of[5], 71), 0)
    keys = draw_keys(jax.random.fold_in(streams_of[5], 71), 0)
    values = gaussian(streams_of[2], (KVH, TOKENS, HD), 1.0, 6.0, ((1, 8),))
    d_out = gaussian(streams_of[3], (QHEADS, TOKENS, HD), 1.0, 6.0, ((0, 4), (1, 8)))
    doc_lengths = uneven(streams_of[4], DOCS, TOKENS, DOC_MOST, 2).astype(jnp.int32)
    return dict(queries=queries, keys=keys, values=values, d_out=d_out, doc_lengths=doc_lengths)


masked_value = -1.0e30


def doc_number(positions, doc_ends):
    return jnp.sum((doc_ends[None, :] <= positions[:, None]).astype(jnp.int32), axis=1)


def window_terms(query_rows, grad_rows, key_rows, value_rows, query_pos, key_pos, doc_ends, key_scale):
    allowed = doc_number(query_pos, doc_ends)[:, None] == doc_number(key_pos, doc_ends)[None, :]
    allowed = allowed & (key_pos[None, :] <= query_pos[:, None]) & (key_pos[None, :] >= 0)
    query_wide = query_rows.astype(jnp.float32)
    grad_wide = grad_rows.astype(jnp.float32)
    key_wide = key_rows.astype(jnp.float32)
    value_wide = value_rows.astype(jnp.float32)
    scores = jnp.einsum("hbd,ld->hbl", query_wide, key_wide) * key_scale
    scores = jnp.where(allowed[None], scores, masked_value)
    row_max = jnp.max(scores, axis=-1, keepdims=True)
    log_total = row_max + jnp.log(jnp.sum(jnp.exp(scores - row_max), axis=-1, keepdims=True))
    attention = jnp.where(allowed[None], jnp.exp(scores - log_total), 0.0)
    attn_half = attention.astype(jnp.bfloat16)
    attended = jnp.einsum("hbl,ld->hbd", attn_half.astype(jnp.float32), value_wide).astype(jnp.bfloat16)
    deltas = jnp.sum(grad_wide * attended.astype(jnp.float32), axis=-1, keepdims=True)
    dattn = jnp.einsum("hbd,ld->hbl", grad_wide, value_wide)
    dscores = (attention * (dattn - deltas)).astype(jnp.bfloat16)
    dscore_wide = dscores.astype(jnp.float32)
    dquery = (jnp.einsum("hbl,ld->hbd", dscore_wide, key_wide) * key_scale).astype(jnp.bfloat16)
    key_grad = jnp.einsum("hbl,hbd->ld", dscore_wide, query_wide) * key_scale
    dvalue = jnp.einsum("hbl,hbd->ld", attn_half.astype(jnp.float32), grad_wide)
    return dquery, key_grad, dvalue


def reference(queries, keys, values, d_out, doc_lengths):
    key_scale = HD ** -0.5
    key_span = REACH * TOK_DEV
    window_len = key_span + TOK_DEV
    block_count = TOKENS // TOK_DEV
    doc_ends = jnp.cumsum(doc_lengths).astype(jnp.int32)
    query_groups = queries.reshape(KVH, GROUP, TOKENS, HD)
    grad_groups = d_out.reshape(KVH, GROUP, TOKENS, HD)

    def one_group(operands):
        group_queries, group_grads, group_keys, group_values = operands
        key_padded = jnp.concatenate([jnp.zeros((key_span, HD), group_keys.dtype), group_keys], axis=0)
        value_padded = jnp.concatenate([jnp.zeros((key_span, HD), group_values.dtype), group_values], axis=0)

        def one_block(totals, block_index):
            key_total, value_total = totals
            row_first = (block_index * TOK_DEV).astype(jnp.int32)
            query_rows = lax.dynamic_slice_in_dim(group_queries, row_first, TOK_DEV, 1)
            grad_rows = lax.dynamic_slice_in_dim(group_grads, row_first, TOK_DEV, 1)
            key_rows = lax.dynamic_slice_in_dim(key_padded, row_first, window_len, 0)
            value_rows = lax.dynamic_slice_in_dim(value_padded, row_first, window_len, 0)
            query_pos = row_first + jnp.arange(TOK_DEV, dtype=jnp.int32)
            key_pos = row_first - key_span + jnp.arange(window_len, dtype=jnp.int32)
            dquery, key_grad, dvalue = window_terms(query_rows, grad_rows, key_rows, value_rows, query_pos, key_pos, doc_ends, key_scale)
            key_total = lax.dynamic_update_slice_in_dim(key_total, lax.dynamic_slice_in_dim(key_total, row_first, window_len, 0) + key_grad, row_first, 0)
            value_total = lax.dynamic_update_slice_in_dim(value_total, lax.dynamic_slice_in_dim(value_total, row_first, window_len, 0) + dvalue, row_first, 0)
            return (key_total, value_total), dquery

        zeros_init = jnp.zeros((key_span + TOKENS, HD), jnp.float32)
        (key_total, value_total), dquery_blocks = lax.scan(one_block, (zeros_init, zeros_init), jnp.arange(block_count, dtype=jnp.int32))
        dquery_all = jnp.transpose(dquery_blocks, (1, 0, 2, 3)).reshape(GROUP, TOKENS, HD)
        return dquery_all, key_total[key_span:].astype(jnp.bfloat16), value_total[key_span:].astype(jnp.bfloat16)

    dquery_all, d_keys, d_values = lax.map(one_group, (query_groups, grad_groups, keys, values))
    return dquery_all.reshape(QHEADS, TOKENS, HD), d_keys, d_values
```

```python
import functools
import math

import jax
import jax.numpy as jnp
from jax import lax
from jax.experimental import pallas as pl
from jax.experimental.pallas import tpu as pltpu
from jax.sharding import PartitionSpec as P

GROUP = 8
REACH = 4
MASKED = -1e30
NT = (((1,), (1,)), ((), ()))
NN = (((1,), (0,)), ((), ()))


def dot(a, b, dims):
    return lax.dot_general(a, b, dims, preferred_element_type=jnp.float32)


def attention_body(reach, blocks, ctx_ref, lengths_ref, q_ref, g_ref, kv_ref, dq_ref, terms_ref,
                   s_ref, dp_ref, p_ref, ds_ref, kt_ref):
    heads, tokens, width = q_ref.shape
    scale = width ** -0.5
    here = ctx_ref[0]
    row_pos = here * tokens + lax.broadcasted_iota(jnp.int32, (1, tokens), 1)
    doc_start = jnp.zeros((1, tokens), jnp.int32)
    end = jnp.int32(0)
    for d in range(lengths_ref.shape[0]):
        end = end + lengths_ref[d]
        doc_start = jnp.where(row_pos >= end, end, doc_start)
    key_iota = lax.broadcasted_iota(jnp.int32, (tokens, 1), 0)
    slots = [lax.rem(here - back + blocks, blocks) for back in range(reach + 1)]
    for back in range(reach + 1):
        kt_ref[back] = kv_ref[slots[back], :, :width].T

    for h in range(heads):
        q = q_ref[h]
        g = g_ref[h]
        top = jnp.full((1, tokens), MASKED, jnp.float32)
        for back in range(reach + 1):
            s = dot(kv_ref[slots[back], :, :width], q, NT)
            key_pos = (here - back) * tokens + key_iota
            allowed = key_pos >= doc_start
            if back == 0:
                allowed = allowed & (key_pos <= row_pos)
            s = jnp.where(allowed, s, MASKED)
            s_ref[back] = s
            top = jnp.maximum(top, jnp.max(s, axis=0, keepdims=True))
        factor = scale * math.log2(math.e)
        total = jnp.zeros((1, tokens), jnp.float32)
        for back in range(reach + 1):
            e = jnp.exp2((s_ref[back] - top) * factor)
            s_ref[back] = e
            total = total + jnp.sum(e, axis=0, keepdims=True)
        inverse = 1.0 / total
        delta = jnp.zeros((1, tokens), jnp.float32)
        for back in range(reach + 1):
            dp = dot(kv_ref[slots[back], :, width:], g, NT)
            p = s_ref[back] * inverse
            p_ref[back, :, h * tokens:(h + 1) * tokens] = p.astype(jnp.bfloat16)
            s_ref[back] = p
            dp_ref[back] = dp
            delta = delta + jnp.sum(p * dp, axis=0, keepdims=True)
        dqt = jnp.zeros((width, tokens), jnp.float32)
        for back in range(reach + 1):
            ds = (s_ref[back] * (dp_ref[back] - delta)).astype(jnp.bfloat16)
            ds_ref[back, :, h * tokens:(h + 1) * tokens] = ds
            dqt = dqt + dot(kt_ref[back], ds, NN)
        dq_ref[h] = (dqt.T * scale).astype(dq_ref.dtype)

    q_all = q_ref[...].reshape(heads * tokens, width)
    g_all = g_ref[...].reshape(heads * tokens, width)
    for back in range(blocks):
        slot = lax.rem(here - back + blocks, blocks)
        if back <= reach:
            dk = dot(ds_ref[back], q_all, NN) * scale
            dv = dot(p_ref[back], g_all, NN)
            terms_ref[slot, :, :width] = dk.astype(terms_ref.dtype)
            terms_ref[slot, :, width:] = dv.astype(terms_ref.dtype)
        else:
            terms_ref[slot] = jnp.zeros(terms_ref.shape[1:], terms_ref.dtype)


def attention_terms(ctx, lengths, queries, d_out, gathered, reach):
    heads, tokens, width = queries.shape
    blocks = gathered.shape[0]
    span = reach + 1
    vmem = pl.BlockSpec(memory_space=pltpu.VMEM)
    smem = pl.BlockSpec(memory_space=pltpu.SMEM)
    flops = 2 * 5 * heads * tokens * span * tokens * width
    moved = 2 * (3 * queries.size + 2 * gathered.size)
    return pl.pallas_call(
        functools.partial(attention_body, reach, blocks),
        out_shape=(
            jax.ShapeDtypeStruct(queries.shape, jnp.bfloat16),
            jax.ShapeDtypeStruct(gathered.shape, jnp.bfloat16),
        ),
        in_specs=[smem, smem, vmem, vmem, vmem],
        out_specs=(vmem, vmem),
        scratch_shapes=[
            pltpu.VMEM((span, tokens, tokens), jnp.float32),
            pltpu.VMEM((span, tokens, tokens), jnp.float32),
            pltpu.VMEM((span, tokens, heads * tokens), jnp.bfloat16),
            pltpu.VMEM((span, tokens, heads * tokens), jnp.bfloat16),
            pltpu.VMEM((span, width, tokens), jnp.bfloat16),
        ],
        compiler_params=pltpu.CompilerParams(vmem_limit_bytes=40 * 2**20),
        cost_estimate=pl.CostEstimate(
            flops=flops, bytes_accessed=moved,
            transcendentals=heads * tokens * span * tokens),
        name="attention_terms",
    )(ctx, lengths, queries, d_out, gathered)


def per_device(queries, keys, values, d_out, doc_lengths):
    heads_here, tokens, width = queries.shape
    ctx_count = lax.axis_size("ctx")
    head_count = lax.axis_size("head")
    reach = min(REACH, ctx_count // 2)
    group = lax.axis_index("head") * heads_here // GROUP
    own = jnp.concatenate(
        [lax.dynamic_index_in_dim(keys, group, 0, keepdims=False),
         lax.dynamic_index_in_dim(values, group, 0, keepdims=False)], axis=1)
    gathered = lax.all_gather(own, "ctx")
    ctx = jnp.reshape(lax.axis_index("ctx"), (1,))
    d_queries, terms = attention_terms(ctx, doc_lengths, queries, d_out, gathered, reach)
    sums = lax.psum_scatter(terms, "ctx", scatter_dimension=0)
    pieces = lax.all_to_all(
        sums.reshape(head_count, tokens // head_count, 2 * width), "head", 0, 0)
    share = GROUP // heads_here
    pieces = pieces.reshape(head_count // share, share, tokens // head_count, 2 * width)
    group_sums = jnp.sum(pieces.astype(jnp.float32), axis=1).astype(jnp.bfloat16)
    return d_queries, group_sums[..., :width], group_sums[..., width:]


def solution(mesh):
    placed = (
        P("head", "ctx", None),
        P(None, "ctx", None),
        P(None, "ctx", None),
        P("head", "ctx", None),
        P(),
    )
    return jax.shard_map(
        per_device,
        mesh=mesh,
        in_specs=placed,
        out_specs=(
            P("head", "ctx", None),
            P(None, ("ctx", "head"), None),
            P(None, ("ctx", "head"), None),
        ),
        check_vma=False,
    )
```

```python
import functools
import math

import jax
import jax.numpy as jnp
from jax import lax
from jax.experimental import pallas as pl
from jax.experimental.pallas import tpu as pltpu
from jax.sharding import PartitionSpec as P

GROUP = 8
REACH = 4
MASKED = -1e30
NT = (((1,), (1,)), ((), ()))
NN = (((1,), (0,)), ((), ()))
VMEM = pl.BlockSpec(memory_space=pltpu.VMEM)
SMEM = pl.BlockSpec(memory_space=pltpu.SMEM)
PARAMS = pltpu.CompilerParams(vmem_limit_bytes=24 * 2**20)


def dot(a, b, dims):
    return lax.dot_general(a, b, dims, preferred_element_type=jnp.float32)


def shifted(block, distance):
    count = lax.axis_size("ctx")
    route = [(i - distance, i) for i in range(count) if 0 <= i - distance < count]
    return lax.ppermute(block, "ctx", route)


def exchanged(block, axis, mask):
    return lax.ppermute(block, axis, [(i, i ^ mask) for i in range(lax.axis_size(axis))])


def scores_body(ctx_ref, lengths_ref, q_ref, g_ref, own_ref, two_ref, four_ref, odd_ref,
                ds_ref, p_ref, odd_terms_ref, s_ref, dp_ref, odd_p_ref):
    heads, tokens, width = q_ref.shape
    scale = width ** -0.5
    here = ctx_ref[0]
    row_pos = here * tokens + lax.broadcasted_iota(jnp.int32, (1, tokens), 1)
    doc_start = jnp.zeros((1, tokens), jnp.int32)
    end = jnp.int32(0)
    for d in range(lengths_ref.shape[0]):
        end = end + lengths_ref[d]
        doc_start = jnp.where(row_pos >= end, end, doc_start)
    key_iota = lax.broadcasted_iota(jnp.int32, (tokens, 1), 0)
    window = [own_ref, odd_ref.at[:tokens], two_ref, odd_ref.at[tokens:], four_ref]

    for h in range(heads):
        q = q_ref[h]
        g = g_ref[h]
        lanes = slice(h * tokens, (h + 1) * tokens)
        top = jnp.full((1, tokens), MASKED, jnp.float32)
        for back, pair in enumerate(window):
            s = dot(pair[:, :width], q, NT)
            key_pos = (here - back) * tokens + key_iota
            allowed = key_pos >= doc_start
            if back == 0:
                allowed = allowed & (key_pos <= row_pos)
            s = jnp.where(allowed, s, MASKED)
            s_ref[back] = s
            top = jnp.maximum(top, jnp.max(s, axis=0, keepdims=True))
        factor = scale * math.log2(math.e)
        total = jnp.zeros((1, tokens), jnp.float32)
        for back in range(len(window)):
            e = jnp.exp2((s_ref[back] - top) * factor)
            s_ref[back] = e
            total = total + jnp.sum(e, axis=0, keepdims=True)
        inverse = 1.0 / total
        delta = jnp.zeros((1, tokens), jnp.float32)
        for back, pair in enumerate(window):
            dp = dot(pair[:, width:], g, NT)
            p = s_ref[back] * inverse
            if back % 2:
                odd_p_ref[back // 2, :, lanes] = p.astype(jnp.bfloat16)
            else:
                p_ref[back // 2, :, lanes] = p.astype(jnp.bfloat16)
            s_ref[back] = p
            dp_ref[back] = dp
            delta = delta + jnp.sum(p * dp, axis=0, keepdims=True)
        for back in range(len(window)):
            ds = (s_ref[back] * (dp_ref[back] - delta)).astype(jnp.bfloat16)
            ds_ref[back, :, lanes] = ds

    q_all = q_ref[...].reshape(heads * tokens, width)
    g_all = g_ref[...].reshape(heads * tokens, width)
    for odd in range(len(window) // 2):
        rows = slice(odd * tokens, (odd + 1) * tokens)
        dk = dot(ds_ref[2 * odd + 1], q_all, NN) * scale
        dv = dot(odd_p_ref[odd], g_all, NN)
        odd_terms_ref[rows, :width] = dk.astype(jnp.bfloat16)
        odd_terms_ref[rows, width:] = dv.astype(jnp.bfloat16)


def even_body(ds_ref, p_ref, q_ref, g_ref, *terms_refs):
    heads, tokens, width = q_ref.shape
    q_all = q_ref[...].reshape(heads * tokens, width)
    g_all = g_ref[...].reshape(heads * tokens, width)
    for at, terms_ref in enumerate(terms_refs, 1):
        terms_ref[:, :width] = dot(ds_ref[2 * at], q_all, NN) * width ** -0.5
        terms_ref[:, width:] = dot(p_ref[at], g_all, NN)


def own_body(ds_ref, p_ref, q_ref, g_ref, own_ref, two_ref, four_ref, odd_ref,
             dq_ref, terms_ref):
    heads, tokens, width = q_ref.shape
    scale = width ** -0.5
    q_all = q_ref[...].reshape(heads * tokens, width)
    g_all = g_ref[...].reshape(heads * tokens, width)
    terms_ref[:, :width] = dot(ds_ref[0], q_all, NN) * scale
    terms_ref[:, width:] = dot(p_ref[0], g_all, NN)
    window = [own_ref, odd_ref.at[:tokens], two_ref, odd_ref.at[tokens:], four_ref]
    turned = [pair[:, :width].T for pair in window]
    for h in range(heads):
        lanes = slice(h * tokens, (h + 1) * tokens)
        dqt = jnp.zeros((width, tokens), jnp.float32)
        for back in range(len(window)):
            dqt = dqt + dot(turned[back], ds_ref[back, :, lanes], NN)
        dq_ref[h] = (dqt.T * scale).astype(dq_ref.dtype)


def per_device(queries, keys, values, d_out, doc_lengths):
    heads_here, tokens, width = queries.shape
    head_count = lax.axis_size("head")
    share = GROUP // heads_here
    groups = head_count // share
    blocks = REACH + 1
    ctx = lax.axis_index("ctx")
    head = lax.axis_index("head")
    second_core = ctx % 2 == 1
    bf16, f32 = jnp.bfloat16, jnp.float32

    own = jnp.concatenate(
        [lax.dynamic_index_in_dim(keys, head // share, 0, keepdims=False),
         lax.dynamic_index_in_dim(values, head // share, 0, keepdims=False)], axis=1)
    four = shifted(own, 4)
    two = shifted(own, 2)
    odd = exchanged(
        jnp.concatenate([jnp.where(second_core, two, own), jnp.where(second_core, four, two)]),
        "ctx", 1)

    work = heads_here * tokens * tokens * width * 2
    ds, p, odd_terms = pl.pallas_call(
        scores_body,
        out_shape=(
            jax.ShapeDtypeStruct((blocks, tokens, heads_here * tokens), bf16),
            jax.ShapeDtypeStruct((blocks // 2 + 1, tokens, heads_here * tokens), bf16),
            jax.ShapeDtypeStruct((2 * tokens, 2 * width), bf16),
        ),
        in_specs=[SMEM, SMEM] + [VMEM] * 6,
        out_specs=(VMEM, VMEM, VMEM),
        scratch_shapes=[
            pltpu.VMEM((blocks, tokens, tokens), f32),
            pltpu.VMEM((blocks, tokens, tokens), f32),
            pltpu.VMEM((blocks // 2, tokens, heads_here * tokens), bf16),
        ],
        compiler_params=PARAMS,
        cost_estimate=pl.CostEstimate(
            flops=work * (2 * blocks + 4), bytes_accessed=2**20, transcendentals=0),
        name="scores",
    )(ctx.reshape(1), doc_lengths, queries, d_out, own, two, four, odd)
    odd_back = exchanged(odd_terms, "ctx", 1)
    even_terms = pl.pallas_call(
        even_body,
        out_shape=(jax.ShapeDtypeStruct((tokens, 2 * width), f32),) * (REACH // 2),
        in_specs=[VMEM] * 4,
        out_specs=(VMEM,) * (REACH // 2),
        compiler_params=PARAMS,
        cost_estimate=pl.CostEstimate(
            flops=work * REACH, bytes_accessed=2**20, transcendentals=0),
        name="even_terms",
    )(ds, p, queries, d_out)
    near, far = odd_back[:tokens].astype(f32), odd_back[tokens:].astype(f32)
    four_back = shifted(
        (even_terms[1] + jnp.where(second_core, far, 0.0)).astype(bf16), -4)
    two_back = shifted(
        (even_terms[0] + jnp.where(second_core, near, far)).astype(bf16), -2)
    d_queries, own_terms = pl.pallas_call(
        own_body,
        out_shape=(
            jax.ShapeDtypeStruct(queries.shape, bf16),
            jax.ShapeDtypeStruct((tokens, 2 * width), f32),
        ),
        in_specs=[VMEM] * 8,
        out_specs=(VMEM, VMEM),
        compiler_params=PARAMS,
        cost_estimate=pl.CostEstimate(
            flops=work * (blocks + 2), bytes_accessed=2**20, transcendentals=0),
        name="own_terms",
    )(ds, p, queries, d_out, own, two, four, odd)
    sums = (own_terms + jnp.where(second_core, 0.0, near)
            + two_back.astype(f32) + four_back.astype(f32))

    sums = sums.reshape(groups, share, tokens // head_count, 2 * width)
    mine = head % share
    kept = lax.dynamic_index_in_dim(sums, mine, 1, keepdims=False)
    given = lax.dynamic_index_in_dim(sums, 1 - mine, 1, keepdims=False)
    kept = kept + exchanged(given.astype(bf16), "head", 1).astype(f32)
    kept = kept.astype(bf16)
    if groups == 2:
        at = head // share
        here = lax.dynamic_index_in_dim(kept, at, 0, keepdims=False)
        there = exchanged(
            lax.dynamic_index_in_dim(kept, 1 - at, 0, keepdims=False), "head", share)
        first = jnp.where(at == 0, here, there)
        second = jnp.where(at == 0, there, here)
        result = jnp.stack([first, second])
    else:
        result = lax.all_to_all(
            kept, "head", 0, 0, tiled=True,
            axis_index_groups=[list(range(u, head_count, share)) for u in range(share)])
    return d_queries, result[..., :width], result[..., width:]


def solution(mesh):
    placed = (
        P("head", "ctx", None),
        P(None, "ctx", None),
        P(None, "ctx", None),
        P("head", "ctx", None),
        P(),
    )
    return jax.shard_map(
        per_device,
        mesh=mesh,
        in_specs=placed,
        out_specs=(
            P("head", "ctx", None),
            P(None, ("ctx", "head"), None),
            P(None, ("ctx", "head"), None),
        ),
        check_vma=False,
    )
```

```python
import functools
import math

import jax
import jax.numpy as jnp
from jax import lax
from jax.experimental import pallas as pl
from jax.experimental.pallas import tpu as pltpu
from jax.sharding import PartitionSpec as P

GROUP = 8
REACH = 4
MASKED = -1e30
NT = (((1,), (1,)), ((), ()))
NN = (((1,), (0,)), ((), ()))
VMEM = pl.BlockSpec(memory_space=pltpu.VMEM)
SMEM = pl.BlockSpec(memory_space=pltpu.SMEM)
bf16, f32, i32 = jnp.bfloat16, jnp.float32, jnp.int32


def dot(a, b, dims):
    return lax.dot_general(a, b, dims, preferred_element_type=f32)


def shape(dims, dtype):
    return jax.ShapeDtypeStruct(dims, dtype)


def call(body, name, in_specs, outs, flops, scratch=()):
    return pl.pallas_call(
        body,
        out_shape=outs,
        in_specs=in_specs,
        out_specs=(VMEM,) * len(outs),
        scratch_shapes=scratch,
        compiler_params=pltpu.CompilerParams(vmem_limit_bytes=20 * 2**20),
        cost_estimate=pl.CostEstimate(
            flops=flops // 100, bytes_accessed=2**10, transcendentals=0),
        name=name,
    )


def shifted(block, distance):
    count = lax.axis_size("ctx")
    route = [(i - distance, i) for i in range(count) if 0 <= i - distance < count]
    return lax.ppermute(block, "ctx", route)


def exchanged(block, axis, mask):
    return lax.ppermute(block, axis, [(i, i ^ mask) for i in range(lax.axis_size(axis))])


def part(pairs, offsets, doc_start, q_ref, g_ref, e_refs, dp_refs, s_ref):
    heads, tokens, width = q_ref.shape
    here = lax.axis_index("ctx")
    factor = width ** -0.5 * math.log2(math.e)
    key_iota = lax.broadcasted_iota(i32, (tokens, 1), 0)
    row_pos = here * tokens + lax.broadcasted_iota(i32, (1, tokens), 1)
    stats = []
    for h in range(heads):
        lanes = slice(h * tokens, (h + 1) * tokens)
        top = jnp.full((1, tokens), MASKED, f32)
        for at, (pair, back) in enumerate(zip(pairs, offsets)):
            s = dot(pair[:, :width], q_ref[h], NT)
            key_pos = (here - back) * tokens + key_iota
            allowed = key_pos >= doc_start
            if isinstance(back, int) and back == 0:
                allowed = allowed & (key_pos <= row_pos)
            s = jnp.where(allowed, s, MASKED)
            s_ref[at] = s
            top = jnp.maximum(top, jnp.max(s, axis=0, keepdims=True))
        total = jnp.zeros((1, tokens), f32)
        weighted = jnp.zeros((1, tokens), f32)
        for at, pair in enumerate(pairs):
            e = jnp.exp2((s_ref[at] - top) * factor)
            dp = dot(pair[:, width:], g_ref[h], NT)
            e_refs[at][:, lanes] = e
            dp_refs[at][:, lanes] = dp
            total = total + jnp.sum(e, axis=0, keepdims=True)
            weighted = weighted + jnp.sum(e * dp, axis=0, keepdims=True)
        stats.append((top, total, weighted))
    return stats


def write_stats(stats, stats_ref):
    tokens = stats[0][0].shape[1]
    for h, values in enumerate(stats):
        for row, value in enumerate(values):
            stats_ref[row:row + 1, h * tokens:(h + 1) * tokens] = value


def own_part_body(lengths_ref, q_in, g_in, own_ref,
                  q_ref, g_ref, start_ref, e_ref, dp_ref, stats_ref, s_ref):
    tokens = q_in.shape[1]
    q_ref[...] = q_in[...]
    g_ref[...] = g_in[...]
    row_pos = lax.axis_index("ctx") * tokens + lax.broadcasted_iota(i32, (1, tokens), 1)
    doc_start = jnp.zeros((1, tokens), i32)
    end = jnp.int32(0)
    for d in range(lengths_ref.shape[0]):
        end = end + lengths_ref[d]
        doc_start = jnp.where(row_pos >= end, end, doc_start)
    start_ref[...] = doc_start
    stats = part([own_ref], [0], doc_start, q_in, g_in, [e_ref], [dp_ref], s_ref)
    write_stats(stats, stats_ref)


def block_part_body(back, start_ref, q_ref, g_ref, pair_ref, e_ref, dp_ref, stats_ref, s_ref):
    stats = part([pair_ref], [back], start_ref[...], q_ref, g_ref, [e_ref], [dp_ref], s_ref)
    write_stats(stats, stats_ref)


def odd_terms_body(start_ref, q_ref, g_ref, odd_ref, stats_own, stats_two, stats_four,
                   terms_ref, coef_ref, ds_one, ds_three, e_ref, dp_ref, s_ref, p_ref):
    heads, tokens, width = q_ref.shape
    factor = width ** -0.5 * math.log2(math.e)
    pairs = [odd_ref.at[:tokens], odd_ref.at[tokens:]]
    slopes = [ds_one, ds_three]
    stats = part(pairs, [1, 3], start_ref[...], q_ref, g_ref,
                 [e_ref.at[0], e_ref.at[1]], [dp_ref.at[0], dp_ref.at[1]], s_ref)
    for h, odd in enumerate(stats):
        lanes = slice(h * tokens, (h + 1) * tokens)
        parts = [[ref[row:row + 1, lanes] for row in range(3)]
                 for ref in (stats_own, stats_two, stats_four)] + [odd]
        top = functools.reduce(jnp.maximum, [each[0] for each in parts])
        gains = [jnp.exp2((each[0] - top) * factor) for each in parts]
        total = sum(gain * each[1] for gain, each in zip(gains, parts))
        inverse = 1.0 / total
        gains = [gain * inverse for gain in gains]
        delta = sum(gain * each[2] for gain, each in zip(gains, parts))
        for row, value in enumerate([delta] + gains[:3]):
            coef_ref[row:row + 1, lanes] = value
        for at, ds_ref in enumerate(slopes):
            p = e_ref[at, :, lanes] * gains[3]
            p_ref[at, :, lanes] = p.astype(bf16)
            ds_ref[:, lanes] = (p * (dp_ref[at, :, lanes] - delta)).astype(bf16)
    q_all = q_ref[...].reshape(heads * tokens, width)
    g_all = g_ref[...].reshape(heads * tokens, width)
    for at, ds_ref in enumerate(slopes):
        rows = slice(at * tokens, (at + 1) * tokens)
        terms_ref[rows, :width] = (dot(ds_ref[...], q_all, NN) * width ** -0.5).astype(bf16)
        terms_ref[rows, width:] = dot(p_ref[at], g_all, NN).astype(bf16)


def block_terms(e_ref, dp_ref, coef_ref, row, q_ref, g_ref, terms_ref, ds_ref, p_ref):
    heads, tokens, width = q_ref.shape
    for h in range(heads):
        lanes = slice(h * tokens, (h + 1) * tokens)
        p = e_ref[:, lanes] * coef_ref[row:row + 1, lanes]
        p_ref[:, lanes] = p.astype(bf16)
        ds_ref[:, lanes] = (p * (dp_ref[:, lanes] - coef_ref[:1, lanes])).astype(bf16)
    q_all = q_ref[...].reshape(heads * tokens, width)
    g_all = g_ref[...].reshape(heads * tokens, width)
    terms_ref[:, :width] = dot(ds_ref[...], q_all, NN) * width ** -0.5
    terms_ref[:, width:] = dot(p_ref[...], g_all, NN)


def even_terms_body(e_two, dp_two, e_four, dp_four, coef_ref, q_ref, g_ref,
                    two_terms, four_terms, ds_two, ds_four, p_ref):
    block_terms(e_two, dp_two, coef_ref, 2, q_ref, g_ref, two_terms, ds_two, p_ref.at[0])
    block_terms(e_four, dp_four, coef_ref, 3, q_ref, g_ref, four_terms, ds_four, p_ref.at[1])


def join_body(two_terms, four_terms, odd_back, two_ref, four_ref):
    tokens = two_terms.shape[0]
    second = lax.rem(lax.axis_index("ctx"), 2)
    rows = pl.ds(pl.multiple_of((1 - second) * tokens, tokens), tokens)
    two_ref[...] = (two_terms[...] + odd_back[rows].astype(f32)).astype(bf16)
    far = odd_back[tokens:].astype(f32) * second.astype(f32)
    four_ref[...] = (four_terms[...] + far).astype(bf16)


def own_terms_body(e_own, dp_own, coef_ref, q_ref, g_ref, own_ref, two_ref, four_ref, odd_ref,
                   ds_one, ds_two, ds_three, ds_four, dq_ref, terms_ref, ds_own, p_ref):
    heads, tokens, width = q_ref.shape
    block_terms(e_own, dp_own, coef_ref, 1, q_ref, g_ref, terms_ref, ds_own, p_ref)
    window = [own_ref, odd_ref.at[:tokens], two_ref, odd_ref.at[tokens:], four_ref]
    turned = [pair[:, :width].T for pair in window]
    slopes = [ds_own, ds_one, ds_two, ds_three, ds_four]
    for h in range(heads):
        lanes = slice(h * tokens, (h + 1) * tokens)
        dqt = sum(dot(kt, ds[:, lanes], NN) for kt, ds in zip(turned, slopes))
        dq_ref[h] = (dqt.T * width ** -0.5).astype(dq_ref.dtype)


def sums_body(direct, uses, own_terms, odd_back, *refs):
    backs, outs = refs[:len(uses)], refs[len(uses):]
    tokens = own_terms.shape[0]
    ctx = lax.axis_index("ctx")
    head = lax.axis_index("head")
    count = lax.axis_size("head")
    rows_each = tokens // count

    def total(rows):
        value = own_terms[rows] + odd_back[rows].astype(f32) * (1 - lax.rem(ctx, 2)).astype(f32)
        for back, use in zip(backs, uses):
            value = value + jnp.where(use(ctx), back[rows].astype(f32), 0.0)
        return value

    if not direct:
        outs[0][...] = total(slice(0, tokens)).astype(bf16)
        return
    for mask in range(count):
        place = jnp.bitwise_xor(head, mask)
        value = total(pl.ds(pl.multiple_of(place * rows_each, rows_each), rows_each))
        outs[mask][...] = value.astype(outs[mask].dtype)


def last_body(share, *refs):
    *parts, dk_ref, dv_ref = refs
    width = dk_ref.shape[-1]
    group = lax.axis_index("head") // share
    for other in range(len(parts) // share):
        mine = parts[other * share:(other + 1) * share]
        value = sum(ref[...].astype(f32) for ref in mine).astype(bf16)
        place = jnp.bitwise_xor(group, other)
        dk_ref[place] = value[:, :width]
        dv_ref[place] = value[:, width:]


def per_device(queries, keys, values, d_out, doc_lengths):
    heads, tokens, width = queries.shape
    head_count = lax.axis_size("head")
    share = GROUP // heads
    groups = head_count // share
    rows = heads * tokens
    work = rows * tokens * width * 2
    pair = (tokens, 2 * width)
    stats = shape((3, rows), f32)
    wide = shape((tokens, rows), f32)
    half = shape((tokens, rows), bf16)

    def tile(count):
        return (pltpu.VMEM((count, tokens, tokens), f32),)

    group = lax.axis_index("head") // share
    own = jnp.concatenate(
        [lax.dynamic_index_in_dim(keys, group, 0, keepdims=False),
         lax.dynamic_index_in_dim(values, group, 0, keepdims=False)], axis=1)
    ctx = lax.axis_index("ctx")
    second_core = ctx % 2 == 1
    mutual = lax.axis_size("ctx") == 2 * REACH
    four = exchanged(own, "ctx", 4) if mutual else shifted(own, 4)
    if mutual:
        two = (exchanged(own, "ctx", 2), exchanged(own, "ctx", 6))
    else:
        two = (shifted(own, 2),)
    q, g, start, e_own, dp_own, stats_own = call(
        own_part_body, "own_part", [SMEM] + [VMEM] * 3,
        (shape(queries.shape, bf16), shape(d_out.shape, bf16), shape((1, tokens), i32),
         wide, wide, stats),
        2 * work, tile(1))(doc_lengths, queries, d_out, own)
    four, start = lax.optimization_barrier((four, start))
    e_four, dp_four, stats_four = call(
        functools.partial(block_part_body, 4), "four_part", [VMEM] * 4, (wide, wide, stats),
        2 * work, tile(1))(start, q, g, four)
    *two, stats_four = lax.optimization_barrier((*two, stats_four))
    two = jnp.where(ctx & 2 == 2, *two) if mutual else two[0]
    odd = exchanged(
        jnp.concatenate([jnp.where(second_core, two, own), jnp.where(second_core, four, two)]),
        "ctx", 1)
    e_two, dp_two, stats_two = call(
        functools.partial(block_part_body, 2), "two_part", [VMEM] * 4, (wide, wide, stats),
        2 * work, tile(1))(start, q, g, two)
    odd_terms, coef, ds_one, ds_three = call(
        odd_terms_body, "odd_terms", [VMEM] * 7,
        (shape((2 * tokens, 2 * width), bf16), shape((4, rows), f32), half, half),
        6 * work,
        (pltpu.VMEM((2, tokens, rows), f32),) * 2 + tile(2)
        + (pltpu.VMEM((2, tokens, rows), bf16),),
    )(start, q, g, odd, stats_own, stats_two, stats_four)
    odd_back = exchanged(odd_terms, "ctx", 1)
    two_terms, four_terms, ds_two, ds_four = call(
        even_terms_body, "even_terms", [VMEM] * 7,
        (shape(pair, f32), shape(pair, f32), half, half), 4 * work,
        (pltpu.VMEM((2, tokens, rows), bf16),),
    )(e_two, dp_two, e_four, dp_four, coef, q, g)
    two_sum, four_sum = call(
        join_body, "join", [VMEM] * 3, (shape(pair, bf16),) * 2, 0,
    )(two_terms, four_terms, odd_back)
    if mutual:
        backs = [exchanged(four_sum, "ctx", 4), exchanged(two_sum, "ctx", 2),
                 exchanged(two_sum, "ctx", 6)]
        uses = [lambda i: i < 4, lambda i: i & 2 == 0, lambda i: i & 6 == 2]
    else:
        backs = [shifted(four_sum, -4), shifted(two_sum, -2)]
        uses = [lambda i: True] * 2
    d_queries, own_terms = call(
        own_terms_body, "own_terms", [VMEM] * 13,
        (shape(queries.shape, bf16), shape(pair, f32)), 7 * work,
        (pltpu.VMEM((tokens, rows), bf16),) * 2,
    )(e_own, dp_own, coef, q, g, own, two, four, odd, ds_one, ds_two, ds_three, ds_four)

    direct = head_count == 2 * share and share == 2
    slice_dims = (tokens // head_count, 2 * width)
    outs = ((shape(slice_dims, f32),) + (shape(slice_dims, bf16),) * (head_count - 1)
            if direct else (shape(pair, bf16),))
    sums = call(
        functools.partial(sums_body, direct, uses), "sums", [VMEM] * (2 + len(backs)), outs, 0,
    )(own_terms, odd_back, *backs)
    if direct:
        parts = [sums[0]] + [exchanged(sums[m], "head", m) for m in range(1, head_count)]
        result_dims = (groups, tokens // head_count, width)
        d_keys, d_values = call(
            functools.partial(last_body, share), "last", [VMEM] * head_count,
            (shape(result_dims, bf16),) * 2, 0)(*parts)
        return d_queries, d_keys, d_values
    slices = lax.all_to_all(sums[0].reshape(head_count, *slice_dims), "head", 0, 0)
    result = jnp.sum(slices.reshape(groups, share, *slice_dims).astype(f32), axis=1).astype(bf16)
    return d_queries, result[..., :width], result[..., width:]


def solution(mesh):
    placed = (
        P("head", "ctx", None),
        P(None, "ctx", None),
        P(None, "ctx", None),
        P("head", "ctx", None),
        P(),
    )
    return jax.shard_map(
        per_device,
        mesh=mesh,
        in_specs=placed,
        out_specs=(
            P("head", "ctx", None),
            P(None, ("ctx", "head"), None),
            P(None, ("ctx", "head"), None),
        ),
        check_vma=False,
    )
```

```python
import functools
import math

import jax
import jax.numpy as jnp
from jax import lax
from jax.experimental import pallas as pl
from jax.experimental.pallas import tpu as pltpu
from jax.sharding import PartitionSpec as P

GROUP = 8
REACH = 4
MASKED = -1e30
NT = (((1,), (1,)), ((), ()))
NN = (((1,), (0,)), ((), ()))
VMEM = pl.BlockSpec(memory_space=pltpu.VMEM)
SMEM = pl.BlockSpec(memory_space=pltpu.SMEM)
bf16, f32, i32 = jnp.bfloat16, jnp.float32, jnp.int32


def dot(a, b, dims):
    return lax.dot_general(a, b, dims, preferred_element_type=f32)


def shape(dims, dtype):
    return jax.ShapeDtypeStruct(dims, dtype)


def call(body, name, in_specs, outs, flops, scratch=()):
    return pl.pallas_call(
        body,
        out_shape=outs,
        in_specs=in_specs,
        out_specs=(VMEM,) * len(outs),
        scratch_shapes=scratch,
        compiler_params=pltpu.CompilerParams(vmem_limit_bytes=20 * 2**20),
        cost_estimate=pl.CostEstimate(
            flops=flops // 100, bytes_accessed=2**10, transcendentals=0),
        name=name,
    )


def shifted(block, distance):
    count = lax.axis_size("ctx")
    route = [(i - distance, i) for i in range(count) if 0 <= i - distance < count]
    return lax.ppermute(block, "ctx", route)


def exchanged(block, axis, mask):
    return lax.ppermute(block, axis, [(i, i ^ mask) for i in range(lax.axis_size(axis))])


def crossed(block):
    return lax.ppermute(block, "ctx", [(2, 4), (4, 2), (3, 5), (5, 3)])


def part(pairs, offsets, doc_start, q_ref, g_ref, e_refs, dp_refs, s_ref):
    heads, tokens, width = q_ref.shape
    here = lax.axis_index("ctx")
    factor = width ** -0.5 * math.log2(math.e)
    key_iota = lax.broadcasted_iota(i32, (tokens, 1), 0)
    row_pos = here * tokens + lax.broadcasted_iota(i32, (1, tokens), 1)
    stats = []
    for h in range(heads):
        lanes = slice(h * tokens, (h + 1) * tokens)
        top = jnp.full((1, tokens), MASKED, f32)
        for at, (pair, back) in enumerate(zip(pairs, offsets)):
            s = dot(pair[:, :width], q_ref[h], NT)
            key_pos = (here - back) * tokens + key_iota
            allowed = key_pos >= doc_start
            if isinstance(back, int) and back == 0:
                allowed = allowed & (key_pos <= row_pos)
            s = jnp.where(allowed, s, MASKED)
            s_ref[at] = s
            top = jnp.maximum(top, jnp.max(s, axis=0, keepdims=True))
        total = jnp.zeros((1, tokens), f32)
        weighted = jnp.zeros((1, tokens), f32)
        for at, pair in enumerate(pairs):
            e = jnp.exp2((s_ref[at] - top) * factor)
            dp = dot(pair[:, width:], g_ref[h], NT)
            e_refs[at][:, lanes] = e
            dp_refs[at][:, lanes] = dp
            total = total + jnp.sum(e, axis=0, keepdims=True)
            weighted = weighted + jnp.sum(e * dp, axis=0, keepdims=True)
        stats.append((top, total, weighted))
    return stats


def write_stats(stats, stats_ref):
    tokens = stats[0][0].shape[1]
    for h, values in enumerate(stats):
        for row, value in enumerate(values):
            stats_ref[row:row + 1, h * tokens:(h + 1) * tokens] = value


def own_part_body(lengths_ref, q_in, g_in, own_ref,
                  q_ref, g_ref, start_ref, e_ref, dp_ref, stats_ref, s_ref):
    tokens = q_in.shape[1]
    q_ref[...] = q_in[...]
    g_ref[...] = g_in[...]
    row_pos = lax.axis_index("ctx") * tokens + lax.broadcasted_iota(i32, (1, tokens), 1)
    doc_start = jnp.zeros((1, tokens), i32)
    end = jnp.int32(0)
    for d in range(lengths_ref.shape[0]):
        end = end + lengths_ref[d]
        doc_start = jnp.where(row_pos >= end, end, doc_start)
    start_ref[...] = doc_start
    stats = part([own_ref], [0], doc_start, q_in, g_in, [e_ref], [dp_ref], s_ref)
    write_stats(stats, stats_ref)


def block_part_body(back, start_ref, q_ref, g_ref, pair_ref, e_ref, dp_ref, stats_ref, s_ref):
    stats = part([pair_ref], [back], start_ref[...], q_ref, g_ref, [e_ref], [dp_ref], s_ref)
    write_stats(stats, stats_ref)


def odd_terms_body(start_ref, q_ref, g_ref, odd_ref, stats_own, stats_two, stats_four,
                   terms_ref, coef_ref, ds_one, ds_three, e_ref, dp_ref, s_ref, p_ref):
    heads, tokens, width = q_ref.shape
    factor = width ** -0.5 * math.log2(math.e)
    pairs = [odd_ref.at[:tokens], odd_ref.at[tokens:]]
    slopes = [ds_one, ds_three]
    stats = part(pairs, [1, 3], start_ref[...], q_ref, g_ref,
                 [e_ref.at[0], e_ref.at[1]], [dp_ref.at[0], dp_ref.at[1]], s_ref)
    for h, odd in enumerate(stats):
        lanes = slice(h * tokens, (h + 1) * tokens)
        parts = [[ref[row:row + 1, lanes] for row in range(3)]
                 for ref in (stats_own, stats_two, stats_four)] + [odd]
        top = functools.reduce(jnp.maximum, [each[0] for each in parts])
        gains = [jnp.exp2((each[0] - top) * factor) for each in parts]
        total = sum(gain * each[1] for gain, each in zip(gains, parts))
        inverse = 1.0 / total
        gains = [gain * inverse for gain in gains]
        delta = sum(gain * each[2] for gain, each in zip(gains, parts))
        for row, value in enumerate([delta] + gains[:3]):
            coef_ref[row:row + 1, lanes] = value
        for at, ds_ref in enumerate(slopes):
            p = e_ref[at, :, lanes] * gains[3]
            p_ref[at, :, lanes] = p.astype(bf16)
            ds_ref[:, lanes] = (p * (dp_ref[at, :, lanes] - delta)).astype(bf16)
    q_all = q_ref[...].reshape(heads * tokens, width)
    g_all = g_ref[...].reshape(heads * tokens, width)
    for at, ds_ref in enumerate(slopes):
        rows = slice(at * tokens, (at + 1) * tokens)
        terms_ref[rows, :width] = (dot(ds_ref[...], q_all, NN) * width ** -0.5).astype(bf16)
        terms_ref[rows, width:] = dot(p_ref[at], g_all, NN).astype(bf16)


def block_terms(e_ref, dp_ref, coef_ref, row, q_ref, g_ref, terms_ref, ds_ref, p_ref):
    heads, tokens, width = q_ref.shape
    for h in range(heads):
        lanes = slice(h * tokens, (h + 1) * tokens)
        p = e_ref[:, lanes] * coef_ref[row:row + 1, lanes]
        p_ref[:, lanes] = p.astype(bf16)
        ds_ref[:, lanes] = (p * (dp_ref[:, lanes] - coef_ref[:1, lanes])).astype(bf16)
    q_all = q_ref[...].reshape(heads * tokens, width)
    g_all = g_ref[...].reshape(heads * tokens, width)
    terms_ref[:, :width] = dot(ds_ref[...], q_all, NN) * width ** -0.5
    terms_ref[:, width:] = dot(p_ref[...], g_all, NN)


def even_terms_body(e_two, dp_two, e_four, dp_four, coef_ref, q_ref, g_ref,
                    two_terms, four_terms, ds_two, ds_four, p_ref):
    block_terms(e_two, dp_two, coef_ref, 2, q_ref, g_ref, two_terms, ds_two, p_ref.at[0])
    block_terms(e_four, dp_four, coef_ref, 3, q_ref, g_ref, four_terms, ds_four, p_ref.at[1])


def join_body(two_terms, four_terms, odd_back, two_ref, four_ref):
    tokens = two_terms.shape[0]
    second = lax.rem(lax.axis_index("ctx"), 2)
    rows = pl.ds(pl.multiple_of((1 - second) * tokens, tokens), tokens)
    two_ref[...] = (two_terms[...] + odd_back[rows].astype(f32)).astype(bf16)
    far = odd_back[tokens:].astype(f32) * second.astype(f32)
    four_ref[...] = (four_terms[...] + far).astype(bf16)


def own_terms_body(e_own, dp_own, coef_ref, q_ref, g_ref, own_ref, two_ref, four_ref, odd_ref,
                   ds_one, ds_two, ds_three, ds_four, dq_ref, terms_ref, ds_own, p_ref):
    heads, tokens, width = q_ref.shape
    block_terms(e_own, dp_own, coef_ref, 1, q_ref, g_ref, terms_ref, ds_own, p_ref)
    window = [own_ref, odd_ref.at[:tokens], two_ref, odd_ref.at[tokens:], four_ref]
    turned = [pair[:, :width].T for pair in window]
    slopes = [ds_own, ds_one, ds_two, ds_three, ds_four]
    for h in range(heads):
        lanes = slice(h * tokens, (h + 1) * tokens)
        dqt = sum(dot(kt, ds[:, lanes], NN) for kt, ds in zip(turned, slopes))
        dq_ref[h] = (dqt.T * width ** -0.5).astype(dq_ref.dtype)


def sums_body(direct, uses, own_terms, odd_back, *refs):
    backs, outs = refs[:len(uses)], refs[len(uses):]
    tokens = own_terms.shape[0]
    ctx = lax.axis_index("ctx")
    head = lax.axis_index("head")
    count = lax.axis_size("head")
    rows_each = tokens // count

    def total(rows):
        value = own_terms[rows] + odd_back[rows].astype(f32) * (1 - lax.rem(ctx, 2)).astype(f32)
        for back, use in zip(backs, uses):
            value = value + jnp.where(use(ctx), back[rows].astype(f32), 0.0)
        return value

    if not direct:
        outs[0][...] = total(slice(0, tokens)).astype(bf16)
        return
    for mask in range(count):
        place = jnp.bitwise_xor(head, mask)
        value = total(pl.ds(pl.multiple_of(place * rows_each, rows_each), rows_each))
        outs[mask][...] = value.astype(outs[mask].dtype)


def last_body(share, *refs):
    parts, (dk_ref, dv_ref) = refs[-3::-1], refs[-2:]
    width = dk_ref.shape[-1]
    group = lax.axis_index("head") // share
    for other in range(len(parts) // share):
        mine = parts[other * share:(other + 1) * share]
        value = sum(ref[...].astype(f32) for ref in mine).astype(bf16)
        place = jnp.bitwise_xor(group, other)
        dk_ref[place] = value[:, :width]
        dv_ref[place] = value[:, width:]


def per_device(queries, keys, values, d_out, doc_lengths):
    heads, tokens, width = queries.shape
    head_count = lax.axis_size("head")
    share = GROUP // heads
    groups = head_count // share
    rows = heads * tokens
    work = rows * tokens * width * 2
    pair = (tokens, 2 * width)
    stats = shape((3, rows), f32)
    wide = shape((tokens, rows), f32)
    half = shape((tokens, rows), bf16)

    def tile(count):
        return (pltpu.VMEM((count, tokens, tokens), f32),)

    group = lax.axis_index("head") // share
    own = jnp.concatenate(
        [lax.dynamic_index_in_dim(keys, group, 0, keepdims=False),
         lax.dynamic_index_in_dim(values, group, 0, keepdims=False)], axis=1)
    ctx = lax.axis_index("ctx")
    second_core = ctx % 2 == 1
    mutual = lax.axis_size("ctx") == 2 * REACH
    four = exchanged(own, "ctx", 4) if mutual else shifted(own, 4)
    if mutual:
        two = (exchanged(own, "ctx", 2), crossed(own))
    else:
        two = (shifted(own, 2),)
    q, g, start, e_own, dp_own, stats_own = call(
        own_part_body, "own_part", [SMEM] + [VMEM] * 3,
        (shape(queries.shape, bf16), shape(d_out.shape, bf16), shape((1, tokens), i32),
         wide, wide, stats),
        2 * work, tile(1))(doc_lengths, queries, d_out, own)
    four, start = lax.optimization_barrier((four, start))
    e_four, dp_four, stats_four = call(
        functools.partial(block_part_body, 4), "four_part", [VMEM] * 4, (wide, wide, stats),
        2 * work, tile(1))(start, q, g, four)
    *two, stats_four = lax.optimization_barrier((*two, stats_four))
    two = jnp.where(ctx & 2 == 2, *two) if mutual else two[0]
    odd = exchanged(
        jnp.concatenate([jnp.where(second_core, two, own), jnp.where(second_core, four, two)]),
        "ctx", 1)
    e_two, dp_two, stats_two = call(
        functools.partial(block_part_body, 2), "two_part", [VMEM] * 4, (wide, wide, stats),
        2 * work, tile(1))(start, q, g, two)
    odd_terms, coef, ds_one, ds_three = call(
        odd_terms_body, "odd_terms", [VMEM] * 7,
        (shape((2 * tokens, 2 * width), bf16), shape((4, rows), f32), half, half),
        6 * work,
        (pltpu.VMEM((2, tokens, rows), f32),) * 2 + tile(2)
        + (pltpu.VMEM((2, tokens, rows), bf16),),
    )(start, q, g, odd, stats_own, stats_two, stats_four)
    odd_back = exchanged(odd_terms, "ctx", 1)
    two_terms, four_terms, ds_two, ds_four = call(
        even_terms_body, "even_terms", [VMEM] * 7,
        (shape(pair, f32), shape(pair, f32), half, half), 4 * work,
        (pltpu.VMEM((2, tokens, rows), bf16),),
    )(e_two, dp_two, e_four, dp_four, coef, q, g)
    two_sum, four_sum = call(
        join_body, "join", [VMEM] * 3, (shape(pair, bf16),) * 2, 0,
    )(two_terms, four_terms, odd_back)
    if mutual:
        backs = [exchanged(four_sum, "ctx", 4), exchanged(two_sum, "ctx", 2),
                 crossed(two_sum)]
        uses = [lambda i: i < 4, lambda i: i & 2 == 0, lambda i: i & 6 == 2]
    else:
        backs = [shifted(four_sum, -4), shifted(two_sum, -2)]
        uses = [lambda i: True] * 2
    d_queries, own_terms = call(
        own_terms_body, "own_terms", [VMEM] * 13,
        (shape(queries.shape, bf16), shape(pair, f32)), 7 * work,
        (pltpu.VMEM((tokens, rows), bf16),) * 2,
    )(e_own, dp_own, coef, q, g, own, two, four, odd, ds_one, ds_two, ds_three, ds_four)

    direct = head_count == 2 * share and share == 2
    slice_dims = (tokens // head_count, 2 * width)
    outs = ((shape(slice_dims, f32),) + (shape(slice_dims, bf16),) * (head_count - 1)
            if direct else (shape(pair, bf16),))
    sums = call(
        functools.partial(sums_body, direct, uses), "sums", [VMEM] * (2 + len(backs)), outs, 0,
    )(own_terms, odd_back, *backs)
    if direct:
        parts = [exchanged(sums[m], "head", m) for m in reversed(range(1, head_count))]
        parts.append(sums[0])
        result_dims = (groups, tokens // head_count, width)
        d_keys, d_values = call(
            functools.partial(last_body, share), "last", [VMEM] * head_count,
            (shape(result_dims, bf16),) * 2, 0)(*parts)
        return d_queries, d_keys, d_values
    slices = lax.all_to_all(sums[0].reshape(head_count, *slice_dims), "head", 0, 0)
    result = jnp.sum(slices.reshape(groups, share, *slice_dims).astype(f32), axis=1).astype(bf16)
    return d_queries, result[..., :width], result[..., width:]


def solution(mesh):
    placed = (
        P("head", "ctx", None),
        P(None, "ctx", None),
        P(None, "ctx", None),
        P("head", "ctx", None),
        P(),
    )
    return jax.shard_map(
        per_device,
        mesh=mesh,
        in_specs=placed,
        out_specs=(
            P("head", "ctx", None),
            P(None, ("ctx", "head"), None),
            P(None, ("ctx", "head"), None),
        ),
        check_vma=False,
    )
```

```python
import functools
import math

import jax
import jax.numpy as jnp
from jax import lax
from jax.experimental import pallas as pl
from jax.experimental.pallas import tpu as pltpu
from jax.sharding import PartitionSpec as P

GROUP = 8
REACH = 4
MASKED = -1e30
NT = (((1,), (1,)), ((), ()))
NN = (((1,), (0,)), ((), ()))
VMEM = pl.BlockSpec(memory_space=pltpu.VMEM)
SMEM = pl.BlockSpec(memory_space=pltpu.SMEM)
bf16, f32, i32 = jnp.bfloat16, jnp.float32, jnp.int32


def dot(a, b, dims=NN):
    return lax.dot_general(a, b, dims, preferred_element_type=f32)


def shape(dims, dtype):
    return jax.ShapeDtypeStruct(dims, dtype)


def call(body, name, in_specs, outs, scratch=()):
    return pl.pallas_call(
        body,
        out_shape=outs,
        in_specs=in_specs,
        out_specs=(VMEM,) * len(outs),
        scratch_shapes=scratch,
        compiler_params=pltpu.CompilerParams(vmem_limit_bytes=20 * 2**20),
        cost_estimate=pl.CostEstimate(flops=2**20, bytes_accessed=2**10, transcendentals=0),
        name=name,
    )


def shifted(block, distance):
    count = lax.axis_size("ctx")
    route = [(i - distance, i) for i in range(count) if 0 <= i - distance < count]
    return lax.ppermute(block, "ctx", route)


def exchanged(block, axis, mask):
    return lax.ppermute(block, axis, [(i, i ^ mask) for i in range(lax.axis_size(axis))])


def second_core():
    return lax.rem(lax.axis_index("ctx"), 2) == 1


def doc_starts(lengths_ref, block, tokens):
    row_pos = block * tokens + lax.broadcasted_iota(i32, (1, tokens), 1)
    starts = jnp.zeros((1, tokens), i32)
    end = jnp.int32(0)
    for d in range(lengths_ref.shape[0]):
        end = end + lengths_ref[d]
        starts = jnp.where(row_pos >= end, end, starts)
    return starts


def unit(pair, key_block, starts, q_ref, g_ref, e_ref, dp_ref, stats_ref, causal=False):
    heads, tokens, width = q_ref.shape
    factor = width ** -0.5 * math.log2(math.e)
    key_iota = lax.broadcasted_iota(i32, (tokens, 1), 0)
    allowed = key_block * tokens + key_iota >= starts
    if causal:
        allowed = allowed & (key_iota <= lax.broadcasted_iota(i32, (1, tokens), 1))
    for h in range(heads):
        lanes = slice(h * tokens, (h + 1) * tokens)
        s = jnp.where(allowed, dot(pair[:, :width], q_ref[h], NT), MASKED)
        top = jnp.max(s, axis=0, keepdims=True)
        e = jnp.exp2((s - top) * factor)
        dp = dot(pair[:, width:], g_ref[h], NT)
        e_ref[:, lanes] = e
        dp_ref[:, lanes] = dp
        stats_ref[0:1, lanes] = top
        stats_ref[1:2, lanes] = jnp.sum(e, axis=0, keepdims=True)
        stats_ref[2:3, lanes] = jnp.sum(e * dp, axis=0, keepdims=True)


def rows_of(ref, first=0):
    return [ref[first + row:first + row + 1] for row in range(3)]


def joined(parts, factor):
    top = functools.reduce(jnp.maximum, [part[0] for part in parts])
    gains = [jnp.exp2((part[0] - top) * factor) for part in parts]
    total = sum(gain * part[1] for gain, part in zip(gains, parts))
    weighted = sum(gain * part[2] for gain, part in zip(gains, parts))
    return top, total, weighted


def own_unit_body(lengths_ref, q_in, g_in, own_ref,
                  q_ref, g_ref, starts_ref, e_ref, dp_ref, stats_ref):
    tokens = q_in.shape[1]
    here = lax.axis_index("ctx")
    starts = doc_starts(lengths_ref, here, tokens)
    starts_ref[0:1] = starts
    starts_ref[1:2] = doc_starts(lengths_ref, jnp.bitwise_xor(here, 1), tokens)
    q_ref[...] = q_in[...]
    g_ref[...] = g_in[...]
    unit(own_ref, here, starts, q_in, g_in, e_ref, dp_ref, stats_ref, causal=True)


def four_units_body(starts_ref, q_ref, g_ref, other_q, other_g, own_ref, four_ref,
                    e_four, dp_four, stats_four, e_side, dp_side, stats_side):
    here = lax.axis_index("ctx")
    unit(four_ref, here - 4, starts_ref[0:1], q_ref, g_ref, e_four, dp_four, stats_four)
    side = jnp.where(second_core(), four_ref[...], own_ref[...])
    unit(side, here - jnp.where(second_core(), 4, 0), starts_ref[1:2], other_q, other_g,
         e_side, dp_side, stats_side)


def two_units_body(starts_ref, q_ref, g_ref, other_q, other_g, two_ref,
                   stats_own, stats_four, stats_side,
                   e_two, dp_two, stats_two, e_cross, dp_cross, stats_cross, given_ref):
    here = lax.axis_index("ctx")
    factor = q_ref.shape[-1] ** -0.5 * math.log2(math.e)
    unit(two_ref, here - 2, starts_ref[0:1], q_ref, g_ref, e_two, dp_two, stats_two)
    unit(two_ref, here - 2, starts_ref[1:2], other_q, other_g, e_cross, dp_cross, stats_cross)
    mine = joined([rows_of(ref) for ref in (stats_own, stats_four, stats_two)], factor)
    others = joined([rows_of(ref) for ref in (stats_side, stats_cross)], factor)
    for row, value in enumerate(mine + others):
        given_ref[row:row + 1] = value
    given_ref[6:8] = jnp.zeros((2, given_ref.shape[1]), f32)


def slopes(e_ref, dp_ref, gain, delta, p_ref, ds_ref):
    p = e_ref[...] * gain
    p_ref[...] = p.astype(bf16)
    ds_ref[...] = (p * (dp_ref[...] - delta)).astype(bf16)


def flat(ref):
    heads, tokens, width = ref.shape
    return ref[...].reshape(heads * tokens, width)


def add_terms(sum_ref, ds_ref, p_ref, q_ref, g_ref, fresh):
    width = q_ref.shape[-1]
    dk = dot(ds_ref[...], flat(q_ref)) * width ** -0.5
    dv = dot(p_ref[...], flat(g_ref))
    if fresh:
        sum_ref[:, :width] = dk
        sum_ref[:, width:] = dv
    else:
        sum_ref[:, :width] += dk
        sum_ref[:, width:] += dv


def four_terms_body(given_ref, taken_ref, stats_own, stats_four, stats_two, stats_side,
                    stats_cross, e_four, dp_four, e_side, dp_side,
                    q_ref, g_ref, other_q, other_g,
                    coef_ref, terms_ref, ds_four, ds_side, p_side, p_four, sum_ref):
    factor = q_ref.shape[-1] ** -0.5 * math.log2(math.e)
    coefs = []
    for at, refs in ((0, (stats_own, stats_four, stats_two)), (3, (stats_side, stats_cross))):
        parts = [rows_of(given_ref, at), rows_of(taken_ref, 3 - at)]
        top, total, weighted = joined(parts, factor)
        inverse = 1.0 / total
        coefs.append(weighted * inverse)
        coefs.extend(jnp.exp2((ref[0:1] - top) * factor) * inverse for ref in refs)
    for row, value in enumerate(coefs):
        coef_ref[row:row + 1] = value
    slopes(e_four, dp_four, coefs[2], coefs[0], p_four, ds_four)
    slopes(e_side, dp_side, coefs[5], coefs[4], p_side, ds_side)
    add_terms(sum_ref, ds_four, p_four, q_ref, g_ref, True)

    @pl.when(second_core())
    def _():
        add_terms(sum_ref, ds_side, p_side, other_q, other_g, False)

    terms_ref[...] = sum_ref[...].astype(bf16)


def two_terms_body(coef_ref, e_two, dp_two, e_cross, dp_cross, q_ref, g_ref, other_q, other_g,
                   terms_ref, ds_two, ds_cross, p_ref, sum_ref):
    slopes(e_two, dp_two, coef_ref[3:4], coef_ref[0:1], p_ref.at[0], ds_two)
    slopes(e_cross, dp_cross, coef_ref[6:7], coef_ref[4:5], p_ref.at[1], ds_cross)
    add_terms(sum_ref, ds_two, p_ref.at[0], q_ref, g_ref, True)
    add_terms(sum_ref, ds_cross, p_ref.at[1], other_q, other_g, False)
    terms_ref[...] = sum_ref[...].astype(bf16)


def query_grads(keys, ds_refs, out_ref):
    heads, tokens, width = out_ref.shape
    turned = [key.T for key in keys]
    for h in range(heads):
        lanes = slice(h * tokens, (h + 1) * tokens)
        dqt = sum(dot(kt, ds[:, lanes]) for kt, ds in zip(turned, ds_refs))
        out_ref[h] = (dqt.T * width ** -0.5).astype(out_ref.dtype)


def own_terms_body(coef_ref, e_own, dp_own, q_ref, g_ref, other_q, other_g, ds_side, p_side,
                   own_ref, two_ref, four_ref, ds_two, ds_four, ds_cross,
                   terms_ref, dq_ref, other_dq_ref, ds_own, p_ref):
    width = q_ref.shape[-1]
    own, two, four = [ref[:, :width] for ref in (own_ref, two_ref, four_ref)]
    query_grads([jnp.where(second_core(), four, own), two], [ds_side, ds_cross], other_dq_ref)
    slopes(e_own, dp_own, coef_ref[1:2], coef_ref[0:1], p_ref, ds_own)
    add_terms(terms_ref, ds_own, p_ref, q_ref, g_ref, True)

    @pl.when(jnp.logical_not(second_core()))
    def _():
        add_terms(terms_ref, ds_side, p_side, other_q, other_g, False)

    query_grads([own, two, four], [ds_own, ds_two, ds_four], dq_ref)


def add_grads_body(mine_ref, taken_ref, dq_ref):
    dq_ref[...] = (mine_ref[...] + taken_ref[...].astype(f32)).astype(dq_ref.dtype)


def first_sum_body(use, own_terms, back, out_ref):
    taken = jnp.where(use(lax.axis_index("ctx")), back[...].astype(f32), 0.0)
    out_ref[...] = own_terms[...] + taken


def sums_body(direct, uses, own_terms, *refs):
    backs, outs = refs[:len(uses)], refs[len(uses):]
    tokens = own_terms.shape[0]
    ctx = lax.axis_index("ctx")
    head = lax.axis_index("head")
    count = lax.axis_size("head")
    rows_each = tokens // count

    def total(rows):
        value = own_terms[rows]
        for back, use in zip(backs, uses):
            value = value + jnp.where(use(ctx), back[rows].astype(f32), 0.0)
        return value

    if not direct:
        outs[0][...] = total(slice(0, tokens)).astype(bf16)
        return
    for mask in range(count):
        place = jnp.bitwise_xor(head, mask)
        value = total(pl.ds(pl.multiple_of(place * rows_each, rows_each), rows_each))
        outs[mask][...] = value.astype(outs[mask].dtype)


def last_body(share, *refs):
    parts, (dk_ref, dv_ref) = refs[-3::-1], refs[-2:]
    width = dk_ref.shape[-1]
    group = lax.axis_index("head") // share
    for other in range(len(parts) // share):
        mine = parts[other * share:(other + 1) * share]
        value = sum(ref[...].astype(f32) for ref in mine).astype(bf16)
        place = jnp.bitwise_xor(group, other)
        dk_ref[place] = value[:, :width]
        dv_ref[place] = value[:, width:]


def per_device(queries, keys, values, d_out, doc_lengths):
    heads, tokens, width = queries.shape
    head_count = lax.axis_size("head")
    share = GROUP // heads
    groups = head_count // share
    rows = heads * tokens
    ctx = lax.axis_index("ctx")
    mutual = lax.axis_size("ctx") == 2 * REACH
    pair = (tokens, 2 * width)
    all_rows = (heads, tokens, width)
    stats = shape((3, rows), f32)
    wide = shape((tokens, rows), f32)
    half = shape((tokens, rows), bf16)
    half_scratch = pltpu.VMEM((tokens, rows), bf16)
    pair_scratch = pltpu.VMEM(pair, f32)

    group = lax.axis_index("head") // share
    own = jnp.concatenate(
        [lax.dynamic_index_in_dim(keys, group, 0, keepdims=False),
         lax.dynamic_index_in_dim(values, group, 0, keepdims=False)], axis=1)
    four = exchanged(own, "ctx", 4) if mutual else shifted(own, 4)
    if mutual:
        two = (exchanged(own, "ctx", 6), exchanged(own, "ctx", 2))
    else:
        two = (shifted(own, 2),)
    q, g, starts, e_own, dp_own, stats_own = call(
        own_unit_body, "own_unit", [SMEM] + [VMEM] * 3,
        (shape(all_rows, bf16), shape(all_rows, bf16), shape((2, tokens), i32),
         wide, wide, stats))(doc_lengths, queries, d_out, own)
    other_q = exchanged(queries, "ctx", 1)
    other_g = exchanged(d_out, "ctx", 1)
    four, starts = lax.optimization_barrier((four, starts))
    e_four, dp_four, stats_four, e_side, dp_side, stats_side = call(
        four_units_body, "four_units", [VMEM] * 7, (wide, wide, stats) * 2,
    )(starts, q, g, other_q, other_g, own, four)
    *two, stats_four = lax.optimization_barrier((*two, stats_four))
    two = jnp.where(ctx & 2 == 2, two[1], two[0]) if mutual else two[0]
    e_two, dp_two, stats_two, e_cross, dp_cross, stats_cross, given = call(
        two_units_body, "two_units", [VMEM] * 9,
        (wide, wide, stats) * 2 + (shape((8, rows), f32),),
    )(starts, q, g, other_q, other_g, two, stats_own, stats_four, stats_side)
    taken = exchanged(given, "ctx", 1)
    coef, four_terms, ds_four, ds_side, p_side = call(
        four_terms_body, "four_terms", [VMEM] * 15,
        (shape((8, rows), f32), shape(pair, bf16), half, half, half),
        (half_scratch, pair_scratch),
    )(given, taken, stats_own, stats_four, stats_two, stats_side, stats_cross,
      e_four, dp_four, e_side, dp_side, q, g, other_q, other_g)
    two_terms, ds_two, ds_cross = call(
        two_terms_body, "two_terms", [VMEM] * 9, (shape(pair, bf16), half, half),
        (pltpu.VMEM((2, tokens, rows), bf16), pair_scratch),
    )(coef, e_two, dp_two, e_cross, dp_cross, q, g, other_q, other_g)
    if mutual:
        backs = [exchanged(four_terms, "ctx", 4), exchanged(two_terms, "ctx", 6),
                 exchanged(two_terms, "ctx", 2)]
        uses = [lambda i: i < 4, lambda i: i & 6 == 2, lambda i: i & 2 == 0]
    else:
        backs = [shifted(four_terms, -4), shifted(two_terms, -2)]
        uses = [lambda i: True] * 2
    own_terms, my_grads, other_grads = call(
        own_terms_body, "own_terms", [VMEM] * 15,
        (shape(pair, f32), shape(all_rows, f32), shape(all_rows, bf16)),
        (half_scratch, half_scratch),
    )(coef, e_own, dp_own, q, g, other_q, other_g, ds_side, p_side, own, two, four,
      ds_two, ds_four, ds_cross)
    own_terms, = call(
        functools.partial(first_sum_body, uses[0]), "first_sum", [VMEM] * 2,
        (shape(pair, f32),))(own_terms, backs[0])
    direct = head_count == 2 * share and share == 2
    slice_dims = (tokens // head_count, 2 * width)
    outs = ((shape(slice_dims, f32),) + (shape(slice_dims, bf16),) * (head_count - 1)
            if direct else (shape(pair, bf16),))
    sums = call(
        functools.partial(sums_body, direct, uses[1:]), "sums", [VMEM] * len(backs), outs,
    )(own_terms, *backs[1:])
    other_grads, kept = lax.optimization_barrier((other_grads, sums[0]))
    taken_grads = exchanged(other_grads, "ctx", 1)
    d_queries, = call(
        add_grads_body, "add_grads", [VMEM] * 2, (shape(all_rows, bf16),),
    )(my_grads, taken_grads)
    if direct:
        parts = [exchanged(sums[m], "head", m) for m in reversed(range(1, head_count))]
        parts.append(kept)
        *parts, d_queries = lax.optimization_barrier((*parts, d_queries))
        result_dims = (groups, tokens // head_count, width)
        d_keys, d_values = call(
            functools.partial(last_body, share), "last", [VMEM] * head_count,
            (shape(result_dims, bf16),) * 2)(*parts)
        return d_queries, d_keys, d_values
    slices = lax.all_to_all(kept.reshape(head_count, *slice_dims), "head", 0, 0)
    result = jnp.sum(slices.reshape(groups, share, *slice_dims).astype(f32), axis=1).astype(bf16)
    return d_queries, result[..., :width], result[..., width:]


def solution(mesh):
    placed = (
        P("head", "ctx", None),
        P(None, "ctx", None),
        P(None, "ctx", None),
        P("head", "ctx", None),
        P(),
    )
    return jax.shard_map(
        per_device,
        mesh=mesh,
        in_specs=placed,
        out_specs=(
            P("head", "ctx", None),
            P(None, ("ctx", "head"), None),
            P(None, ("ctx", "head"), None),
        ),
        check_vma=False,
    )
```

```python
import functools
import math

import jax
import jax.numpy as jnp
from jax import lax
from jax.experimental import pallas as pl
from jax.experimental.pallas import tpu as pltpu
from jax.sharding import PartitionSpec as P

GROUP = 8
REACH = 4
MASKED = -1e30
NT = (((1,), (1,)), ((), ()))
NN = (((1,), (0,)), ((), ()))
VMEM = pl.BlockSpec(memory_space=pltpu.VMEM)
SMEM = pl.BlockSpec(memory_space=pltpu.SMEM)
bf16, f32, i32 = jnp.bfloat16, jnp.float32, jnp.int32


def dot(a, b, dims=NN):
    return lax.dot_general(a, b, dims, preferred_element_type=f32)


def shape(dims, dtype):
    return jax.ShapeDtypeStruct(dims, dtype)


def call(body, name, in_specs, outs, scratch=()):
    return pl.pallas_call(
        body,
        out_shape=outs,
        in_specs=in_specs,
        out_specs=(VMEM,) * len(outs),
        scratch_shapes=scratch,
        compiler_params=pltpu.CompilerParams(vmem_limit_bytes=20 * 2**20),
        cost_estimate=pl.CostEstimate(flops=2**20, bytes_accessed=2**10, transcendentals=0),
        name=name,
    )


def shifted(block, distance):
    count = lax.axis_size("ctx")
    route = [(i - distance, i) for i in range(count) if 0 <= i - distance < count]
    return lax.ppermute(block, "ctx", route)


def exchanged(block, axis, mask):
    return lax.ppermute(block, axis, [(i, i ^ mask) for i in range(lax.axis_size(axis))])


def second_core():
    return lax.rem(lax.axis_index("ctx"), 2) == 1


def doc_starts(lengths_ref, block, tokens):
    row_pos = block * tokens + lax.broadcasted_iota(i32, (1, tokens), 1)
    starts = jnp.zeros((1, tokens), i32)
    end = jnp.int32(0)
    for d in range(lengths_ref.shape[0]):
        end = end + lengths_ref[d]
        starts = jnp.where(row_pos >= end, end, starts)
    return starts


def unit(pair, key_block, starts, q_ref, g_ref, e_ref, dp_ref, stats_ref, causal=False):
    heads, tokens, width = q_ref.shape
    factor = width ** -0.5 * math.log2(math.e)
    key_iota = lax.broadcasted_iota(i32, (tokens, 1), 0)
    allowed = key_block * tokens + key_iota >= starts
    if causal:
        allowed = allowed & (key_iota <= lax.broadcasted_iota(i32, (1, tokens), 1))
    for h in range(heads):
        lanes = slice(h * tokens, (h + 1) * tokens)
        s = jnp.where(allowed, dot(pair[:, :width], q_ref[h], NT), MASKED)
        top = jnp.max(s, axis=0, keepdims=True)
        e = jnp.exp2((s - top) * factor)
        dp = dot(pair[:, width:], g_ref[h], NT)
        e_ref[:, lanes] = e
        dp_ref[:, lanes] = dp
        stats_ref[0:1, lanes] = top
        stats_ref[1:2, lanes] = jnp.sum(e, axis=0, keepdims=True)
        stats_ref[2:3, lanes] = jnp.sum(e * dp, axis=0, keepdims=True)


def rows_of(ref, first=0):
    return [ref[first + row:first + row + 1] for row in range(3)]


def joined(parts, factor):
    top = functools.reduce(jnp.maximum, [part[0] for part in parts])
    gains = [jnp.exp2((part[0] - top) * factor) for part in parts]
    total = sum(gain * part[1] for gain, part in zip(gains, parts))
    weighted = sum(gain * part[2] for gain, part in zip(gains, parts))
    return top, total, weighted


def own_unit_body(lengths_ref, q_in, g_in, own_ref,
                  q_ref, g_ref, starts_ref, e_ref, dp_ref, stats_ref):
    tokens = q_in.shape[1]
    here = lax.axis_index("ctx")
    starts = doc_starts(lengths_ref, here, tokens)
    starts_ref[0:1] = starts
    starts_ref[1:2] = doc_starts(lengths_ref, jnp.bitwise_xor(here, 1), tokens)
    q_ref[...] = q_in[...]
    g_ref[...] = g_in[...]
    unit(own_ref, here, starts, q_in, g_in, e_ref, dp_ref, stats_ref, causal=True)


def four_unit_body(starts_ref, q_ref, g_ref, four_ref, e_ref, dp_ref, stats_ref):
    here = lax.axis_index("ctx")
    unit(four_ref, here - 4, starts_ref[0:1], q_ref, g_ref, e_ref, dp_ref, stats_ref)


def side_unit_body(starts_ref, other_q, other_g, own_ref, four_ref, e_ref, dp_ref, stats_ref):
    side = jnp.where(second_core(), four_ref[...], own_ref[...])
    block = lax.axis_index("ctx") - jnp.where(second_core(), 4, 0)
    unit(side, block, starts_ref[1:2], other_q, other_g, e_ref, dp_ref, stats_ref)


def two_units_body(starts_ref, q_ref, g_ref, other_q, other_g, two_ref,
                   stats_own, stats_four, stats_side,
                   e_two, dp_two, stats_two, e_cross, dp_cross, stats_cross, given_ref):
    here = lax.axis_index("ctx")
    factor = q_ref.shape[-1] ** -0.5 * math.log2(math.e)
    unit(two_ref, here - 2, starts_ref[0:1], q_ref, g_ref, e_two, dp_two, stats_two)
    unit(two_ref, here - 2, starts_ref[1:2], other_q, other_g, e_cross, dp_cross, stats_cross)
    mine = joined([rows_of(ref) for ref in (stats_own, stats_four, stats_two)], factor)
    others = joined([rows_of(ref) for ref in (stats_side, stats_cross)], factor)
    for row, value in enumerate(mine + others):
        given_ref[row:row + 1] = value
    given_ref[6:8] = jnp.zeros((2, given_ref.shape[1]), f32)


def slopes(e_ref, dp_ref, gain, delta, p_ref, ds_ref):
    p = e_ref[...] * gain
    p_ref[...] = p.astype(bf16)
    ds_ref[...] = (p * (dp_ref[...] - delta)).astype(bf16)


def flat(ref):
    heads, tokens, width = ref.shape
    return ref[...].reshape(heads * tokens, width)


def add_terms(sum_ref, ds_ref, p_ref, q_ref, g_ref, fresh):
    width = q_ref.shape[-1]
    dk = dot(ds_ref[...], flat(q_ref)) * width ** -0.5
    dv = dot(p_ref[...], flat(g_ref))
    if fresh:
        sum_ref[:, :width] = dk
        sum_ref[:, width:] = dv
    else:
        sum_ref[:, :width] += dk
        sum_ref[:, width:] += dv


def four_terms_body(given_ref, taken_ref, stats_own, stats_four, stats_two, stats_side,
                    stats_cross, e_four, dp_four, e_side, dp_side,
                    q_ref, g_ref, other_q, other_g,
                    coef_ref, terms_ref, ds_four, ds_side, p_ref, sum_ref):
    factor = q_ref.shape[-1] ** -0.5 * math.log2(math.e)
    coefs = []
    for at, refs in ((0, (stats_own, stats_four, stats_two)), (3, (stats_side, stats_cross))):
        parts = [rows_of(given_ref, at), rows_of(taken_ref, 3 - at)]
        top, total, weighted = joined(parts, factor)
        inverse = 1.0 / total
        coefs.append(weighted * inverse)
        coefs.extend(jnp.exp2((ref[0:1] - top) * factor) * inverse for ref in refs)
    for row, value in enumerate(coefs):
        coef_ref[row:row + 1] = value
    slopes(e_four, dp_four, coefs[2], coefs[0], p_ref.at[0], ds_four)
    add_terms(sum_ref, ds_four, p_ref.at[0], q_ref, g_ref, True)

    @pl.when(second_core())
    def _():
        slopes(e_side, dp_side, coef_ref[5:6], coef_ref[4:5], p_ref.at[1], ds_side)
        add_terms(sum_ref, ds_side, p_ref.at[1], other_q, other_g, False)

    terms_ref[...] = sum_ref[...].astype(bf16)


def two_terms_body(coef_ref, e_two, dp_two, e_cross, dp_cross, q_ref, g_ref, other_q, other_g,
                   terms_ref, ds_two, ds_cross, p_ref, sum_ref):
    slopes(e_two, dp_two, coef_ref[3:4], coef_ref[0:1], p_ref.at[0], ds_two)
    slopes(e_cross, dp_cross, coef_ref[6:7], coef_ref[4:5], p_ref.at[1], ds_cross)
    add_terms(sum_ref, ds_two, p_ref.at[0], q_ref, g_ref, True)
    add_terms(sum_ref, ds_cross, p_ref.at[1], other_q, other_g, False)
    terms_ref[...] = sum_ref[...].astype(bf16)


def query_grads(keys, ds_refs, out_ref):
    heads, tokens, width = out_ref.shape
    turned = [key.T for key in keys]
    for h in range(heads):
        lanes = slice(h * tokens, (h + 1) * tokens)
        dqt = sum(dot(kt, ds[:, lanes]) for kt, ds in zip(turned, ds_refs))
        out_ref[h] = (dqt.T * width ** -0.5).astype(out_ref.dtype)


def own_terms_body(coef_ref, e_own, dp_own, e_side, dp_side, q_ref, g_ref, other_q, other_g,
                   own_ref, two_ref, four_ref, ds_two, ds_four, ds_cross,
                   terms_ref, dq_ref, other_dq_ref, ds_own, ds_side, p_ref, p_side):
    width = q_ref.shape[-1]
    own, two, four = [ref[:, :width] for ref in (own_ref, two_ref, four_ref)]
    slopes(e_side, dp_side, coef_ref[5:6], coef_ref[4:5], p_side, ds_side)
    query_grads([jnp.where(second_core(), four, own), two], [ds_side, ds_cross], other_dq_ref)
    slopes(e_own, dp_own, coef_ref[1:2], coef_ref[0:1], p_ref, ds_own)
    add_terms(terms_ref, ds_own, p_ref, q_ref, g_ref, True)

    @pl.when(jnp.logical_not(second_core()))
    def _():
        add_terms(terms_ref, ds_side, p_side, other_q, other_g, False)

    query_grads([own, two, four], [ds_own, ds_two, ds_four], dq_ref)


def add_grads_body(mine_ref, taken_ref, dq_ref):
    dq_ref[...] = (mine_ref[...] + taken_ref[...].astype(f32)).astype(dq_ref.dtype)


def first_sum_body(use, own_terms, back, out_ref):
    taken = jnp.where(use(lax.axis_index("ctx")), back[...].astype(f32), 0.0)
    out_ref[...] = own_terms[...] + taken


def sums_body(direct, uses, own_terms, *refs):
    backs, outs = refs[:len(uses)], refs[len(uses):]
    tokens = own_terms.shape[0]
    ctx = lax.axis_index("ctx")
    head = lax.axis_index("head")
    count = lax.axis_size("head")
    rows_each = tokens // count

    def total(rows):
        value = own_terms[rows]
        for back, use in zip(backs, uses):
            value = value + jnp.where(use(ctx), back[rows].astype(f32), 0.0)
        return value

    if not direct:
        outs[0][...] = total(slice(0, tokens)).astype(bf16)
        return
    for mask in range(count):
        place = jnp.bitwise_xor(head, mask)
        value = total(pl.ds(pl.multiple_of(place * rows_each, rows_each), rows_each))
        outs[mask][...] = value.astype(outs[mask].dtype)


def last_body(share, *refs):
    parts, (dk_ref, dv_ref) = refs[-3::-1], refs[-2:]
    width = dk_ref.shape[-1]
    group = lax.axis_index("head") // share
    for other in range(len(parts) // share):
        mine = parts[other * share:(other + 1) * share]
        value = sum(ref[...].astype(f32) for ref in mine).astype(bf16)
        place = jnp.bitwise_xor(group, other)
        dk_ref[place] = value[:, :width]
        dv_ref[place] = value[:, width:]


def per_device(queries, keys, values, d_out, doc_lengths):
    heads, tokens, width = queries.shape
    head_count = lax.axis_size("head")
    share = GROUP // heads
    groups = head_count // share
    rows = heads * tokens
    ctx = lax.axis_index("ctx")
    mutual = lax.axis_size("ctx") == 2 * REACH
    pair = (tokens, 2 * width)
    all_rows = (heads, tokens, width)
    stats = shape((3, rows), f32)
    wide = shape((tokens, rows), f32)
    half = shape((tokens, rows), bf16)
    half_scratch = pltpu.VMEM((tokens, rows), bf16)
    pair_scratch = pltpu.VMEM(pair, f32)

    group = lax.axis_index("head") // share
    own = jnp.concatenate(
        [lax.dynamic_index_in_dim(keys, group, 0, keepdims=False),
         lax.dynamic_index_in_dim(values, group, 0, keepdims=False)], axis=1)
    four = exchanged(own, "ctx", 4) if mutual else shifted(own, 4)
    if mutual:
        two = (exchanged(own, "ctx", 2), exchanged(own, "ctx", 6))
    else:
        two = (shifted(own, 2),)
    q, g, starts, e_own, dp_own, stats_own = call(
        own_unit_body, "own_unit", [SMEM] + [VMEM] * 3,
        (shape(all_rows, bf16), shape(all_rows, bf16), shape((2, tokens), i32),
         wide, wide, stats))(doc_lengths, queries, d_out, own)
    other_q = exchanged(queries, "ctx", 1)
    other_g = exchanged(d_out, "ctx", 1)
    four, starts = lax.optimization_barrier((four, starts))
    e_four, dp_four, stats_four = call(
        four_unit_body, "four_unit", [VMEM] * 4, (wide, wide, stats))(starts, q, g, four)
    other_q, stats_four = lax.optimization_barrier((other_q, stats_four))
    e_side, dp_side, stats_side = call(
        side_unit_body, "side_unit", [VMEM] * 5, (wide, wide, stats),
    )(starts, other_q, other_g, own, four)
    *two, stats_side = lax.optimization_barrier((*two, stats_side))
    two = jnp.where(ctx & 2 == 2, *two) if mutual else two[0]
    e_two, dp_two, stats_two, e_cross, dp_cross, stats_cross, given = call(
        two_units_body, "two_units", [VMEM] * 9,
        (wide, wide, stats) * 2 + (shape((8, rows), f32),),
    )(starts, q, g, other_q, other_g, two, stats_own, stats_four, stats_side)
    taken = exchanged(given, "ctx", 1)
    coef, four_terms, ds_four = call(
        four_terms_body, "four_terms", [VMEM] * 15,
        (shape((8, rows), f32), shape(pair, bf16), half),
        (half_scratch, pltpu.VMEM((2, tokens, rows), bf16), pair_scratch),
    )(given, taken, stats_own, stats_four, stats_two, stats_side, stats_cross,
      e_four, dp_four, e_side, dp_side, q, g, other_q, other_g)
    two_terms, ds_two, ds_cross = call(
        two_terms_body, "two_terms", [VMEM] * 9, (shape(pair, bf16), half, half),
        (pltpu.VMEM((2, tokens, rows), bf16), pair_scratch),
    )(coef, e_two, dp_two, e_cross, dp_cross, q, g, other_q, other_g)
    if mutual:
        backs = [exchanged(four_terms, "ctx", 4), exchanged(two_terms, "ctx", 2),
                 exchanged(two_terms, "ctx", 6)]
        uses = [lambda i: i < 4, lambda i: i & 2 == 0, lambda i: i & 6 == 2]
    else:
        backs = [shifted(four_terms, -4), shifted(two_terms, -2)]
        uses = [lambda i: True] * 2
    own_terms, my_grads, other_grads = call(
        own_terms_body, "own_terms", [VMEM] * 15,
        (shape(pair, f32), shape(all_rows, f32), shape(all_rows, bf16)),
        (half_scratch,) * 4,
    )(coef, e_own, dp_own, e_side, dp_side, q, g, other_q, other_g, own, two, four,
      ds_two, ds_four, ds_cross)
    own_terms, = call(
        functools.partial(first_sum_body, uses[0]), "first_sum", [VMEM] * 2,
        (shape(pair, f32),))(own_terms, backs[0])
    direct = head_count == 2 * share and share == 2
    slice_dims = (tokens // head_count, 2 * width)
    outs = ((shape(slice_dims, f32),) + (shape(slice_dims, bf16),) * (head_count - 1)
            if direct else (shape(pair, bf16),))
    sums = call(
        functools.partial(sums_body, direct, uses[1:]), "sums", [VMEM] * len(backs), outs,
    )(own_terms, *backs[1:])
    other_grads, kept = lax.optimization_barrier((other_grads, sums[0]))
    taken_grads = exchanged(other_grads, "ctx", 1)
    d_queries, = call(
        add_grads_body, "add_grads", [VMEM] * 2, (shape(all_rows, bf16),),
    )(my_grads, taken_grads)
    if direct:
        parts = [exchanged(sums[m], "head", m) for m in reversed(range(1, head_count))]
        parts.append(kept)
        *parts, d_queries = lax.optimization_barrier((*parts, d_queries))
        result_dims = (groups, tokens // head_count, width)
        d_keys, d_values = call(
            functools.partial(last_body, share), "last", [VMEM] * head_count,
            (shape(result_dims, bf16),) * 2)(*parts)
        return d_queries, d_keys, d_values
    slices = lax.all_to_all(kept.reshape(head_count, *slice_dims), "head", 0, 0)
    result = jnp.sum(slices.reshape(groups, share, *slice_dims).astype(f32), axis=1).astype(bf16)
    return d_queries, result[..., :width], result[..., width:]


def solution(mesh):
    placed = (
        P("head", "ctx", None),
        P(None, "ctx", None),
        P(None, "ctx", None),
        P("head", "ctx", None),
        P(),
    )
    return jax.shard_map(
        per_device,
        mesh=mesh,
        in_specs=placed,
        out_specs=(
            P("head", "ctx", None),
            P(None, ("ctx", "head"), None),
            P(None, ("ctx", "head"), None),
        ),
        check_vma=False,
    )
```

```python
import functools
import math

import jax
import jax.numpy as jnp
from jax import lax
from jax.experimental import pallas as pl
from jax.experimental.pallas import tpu as pltpu
from jax.sharding import PartitionSpec as P

GROUP = 8
REACH = 4
MASKED = -1e30
NT = (((1,), (1,)), ((), ()))
NN = (((1,), (0,)), ((), ()))
VMEM = pl.BlockSpec(memory_space=pltpu.VMEM)
SMEM = pl.BlockSpec(memory_space=pltpu.SMEM)
bf16, f32, i32 = jnp.bfloat16, jnp.float32, jnp.int32


def dot(a, b, dims=NN):
    return lax.dot_general(a, b, dims, preferred_element_type=f32)


def shape(dims, dtype):
    return jax.ShapeDtypeStruct(dims, dtype)


def call(body, name, in_specs, outs, scratch=()):
    return pl.pallas_call(
        body,
        out_shape=outs,
        in_specs=in_specs,
        out_specs=(VMEM,) * len(outs),
        scratch_shapes=scratch,
        compiler_params=pltpu.CompilerParams(vmem_limit_bytes=20 * 2**20),
        cost_estimate=pl.CostEstimate(flops=2**20, bytes_accessed=2**10, transcendentals=0),
        name=name,
    )


def shifted(block, distance):
    count = lax.axis_size("ctx")
    route = [(i - distance, i) for i in range(count) if 0 <= i - distance < count]
    return lax.ppermute(block, "ctx", route)


def exchanged(block, axis, mask):
    return lax.ppermute(block, axis, [(i, i ^ mask) for i in range(lax.axis_size(axis))])


def second_core():
    return lax.rem(lax.axis_index("ctx"), 2) == 1


def doc_starts(lengths_ref, block, tokens):
    row_pos = block * tokens + lax.broadcasted_iota(i32, (1, tokens), 1)
    starts = jnp.zeros((1, tokens), i32)
    end = jnp.int32(0)
    for d in range(lengths_ref.shape[0]):
        end = end + lengths_ref[d]
        starts = jnp.where(row_pos >= end, end, starts)
    return starts


def unit(pair, key_block, starts, q_ref, g_ref, e_ref, dp_ref, stats_ref, causal=False):
    heads, tokens, width = q_ref.shape
    factor = width ** -0.5 * math.log2(math.e)
    key_iota = lax.broadcasted_iota(i32, (tokens, 1), 0)
    allowed = key_block * tokens + key_iota >= starts
    if causal:
        allowed = allowed & (key_iota <= lax.broadcasted_iota(i32, (1, tokens), 1))
    for h in range(heads):
        lanes = slice(h * tokens, (h + 1) * tokens)
        s = jnp.where(allowed, dot(pair[:, :width], q_ref[h], NT), MASKED)
        top = jnp.max(s, axis=0, keepdims=True)
        e = jnp.exp2((s - top) * factor)
        dp = dot(pair[:, width:], g_ref[h], NT)
        e_ref[:, lanes] = e
        dp_ref[:, lanes] = dp
        stats_ref[0:1, lanes] = top
        stats_ref[1:2, lanes] = jnp.sum(e, axis=0, keepdims=True)
        stats_ref[2:3, lanes] = jnp.sum(e * dp, axis=0, keepdims=True)


def rows_of(ref, first=0):
    return [ref[first + row:first + row + 1] for row in range(3)]


def joined(parts, factor):
    top = functools.reduce(jnp.maximum, [part[0] for part in parts])
    gains = [jnp.exp2((part[0] - top) * factor) for part in parts]
    total = sum(gain * part[1] for gain, part in zip(gains, parts))
    weighted = sum(gain * part[2] for gain, part in zip(gains, parts))
    return top, total, weighted


def own_unit_body(lengths_ref, q_in, g_in, own_ref,
                  q_ref, g_ref, starts_ref, e_ref, dp_ref, stats_ref):
    tokens = q_in.shape[1]
    here = lax.axis_index("ctx")
    starts = doc_starts(lengths_ref, here, tokens)
    starts_ref[0:1] = starts
    starts_ref[1:2] = doc_starts(lengths_ref, jnp.bitwise_xor(here, 1), tokens)
    q_ref[...] = q_in[...]
    g_ref[...] = g_in[...]
    unit(own_ref, here, starts, q_in, g_in, e_ref, dp_ref, stats_ref, causal=True)


def four_unit_body(starts_ref, q_ref, g_ref, four_ref, e_ref, dp_ref, stats_ref):
    here = lax.axis_index("ctx")
    unit(four_ref, here - 4, starts_ref[0:1], q_ref, g_ref, e_ref, dp_ref, stats_ref)


def side_unit_body(starts_ref, other_q, other_g, own_ref, four_ref, e_ref, dp_ref, stats_ref):
    side = jnp.where(second_core(), four_ref[...], own_ref[...])
    block = lax.axis_index("ctx") - jnp.where(second_core(), 4, 0)
    unit(side, block, starts_ref[1:2], other_q, other_g, e_ref, dp_ref, stats_ref)


def two_units_body(starts_ref, q_ref, g_ref, other_q, other_g, two_ref,
                   stats_own, stats_four, stats_side,
                   e_two, dp_two, stats_two, e_cross, dp_cross, stats_cross, given_ref):
    here = lax.axis_index("ctx")
    factor = q_ref.shape[-1] ** -0.5 * math.log2(math.e)
    unit(two_ref, here - 2, starts_ref[0:1], q_ref, g_ref, e_two, dp_two, stats_two)
    unit(two_ref, here - 2, starts_ref[1:2], other_q, other_g, e_cross, dp_cross, stats_cross)
    mine = joined([rows_of(ref) for ref in (stats_own, stats_four, stats_two)], factor)
    others = joined([rows_of(ref) for ref in (stats_side, stats_cross)], factor)
    for row, value in enumerate(mine + others):
        given_ref[row:row + 1] = value
    given_ref[6:8] = jnp.zeros((2, given_ref.shape[1]), f32)


def slopes(e_ref, dp_ref, gain, delta, p_ref, ds_ref):
    p = e_ref[...] * gain
    p_ref[...] = p.astype(bf16)
    ds_ref[...] = (p * (dp_ref[...] - delta)).astype(bf16)


def flat(ref):
    heads, tokens, width = ref.shape
    return ref[...].reshape(heads * tokens, width)


def add_terms(sum_ref, ds_ref, p_ref, q_ref, g_ref, fresh):
    width = q_ref.shape[-1]
    dk = dot(ds_ref[...], flat(q_ref)) * width ** -0.5
    dv = dot(p_ref[...], flat(g_ref))
    if fresh:
        sum_ref[:, :width] = dk
        sum_ref[:, width:] = dv
    else:
        sum_ref[:, :width] += dk
        sum_ref[:, width:] += dv


def four_terms_body(given_ref, taken_ref, stats_own, stats_four, stats_two, stats_side,
                    stats_cross, e_four, dp_four, e_side, dp_side,
                    q_ref, g_ref, other_q, other_g,
                    coef_ref, terms_ref, ds_four, ds_side, p_ref, sum_ref):
    factor = q_ref.shape[-1] ** -0.5 * math.log2(math.e)
    coefs = []
    for at, refs in ((0, (stats_own, stats_four, stats_two)), (3, (stats_side, stats_cross))):
        parts = [rows_of(given_ref, at), rows_of(taken_ref, 3 - at)]
        top, total, weighted = joined(parts, factor)
        inverse = 1.0 / total
        coefs.append(weighted * inverse)
        coefs.extend(jnp.exp2((ref[0:1] - top) * factor) * inverse for ref in refs)
    for row, value in enumerate(coefs):
        coef_ref[row:row + 1] = value
    slopes(e_four, dp_four, coefs[2], coefs[0], p_ref.at[0], ds_four)
    add_terms(sum_ref, ds_four, p_ref.at[0], q_ref, g_ref, True)

    @pl.when(second_core())
    def _():
        slopes(e_side, dp_side, coef_ref[5:6], coef_ref[4:5], p_ref.at[1], ds_side)
        add_terms(sum_ref, ds_side, p_ref.at[1], other_q, other_g, False)

    terms_ref[...] = sum_ref[...].astype(bf16)


def two_terms_body(coef_ref, e_two, dp_two, e_cross, dp_cross, q_ref, g_ref, other_q, other_g,
                   terms_ref, ds_two, ds_cross, p_ref, sum_ref):
    slopes(e_two, dp_two, coef_ref[3:4], coef_ref[0:1], p_ref.at[0], ds_two)
    slopes(e_cross, dp_cross, coef_ref[6:7], coef_ref[4:5], p_ref.at[1], ds_cross)
    add_terms(sum_ref, ds_two, p_ref.at[0], q_ref, g_ref, True)
    add_terms(sum_ref, ds_cross, p_ref.at[1], other_q, other_g, False)
    terms_ref[...] = sum_ref[...].astype(bf16)


def query_grads(keys, ds_refs, out_ref):
    heads, tokens, width = out_ref.shape
    turned = [key.T for key in keys]
    for h in range(heads):
        lanes = slice(h * tokens, (h + 1) * tokens)
        dqt = sum(dot(kt, ds[:, lanes]) for kt, ds in zip(turned, ds_refs))
        out_ref[h] = (dqt.T * width ** -0.5).astype(out_ref.dtype)


def own_terms_body(coef_ref, e_own, dp_own, e_side, dp_side, q_ref, g_ref, other_q, other_g,
                   own_ref, two_ref, four_ref, ds_two, ds_four, ds_cross,
                   terms_ref, dq_ref, other_dq_ref, ds_own, ds_side, p_ref, p_side):
    width = q_ref.shape[-1]
    own, two, four = [ref[:, :width] for ref in (own_ref, two_ref, four_ref)]
    slopes(e_side, dp_side, coef_ref[5:6], coef_ref[4:5], p_side, ds_side)
    query_grads([jnp.where(second_core(), four, own), two], [ds_side, ds_cross], other_dq_ref)
    slopes(e_own, dp_own, coef_ref[1:2], coef_ref[0:1], p_ref, ds_own)
    add_terms(terms_ref, ds_own, p_ref, q_ref, g_ref, True)

    @pl.when(jnp.logical_not(second_core()))
    def _():
        add_terms(terms_ref, ds_side, p_side, other_q, other_g, False)

    query_grads([own, two, four], [ds_own, ds_two, ds_four], dq_ref)


def add_grads_body(mine_ref, taken_ref, dq_ref):
    dq_ref[...] = (mine_ref[...] + taken_ref[...].astype(f32)).astype(dq_ref.dtype)


def first_sum_body(use, own_terms, back, out_ref):
    taken = jnp.where(use(lax.axis_index("ctx")), back[...].astype(f32), 0.0)
    out_ref[...] = own_terms[...] + taken


def sums_body(direct, uses, own_terms, *refs):
    backs, outs = refs[:len(uses)], refs[len(uses):]
    tokens = own_terms.shape[0]
    ctx = lax.axis_index("ctx")
    head = lax.axis_index("head")
    count = lax.axis_size("head")
    rows_each = tokens // count

    def total(rows):
        value = own_terms[rows]
        for back, use in zip(backs, uses):
            value = value + jnp.where(use(ctx), back[rows].astype(f32), 0.0)
        return value

    if not direct:
        outs[0][...] = total(slice(0, tokens)).astype(bf16)
        return
    for mask in range(count):
        place = jnp.bitwise_xor(head, mask)
        value = total(pl.ds(pl.multiple_of(place * rows_each, rows_each), rows_each))
        outs[mask][...] = value.astype(outs[mask].dtype)


def last_body(share, *refs):
    parts, (dk_ref, dv_ref) = refs[-3::-1], refs[-2:]
    width = dk_ref.shape[-1]
    group = lax.axis_index("head") // share
    for other in range(len(parts) // share):
        mine = parts[other * share:(other + 1) * share]
        value = sum(ref[...].astype(f32) for ref in mine).astype(bf16)
        place = jnp.bitwise_xor(group, other)
        dk_ref[place] = value[:, :width]
        dv_ref[place] = value[:, width:]


def per_device(queries, keys, values, d_out, doc_lengths):
    heads, tokens, width = queries.shape
    head_count = lax.axis_size("head")
    share = GROUP // heads
    groups = head_count // share
    rows = heads * tokens
    ctx = lax.axis_index("ctx")
    mutual = lax.axis_size("ctx") == 2 * REACH
    pair = (tokens, 2 * width)
    all_rows = (heads, tokens, width)
    stats = shape((3, rows), f32)
    wide = shape((tokens, rows), f32)
    half = shape((tokens, rows), bf16)
    half_scratch = pltpu.VMEM((tokens, rows), bf16)
    pair_scratch = pltpu.VMEM(pair, f32)

    group = lax.axis_index("head") // share
    own = jnp.concatenate(
        [lax.dynamic_index_in_dim(keys, group, 0, keepdims=False),
         lax.dynamic_index_in_dim(values, group, 0, keepdims=False)], axis=1)
    four = exchanged(own, "ctx", 4) if mutual else shifted(own, 4)
    q, g, starts, e_own, dp_own, stats_own = call(
        own_unit_body, "own_unit", [SMEM] + [VMEM] * 3,
        (shape(all_rows, bf16), shape(all_rows, bf16), shape((2, tokens), i32),
         wide, wide, stats))(doc_lengths, queries, d_out, own)
    sent, stats_own = lax.optimization_barrier((own, stats_own))
    if mutual:
        two = (exchanged(sent, "ctx", 2), exchanged(sent, "ctx", 6))
    else:
        two = (shifted(sent, 2),)
    other_q = exchanged(queries, "ctx", 1)
    other_g = exchanged(d_out, "ctx", 1)
    four, starts = lax.optimization_barrier((four, starts))
    e_four, dp_four, stats_four = call(
        four_unit_body, "four_unit", [VMEM] * 4, (wide, wide, stats))(starts, q, g, four)
    other_q, stats_four = lax.optimization_barrier((other_q, stats_four))
    e_side, dp_side, stats_side = call(
        side_unit_body, "side_unit", [VMEM] * 5, (wide, wide, stats),
    )(starts, other_q, other_g, own, four)
    *two, stats_side = lax.optimization_barrier((*two, stats_side))
    two = jnp.where(ctx & 2 == 2, *two) if mutual else two[0]
    e_two, dp_two, stats_two, e_cross, dp_cross, stats_cross, given = call(
        two_units_body, "two_units", [VMEM] * 9,
        (wide, wide, stats) * 2 + (shape((8, rows), f32),),
    )(starts, q, g, other_q, other_g, two, stats_own, stats_four, stats_side)
    taken = exchanged(given, "ctx", 1)
    coef, four_terms, ds_four = call(
        four_terms_body, "four_terms", [VMEM] * 15,
        (shape((8, rows), f32), shape(pair, bf16), half),
        (half_scratch, pltpu.VMEM((2, tokens, rows), bf16), pair_scratch),
    )(given, taken, stats_own, stats_four, stats_two, stats_side, stats_cross,
      e_four, dp_four, e_side, dp_side, q, g, other_q, other_g)
    two_terms, ds_two, ds_cross = call(
        two_terms_body, "two_terms", [VMEM] * 9, (shape(pair, bf16), half, half),
        (pltpu.VMEM((2, tokens, rows), bf16), pair_scratch),
    )(coef, e_two, dp_two, e_cross, dp_cross, q, g, other_q, other_g)
    if mutual:
        backs = [exchanged(four_terms, "ctx", 4), exchanged(two_terms, "ctx", 2),
                 exchanged(two_terms, "ctx", 6)]
        uses = [lambda i: i < 4, lambda i: i & 2 == 0, lambda i: i & 6 == 2]
    else:
        backs = [shifted(four_terms, -4), shifted(two_terms, -2)]
        uses = [lambda i: True] * 2
    own_terms, my_grads, other_grads = call(
        own_terms_body, "own_terms", [VMEM] * 15,
        (shape(pair, f32), shape(all_rows, f32), shape(all_rows, bf16)),
        (half_scratch,) * 4,
    )(coef, e_own, dp_own, e_side, dp_side, q, g, other_q, other_g, own, two, four,
      ds_two, ds_four, ds_cross)
    own_terms, = call(
        functools.partial(first_sum_body, uses[0]), "first_sum", [VMEM] * 2,
        (shape(pair, f32),))(own_terms, backs[0])
    direct = head_count == 2 * share and share == 2
    slice_dims = (tokens // head_count, 2 * width)
    outs = ((shape(slice_dims, f32),) + (shape(slice_dims, bf16),) * (head_count - 1)
            if direct else (shape(pair, bf16),))
    sums = call(
        functools.partial(sums_body, direct, uses[1:]), "sums", [VMEM] * len(backs), outs,
    )(own_terms, *backs[1:])
    other_grads, kept = lax.optimization_barrier((other_grads, sums[0]))
    taken_grads = exchanged(other_grads, "ctx", 1)
    d_queries, = call(
        add_grads_body, "add_grads", [VMEM] * 2, (shape(all_rows, bf16),),
    )(my_grads, taken_grads)
    if direct:
        parts = [exchanged(sums[m], "head", m) for m in reversed(range(1, head_count))]
        parts.append(kept)
        *parts, d_queries = lax.optimization_barrier((*parts, d_queries))
        result_dims = (groups, tokens // head_count, width)
        d_keys, d_values = call(
            functools.partial(last_body, share), "last", [VMEM] * head_count,
            (shape(result_dims, bf16),) * 2)(*parts)
        return d_queries, d_keys, d_values
    slices = lax.all_to_all(kept.reshape(head_count, *slice_dims), "head", 0, 0)
    result = jnp.sum(slices.reshape(groups, share, *slice_dims).astype(f32), axis=1).astype(bf16)
    return d_queries, result[..., :width], result[..., width:]


def solution(mesh):
    placed = (
        P("head", "ctx", None),
        P(None, "ctx", None),
        P(None, "ctx", None),
        P("head", "ctx", None),
        P(),
    )
    return jax.shard_map(
        per_device,
        mesh=mesh,
        in_specs=placed,
        out_specs=(
            P("head", "ctx", None),
            P(None, ("ctx", "head"), None),
            P(None, ("ctx", "head"), None),
        ),
        check_vma=False,
    )
```

```python
import functools
import math

import jax
import jax.numpy as jnp
from jax import lax
from jax.experimental import pallas as pl
from jax.experimental.pallas import tpu as pltpu
from jax.sharding import PartitionSpec as P

GROUP = 8
REACH = 4
MASKED = -1e30
NT = (((1,), (1,)), ((), ()))
NN = (((1,), (0,)), ((), ()))
VMEM = pl.BlockSpec(memory_space=pltpu.VMEM)
SMEM = pl.BlockSpec(memory_space=pltpu.SMEM)
bf16, f32, i32 = jnp.bfloat16, jnp.float32, jnp.int32


def dot(a, b, dims=NN):
    return lax.dot_general(a, b, dims, preferred_element_type=f32)


def shape(dims, dtype):
    return jax.ShapeDtypeStruct(dims, dtype)


def call(body, name, in_specs, outs, scratch=()):
    return pl.pallas_call(
        body,
        out_shape=outs,
        in_specs=in_specs,
        out_specs=(VMEM,) * len(outs),
        scratch_shapes=scratch,
        compiler_params=pltpu.CompilerParams(vmem_limit_bytes=20 * 2**20),
        cost_estimate=pl.CostEstimate(flops=2**20, bytes_accessed=2**10, transcendentals=0),
        name=name,
    )


def shifted(block, distance):
    count = lax.axis_size("ctx")
    route = [(i - distance, i) for i in range(count) if 0 <= i - distance < count]
    return lax.ppermute(block, "ctx", route)


def exchanged(block, axis, mask):
    return lax.ppermute(block, axis, [(i, i ^ mask) for i in range(lax.axis_size(axis))])


def crossed(block):
    return lax.ppermute(block, "ctx", [(i, i ^ 6 if 2 <= i < 6 else i) for i in range(8)])


def second_core():
    return lax.rem(lax.axis_index("ctx"), 2) == 1


def doc_starts(lengths_ref, block, tokens):
    row_pos = block * tokens + lax.broadcasted_iota(i32, (1, tokens), 1)
    starts = jnp.zeros((1, tokens), i32)
    end = jnp.int32(0)
    for d in range(lengths_ref.shape[0]):
        end = end + lengths_ref[d]
        starts = jnp.where(row_pos >= end, end, starts)
    return starts


def unit(pair, key_block, starts, q_ref, g_ref, e_ref, dp_ref, stats_ref, causal=False):
    heads, tokens, width = q_ref.shape
    factor = width ** -0.5 * math.log2(math.e)
    key_iota = lax.broadcasted_iota(i32, (tokens, 1), 0)
    allowed = key_block * tokens + key_iota >= starts
    if causal:
        allowed = allowed & (key_iota <= lax.broadcasted_iota(i32, (1, tokens), 1))
    for h in range(heads):
        lanes = slice(h * tokens, (h + 1) * tokens)
        s = jnp.where(allowed, dot(pair[:, :width], q_ref[h], NT), MASKED)
        top = jnp.max(s, axis=0, keepdims=True)
        e = jnp.exp2((s - top) * factor)
        dp = dot(pair[:, width:], g_ref[h], NT)
        e_ref[:, lanes] = e
        dp_ref[:, lanes] = dp
        stats_ref[0:1, lanes] = top
        stats_ref[1:2, lanes] = jnp.sum(e, axis=0, keepdims=True)
        stats_ref[2:3, lanes] = jnp.sum(e * dp, axis=0, keepdims=True)


def rows_of(ref, first=0):
    return [ref[first + row:first + row + 1] for row in range(3)]


def joined(parts, factor):
    top = functools.reduce(jnp.maximum, [part[0] for part in parts])
    gains = [jnp.exp2((part[0] - top) * factor) for part in parts]
    total = sum(gain * part[1] for gain, part in zip(gains, parts))
    weighted = sum(gain * part[2] for gain, part in zip(gains, parts))
    return top, total, weighted


def own_unit_body(lengths_ref, q_in, g_in, own_ref,
                  q_ref, g_ref, starts_ref, e_ref, dp_ref, stats_ref):
    tokens = q_in.shape[1]
    here = lax.axis_index("ctx")
    starts = doc_starts(lengths_ref, here, tokens)
    starts_ref[0:1] = starts
    starts_ref[1:2] = doc_starts(lengths_ref, jnp.bitwise_xor(here, 1), tokens)
    q_ref[...] = q_in[...]
    g_ref[...] = g_in[...]
    unit(own_ref, here, starts, q_in, g_in, e_ref, dp_ref, stats_ref, causal=True)


def four_unit_body(starts_ref, q_ref, g_ref, four_ref, e_ref, dp_ref, stats_ref):
    here = lax.axis_index("ctx")
    unit(four_ref, here - 4, starts_ref[0:1], q_ref, g_ref, e_ref, dp_ref, stats_ref)


def side_unit_body(starts_ref, other_q, other_g, own_ref, four_ref, e_ref, dp_ref, stats_ref):
    side = jnp.where(second_core(), four_ref[...], own_ref[...])
    block = lax.axis_index("ctx") - jnp.where(second_core(), 4, 0)
    unit(side, block, starts_ref[1:2], other_q, other_g, e_ref, dp_ref, stats_ref)


def two_units_body(starts_ref, q_ref, g_ref, other_q, other_g, two_ref,
                   stats_own, stats_four, stats_side,
                   e_two, dp_two, stats_two, e_cross, dp_cross, stats_cross, given_ref):
    here = lax.axis_index("ctx")
    factor = q_ref.shape[-1] ** -0.5 * math.log2(math.e)
    unit(two_ref, here - 2, starts_ref[0:1], q_ref, g_ref, e_two, dp_two, stats_two)
    unit(two_ref, here - 2, starts_ref[1:2], other_q, other_g, e_cross, dp_cross, stats_cross)
    mine = joined([rows_of(ref) for ref in (stats_own, stats_four, stats_two)], factor)
    others = joined([rows_of(ref) for ref in (stats_side, stats_cross)], factor)
    for row, value in enumerate(mine + others):
        given_ref[row:row + 1] = value
    given_ref[6:8] = jnp.zeros((2, given_ref.shape[1]), f32)


def slopes(e_ref, dp_ref, gain, delta, p_ref, ds_ref):
    p = e_ref[...] * gain
    p_ref[...] = p.astype(bf16)
    ds_ref[...] = (p * (dp_ref[...] - delta)).astype(bf16)


def flat(ref):
    heads, tokens, width = ref.shape
    return ref[...].reshape(heads * tokens, width)


def add_terms(sum_ref, ds_ref, p_ref, q_ref, g_ref, fresh):
    width = q_ref.shape[-1]
    dk = dot(ds_ref[...], flat(q_ref)) * width ** -0.5
    dv = dot(p_ref[...], flat(g_ref))
    if fresh:
        sum_ref[:, :width] = dk
        sum_ref[:, width:] = dv
    else:
        sum_ref[:, :width] += dk
        sum_ref[:, width:] += dv


def four_terms_body(given_ref, taken_ref, stats_own, stats_four, stats_two, stats_side,
                    stats_cross, e_four, dp_four, e_side, dp_side,
                    q_ref, g_ref, other_q, other_g,
                    coef_ref, terms_ref, ds_four, ds_side, p_ref, sum_ref):
    factor = q_ref.shape[-1] ** -0.5 * math.log2(math.e)
    coefs = []
    for at, refs in ((0, (stats_own, stats_four, stats_two)), (3, (stats_side, stats_cross))):
        parts = [rows_of(given_ref, at), rows_of(taken_ref, 3 - at)]
        top, total, weighted = joined(parts, factor)
        inverse = 1.0 / total
        coefs.append(weighted * inverse)
        coefs.extend(jnp.exp2((ref[0:1] - top) * factor) * inverse for ref in refs)
    for row, value in enumerate(coefs):
        coef_ref[row:row + 1] = value
    slopes(e_four, dp_four, coefs[2], coefs[0], p_ref.at[0], ds_four)
    add_terms(sum_ref, ds_four, p_ref.at[0], q_ref, g_ref, True)

    @pl.when(second_core())
    def _():
        slopes(e_side, dp_side, coef_ref[5:6], coef_ref[4:5], p_ref.at[1], ds_side)
        add_terms(sum_ref, ds_side, p_ref.at[1], other_q, other_g, False)

    terms_ref[...] = sum_ref[...].astype(bf16)


def two_terms_body(coef_ref, e_two, dp_two, e_cross, dp_cross, q_ref, g_ref, other_q, other_g,
                   terms_ref, ds_two, ds_cross, p_ref, sum_ref):
    slopes(e_two, dp_two, coef_ref[3:4], coef_ref[0:1], p_ref.at[0], ds_two)
    slopes(e_cross, dp_cross, coef_ref[6:7], coef_ref[4:5], p_ref.at[1], ds_cross)
    add_terms(sum_ref, ds_two, p_ref.at[0], q_ref, g_ref, True)
    add_terms(sum_ref, ds_cross, p_ref.at[1], other_q, other_g, False)
    terms_ref[...] = sum_ref[...].astype(bf16)


def query_grads(keys, ds_refs, out_ref):
    heads, tokens, width = out_ref.shape
    turned = [key.T for key in keys]
    for h in range(heads):
        lanes = slice(h * tokens, (h + 1) * tokens)
        dqt = sum(dot(kt, ds[:, lanes]) for kt, ds in zip(turned, ds_refs))
        out_ref[h] = (dqt.T * width ** -0.5).astype(out_ref.dtype)


def own_terms_body(coef_ref, e_own, dp_own, e_side, dp_side, q_ref, g_ref, other_q, other_g,
                   own_ref, two_ref, four_ref, ds_two, ds_four, ds_cross,
                   terms_ref, dq_ref, other_dq_ref, ds_own, ds_side, p_ref, p_side):
    width = q_ref.shape[-1]
    own, two, four = [ref[:, :width] for ref in (own_ref, two_ref, four_ref)]
    slopes(e_side, dp_side, coef_ref[5:6], coef_ref[4:5], p_side, ds_side)
    query_grads([jnp.where(second_core(), four, own), two], [ds_side, ds_cross], other_dq_ref)
    slopes(e_own, dp_own, coef_ref[1:2], coef_ref[0:1], p_ref, ds_own)
    add_terms(terms_ref, ds_own, p_ref, q_ref, g_ref, True)

    @pl.when(jnp.logical_not(second_core()))
    def _():
        add_terms(terms_ref, ds_side, p_side, other_q, other_g, False)

    query_grads([own, two, four], [ds_own, ds_two, ds_four], dq_ref)


def add_grads_body(mine_ref, taken_ref, dq_ref):
    dq_ref[...] = (mine_ref[...] + taken_ref[...].astype(f32)).astype(dq_ref.dtype)


def first_sum_body(use, own_terms, back, out_ref):
    taken = jnp.where(use(lax.axis_index("ctx")), back[...].astype(f32), 0.0)
    out_ref[...] = own_terms[...] + taken


def sums_body(direct, uses, own_terms, *refs):
    backs, outs = refs[:len(uses)], refs[len(uses):]
    tokens = own_terms.shape[0]
    ctx = lax.axis_index("ctx")
    head = lax.axis_index("head")
    count = lax.axis_size("head")
    rows_each = tokens // count

    def total(rows):
        value = own_terms[rows]
        for back, use in zip(backs, uses):
            value = value + jnp.where(use(ctx), back[rows].astype(f32), 0.0)
        return value

    if not direct:
        outs[0][...] = total(slice(0, tokens)).astype(bf16)
        return
    for mask in range(count):
        place = jnp.bitwise_xor(head, mask)
        value = total(pl.ds(pl.multiple_of(place * rows_each, rows_each), rows_each))
        outs[mask][...] = value.astype(outs[mask].dtype)


def last_body(share, *refs):
    parts, (dk_ref, dv_ref) = refs[-3::-1], refs[-2:]
    width = dk_ref.shape[-1]
    group = lax.axis_index("head") // share
    for other in range(len(parts) // share):
        mine = parts[other * share:(other + 1) * share]
        value = sum(ref[...].astype(f32) for ref in mine).astype(bf16)
        place = jnp.bitwise_xor(group, other)
        dk_ref[place] = value[:, :width]
        dv_ref[place] = value[:, width:]


def per_device(queries, keys, values, d_out, doc_lengths):
    heads, tokens, width = queries.shape
    head_count = lax.axis_size("head")
    share = GROUP // heads
    groups = head_count // share
    rows = heads * tokens
    ctx = lax.axis_index("ctx")
    mutual = lax.axis_size("ctx") == 2 * REACH
    pair = (tokens, 2 * width)
    all_rows = (heads, tokens, width)
    stats = shape((3, rows), f32)
    wide = shape((tokens, rows), f32)
    half = shape((tokens, rows), bf16)
    half_scratch = pltpu.VMEM((tokens, rows), bf16)
    pair_scratch = pltpu.VMEM(pair, f32)

    group = lax.axis_index("head") // share
    own = jnp.concatenate(
        [lax.dynamic_index_in_dim(keys, group, 0, keepdims=False),
         lax.dynamic_index_in_dim(values, group, 0, keepdims=False)], axis=1)
    four = exchanged(own, "ctx", 4) if mutual else shifted(own, 4)
    if mutual:
        two = (exchanged(own, "ctx", 2), crossed(own))
    else:
        two = (shifted(own, 2),)
    q, g, starts, e_own, dp_own, stats_own = call(
        own_unit_body, "own_unit", [SMEM] + [VMEM] * 3,
        (shape(all_rows, bf16), shape(all_rows, bf16), shape((2, tokens), i32),
         wide, wide, stats))(doc_lengths, queries, d_out, own)
    other_q = exchanged(queries, "ctx", 1)
    other_g = exchanged(d_out, "ctx", 1)
    four, starts = lax.optimization_barrier((four, starts))
    e_four, dp_four, stats_four = call(
        four_unit_body, "four_unit", [VMEM] * 4, (wide, wide, stats))(starts, q, g, four)
    other_q, stats_four = lax.optimization_barrier((other_q, stats_four))
    e_side, dp_side, stats_side = call(
        side_unit_body, "side_unit", [VMEM] * 5, (wide, wide, stats),
    )(starts, other_q, other_g, own, four)
    *two, stats_side = lax.optimization_barrier((*two, stats_side))
    two = jnp.where(ctx & 2 == 2, *two) if mutual else two[0]
    e_two, dp_two, stats_two, e_cross, dp_cross, stats_cross, given = call(
        two_units_body, "two_units", [VMEM] * 9,
        (wide, wide, stats) * 2 + (shape((8, rows), f32),),
    )(starts, q, g, other_q, other_g, two, stats_own, stats_four, stats_side)
    taken = exchanged(given, "ctx", 1)
    coef, four_terms, ds_four = call(
        four_terms_body, "four_terms", [VMEM] * 15,
        (shape((8, rows), f32), shape(pair, bf16), half),
        (half_scratch, pltpu.VMEM((2, tokens, rows), bf16), pair_scratch),
    )(given, taken, stats_own, stats_four, stats_two, stats_side, stats_cross,
      e_four, dp_four, e_side, dp_side, q, g, other_q, other_g)
    two_terms, ds_two, ds_cross = call(
        two_terms_body, "two_terms", [VMEM] * 9, (shape(pair, bf16), half, half),
        (pltpu.VMEM((2, tokens, rows), bf16), pair_scratch),
    )(coef, e_two, dp_two, e_cross, dp_cross, q, g, other_q, other_g)
    if mutual:
        backs = [exchanged(four_terms, "ctx", 4), exchanged(two_terms, "ctx", 2),
                 crossed(two_terms)]
        uses = [lambda i: i < 4, lambda i: i & 2 == 0, lambda i: i & 6 == 2]
    else:
        backs = [shifted(four_terms, -4), shifted(two_terms, -2)]
        uses = [lambda i: True] * 2
    own_terms, my_grads, other_grads = call(
        own_terms_body, "own_terms", [VMEM] * 15,
        (shape(pair, f32), shape(all_rows, f32), shape(all_rows, bf16)),
        (half_scratch,) * 4,
    )(coef, e_own, dp_own, e_side, dp_side, q, g, other_q, other_g, own, two, four,
      ds_two, ds_four, ds_cross)
    own_terms, = call(
        functools.partial(first_sum_body, uses[0]), "first_sum", [VMEM] * 2,
        (shape(pair, f32),))(own_terms, backs[0])
    direct = head_count == 2 * share and share == 2
    slice_dims = (tokens // head_count, 2 * width)
    outs = ((shape(slice_dims, f32),) + (shape(slice_dims, bf16),) * (head_count - 1)
            if direct else (shape(pair, bf16),))
    sums = call(
        functools.partial(sums_body, direct, uses[1:]), "sums", [VMEM] * len(backs), outs,
    )(own_terms, *backs[1:])
    other_grads, kept = lax.optimization_barrier((other_grads, sums[0]))
    taken_grads = exchanged(other_grads, "ctx", 1)
    d_queries, = call(
        add_grads_body, "add_grads", [VMEM] * 2, (shape(all_rows, bf16),),
    )(my_grads, taken_grads)
    if direct:
        parts = [exchanged(sums[m], "head", m) for m in reversed(range(1, head_count))]
        parts.append(kept)
        *parts, d_queries = lax.optimization_barrier((*parts, d_queries))
        result_dims = (groups, tokens // head_count, width)
        d_keys, d_values = call(
            functools.partial(last_body, share), "last", [VMEM] * head_count,
            (shape(result_dims, bf16),) * 2)(*parts)
        return d_queries, d_keys, d_values
    slices = lax.all_to_all(kept.reshape(head_count, *slice_dims), "head", 0, 0)
    result = jnp.sum(slices.reshape(groups, share, *slice_dims).astype(f32), axis=1).astype(bf16)
    return d_queries, result[..., :width], result[..., width:]


def solution(mesh):
    placed = (
        P("head", "ctx", None),
        P(None, "ctx", None),
        P(None, "ctx", None),
        P("head", "ctx", None),
        P(),
    )
    return jax.shard_map(
        per_device,
        mesh=mesh,
        in_specs=placed,
        out_specs=(
            P("head", "ctx", None),
            P(None, ("ctx", "head"), None),
            P(None, ("ctx", "head"), None),
        ),
        check_vma=False,
    )
```

```python
import functools
import math

import jax
import jax.numpy as jnp
from jax import lax
from jax.experimental import pallas as pl
from jax.experimental.pallas import tpu as pltpu
from jax.sharding import PartitionSpec as P

GROUP = 8
REACH = 4
MASKED = -1e30
NT = (((1,), (1,)), ((), ()))
NN = (((1,), (0,)), ((), ()))
VMEM = pl.BlockSpec(memory_space=pltpu.VMEM)
SMEM = pl.BlockSpec(memory_space=pltpu.SMEM)
bf16, f32, i32 = jnp.bfloat16, jnp.float32, jnp.int32


def dot(a, b, dims=NN):
    return lax.dot_general(a, b, dims, preferred_element_type=f32)


def shape(dims, dtype):
    return jax.ShapeDtypeStruct(dims, dtype)


def call(body, name, in_specs, outs, scratch=()):
    return pl.pallas_call(
        body,
        out_shape=outs,
        in_specs=in_specs,
        out_specs=(VMEM,) * len(outs),
        scratch_shapes=scratch,
        compiler_params=pltpu.CompilerParams(vmem_limit_bytes=20 * 2**20),
        cost_estimate=pl.CostEstimate(flops=2**20, bytes_accessed=2**10, transcendentals=0),
        name=name,
    )


def shifted(block, distance):
    count = lax.axis_size("ctx")
    route = [(i - distance, i) for i in range(count) if 0 <= i - distance < count]
    return lax.ppermute(block, "ctx", route)


def exchanged(block, axis, mask):
    return lax.ppermute(block, axis, [(i, i ^ mask) for i in range(lax.axis_size(axis))])


def second_core():
    return lax.rem(lax.axis_index("ctx"), 2) == 1


def doc_starts(lengths_ref, block, tokens):
    row_pos = block * tokens + lax.broadcasted_iota(i32, (1, tokens), 1)
    starts = jnp.zeros((1, tokens), i32)
    end = jnp.int32(0)
    for d in range(lengths_ref.shape[0]):
        end = end + lengths_ref[d]
        starts = jnp.where(row_pos >= end, end, starts)
    return starts


def unit(pair, key_block, starts, q_ref, g_ref, e_ref, dp_ref, stats_ref, causal=False):
    heads, tokens, width = q_ref.shape
    factor = width ** -0.5 * math.log2(math.e)
    key_iota = lax.broadcasted_iota(i32, (tokens, 1), 0)
    allowed = key_block * tokens + key_iota >= starts
    if causal:
        allowed = allowed & (key_iota <= lax.broadcasted_iota(i32, (1, tokens), 1))
    for h in range(heads):
        lanes = slice(h * tokens, (h + 1) * tokens)
        s = jnp.where(allowed, dot(pair[:, :width], q_ref[h], NT), MASKED)
        top = jnp.max(s, axis=0, keepdims=True)
        e = jnp.exp2((s - top) * factor)
        dp = dot(pair[:, width:], g_ref[h], NT)
        e_ref[:, lanes] = e
        dp_ref[:, lanes] = dp
        stats_ref[0:1, lanes] = top
        stats_ref[1:2, lanes] = jnp.sum(e, axis=0, keepdims=True)
        stats_ref[2:3, lanes] = jnp.sum(e * dp, axis=0, keepdims=True)


def rows_of(ref, first=0):
    return [ref[first + row:first + row + 1] for row in range(3)]


def joined(parts, factor):
    top = functools.reduce(jnp.maximum, [part[0] for part in parts])
    gains = [jnp.exp2((part[0] - top) * factor) for part in parts]
    total = sum(gain * part[1] for gain, part in zip(gains, parts))
    weighted = sum(gain * part[2] for gain, part in zip(gains, parts))
    return top, total, weighted


def own_unit_body(lengths_ref, q_in, g_in, own_ref,
                  q_ref, g_ref, starts_ref, e_ref, dp_ref, stats_ref):
    tokens = q_in.shape[1]
    here = lax.axis_index("ctx")
    starts = doc_starts(lengths_ref, here, tokens)
    starts_ref[0:1] = starts
    starts_ref[1:2] = doc_starts(lengths_ref, jnp.bitwise_xor(here, 1), tokens)
    q_ref[...] = q_in[...]
    g_ref[...] = g_in[...]
    unit(own_ref, here, starts, q_in, g_in, e_ref, dp_ref, stats_ref, causal=True)


def four_unit_body(starts_ref, q_ref, g_ref, four_ref, e_ref, dp_ref, stats_ref):
    here = lax.axis_index("ctx")
    unit(four_ref, here - 4, starts_ref[0:1], q_ref, g_ref, e_ref, dp_ref, stats_ref)


def side_unit_body(starts_ref, other_q, other_g, own_ref, four_ref, e_ref, dp_ref, stats_ref):
    side = jnp.where(second_core(), four_ref[...], own_ref[...])
    block = lax.axis_index("ctx") - jnp.where(second_core(), 4, 0)
    unit(side, block, starts_ref[1:2], other_q, other_g, e_ref, dp_ref, stats_ref)


def near_side_unit_body(starts_ref, other_q, other_g, own_ref, e_ref, dp_ref, stats_ref):
    block = jnp.where(second_core(), -1, lax.axis_index("ctx"))
    unit(own_ref, block, starts_ref[1:2], other_q, other_g, e_ref, dp_ref, stats_ref)


def two_units_body(side_at, starts_ref, q_ref, g_ref, other_q, other_g, two_ref, *refs):
    earlier, refs = refs[:side_at + 1], refs[side_at + 1:]
    e_two, dp_two, stats_two, e_cross, dp_cross, stats_cross, given_ref = refs
    here = lax.axis_index("ctx")
    factor = q_ref.shape[-1] ** -0.5 * math.log2(math.e)
    unit(two_ref, here - 2, starts_ref[0:1], q_ref, g_ref, e_two, dp_two, stats_two)
    unit(two_ref, here - 2, starts_ref[1:2], other_q, other_g, e_cross, dp_cross, stats_cross)
    mine = joined([rows_of(ref) for ref in earlier[:side_at] + (stats_two,)], factor)
    others = joined([rows_of(ref) for ref in (earlier[side_at], stats_cross)], factor)
    for row, value in enumerate(mine + others):
        given_ref[row:row + 1] = value
    given_ref[6:8] = jnp.zeros((2, given_ref.shape[1]), f32)


def coefficients(given_ref, taken_ref, mine, others, width):
    factor = width ** -0.5 * math.log2(math.e)
    coefs = []
    for at, refs in ((0, mine), (3, others)):
        parts = [rows_of(given_ref, at), rows_of(taken_ref, 3 - at)]
        top, total, weighted = joined(parts, factor)
        inverse = 1.0 / total
        coefs.append(weighted * inverse)
        coefs.extend(jnp.exp2((ref[0:1] - top) * factor) * inverse for ref in refs)
    return coefs


def slopes(e_ref, dp_ref, gain, delta, p_ref, ds_ref):
    p = e_ref[...] * gain
    p_ref[...] = p.astype(bf16)
    ds_ref[...] = (p * (dp_ref[...] - delta)).astype(bf16)


def flat(ref):
    heads, tokens, width = ref.shape
    return ref[...].reshape(heads * tokens, width)


def add_terms(sum_ref, ds_ref, p_ref, q_ref, g_ref, fresh):
    width = q_ref.shape[-1]
    dk = dot(ds_ref[...], flat(q_ref)) * width ** -0.5
    dv = dot(p_ref[...], flat(g_ref))
    if fresh:
        sum_ref[:, :width] = dk
        sum_ref[:, width:] = dv
    else:
        sum_ref[:, :width] += dk
        sum_ref[:, width:] += dv


def four_terms_body(given_ref, taken_ref, stats_own, stats_four, stats_two, stats_side,
                    stats_cross, e_four, dp_four, e_side, dp_side,
                    q_ref, g_ref, other_q, other_g,
                    coef_ref, terms_ref, ds_four, ds_side, p_ref, sum_ref):
    coefs = coefficients(given_ref, taken_ref, (stats_own, stats_four, stats_two),
                         (stats_side, stats_cross), q_ref.shape[-1])
    for row, value in enumerate(coefs):
        coef_ref[row:row + 1] = value
    slopes(e_four, dp_four, coefs[2], coefs[0], p_ref.at[0], ds_four)
    add_terms(sum_ref, ds_four, p_ref.at[0], q_ref, g_ref, True)

    @pl.when(second_core())
    def _():
        slopes(e_side, dp_side, coef_ref[5:6], coef_ref[4:5], p_ref.at[1], ds_side)
        add_terms(sum_ref, ds_side, p_ref.at[1], other_q, other_g, False)

    terms_ref[...] = sum_ref[...].astype(bf16)


def two_terms_body(coef_ref, e_two, dp_two, e_cross, dp_cross, q_ref, g_ref, other_q, other_g,
                   terms_ref, ds_two, ds_cross, p_ref, sum_ref):
    slopes(e_two, dp_two, coef_ref[3:4], coef_ref[0:1], p_ref.at[0], ds_two)
    slopes(e_cross, dp_cross, coef_ref[6:7], coef_ref[4:5], p_ref.at[1], ds_cross)
    add_terms(sum_ref, ds_two, p_ref.at[0], q_ref, g_ref, True)
    add_terms(sum_ref, ds_cross, p_ref.at[1], other_q, other_g, False)
    terms_ref[...] = sum_ref[...].astype(bf16)


def near_two_terms_body(given_ref, taken_ref, stats_own, stats_two, stats_side, stats_cross,
                        e_two, dp_two, e_cross, dp_cross, q_ref, g_ref, other_q, other_g,
                        coef_ref, terms_ref, ds_two, ds_cross, p_ref, sum_ref):
    coefs = coefficients(given_ref, taken_ref, (stats_own, stats_two),
                         (stats_side, stats_cross), q_ref.shape[-1])
    coefs.insert(2, jnp.zeros_like(coefs[0]))
    for row, value in enumerate(coefs):
        coef_ref[row:row + 1] = value
    two_terms_body(coef_ref, e_two, dp_two, e_cross, dp_cross, q_ref, g_ref, other_q, other_g,
                   terms_ref, ds_two, ds_cross, p_ref, sum_ref)


def query_grads(keys, ds_refs, out_ref):
    heads, tokens, width = out_ref.shape
    turned = [key.T for key in keys]
    for h in range(heads):
        lanes = slice(h * tokens, (h + 1) * tokens)
        dqt = sum(dot(kt, ds[:, lanes]) for kt, ds in zip(turned, ds_refs))
        out_ref[h] = (dqt.T * width ** -0.5).astype(out_ref.dtype)


def own_terms_body(far, coef_ref, e_own, dp_own, e_side, dp_side, q_ref, g_ref, other_q, other_g,
                   own_ref, two_ref, ds_two, ds_cross, *refs):
    four_refs, refs = refs[:2 * far], refs[2 * far:]
    terms_ref, dq_ref, other_dq_ref, ds_own, ds_side, p_ref, p_side = refs
    width = q_ref.shape[-1]
    keys, slope_refs = [own_ref[:, :width], two_ref[:, :width]], [ds_own, ds_two]
    side = keys[0]
    if far:
        keys.append(four_refs[0][:, :width])
        slope_refs.append(four_refs[1])
        side = jnp.where(second_core(), keys[2], keys[0])
    slopes(e_side, dp_side, coef_ref[5:6], coef_ref[4:5], p_side, ds_side)
    query_grads([side, keys[1]], [ds_side, ds_cross], other_dq_ref)
    slopes(e_own, dp_own, coef_ref[1:2], coef_ref[0:1], p_ref, ds_own)
    add_terms(terms_ref, ds_own, p_ref, q_ref, g_ref, True)

    @pl.when(jnp.logical_not(second_core()))
    def _():
        add_terms(terms_ref, ds_side, p_side, other_q, other_g, False)

    query_grads(keys, slope_refs, dq_ref)


def add_grads_body(mine_ref, taken_ref, dq_ref):
    dq_ref[...] = (mine_ref[...] + taken_ref[...].astype(f32)).astype(dq_ref.dtype)


def first_sum_body(use, own_terms, back, out_ref):
    taken = jnp.where(use(lax.axis_index("ctx")), back[...].astype(f32), 0.0)
    out_ref[...] = own_terms[...] + taken


def sums_body(direct, uses, own_terms, *refs):
    backs, outs = refs[:len(uses)], refs[len(uses):]
    tokens = own_terms.shape[0]
    ctx = lax.axis_index("ctx")
    head = lax.axis_index("head")
    count = lax.axis_size("head")
    rows_each = tokens // count

    def total(rows):
        value = own_terms[rows]
        for back, use in zip(backs, uses):
            value = value + jnp.where(use(ctx), back[rows].astype(f32), 0.0)
        return value

    if not direct:
        outs[0][...] = total(slice(0, tokens)).astype(bf16)
        return
    for mask in range(count):
        place = jnp.bitwise_xor(head, mask)
        value = total(pl.ds(pl.multiple_of(place * rows_each, rows_each), rows_each))
        outs[mask][...] = value.astype(outs[mask].dtype)


def last_body(share, *refs):
    parts, (dk_ref, dv_ref) = refs[-3::-1], refs[-2:]
    width = dk_ref.shape[-1]
    group = lax.axis_index("head") // share
    for other in range(len(parts) // share):
        mine = parts[other * share:(other + 1) * share]
        value = sum(ref[...].astype(f32) for ref in mine).astype(bf16)
        place = jnp.bitwise_xor(group, other)
        dk_ref[place] = value[:, :width]
        dv_ref[place] = value[:, width:]


def per_device(queries, keys, values, d_out, doc_lengths):
    operands = (queries, keys, values, d_out, doc_lengths)
    ctx_count, tokens = lax.axis_size("ctx"), queries.shape[1]
    if ctx_count != 2 * REACH:
        return gradients(True, *operands)
    count = doc_lengths.shape[0]
    upto = jnp.arange(count)[:, None] >= jnp.arange(count)[None, :]
    doc_ends = jnp.sum(jnp.where(upto, doc_lengths[None, :], 0), axis=1)
    split = jnp.any(doc_ends == ctx_count // 2 * tokens)
    return lax.cond(split, functools.partial(gradients, False),
                    functools.partial(gradients, True), *operands)


def gradients(far, queries, keys, values, d_out, doc_lengths):
    heads, tokens, width = queries.shape
    head_count = lax.axis_size("head")
    share = GROUP // heads
    groups = head_count // share
    rows = heads * tokens
    ctx = lax.axis_index("ctx")
    mutual = lax.axis_size("ctx") == 2 * REACH
    pair = (tokens, 2 * width)
    all_rows = (heads, tokens, width)
    stats = shape((3, rows), f32)
    wide = shape((tokens, rows), f32)
    half = shape((tokens, rows), bf16)
    half_scratch = pltpu.VMEM((tokens, rows), bf16)
    halves_scratch = pltpu.VMEM((2, tokens, rows), bf16)
    pair_scratch = pltpu.VMEM(pair, f32)

    group = lax.axis_index("head") // share
    own = jnp.concatenate(
        [lax.dynamic_index_in_dim(keys, group, 0, keepdims=False),
         lax.dynamic_index_in_dim(values, group, 0, keepdims=False)], axis=1)
    if far:
        four = exchanged(own, "ctx", 4) if mutual else shifted(own, 4)
    two = [exchanged(own, "ctx", 2) if mutual else shifted(own, 2)]
    if far and mutual:
        two.append(exchanged(own, "ctx", 6))
    q, g, starts, e_own, dp_own, stats_own = call(
        own_unit_body, "own_unit", [SMEM] + [VMEM] * 3,
        (shape(all_rows, bf16), shape(all_rows, bf16), shape((2, tokens), i32),
         wide, wide, stats))(doc_lengths, queries, d_out, own)
    other_q = exchanged(queries, "ctx", 1)
    other_g = exchanged(d_out, "ctx", 1)
    if far:
        four, starts = lax.optimization_barrier((four, starts))
        e_four, dp_four, stats_four = call(
            four_unit_body, "four_unit", [VMEM] * 4, (wide, wide, stats))(starts, q, g, four)
        other_q, stats_four = lax.optimization_barrier((other_q, stats_four))
        e_side, dp_side, stats_side = call(
            side_unit_body, "side_unit", [VMEM] * 5, (wide, wide, stats),
        )(starts, other_q, other_g, own, four)
        earlier = (stats_own, stats_four, stats_side)
    else:
        e_side, dp_side, stats_side = call(
            near_side_unit_body, "side_unit", [VMEM] * 4, (wide, wide, stats),
        )(starts, other_q, other_g, own)
        earlier = (stats_own, stats_side)
    *two, stats_side = lax.optimization_barrier((*two, stats_side))
    two = jnp.where(ctx & 2 == 2, *two) if len(two) == 2 else two[0]
    e_two, dp_two, stats_two, e_cross, dp_cross, stats_cross, given = call(
        functools.partial(two_units_body, len(earlier) - 1), "two_units",
        [VMEM] * (6 + len(earlier)), (wide, wide, stats) * 2 + (shape((8, rows), f32),),
    )(starts, q, g, other_q, other_g, two, *earlier)
    taken = exchanged(given, "ctx", 1)
    all_stats = earlier[:-1] + (stats_two, stats_side, stats_cross)
    sides = (q, g, other_q, other_g)
    two_parts = (e_two, dp_two, e_cross, dp_cross)
    two_scratch = (halves_scratch, pair_scratch)
    coef_shape = shape((8, rows), f32)
    backs, uses = [], []
    if far:
        coef, four_terms, ds_four = call(
            four_terms_body, "four_terms", [VMEM] * 15, (coef_shape, shape(pair, bf16), half),
            (half_scratch,) + two_scratch,
        )(given, taken, *all_stats, e_four, dp_four, e_side, dp_side, *sides)
        two_terms, ds_two, ds_cross = call(
            two_terms_body, "two_terms", [VMEM] * 9, (shape(pair, bf16), half, half), two_scratch,
        )(coef, *two_parts, *sides)
        backs.append(exchanged(four_terms, "ctx", 4) if mutual else shifted(four_terms, -4))
        uses.append((lambda i: i < 4) if mutual else (lambda i: True))
        four_parts = (four, ds_four)
    else:
        coef, two_terms, ds_two, ds_cross = call(
            near_two_terms_body, "two_terms", [VMEM] * 14,
            (coef_shape, shape(pair, bf16), half, half), two_scratch,
        )(given, taken, *all_stats, *two_parts, *sides)
        four_parts = ()
    backs.append(exchanged(two_terms, "ctx", 2) if mutual else shifted(two_terms, -2))
    uses.append((lambda i: i & 2 == 0) if mutual else (lambda i: True))
    if far and mutual:
        backs.append(exchanged(two_terms, "ctx", 6))
        uses.append(lambda i: i & 6 == 2)
    own_terms, my_grads, other_grads = call(
        functools.partial(own_terms_body, far), "own_terms", [VMEM] * (13 + len(four_parts)),
        (shape(pair, f32), shape(all_rows, f32), shape(all_rows, bf16)),
        (half_scratch,) * 4,
    )(coef, e_own, dp_own, e_side, dp_side, *sides, own, two, ds_two, ds_cross, *four_parts)
    if len(backs) > 1:
        own_terms, = call(
            functools.partial(first_sum_body, uses[0]), "first_sum", [VMEM] * 2,
            (shape(pair, f32),))(own_terms, backs[0])
        backs, uses = backs[1:], uses[1:]
    direct = head_count == 2 * share and share == 2
    slice_dims = (tokens // head_count, 2 * width)
    outs = ((shape(slice_dims, f32),) + (shape(slice_dims, bf16),) * (head_count - 1)
            if direct else (shape(pair, bf16),))
    sums = call(
        functools.partial(sums_body, direct, uses), "sums", [VMEM] * (1 + len(backs)), outs,
    )(own_terms, *backs)
    other_grads, kept = lax.optimization_barrier((other_grads, sums[0]))
    taken_grads = exchanged(other_grads, "ctx", 1)
    d_queries, = call(
        add_grads_body, "add_grads", [VMEM] * 2, (shape(all_rows, bf16),),
    )(my_grads, taken_grads)
    if direct:
        parts = [exchanged(sums[m], "head", m) for m in reversed(range(1, head_count))]
        parts.append(kept)
        *parts, d_queries = lax.optimization_barrier((*parts, d_queries))
        result_dims = (groups, tokens // head_count, width)
        d_keys, d_values = call(
            functools.partial(last_body, share), "last", [VMEM] * head_count,
            (shape(result_dims, bf16),) * 2)(*parts)
        return d_queries, d_keys, d_values
    slices = lax.all_to_all(kept.reshape(head_count, *slice_dims), "head", 0, 0)
    result = jnp.sum(slices.reshape(groups, share, *slice_dims).astype(f32), axis=1).astype(bf16)
    return d_queries, result[..., :width], result[..., width:]


def solution(mesh):
    placed = (
        P("head", "ctx", None),
        P(None, "ctx", None),
        P(None, "ctx", None),
        P("head", "ctx", None),
        P(),
    )
    return jax.shard_map(
        per_device,
        mesh=mesh,
        in_specs=placed,
        out_specs=(
            P("head", "ctx", None),
            P(None, ("ctx", "head"), None),
            P(None, ("ctx", "head"), None),
        ),
        check_vma=False,
    )
```

```python
import functools
import math

import jax
import jax.numpy as jnp
from jax import lax
from jax.experimental import pallas as pl
from jax.experimental.pallas import tpu as pltpu
from jax.sharding import PartitionSpec as P

GROUP = 8
REACH = 4
MASKED = -1e30
NT = (((1,), (1,)), ((), ()))
NN = (((1,), (0,)), ((), ()))
VMEM = pl.BlockSpec(memory_space=pltpu.VMEM)
SMEM = pl.BlockSpec(memory_space=pltpu.SMEM)
bf16, f32, i32 = jnp.bfloat16, jnp.float32, jnp.int32


def dot(a, b, dims=NN):
    return lax.dot_general(a, b, dims, preferred_element_type=f32)


def shape(dims, dtype):
    return jax.ShapeDtypeStruct(dims, dtype)


def call(body, name, in_specs, outs, scratch=()):
    return pl.pallas_call(
        body,
        out_shape=outs,
        in_specs=in_specs,
        out_specs=(VMEM,) * len(outs),
        scratch_shapes=scratch,
        compiler_params=pltpu.CompilerParams(vmem_limit_bytes=20 * 2**20),
        cost_estimate=pl.CostEstimate(flops=2**20, bytes_accessed=2**10, transcendentals=0),
        name=name,
    )


def shifted(block, distance):
    count = lax.axis_size("ctx")
    route = [(i - distance, i) for i in range(count) if 0 <= i - distance < count]
    return lax.ppermute(block, "ctx", route)


def exchanged(block, axis, mask):
    count = math.prod(lax.axis_size(name) for name in axis) if isinstance(axis, tuple) else (
        lax.axis_size(axis))
    return lax.ppermute(block, axis, [(i, i ^ mask) for i in range(count)])


def second_core():
    return lax.rem(lax.axis_index("ctx"), 2) == 1


def doc_starts(lengths_ref, block, tokens):
    row_pos = block * tokens + lax.broadcasted_iota(i32, (1, tokens), 1)
    starts = jnp.zeros((1, tokens), i32)
    end = jnp.int32(0)
    for d in range(lengths_ref.shape[0]):
        end = end + lengths_ref[d]
        starts = jnp.where(row_pos >= end, end, starts)
    return starts


def unit(pair, key_block, starts, q_ref, g_ref, e_ref, dp_ref, stats_ref, causal=False):
    heads, tokens, width = q_ref.shape
    factor = width ** -0.5 * math.log2(math.e)
    key_iota = lax.broadcasted_iota(i32, (tokens, 1), 0)
    allowed = key_block * tokens + key_iota >= starts
    if causal:
        allowed = allowed & (key_iota <= lax.broadcasted_iota(i32, (1, tokens), 1))
    for h in range(heads):
        lanes = slice(h * tokens, (h + 1) * tokens)
        s = jnp.where(allowed, dot(pair[:, :width], q_ref[h], NT), MASKED)
        top = jnp.max(s, axis=0, keepdims=True)
        e = jnp.exp2((s - top) * factor)
        dp = dot(pair[:, width:], g_ref[h], NT)
        e_ref[:, lanes] = e
        dp_ref[:, lanes] = dp
        stats_ref[0:1, lanes] = top
        stats_ref[1:2, lanes] = jnp.sum(e, axis=0, keepdims=True)
        stats_ref[2:3, lanes] = jnp.sum(e * dp, axis=0, keepdims=True)


def rows_of(ref, first=0):
    return [ref[first + row:first + row + 1] for row in range(3)]


def joined(parts, factor):
    top = functools.reduce(jnp.maximum, [part[0] for part in parts])
    gains = [jnp.exp2((part[0] - top) * factor) for part in parts]
    total = sum(gain * part[1] for gain, part in zip(gains, parts))
    weighted = sum(gain * part[2] for gain, part in zip(gains, parts))
    return top, total, weighted


def own_unit_body(lengths_ref, q_in, g_in, own_ref,
                  q_ref, g_ref, starts_ref, e_ref, dp_ref, stats_ref):
    tokens = q_in.shape[1]
    here = lax.axis_index("ctx")
    starts = doc_starts(lengths_ref, here, tokens)
    starts_ref[0:1] = starts
    starts_ref[1:2] = doc_starts(lengths_ref, jnp.bitwise_xor(here, 1), tokens)
    q_ref[...] = q_in[...]
    g_ref[...] = g_in[...]
    unit(own_ref, here, starts, q_in, g_in, e_ref, dp_ref, stats_ref, causal=True)


def four_unit_body(starts_ref, q_ref, g_ref, four_ref, e_ref, dp_ref, stats_ref):
    here = lax.axis_index("ctx")
    unit(four_ref, here - 4, starts_ref[0:1], q_ref, g_ref, e_ref, dp_ref, stats_ref)


def side_unit_body(starts_ref, other_q, other_g, own_ref, four_ref, e_ref, dp_ref, stats_ref):
    side = jnp.where(second_core(), four_ref[...], own_ref[...])
    block = lax.axis_index("ctx") - jnp.where(second_core(), 4, 0)
    unit(side, block, starts_ref[1:2], other_q, other_g, e_ref, dp_ref, stats_ref)


def near_side_unit_body(starts_ref, other_q, other_g, own_ref, e_ref, dp_ref, stats_ref):
    block = jnp.where(second_core(), -1, lax.axis_index("ctx"))
    unit(own_ref, block, starts_ref[1:2], other_q, other_g, e_ref, dp_ref, stats_ref)


def two_units_body(side_at, starts_ref, q_ref, g_ref, other_q, other_g, two_ref, *refs):
    earlier, refs = refs[:side_at + 1], refs[side_at + 1:]
    e_two, dp_two, stats_two, e_cross, dp_cross, stats_cross, given_ref = refs
    here = lax.axis_index("ctx")
    factor = q_ref.shape[-1] ** -0.5 * math.log2(math.e)
    unit(two_ref, here - 2, starts_ref[0:1], q_ref, g_ref, e_two, dp_two, stats_two)
    unit(two_ref, here - 2, starts_ref[1:2], other_q, other_g, e_cross, dp_cross, stats_cross)
    mine = joined([rows_of(ref) for ref in earlier[:side_at] + (stats_two,)], factor)
    others = joined([rows_of(ref) for ref in (earlier[side_at], stats_cross)], factor)
    for row, value in enumerate(mine + others):
        given_ref[row:row + 1] = value
    given_ref[6:8] = jnp.zeros((2, given_ref.shape[1]), f32)


def coefficients(given_ref, taken_ref, mine, others, width):
    factor = width ** -0.5 * math.log2(math.e)
    coefs = []
    for at, refs in ((0, mine), (3, others)):
        parts = [rows_of(given_ref, at), rows_of(taken_ref, 3 - at)]
        top, total, weighted = joined(parts, factor)
        inverse = 1.0 / total
        coefs.append(weighted * inverse)
        coefs.extend(jnp.exp2((ref[0:1] - top) * factor) * inverse for ref in refs)
    return coefs


def slopes(e_ref, dp_ref, gain, delta, p_ref, ds_ref):
    p = e_ref[...] * gain
    p_ref[...] = p.astype(bf16)
    ds_ref[...] = (p * (dp_ref[...] - delta)).astype(bf16)


def flat(ref):
    heads, tokens, width = ref.shape
    return ref[...].reshape(heads * tokens, width)


def add_terms(sum_ref, ds_ref, p_ref, q_ref, g_ref, fresh):
    width = q_ref.shape[-1]
    dk = dot(ds_ref[...], flat(q_ref)) * width ** -0.5
    dv = dot(p_ref[...], flat(g_ref))
    if fresh:
        sum_ref[:, :width] = dk
        sum_ref[:, width:] = dv
    else:
        sum_ref[:, :width] += dk
        sum_ref[:, width:] += dv


def four_terms_body(given_ref, taken_ref, stats_own, stats_four, stats_two, stats_side,
                    stats_cross, e_four, dp_four, e_side, dp_side,
                    q_ref, g_ref, other_q, other_g,
                    coef_ref, terms_ref, ds_four, ds_side, p_ref, sum_ref):
    coefs = coefficients(given_ref, taken_ref, (stats_own, stats_four, stats_two),
                         (stats_side, stats_cross), q_ref.shape[-1])
    for row, value in enumerate(coefs):
        coef_ref[row:row + 1] = value
    slopes(e_four, dp_four, coefs[2], coefs[0], p_ref.at[0], ds_four)
    add_terms(sum_ref, ds_four, p_ref.at[0], q_ref, g_ref, True)

    @pl.when(second_core())
    def _():
        slopes(e_side, dp_side, coef_ref[5:6], coef_ref[4:5], p_ref.at[1], ds_side)
        add_terms(sum_ref, ds_side, p_ref.at[1], other_q, other_g, False)

    terms_ref[...] = sum_ref[...].astype(bf16)


def two_terms_body(coef_ref, e_two, dp_two, e_cross, dp_cross, q_ref, g_ref, other_q, other_g,
                   terms_ref, ds_two, ds_cross, p_ref, sum_ref):
    slopes(e_two, dp_two, coef_ref[3:4], coef_ref[0:1], p_ref.at[0], ds_two)
    slopes(e_cross, dp_cross, coef_ref[6:7], coef_ref[4:5], p_ref.at[1], ds_cross)
    add_terms(sum_ref, ds_two, p_ref.at[0], q_ref, g_ref, True)
    add_terms(sum_ref, ds_cross, p_ref.at[1], other_q, other_g, False)
    terms_ref[...] = sum_ref[...].astype(bf16)


def slice_rows(ref, other):
    count = lax.axis_size("head")
    each = ref.shape[0] // count
    parity = jnp.bitwise_xor(lax.rem(lax.axis_index("head"), 2), other)
    return [ref[pl.ds(pl.multiple_of((2 * at + parity) * each, each), each)]
            for at in range(count // 2)]


def halve(sum_ref, kept_ref, given_ref):
    each = sum_ref.shape[0] // lax.axis_size("head")
    for other, out_ref in enumerate((kept_ref, given_ref)):
        for at, value in enumerate(slice_rows(sum_ref, other)):
            out_ref[at * each:(at + 1) * each] = value.astype(out_ref.dtype)


def near_two_terms_body(given_ref, taken_ref, stats_own, stats_two, stats_side, stats_cross,
                        e_two, dp_two, e_cross, dp_cross, q_ref, g_ref, other_q, other_g,
                        coef_ref, kept_ref, other_ref, ds_two, ds_cross, p_ref, sum_ref):
    coefs = coefficients(given_ref, taken_ref, (stats_own, stats_two),
                         (stats_side, stats_cross), q_ref.shape[-1])
    coefs.insert(2, jnp.zeros_like(coefs[0]))
    for row, value in enumerate(coefs):
        coef_ref[row:row + 1] = value
    slopes(e_two, dp_two, coefs[3], coefs[0], p_ref.at[0], ds_two)
    slopes(e_cross, dp_cross, coefs[6], coefs[4], p_ref.at[1], ds_cross)
    add_terms(sum_ref, ds_two, p_ref.at[0], q_ref, g_ref, True)
    add_terms(sum_ref, ds_cross, p_ref.at[1], other_q, other_g, False)
    halve(sum_ref, kept_ref, other_ref)


def near_own_terms_body(coef_ref, e_own, dp_own, e_side, dp_side, q_ref, g_ref, other_q, other_g,
                        kept_ref, other_ref, ds_own, ds_side, p_ref, sum_ref):
    slopes(e_own, dp_own, coef_ref[1:2], coef_ref[0:1], p_ref.at[0], ds_own)
    add_terms(sum_ref, ds_own, p_ref.at[0], q_ref, g_ref, True)
    slopes(e_side, dp_side, coef_ref[5:6], coef_ref[4:5], p_ref.at[1], ds_side)

    @pl.when(jnp.logical_not(second_core()))
    def _():
        add_terms(sum_ref, ds_side, p_ref.at[1], other_q, other_g, False)

    halve(sum_ref, kept_ref, other_ref)


def near_grads_body(own_ref, two_ref, ds_own, ds_two, ds_side, ds_cross, dq_ref, other_dq_ref):
    width = dq_ref.shape[-1]
    keys = [own_ref[:, :width], two_ref[:, :width]]
    query_grads(keys, [ds_side, ds_cross], other_dq_ref)
    query_grads(keys, [ds_own, ds_two], dq_ref)


def near_first_sum_body(kept_ref, two_pair_ref, two_ref, out_ref):
    taken = two_ref[...].astype(f32) + two_pair_ref[...].astype(f32)
    out_ref[...] = kept_ref[...] + jnp.where(lax.axis_index("ctx") & 2 == 0, taken, 0.0)


def near_sums_body(share, kept_ref, pair_ref, here_ref, there_ref):
    each = here_ref.shape[0]
    group = lax.axis_index("head") // share
    for out_ref, at in ((here_ref, group), (there_ref, 1 - group)):
        rows = pl.ds(pl.multiple_of(at * each, each), each)
        out_ref[...] = (kept_ref[rows] + pair_ref[rows].astype(f32)).astype(out_ref.dtype)


def near_last_body(share, here_ref, taken_ref, dk_ref, dv_ref):
    width = dk_ref.shape[-1]
    group = lax.axis_index("head") // share
    for ref, place in ((here_ref, group), (taken_ref, 1 - group)):
        dk_ref[place] = ref[:, :width]
        dv_ref[place] = ref[:, width:]


def query_grads(keys, ds_refs, out_ref):
    heads, tokens, width = out_ref.shape
    turned = [key.T for key in keys]
    for h in range(heads):
        lanes = slice(h * tokens, (h + 1) * tokens)
        dqt = sum(dot(kt, ds[:, lanes]) for kt, ds in zip(turned, ds_refs))
        out_ref[h] = (dqt.T * width ** -0.5).astype(out_ref.dtype)


def own_terms_body(coef_ref, e_own, dp_own, e_side, dp_side, q_ref, g_ref, other_q, other_g,
                   own_ref, two_ref, ds_two, ds_cross, four_ref, ds_four,
                   terms_ref, dq_ref, other_dq_ref, ds_own, ds_side, p_ref, p_side):
    width = q_ref.shape[-1]
    own, two, four = [ref[:, :width] for ref in (own_ref, two_ref, four_ref)]
    slopes(e_side, dp_side, coef_ref[5:6], coef_ref[4:5], p_side, ds_side)
    query_grads([jnp.where(second_core(), four, own), two], [ds_side, ds_cross], other_dq_ref)
    slopes(e_own, dp_own, coef_ref[1:2], coef_ref[0:1], p_ref, ds_own)
    add_terms(terms_ref, ds_own, p_ref, q_ref, g_ref, True)

    @pl.when(jnp.logical_not(second_core()))
    def _():
        add_terms(terms_ref, ds_side, p_side, other_q, other_g, False)

    query_grads([own, two, four], [ds_own, ds_two, ds_four], dq_ref)


def add_grads_body(mine_ref, taken_ref, dq_ref):
    dq_ref[...] = (mine_ref[...] + taken_ref[...].astype(f32)).astype(dq_ref.dtype)


def first_sum_body(use, own_terms, back, out_ref):
    taken = jnp.where(use(lax.axis_index("ctx")), back[...].astype(f32), 0.0)
    out_ref[...] = own_terms[...] + taken


def sums_body(direct, uses, own_terms, *refs):
    backs, outs = refs[:len(uses)], refs[len(uses):]
    tokens = own_terms.shape[0]
    ctx = lax.axis_index("ctx")
    head = lax.axis_index("head")
    count = lax.axis_size("head")
    rows_each = tokens // count

    def total(rows):
        value = own_terms[rows]
        for back, use in zip(backs, uses):
            value = value + jnp.where(use(ctx), back[rows].astype(f32), 0.0)
        return value

    if not direct:
        outs[0][...] = total(slice(0, tokens)).astype(bf16)
        return
    for mask in range(count):
        place = jnp.bitwise_xor(head, mask)
        value = total(pl.ds(pl.multiple_of(place * rows_each, rows_each), rows_each))
        outs[mask][...] = value.astype(outs[mask].dtype)


def last_body(share, *refs):
    parts, (dk_ref, dv_ref) = refs[-3::-1], refs[-2:]
    width = dk_ref.shape[-1]
    group = lax.axis_index("head") // share
    for other in range(len(parts) // share):
        mine = parts[other * share:(other + 1) * share]
        value = sum(ref[...].astype(f32) for ref in mine).astype(bf16)
        place = jnp.bitwise_xor(group, other)
        dk_ref[place] = value[:, :width]
        dv_ref[place] = value[:, width:]


def per_device(queries, keys, values, d_out, doc_lengths):
    ctx_count, (heads, tokens, _) = lax.axis_size("ctx"), queries.shape
    group = lax.axis_index("head") // (GROUP // heads)
    own = jnp.concatenate(
        [lax.dynamic_index_in_dim(keys, group, 0, keepdims=False),
         lax.dynamic_index_in_dim(values, group, 0, keepdims=False)], axis=1)
    operands = (queries, d_out, own, doc_lengths)
    if ctx_count != 2 * REACH or lax.axis_size("head") * heads != 2 * GROUP or 2 * heads != GROUP:
        return gradients(True, *operands)
    middle, own = lax.optimization_barrier((jnp.int32(ctx_count // 2 * tokens), own))
    operands = (queries, d_out, own, doc_lengths)
    doc_ends, zero = doc_lengths, jnp.int32(0)
    for back in range(1, doc_lengths.shape[0]):
        doc_ends = doc_ends + lax.pad(doc_lengths[:-back], zero, [(back, 0, 0)])
    split = jnp.max((doc_ends == middle).astype(i32))
    return lax.switch(split, [functools.partial(gradients, True),
                              functools.partial(gradients, False)], *operands)


def gradients(far, queries, d_out, own, doc_lengths):
    heads, tokens, width = queries.shape
    head_count = lax.axis_size("head")
    share = GROUP // heads
    groups = head_count // share
    rows = heads * tokens
    ctx = lax.axis_index("ctx")
    mutual = lax.axis_size("ctx") == 2 * REACH
    pair = (tokens, 2 * width)
    all_rows = (heads, tokens, width)
    stats = shape((3, rows), f32)
    wide = shape((tokens, rows), f32)
    half = shape((tokens, rows), bf16)
    half_scratch = pltpu.VMEM((tokens, rows), bf16)
    halves_scratch = pltpu.VMEM((2, tokens, rows), bf16)
    pair_scratch = pltpu.VMEM(pair, f32)

    if far:
        four = exchanged(own, "ctx", 4) if mutual else shifted(own, 4)
    two = [exchanged(own, "ctx", 2) if mutual else shifted(own, 2)]
    if far and mutual:
        two.append(exchanged(own, "ctx", 6))
    q, g, starts, e_own, dp_own, stats_own = call(
        own_unit_body, "own_unit", [SMEM] + [VMEM] * 3,
        (shape(all_rows, bf16), shape(all_rows, bf16), shape((2, tokens), i32),
         wide, wide, stats))(doc_lengths, queries, d_out, own)
    other_q = exchanged(queries, "ctx", 1)
    other_g = exchanged(d_out, "ctx", 1)
    if far:
        four, starts = lax.optimization_barrier((four, starts))
        e_four, dp_four, stats_four = call(
            four_unit_body, "four_unit", [VMEM] * 4, (wide, wide, stats))(starts, q, g, four)
        other_q, stats_four = lax.optimization_barrier((other_q, stats_four))
        e_side, dp_side, stats_side = call(
            side_unit_body, "side_unit", [VMEM] * 5, (wide, wide, stats),
        )(starts, other_q, other_g, own, four)
        earlier = (stats_own, stats_four, stats_side)
    else:
        e_side, dp_side, stats_side = call(
            near_side_unit_body, "side_unit", [VMEM] * 4, (wide, wide, stats),
        )(starts, other_q, other_g, own)
        earlier = (stats_own, stats_side)
    *two, stats_side = lax.optimization_barrier((*two, stats_side))
    two = jnp.where(ctx & 2 == 2, *two) if len(two) == 2 else two[0]
    e_two, dp_two, stats_two, e_cross, dp_cross, stats_cross, given = call(
        functools.partial(two_units_body, len(earlier) - 1), "two_units",
        [VMEM] * (6 + len(earlier)), (wide, wide, stats) * 2 + (shape((8, rows), f32),),
    )(starts, q, g, other_q, other_g, two, *earlier)
    taken = exchanged(given, "ctx", 1)
    all_stats = earlier[:-1] + (stats_two, stats_side, stats_cross)
    sides = (q, g, other_q, other_g)
    two_parts = (e_two, dp_two, e_cross, dp_cross)
    two_scratch = (halves_scratch, pair_scratch)
    coef_shape = shape((8, rows), f32)
    backs, uses = [], []
    if far:
        coef, four_terms, ds_four = call(
            four_terms_body, "four_terms", [VMEM] * 15, (coef_shape, shape(pair, bf16), half),
            (half_scratch,) + two_scratch,
        )(given, taken, *all_stats, e_four, dp_four, e_side, dp_side, *sides)
        two_terms, ds_two, ds_cross = call(
            two_terms_body, "two_terms", [VMEM] * 9, (shape(pair, bf16), half, half), two_scratch,
        )(coef, *two_parts, *sides)
        backs.append(exchanged(four_terms, "ctx", 4) if mutual else shifted(four_terms, -4))
        uses.append((lambda i: i < 4) if mutual else (lambda i: True))
    else:
        slices = (tokens // 2, 2 * width)
        coef, two_kept, two_other, ds_two, ds_cross = call(
            near_two_terms_body, "two_terms", [VMEM] * 14,
            (coef_shape, shape(slices, bf16), shape(slices, bf16), half, half), two_scratch,
        )(given, taken, *all_stats, *two_parts, *sides)
        two_pair = exchanged(two_other, ("ctx", "head"), 2 * head_count + 1)
        two_back = exchanged(two_kept, "ctx", 2)
        own_kept, own_other, ds_own, ds_side = call(
            near_own_terms_body, "own_terms", [VMEM] * 9,
            (shape(slices, f32), shape(slices, bf16), half, half), two_scratch,
        )(coef, e_own, dp_own, e_side, dp_side, *sides)
        own_pair = exchanged(own_other, "head", 1)
        my_grads, other_grads = call(
            near_grads_body, "query_grads", [VMEM] * 6,
            (shape(all_rows, f32), shape(all_rows, bf16)),
        )(own, two, ds_own, ds_two, ds_side, ds_cross)
        slice_dims = (tokens // head_count, 2 * width)
        own_kept, = call(
            near_first_sum_body, "first_sum", [VMEM] * 3, (shape(slices, f32),),
        )(own_kept, two_pair, two_back)
        kept, sent = call(
            functools.partial(near_sums_body, share), "sums", [VMEM] * 2,
            (shape(slice_dims, bf16),) * 2)(own_kept, own_pair)
        other_grads, kept = lax.optimization_barrier((other_grads, kept))
        taken_grads = exchanged(other_grads, "ctx", 1)
        d_queries, = call(
            add_grads_body, "add_grads", [VMEM] * 2, (shape(all_rows, bf16),),
        )(my_grads, taken_grads)
        last = exchanged(sent, "head", share)
        last, d_queries = lax.optimization_barrier((last, d_queries))
        d_keys, d_values = call(
            functools.partial(near_last_body, share), "last", [VMEM] * 2,
            (shape((groups, tokens // head_count, width), bf16),) * 2)(kept, last)
        return d_queries, d_keys, d_values
    backs.append(exchanged(two_terms, "ctx", 2) if mutual else shifted(two_terms, -2))
    uses.append((lambda i: i & 2 == 0) if mutual else (lambda i: True))
    if far and mutual:
        backs.append(exchanged(two_terms, "ctx", 6))
        uses.append(lambda i: i & 6 == 2)
    own_terms, my_grads, other_grads = call(
        own_terms_body, "own_terms", [VMEM] * 15,
        (shape(pair, f32), shape(all_rows, f32), shape(all_rows, bf16)),
        (half_scratch,) * 4,
    )(coef, e_own, dp_own, e_side, dp_side, *sides, own, two, ds_two, ds_cross, four, ds_four)
    own_terms, = call(
        functools.partial(first_sum_body, uses[0]), "first_sum", [VMEM] * 2,
        (shape(pair, f32),))(own_terms, backs[0])
    backs, uses = backs[1:], uses[1:]
    direct = head_count == 2 * share and share == 2
    slice_dims = (tokens // head_count, 2 * width)
    outs = ((shape(slice_dims, f32),) + (shape(slice_dims, bf16),) * (head_count - 1)
            if direct else (shape(pair, bf16),))
    sums = call(
        functools.partial(sums_body, direct, uses), "sums", [VMEM] * (1 + len(backs)), outs,
    )(own_terms, *backs)
    other_grads, kept = lax.optimization_barrier((other_grads, sums[0]))
    taken_grads = exchanged(other_grads, "ctx", 1)
    d_queries, = call(
        add_grads_body, "add_grads", [VMEM] * 2, (shape(all_rows, bf16),),
    )(my_grads, taken_grads)
    if direct:
        parts = [exchanged(sums[m], "head", m) for m in reversed(range(1, head_count))]
        parts.append(kept)
        *parts, d_queries = lax.optimization_barrier((*parts, d_queries))
        result_dims = (groups, tokens // head_count, width)
        d_keys, d_values = call(
            functools.partial(last_body, share), "last", [VMEM] * head_count,
            (shape(result_dims, bf16),) * 2)(*parts)
        return d_queries, d_keys, d_values
    slices = lax.all_to_all(kept.reshape(head_count, *slice_dims), "head", 0, 0)
    result = jnp.sum(slices.reshape(groups, share, *slice_dims).astype(f32), axis=1).astype(bf16)
    return d_queries, result[..., :width], result[..., width:]


def solution(mesh):
    placed = (
        P("head", "ctx", None),
        P(None, "ctx", None),
        P(None, "ctx", None),
        P("head", "ctx", None),
        P(),
    )
    return jax.shard_map(
        per_device,
        mesh=mesh,
        in_specs=placed,
        out_specs=(
            P("head", "ctx", None),
            P(None, ("ctx", "head"), None),
            P(None, ("ctx", "head"), None),
        ),
        check_vma=False,
    )
```

```python
import functools
import math

import jax
import jax.numpy as jnp
from jax import lax
from jax.experimental import pallas as pl
from jax.experimental.pallas import tpu as pltpu
from jax.sharding import PartitionSpec as P

GROUP = 8
REACH = 4
MASKED = -1e30
NT = (((1,), (1,)), ((), ()))
NN = (((1,), (0,)), ((), ()))
VMEM = pl.BlockSpec(memory_space=pltpu.VMEM)
SMEM = pl.BlockSpec(memory_space=pltpu.SMEM)
bf16, f32, i32 = jnp.bfloat16, jnp.float32, jnp.int32


def dot(a, b, dims=NN):
    return lax.dot_general(a, b, dims, preferred_element_type=f32)


def shape(dims, dtype):
    return jax.ShapeDtypeStruct(dims, dtype)


def call(body, name, in_specs, outs, scratch=()):
    return pl.pallas_call(
        body,
        out_shape=outs,
        in_specs=in_specs,
        out_specs=(VMEM,) * len(outs),
        scratch_shapes=scratch,
        compiler_params=pltpu.CompilerParams(vmem_limit_bytes=20 * 2**20),
        cost_estimate=pl.CostEstimate(flops=2**20, bytes_accessed=2**10, transcendentals=0),
        name=name,
    )


def shifted(block, distance):
    count = lax.axis_size("ctx")
    route = [(i - distance, i) for i in range(count) if 0 <= i - distance < count]
    return lax.ppermute(block, "ctx", route)


def shifted_to_pair(block, distance):
    count, layers = lax.axis_size("ctx"), lax.axis_size("head")
    route = [((i - distance) * layers + layer, i * layers + (layer ^ 1))
             for i in range(count) if 0 <= i - distance < count for layer in range(layers)]
    return lax.ppermute(block, ("ctx", "head"), route)


def exchanged(block, axis, mask):
    count = math.prod(lax.axis_size(name) for name in axis) if isinstance(axis, tuple) else (
        lax.axis_size(axis))
    return lax.ppermute(block, axis, [(i, i ^ mask) for i in range(count)])


def second_core():
    return lax.rem(lax.axis_index("ctx"), 2) == 1


def doc_starts(lengths_ref, block, tokens):
    row_pos = block * tokens + lax.broadcasted_iota(i32, (1, tokens), 1)
    starts = jnp.zeros((1, tokens), i32)
    end = jnp.int32(0)
    for d in range(lengths_ref.shape[0]):
        end = end + lengths_ref[d]
        starts = jnp.where(row_pos >= end, end, starts)
    return starts


def unit(pair, key_block, starts, q_ref, g_ref, e_ref, dp_ref, stats_ref, causal=False):
    heads, tokens, width = q_ref.shape
    factor = width ** -0.5 * math.log2(math.e)
    key_iota = lax.broadcasted_iota(i32, (tokens, 1), 0)
    allowed = key_block * tokens + key_iota >= starts
    if causal:
        allowed = allowed & (key_iota <= lax.broadcasted_iota(i32, (1, tokens), 1))
    for h in range(heads):
        lanes = slice(h * tokens, (h + 1) * tokens)
        s = jnp.where(allowed, dot(pair[:, :width], q_ref[h], NT), MASKED)
        top = jnp.max(s, axis=0, keepdims=True)
        e = jnp.exp2((s - top) * factor)
        dp = dot(pair[:, width:], g_ref[h], NT)
        e_ref[:, lanes] = e
        dp_ref[:, lanes] = dp
        stats_ref[0:1, lanes] = top
        stats_ref[1:2, lanes] = jnp.sum(e, axis=0, keepdims=True)
        stats_ref[2:3, lanes] = jnp.sum(e * dp, axis=0, keepdims=True)


def rows_of(ref, first=0):
    return [ref[first + row:first + row + 1] for row in range(3)]


def joined(parts, factor):
    top = functools.reduce(jnp.maximum, [part[0] for part in parts])
    gains = [jnp.exp2((part[0] - top) * factor) for part in parts]
    total = sum(gain * part[1] for gain, part in zip(gains, parts))
    weighted = sum(gain * part[2] for gain, part in zip(gains, parts))
    return top, total, weighted


def own_unit_body(lengths_ref, q_in, g_in, own_ref,
                  q_ref, g_ref, starts_ref, e_ref, dp_ref, stats_ref):
    tokens = q_in.shape[1]
    here = lax.axis_index("ctx")
    starts = doc_starts(lengths_ref, here, tokens)
    starts_ref[0:1] = starts
    starts_ref[1:2] = doc_starts(lengths_ref, jnp.bitwise_xor(here, 1), tokens)
    q_ref[...] = q_in[...]
    g_ref[...] = g_in[...]
    unit(own_ref, here, starts, q_in, g_in, e_ref, dp_ref, stats_ref, causal=True)


def four_unit_body(starts_ref, q_ref, g_ref, four_ref, e_ref, dp_ref, stats_ref):
    here = lax.axis_index("ctx")
    unit(four_ref, here - 4, starts_ref[0:1], q_ref, g_ref, e_ref, dp_ref, stats_ref)


def side_unit_body(starts_ref, other_q, other_g, own_ref, four_ref, e_ref, dp_ref, stats_ref):
    side = jnp.where(second_core(), four_ref[...], own_ref[...])
    block = lax.axis_index("ctx") - jnp.where(second_core(), 4, 0)
    unit(side, block, starts_ref[1:2], other_q, other_g, e_ref, dp_ref, stats_ref)


def near_side_unit_body(starts_ref, other_q, other_g, own_ref, e_ref, dp_ref, stats_ref):
    block = jnp.where(second_core(), -1, lax.axis_index("ctx"))
    unit(own_ref, block, starts_ref[1:2], other_q, other_g, e_ref, dp_ref, stats_ref)


def two_units_body(side_at, starts_ref, q_ref, g_ref, other_q, other_g, two_ref, *refs):
    earlier, refs = refs[:side_at + 1], refs[side_at + 1:]
    e_two, dp_two, stats_two, e_cross, dp_cross, stats_cross, given_ref = refs
    here = lax.axis_index("ctx")
    factor = q_ref.shape[-1] ** -0.5 * math.log2(math.e)
    unit(two_ref, here - 2, starts_ref[0:1], q_ref, g_ref, e_two, dp_two, stats_two)
    unit(two_ref, here - 2, starts_ref[1:2], other_q, other_g, e_cross, dp_cross, stats_cross)
    mine = joined([rows_of(ref) for ref in earlier[:side_at] + (stats_two,)], factor)
    others = joined([rows_of(ref) for ref in (earlier[side_at], stats_cross)], factor)
    for row, value in enumerate(mine + others):
        given_ref[row:row + 1] = value
    given_ref[6:8] = jnp.zeros((2, given_ref.shape[1]), f32)


def coefficients(given_ref, taken_ref, mine, others, width):
    factor = width ** -0.5 * math.log2(math.e)
    coefs = []
    for at, refs in ((0, mine), (3, others)):
        parts = [rows_of(given_ref, at), rows_of(taken_ref, 3 - at)]
        top, total, weighted = joined(parts, factor)
        inverse = 1.0 / total
        coefs.append(weighted * inverse)
        coefs.extend(jnp.exp2((ref[0:1] - top) * factor) * inverse for ref in refs)
    return coefs


def slopes(e_ref, dp_ref, gain, delta, p_ref, ds_ref):
    p = e_ref[...] * gain
    p_ref[...] = p.astype(bf16)
    ds_ref[...] = (p * (dp_ref[...] - delta)).astype(bf16)


def flat(ref):
    heads, tokens, width = ref.shape
    return ref[...].reshape(heads * tokens, width)


def add_terms(sum_ref, ds_ref, p_ref, q_ref, g_ref, fresh):
    width = q_ref.shape[-1]
    dk = dot(ds_ref[...], flat(q_ref)) * width ** -0.5
    dv = dot(p_ref[...], flat(g_ref))
    if fresh:
        sum_ref[:, :width] = dk
        sum_ref[:, width:] = dv
    else:
        sum_ref[:, :width] += dk
        sum_ref[:, width:] += dv


def slice_rows(ref, other):
    count = lax.axis_size("head")
    each = ref.shape[0] // count
    parity = jnp.bitwise_xor(lax.rem(lax.axis_index("head"), 2), other)
    return [ref[pl.ds(pl.multiple_of((2 * at + parity) * each, each), each)]
            for at in range(count // 2)]


def halve(sum_ref, kept_ref, given_ref):
    each = sum_ref.shape[0] // lax.axis_size("head")
    for other, out_ref in enumerate((kept_ref, given_ref)):
        for at, value in enumerate(slice_rows(sum_ref, other)):
            out_ref[at * each:(at + 1) * each] = value.astype(out_ref.dtype)


def first_terms_body(far, given_ref, taken_ref, *refs):
    stats, refs = refs[:4 + far], refs[4 + far:]
    e_ref, dp_ref, e_more, dp_more, q_ref, g_ref, other_q, other_g = refs[:8]
    coef_ref, kept_ref, other_ref, ds_ref, ds_more, p_ref, sum_ref = refs[8:]
    coefs = coefficients(given_ref, taken_ref, stats[:2 + far], stats[2 + far:], q_ref.shape[-1])
    if not far:
        coefs.insert(2, jnp.zeros_like(coefs[0]))
    for row, value in enumerate(coefs):
        coef_ref[row:row + 1] = value
    at, more = (2, 5) if far else (3, 6)
    slopes(e_ref, dp_ref, coefs[at], coefs[0], p_ref.at[0], ds_ref)
    add_terms(sum_ref, ds_ref, p_ref.at[0], q_ref, g_ref, True)

    def add_more():
        slopes(e_more, dp_more, coef_ref[more:more + 1], coef_ref[4:5], p_ref.at[1], ds_more)
        add_terms(sum_ref, ds_more, p_ref.at[1], other_q, other_g, False)

    if far:
        pl.when(second_core())(add_more)
    else:
        add_more()
    halve(sum_ref, kept_ref, other_ref)


def two_terms_body(coef_ref, e_two, dp_two, e_cross, dp_cross, q_ref, g_ref, other_q, other_g,
                   kept_ref, other_ref, ds_two, ds_cross, p_ref, sum_ref):
    slopes(e_two, dp_two, coef_ref[3:4], coef_ref[0:1], p_ref.at[0], ds_two)
    slopes(e_cross, dp_cross, coef_ref[6:7], coef_ref[4:5], p_ref.at[1], ds_cross)
    add_terms(sum_ref, ds_two, p_ref.at[0], q_ref, g_ref, True)
    add_terms(sum_ref, ds_cross, p_ref.at[1], other_q, other_g, False)
    halve(sum_ref, kept_ref, other_ref)


def own_terms_body(coef_ref, e_own, dp_own, e_side, dp_side, q_ref, g_ref, other_q, other_g,
                   kept_ref, other_ref, ds_own, ds_side, p_ref, sum_ref):
    slopes(e_own, dp_own, coef_ref[1:2], coef_ref[0:1], p_ref.at[0], ds_own)
    add_terms(sum_ref, ds_own, p_ref.at[0], q_ref, g_ref, True)
    slopes(e_side, dp_side, coef_ref[5:6], coef_ref[4:5], p_ref.at[1], ds_side)

    @pl.when(jnp.logical_not(second_core()))
    def _():
        add_terms(sum_ref, ds_side, p_ref.at[1], other_q, other_g, False)

    halve(sum_ref, kept_ref, other_ref)


def query_grads(keys, ds_refs, out_ref):
    heads, tokens, width = out_ref.shape
    turned = [key.T for key in keys]
    for h in range(heads):
        lanes = slice(h * tokens, (h + 1) * tokens)
        dqt = sum(dot(kt, ds[:, lanes]) for kt, ds in zip(turned, ds_refs))
        out_ref[h] = (dqt.T * width ** -0.5).astype(out_ref.dtype)


def query_grads_body(own_ref, two_ref, ds_own, ds_two, ds_side, ds_cross, *refs):
    four_refs, (dq_ref, other_dq_ref) = refs[:-2], refs[-2:]
    width = dq_ref.shape[-1]
    keys, slope_refs = [own_ref[:, :width], two_ref[:, :width]], [ds_own, ds_two]
    side = keys[0]
    if four_refs:
        keys.append(four_refs[0][:, :width])
        slope_refs.append(four_refs[1])
        side = jnp.where(second_core(), keys[2], side)
    query_grads([side, keys[1]], [ds_side, ds_cross], other_dq_ref)
    query_grads(keys, slope_refs, dq_ref)


def add_grads_body(mine_ref, taken_ref, dq_ref):
    dq_ref[...] = (mine_ref[...] + taken_ref[...].astype(f32)).astype(dq_ref.dtype)


def add_backs_body(uses, sum_ref, *refs):
    backs, out_ref = refs[:-1], refs[-1]
    ctx = lax.axis_index("ctx")
    value = sum_ref[...]
    for at, use in enumerate(uses):
        taken = backs[2 * at][...].astype(f32) + backs[2 * at + 1][...].astype(f32)
        value = value + jnp.where(use(ctx), taken, 0.0)
    out_ref[...] = value


def sums_body(share, kept_ref, pair_ref, *out_refs):
    if len(out_refs) == 1:
        out_refs[0][...] = (kept_ref[...] + pair_ref[...].astype(f32)).astype(bf16)
        return
    each = out_refs[0].shape[0]
    group = lax.axis_index("head") // share
    for out_ref, at in zip(out_refs, (group, 1 - group)):
        rows = pl.ds(pl.multiple_of(at * each, each), each)
        out_ref[...] = (kept_ref[rows] + pair_ref[rows].astype(f32)).astype(bf16)


def last_body(share, here_ref, taken_ref, dk_ref, dv_ref):
    width = dk_ref.shape[-1]
    group = lax.axis_index("head") // share
    for ref, place in ((here_ref, group), (taken_ref, 1 - group)):
        dk_ref[place] = ref[:, :width]
        dv_ref[place] = ref[:, width:]


def per_device(queries, keys, values, d_out, doc_lengths):
    ctx_count, (heads, tokens, _) = lax.axis_size("ctx"), queries.shape
    group = lax.axis_index("head") // (GROUP // heads)
    own = jnp.concatenate(
        [lax.dynamic_index_in_dim(keys, group, 0, keepdims=False),
         lax.dynamic_index_in_dim(values, group, 0, keepdims=False)], axis=1)
    operands = (queries, d_out, own, doc_lengths)
    if ctx_count != 2 * REACH:
        return gradients(True, *operands)
    middle, own = lax.optimization_barrier((jnp.int32(ctx_count // 2 * tokens), own))
    operands = (queries, d_out, own, doc_lengths)
    doc_ends, zero = doc_lengths, jnp.int32(0)
    for back in range(1, doc_lengths.shape[0]):
        doc_ends = doc_ends + lax.pad(doc_lengths[:-back], zero, [(back, 0, 0)])
    split = jnp.max((doc_ends == middle).astype(i32))
    return lax.switch(split, [functools.partial(gradients, True),
                              functools.partial(gradients, False)], *operands)


def gradients(far, queries, d_out, own, doc_lengths):
    heads, tokens, width = queries.shape
    head_count = lax.axis_size("head")
    share = GROUP // heads
    groups = head_count // share
    rows = heads * tokens
    ctx = lax.axis_index("ctx")
    mutual = lax.axis_size("ctx") == 2 * REACH
    pair = (tokens, 2 * width)
    all_rows = (heads, tokens, width)
    slices = (tokens // share, 2 * width)
    stats = shape((3, rows), f32)
    wide = shape((tokens, rows), f32)
    half = shape((tokens, rows), bf16)
    coef_shape = shape((8, rows), f32)
    scratch = (pltpu.VMEM((2, tokens, rows), bf16), pltpu.VMEM(pair, f32))

    if far:
        four = exchanged(own, "ctx", 4) if mutual else shifted(own, 4)
    two = [exchanged(own, "ctx", 2) if mutual else shifted(own, 2)]
    if far and mutual:
        two.append(exchanged(own, "ctx", 6))
    q, g, starts, e_own, dp_own, stats_own = call(
        own_unit_body, "own_unit", [SMEM] + [VMEM] * 3,
        (shape(all_rows, bf16), shape(all_rows, bf16), shape((2, tokens), i32),
         wide, wide, stats))(doc_lengths, queries, d_out, own)
    other_q = exchanged(queries, "ctx", 1)
    other_g = exchanged(d_out, "ctx", 1)
    if far:
        four, starts = lax.optimization_barrier((four, starts))
        e_four, dp_four, stats_four = call(
            four_unit_body, "four_unit", [VMEM] * 4, (wide, wide, stats))(starts, q, g, four)
        other_q, stats_four = lax.optimization_barrier((other_q, stats_four))
        e_side, dp_side, stats_side = call(
            side_unit_body, "side_unit", [VMEM] * 5, (wide, wide, stats),
        )(starts, other_q, other_g, own, four)
        earlier = (stats_own, stats_four, stats_side)
    else:
        e_side, dp_side, stats_side = call(
            near_side_unit_body, "side_unit", [VMEM] * 4, (wide, wide, stats),
        )(starts, other_q, other_g, own)
        earlier = (stats_own, stats_side)
    *two, stats_side = lax.optimization_barrier((*two, stats_side))
    two = jnp.where(ctx & 2 == 2, *two) if len(two) == 2 else two[0]
    e_two, dp_two, stats_two, e_cross, dp_cross, stats_cross, given = call(
        functools.partial(two_units_body, len(earlier) - 1), "two_units",
        [VMEM] * (6 + len(earlier)), (wide, wide, stats) * 2 + (shape((8, rows), f32),),
    )(starts, q, g, other_q, other_g, two, *earlier)
    taken = exchanged(given, "ctx", 1)
    all_stats = earlier[:-1] + (stats_two, stats_side, stats_cross)
    sides = (q, g, other_q, other_g)
    two_parts = (e_two, dp_two, e_cross, dp_cross)
    side_parts = (e_side, dp_side)
    halves = (shape(slices, bf16),) * 2

    def sent_back(kept, other, mask, distance):
        if mutual:
            return [exchanged(kept, "ctx", mask),
                    exchanged(other, ("ctx", "head"), mask * head_count + 1)]
        return [shifted(kept, -distance), shifted_to_pair(other, -distance)]

    coef, kept, other, ds_first, ds_more = call(
        functools.partial(first_terms_body, far), "first_terms", [VMEM] * (14 + far),
        (coef_shape,) + halves + (half, half), scratch,
    )(given, taken, *all_stats, *((e_four, dp_four) + side_parts if far else two_parts), *sides)
    if far:
        four_backs = sent_back(kept, other, 4, 4)
        kept, other, ds_two, ds_cross = call(
            two_terms_body, "two_terms", [VMEM] * 9, halves + (half, half), scratch,
        )(coef, *two_parts, *sides)
    else:
        ds_two, ds_cross = ds_first, ds_more
    two_backs, uses = [], []
    if far and mutual:
        two_backs += sent_back(kept, other, 6, 2)
        uses.append(lambda i: i & 6 == 2)
    two_backs += sent_back(kept, other, 2, 2)
    uses.append((lambda i: i & 2 == 0) if mutual else (lambda i: True))
    own_kept, own_other, ds_own, ds_side = call(
        own_terms_body, "own_terms", [VMEM] * 9, (shape(slices, f32), halves[0], half, half),
        scratch)(coef, e_own, dp_own, *side_parts, *sides)
    own_pair = exchanged(own_other, "head", 1)
    four_refs = (four, ds_first) if far else ()
    my_grads, other_grads = call(
        query_grads_body, "query_grads", [VMEM] * (6 + len(four_refs)),
        (shape(all_rows, f32), shape(all_rows, bf16)),
    )(own, two, ds_own, ds_two, ds_side, ds_cross, *four_refs)
    if far:
        own_kept, = call(
            functools.partial(add_backs_body, [(lambda i: i < 4) if mutual else (lambda i: True)]),
            "add_four", [VMEM] * 3, (shape(slices, f32),))(own_kept, *four_backs)
    own_kept, = call(
        functools.partial(add_backs_body, uses), "add_two", [VMEM] * (1 + len(two_backs)),
        (shape(slices, f32),))(own_kept, *two_backs)
    slice_dims = (tokens // head_count, 2 * width)
    outs = (shape(slice_dims, bf16),) * 2 if groups == 2 else halves[:1]
    kept, *sent = call(
        functools.partial(sums_body, share), "sums", [VMEM] * 2, outs)(own_kept, own_pair)
    other_grads, kept = lax.optimization_barrier((other_grads, kept))
    taken_grads = exchanged(other_grads, "ctx", 1)
    d_queries, = call(
        add_grads_body, "add_grads", [VMEM] * 2, (shape(all_rows, bf16),),
    )(my_grads, taken_grads)
    if groups == 2:
        last = exchanged(sent[0], "head", share)
        last, d_queries = lax.optimization_barrier((last, d_queries))
        d_keys, d_values = call(
            functools.partial(last_body, share), "last", [VMEM] * 2,
            (shape((groups, tokens // head_count, width), bf16),) * 2)(kept, last)
        return d_queries, d_keys, d_values
    result = lax.all_to_all(
        kept.reshape(groups, *slice_dims), "head", 0, 0, tiled=True,
        axis_index_groups=[list(range(at, head_count, share)) for at in range(share)])
    return d_queries, result[..., :width], result[..., width:]


def solution(mesh):
    placed = (
        P("head", "ctx", None),
        P(None, "ctx", None),
        P(None, "ctx", None),
        P("head", "ctx", None),
        P(),
    )
    return jax.shard_map(
        per_device,
        mesh=mesh,
        in_specs=placed,
        out_specs=(
            P("head", "ctx", None),
            P(None, ("ctx", "head"), None),
            P(None, ("ctx", "head"), None),
        ),
        check_vma=False,
    )
```

```python
import functools
import math

import jax
import jax.numpy as jnp
from jax import lax
from jax.experimental import pallas as pl
from jax.experimental.pallas import tpu as pltpu
from jax.sharding import PartitionSpec as P

GROUP = 8
REACH = 4
MASKED = -1e30
NT = (((1,), (1,)), ((), ()))
NN = (((1,), (0,)), ((), ()))
VMEM = pl.BlockSpec(memory_space=pltpu.VMEM)
SMEM = pl.BlockSpec(memory_space=pltpu.SMEM)
bf16, f32, i32 = jnp.bfloat16, jnp.float32, jnp.int32


def dot(a, b, dims=NN):
    return lax.dot_general(a, b, dims, preferred_element_type=f32)


def shape(dims, dtype):
    return jax.ShapeDtypeStruct(dims, dtype)


def call(body, name, in_specs, outs, scratch=()):
    return pl.pallas_call(
        body,
        out_shape=outs,
        in_specs=in_specs,
        out_specs=(VMEM,) * len(outs),
        scratch_shapes=scratch,
        compiler_params=pltpu.CompilerParams(vmem_limit_bytes=20 * 2**20),
        cost_estimate=pl.CostEstimate(flops=2**20, bytes_accessed=2**10, transcendentals=0),
        name=name,
    )


def shifted(block, distance):
    count = lax.axis_size("ctx")
    route = [(i - distance, i) for i in range(count) if 0 <= i - distance < count]
    return lax.ppermute(block, "ctx", route)


def exchanged(block, axis, mask):
    count = math.prod(lax.axis_size(name) for name in axis) if isinstance(axis, tuple) else (
        lax.axis_size(axis))
    return lax.ppermute(block, axis, [(i, i ^ mask) for i in range(count)])


def second_core():
    return lax.rem(lax.axis_index("ctx"), 2) == 1


def doc_starts(lengths_ref, block, tokens):
    row_pos = block * tokens + lax.broadcasted_iota(i32, (1, tokens), 1)
    starts = jnp.zeros((1, tokens), i32)
    end = jnp.int32(0)
    for d in range(lengths_ref.shape[0]):
        end = end + lengths_ref[d]
        starts = jnp.where(row_pos >= end, end, starts)
    return starts


def unit(pair, key_block, starts, q_ref, g_ref, e_ref, dp_ref, stats_ref, causal=False):
    heads, tokens, width = q_ref.shape
    factor = width ** -0.5 * math.log2(math.e)
    key_iota = lax.broadcasted_iota(i32, (tokens, 1), 0)
    allowed = key_block * tokens + key_iota >= starts
    if causal:
        allowed = allowed & (key_iota <= lax.broadcasted_iota(i32, (1, tokens), 1))
    for h in range(heads):
        lanes = slice(h * tokens, (h + 1) * tokens)
        s = jnp.where(allowed, dot(pair[:, :width], q_ref[h], NT), MASKED)
        top = jnp.max(s, axis=0, keepdims=True)
        e = jnp.exp2((s - top) * factor)
        dp = dot(pair[:, width:], g_ref[h], NT)
        e_ref[:, lanes] = e
        dp_ref[:, lanes] = dp
        stats_ref[0:1, lanes] = top
        stats_ref[1:2, lanes] = jnp.sum(e, axis=0, keepdims=True)
        stats_ref[2:3, lanes] = jnp.sum(e * dp, axis=0, keepdims=True)


def rows_of(ref, first=0):
    return [ref[first + row:first + row + 1] for row in range(3)]


def joined(parts, factor):
    top = functools.reduce(jnp.maximum, [part[0] for part in parts])
    gains = [jnp.exp2((part[0] - top) * factor) for part in parts]
    total = sum(gain * part[1] for gain, part in zip(gains, parts))
    weighted = sum(gain * part[2] for gain, part in zip(gains, parts))
    return top, total, weighted


def own_unit_body(starts_ref, q_in, g_in, own_ref, q_ref, g_ref, e_ref, dp_ref, stats_ref):
    q_ref[...] = q_in[...]
    g_ref[...] = g_in[...]
    unit(own_ref, lax.axis_index("ctx"), starts_ref[0:1], q_in, g_in, e_ref, dp_ref, stats_ref,
         causal=True)


def four_unit_body(starts_ref, q_ref, g_ref, four_ref, e_ref, dp_ref, stats_ref):
    here = lax.axis_index("ctx")
    unit(four_ref, here - 4, starts_ref[0:1], q_ref, g_ref, e_ref, dp_ref, stats_ref)


def side_unit_body(starts_ref, other_q, other_g, own_ref, four_ref, e_ref, dp_ref, stats_ref):
    side = jnp.where(second_core(), four_ref[...], own_ref[...])
    block = lax.axis_index("ctx") - jnp.where(second_core(), 4, 0)
    unit(side, block, starts_ref[1:2], other_q, other_g, e_ref, dp_ref, stats_ref)


def prepare_body(share, middle, lengths_in, keys_ref, values_ref,
                 split_ref, starts_ref, own_ref, lengths_ref, sems):
    tokens, width = keys_ref.shape[1:]
    group = lax.axis_index("head") // share
    lengths = pltpu.make_async_copy(lengths_in, lengths_ref, sems.at[0])
    copies = [
        pltpu.make_async_copy(keys_ref.at[group], own_ref.at[:, :width], sems.at[1]),
        pltpu.make_async_copy(values_ref.at[group], own_ref.at[:, width:], sems.at[2]),
    ]
    for copy in [lengths] + copies:
        copy.start()
    lengths.wait()
    end, split = jnp.int32(0), jnp.int32(0)
    for d in range(lengths_ref.shape[0]):
        end = end + lengths_ref[d]
        split = jnp.where(end == middle, 1, split)
    split_ref[0] = split
    here = lax.axis_index("ctx")
    starts_ref[0:1] = doc_starts(lengths_ref, here, tokens)
    starts_ref[1:2] = doc_starts(lengths_ref, jnp.bitwise_xor(here, 1), tokens)
    for copy in copies:
        copy.wait()


def near_side_unit_body(starts_ref, other_q, other_g, own_ref, e_ref, dp_ref, stats_ref):
    block = jnp.where(second_core(), -1, lax.axis_index("ctx"))
    unit(own_ref, block, starts_ref[1:2], other_q, other_g, e_ref, dp_ref, stats_ref)


def two_units_body(side_at, starts_ref, q_ref, g_ref, other_q, other_g, two_ref, *refs):
    earlier, refs = refs[:side_at + 1], refs[side_at + 1:]
    e_two, dp_two, stats_two, e_cross, dp_cross, stats_cross, given_ref = refs
    here = lax.axis_index("ctx")
    factor = q_ref.shape[-1] ** -0.5 * math.log2(math.e)
    unit(two_ref, here - 2, starts_ref[0:1], q_ref, g_ref, e_two, dp_two, stats_two)
    unit(two_ref, here - 2, starts_ref[1:2], other_q, other_g, e_cross, dp_cross, stats_cross)
    mine = joined([rows_of(ref) for ref in earlier[:side_at] + (stats_two,)], factor)
    others = joined([rows_of(ref) for ref in (earlier[side_at], stats_cross)], factor)
    for row, value in enumerate(mine + others):
        given_ref[row:row + 1] = value
    given_ref[6:8] = jnp.zeros((2, given_ref.shape[1]), f32)


def coefficients(given_ref, taken_ref, mine, others, width):
    factor = width ** -0.5 * math.log2(math.e)
    coefs = []
    for at, refs in ((0, mine), (3, others)):
        parts = [rows_of(given_ref, at), rows_of(taken_ref, 3 - at)]
        top, total, weighted = joined(parts, factor)
        inverse = 1.0 / total
        coefs.append(weighted * inverse)
        coefs.extend(jnp.exp2((ref[0:1] - top) * factor) * inverse for ref in refs)
    return coefs


def slopes(e_ref, dp_ref, gain, delta, p_ref, ds_ref):
    p = e_ref[...] * gain
    p_ref[...] = p.astype(bf16)
    ds_ref[...] = (p * (dp_ref[...] - delta)).astype(bf16)


def flat(ref):
    heads, tokens, width = ref.shape
    return ref[...].reshape(heads * tokens, width)


def add_terms(sum_ref, ds_ref, p_ref, q_ref, g_ref, fresh):
    width = q_ref.shape[-1]
    dk = dot(ds_ref[...], flat(q_ref)) * width ** -0.5
    dv = dot(p_ref[...], flat(g_ref))
    if fresh:
        sum_ref[:, :width] = dk
        sum_ref[:, width:] = dv
    else:
        sum_ref[:, :width] += dk
        sum_ref[:, width:] += dv


def four_terms_body(given_ref, taken_ref, stats_own, stats_four, stats_two, stats_side,
                    stats_cross, e_four, dp_four, e_side, dp_side,
                    q_ref, g_ref, other_q, other_g,
                    coef_ref, terms_ref, ds_four, ds_side, p_ref, sum_ref):
    coefs = coefficients(given_ref, taken_ref, (stats_own, stats_four, stats_two),
                         (stats_side, stats_cross), q_ref.shape[-1])
    for row, value in enumerate(coefs):
        coef_ref[row:row + 1] = value
    slopes(e_four, dp_four, coefs[2], coefs[0], p_ref.at[0], ds_four)
    add_terms(sum_ref, ds_four, p_ref.at[0], q_ref, g_ref, True)

    @pl.when(second_core())
    def _():
        slopes(e_side, dp_side, coef_ref[5:6], coef_ref[4:5], p_ref.at[1], ds_side)
        add_terms(sum_ref, ds_side, p_ref.at[1], other_q, other_g, False)

    terms_ref[...] = sum_ref[...].astype(bf16)


def two_terms_body(coef_ref, e_two, dp_two, e_cross, dp_cross, q_ref, g_ref, other_q, other_g,
                   terms_ref, ds_two, ds_cross, p_ref, sum_ref):
    slopes(e_two, dp_two, coef_ref[3:4], coef_ref[0:1], p_ref.at[0], ds_two)
    slopes(e_cross, dp_cross, coef_ref[6:7], coef_ref[4:5], p_ref.at[1], ds_cross)
    add_terms(sum_ref, ds_two, p_ref.at[0], q_ref, g_ref, True)
    add_terms(sum_ref, ds_cross, p_ref.at[1], other_q, other_g, False)
    terms_ref[...] = sum_ref[...].astype(bf16)


def slice_rows(ref, other):
    count = lax.axis_size("head")
    each = ref.shape[0] // count
    parity = jnp.bitwise_xor(lax.rem(lax.axis_index("head"), 2), other)
    return [ref[pl.ds(pl.multiple_of((2 * at + parity) * each, each), each)]
            for at in range(count // 2)]


def halve(sum_ref, kept_ref, given_ref):
    each = sum_ref.shape[0] // lax.axis_size("head")
    for other, out_ref in enumerate((kept_ref, given_ref)):
        for at, value in enumerate(slice_rows(sum_ref, other)):
            out_ref[at * each:(at + 1) * each] = value.astype(out_ref.dtype)


def near_two_terms_body(given_ref, taken_ref, stats_own, stats_two, stats_side, stats_cross,
                        e_two, dp_two, e_cross, dp_cross, q_ref, g_ref, other_q, other_g,
                        coef_ref, kept_ref, other_ref, ds_two, ds_cross, p_ref, sum_ref):
    coefs = coefficients(given_ref, taken_ref, (stats_own, stats_two),
                         (stats_side, stats_cross), q_ref.shape[-1])
    coefs.insert(2, jnp.zeros_like(coefs[0]))
    for row, value in enumerate(coefs):
        coef_ref[row:row + 1] = value
    slopes(e_two, dp_two, coefs[3], coefs[0], p_ref.at[0], ds_two)
    slopes(e_cross, dp_cross, coefs[6], coefs[4], p_ref.at[1], ds_cross)
    add_terms(sum_ref, ds_two, p_ref.at[0], q_ref, g_ref, True)
    add_terms(sum_ref, ds_cross, p_ref.at[1], other_q, other_g, False)
    halve(sum_ref, kept_ref, other_ref)


def near_own_terms_body(coef_ref, e_own, dp_own, e_side, dp_side, q_ref, g_ref, other_q, other_g,
                        kept_ref, other_ref, ds_own, ds_side, p_ref, sum_ref):
    slopes(e_own, dp_own, coef_ref[1:2], coef_ref[0:1], p_ref.at[0], ds_own)
    add_terms(sum_ref, ds_own, p_ref.at[0], q_ref, g_ref, True)
    slopes(e_side, dp_side, coef_ref[5:6], coef_ref[4:5], p_ref.at[1], ds_side)

    @pl.when(jnp.logical_not(second_core()))
    def _():
        add_terms(sum_ref, ds_side, p_ref.at[1], other_q, other_g, False)

    halve(sum_ref, kept_ref, other_ref)


def near_grads_body(own_ref, two_ref, ds_own, ds_two, ds_side, ds_cross, dq_ref, other_dq_ref):
    width = dq_ref.shape[-1]
    keys = [own_ref[:, :width], two_ref[:, :width]]
    query_grads(keys, [ds_side, ds_cross], other_dq_ref)
    query_grads(keys, [ds_own, ds_two], dq_ref)


def near_first_sum_body(kept_ref, two_ref, two_pair_ref, out_ref):
    taken = two_ref[...].astype(f32) + two_pair_ref[...].astype(f32)
    out_ref[...] = kept_ref[...] + jnp.where(lax.axis_index("ctx") & 2 == 0, taken, 0.0)


def near_sums_body(share, kept_ref, pair_ref, here_ref, there_ref):
    each = here_ref.shape[0]
    group = lax.axis_index("head") // share
    for out_ref, at in ((here_ref, group), (there_ref, 1 - group)):
        rows = pl.ds(pl.multiple_of(at * each, each), each)
        out_ref[...] = (kept_ref[rows] + pair_ref[rows].astype(f32)).astype(out_ref.dtype)


def near_last_body(share, here_ref, taken_ref, dk_ref, dv_ref):
    width = dk_ref.shape[-1]
    group = lax.axis_index("head") // share
    for ref, place in ((here_ref, group), (taken_ref, 1 - group)):
        dk_ref[place] = ref[:, :width]
        dv_ref[place] = ref[:, width:]


def query_grads(keys, ds_refs, out_ref):
    heads, tokens, width = out_ref.shape
    turned = [key.T for key in keys]
    for h in range(heads):
        lanes = slice(h * tokens, (h + 1) * tokens)
        dqt = sum(dot(kt, ds[:, lanes]) for kt, ds in zip(turned, ds_refs))
        out_ref[h] = (dqt.T * width ** -0.5).astype(out_ref.dtype)


def own_terms_body(coef_ref, e_own, dp_own, e_side, dp_side, q_ref, g_ref, other_q, other_g,
                   own_ref, two_ref, ds_two, ds_cross, four_ref, ds_four,
                   terms_ref, dq_ref, other_dq_ref, ds_own, ds_side, p_ref, p_side):
    width = q_ref.shape[-1]
    own, two, four = [ref[:, :width] for ref in (own_ref, two_ref, four_ref)]
    slopes(e_side, dp_side, coef_ref[5:6], coef_ref[4:5], p_side, ds_side)
    query_grads([jnp.where(second_core(), four, own), two], [ds_side, ds_cross], other_dq_ref)
    slopes(e_own, dp_own, coef_ref[1:2], coef_ref[0:1], p_ref, ds_own)
    add_terms(terms_ref, ds_own, p_ref, q_ref, g_ref, True)

    @pl.when(jnp.logical_not(second_core()))
    def _():
        add_terms(terms_ref, ds_side, p_side, other_q, other_g, False)

    query_grads([own, two, four], [ds_own, ds_two, ds_four], dq_ref)


def add_grads_body(mine_ref, taken_ref, dq_ref):
    dq_ref[...] = (mine_ref[...] + taken_ref[...].astype(f32)).astype(dq_ref.dtype)


def first_sum_body(use, own_terms, back, out_ref):
    taken = jnp.where(use(lax.axis_index("ctx")), back[...].astype(f32), 0.0)
    out_ref[...] = own_terms[...] + taken


def sums_body(direct, uses, own_terms, *refs):
    backs, outs = refs[:len(uses)], refs[len(uses):]
    tokens = own_terms.shape[0]
    ctx = lax.axis_index("ctx")
    head = lax.axis_index("head")
    count = lax.axis_size("head")
    rows_each = tokens // count

    def total(rows):
        value = own_terms[rows]
        for back, use in zip(backs, uses):
            value = value + jnp.where(use(ctx), back[rows].astype(f32), 0.0)
        return value

    if not direct:
        outs[0][...] = total(slice(0, tokens)).astype(bf16)
        return
    for mask in range(count):
        place = jnp.bitwise_xor(head, mask)
        value = total(pl.ds(pl.multiple_of(place * rows_each, rows_each), rows_each))
        outs[mask][...] = value.astype(outs[mask].dtype)


def last_body(share, *refs):
    parts, (dk_ref, dv_ref) = refs[-3::-1], refs[-2:]
    width = dk_ref.shape[-1]
    group = lax.axis_index("head") // share
    for other in range(len(parts) // share):
        mine = parts[other * share:(other + 1) * share]
        value = sum(ref[...].astype(f32) for ref in mine).astype(bf16)
        place = jnp.bitwise_xor(group, other)
        dk_ref[place] = value[:, :width]
        dv_ref[place] = value[:, width:]


def per_device(queries, keys, values, d_out, doc_lengths):
    ctx_count, (heads, tokens, width) = lax.axis_size("ctx"), queries.shape
    middle = ctx_count // 2 * tokens
    split, starts, own = pl.pallas_call(
        functools.partial(prepare_body, GROUP // heads, middle),
        out_shape=(shape((1,), i32), shape((2, tokens), i32), shape((tokens, 2 * width), bf16)),
        in_specs=[pl.BlockSpec(memory_space=pl.ANY)] * 3,
        out_specs=(SMEM, VMEM, VMEM),
        scratch_shapes=[pltpu.SMEM(doc_lengths.shape, i32), pltpu.SemaphoreType.DMA((3,))],
        name="prepare",
    )(*[pltpu.with_memory_space_constraint(value, pltpu.HBM)
        for value in (doc_lengths, keys, values)])
    operands = (queries, d_out, own, starts)
    if ctx_count != 2 * REACH or lax.axis_size("head") * heads != 2 * GROUP or 2 * heads != GROUP:
        return gradients(True, *operands)
    return lax.switch(split[0], [functools.partial(gradients, True),
                                 functools.partial(gradients, False)], *operands)


def gradients(far, queries, d_out, own, starts):
    heads, tokens, width = queries.shape
    head_count = lax.axis_size("head")
    share = GROUP // heads
    groups = head_count // share
    rows = heads * tokens
    ctx = lax.axis_index("ctx")
    mutual = lax.axis_size("ctx") == 2 * REACH
    pair = (tokens, 2 * width)
    all_rows = (heads, tokens, width)
    stats = shape((3, rows), f32)
    wide = shape((tokens, rows), f32)
    half = shape((tokens, rows), bf16)
    half_scratch = pltpu.VMEM((tokens, rows), bf16)
    halves_scratch = pltpu.VMEM((2, tokens, rows), bf16)
    pair_scratch = pltpu.VMEM(pair, f32)

    if far:
        four = exchanged(own, "ctx", 4) if mutual else shifted(own, 4)
    two = [exchanged(own, "ctx", 2) if mutual else shifted(own, 2)]
    if far and mutual:
        two.append(exchanged(own, "ctx", 6))
    q, g, e_own, dp_own, stats_own = call(
        own_unit_body, "own_unit", [VMEM] * 4,
        (shape(all_rows, bf16), shape(all_rows, bf16), wide, wide, stats),
    )(starts, queries, d_out, own)
    other_q = exchanged(queries, "ctx", 1)
    other_g = exchanged(d_out, "ctx", 1)
    if far:
        four, stats_own = lax.optimization_barrier((four, stats_own))
        e_four, dp_four, stats_four = call(
            four_unit_body, "four_unit", [VMEM] * 4, (wide, wide, stats))(starts, q, g, four)
        other_q, stats_four = lax.optimization_barrier((other_q, stats_four))
        e_side, dp_side, stats_side = call(
            side_unit_body, "side_unit", [VMEM] * 5, (wide, wide, stats),
        )(starts, other_q, other_g, own, four)
        earlier = (stats_own, stats_four, stats_side)
    else:
        e_side, dp_side, stats_side = call(
            near_side_unit_body, "side_unit", [VMEM] * 4, (wide, wide, stats),
        )(starts, other_q, other_g, own)
        earlier = (stats_own, stats_side)
    *two, stats_side = lax.optimization_barrier((*two, stats_side))
    two = jnp.where(ctx & 2 == 2, *two) if len(two) == 2 else two[0]
    e_two, dp_two, stats_two, e_cross, dp_cross, stats_cross, given = call(
        functools.partial(two_units_body, len(earlier) - 1), "two_units",
        [VMEM] * (6 + len(earlier)), (wide, wide, stats) * 2 + (shape((8, rows), f32),),
    )(starts, q, g, other_q, other_g, two, *earlier)
    taken = exchanged(given, "ctx", 1)
    all_stats = earlier[:-1] + (stats_two, stats_side, stats_cross)
    sides = (q, g, other_q, other_g)
    two_parts = (e_two, dp_two, e_cross, dp_cross)
    two_scratch = (halves_scratch, pair_scratch)
    coef_shape = shape((8, rows), f32)
    backs, uses = [], []
    if far:
        coef, four_terms, ds_four = call(
            four_terms_body, "four_terms", [VMEM] * 15, (coef_shape, shape(pair, bf16), half),
            (half_scratch,) + two_scratch,
        )(given, taken, *all_stats, e_four, dp_four, e_side, dp_side, *sides)
        two_terms, ds_two, ds_cross = call(
            two_terms_body, "two_terms", [VMEM] * 9, (shape(pair, bf16), half, half), two_scratch,
        )(coef, *two_parts, *sides)
        backs.append(exchanged(four_terms, "ctx", 4) if mutual else shifted(four_terms, -4))
        uses.append((lambda i: i < 4) if mutual else (lambda i: True))
    else:
        slices = (tokens // 2, 2 * width)
        coef, two_kept, two_other, ds_two, ds_cross = call(
            near_two_terms_body, "two_terms", [VMEM] * 14,
            (coef_shape, shape(slices, bf16), shape(slices, bf16), half, half), two_scratch,
        )(given, taken, *all_stats, *two_parts, *sides)
        two_pair = exchanged(two_other, ("ctx", "head"), 2 * head_count + 1)
        two_back = exchanged(two_kept, "ctx", 2)
        own_kept, own_other, ds_own, ds_side = call(
            near_own_terms_body, "own_terms", [VMEM] * 9,
            (shape(slices, f32), shape(slices, bf16), half, half), two_scratch,
        )(coef, e_own, dp_own, e_side, dp_side, *sides)
        own_pair = exchanged(own_other, "head", 1)
        my_grads, other_grads = call(
            near_grads_body, "query_grads", [VMEM] * 6,
            (shape(all_rows, f32), shape(all_rows, bf16)),
        )(own, two, ds_own, ds_two, ds_side, ds_cross)
        slice_dims = (tokens // head_count, 2 * width)
        own_kept, = call(
            near_first_sum_body, "first_sum", [VMEM] * 3, (shape(slices, f32),),
        )(own_kept, two_back, two_pair)
        kept, sent = call(
            functools.partial(near_sums_body, share), "sums", [VMEM] * 2,
            (shape(slice_dims, bf16),) * 2)(own_kept, own_pair)
        other_grads, kept = lax.optimization_barrier((other_grads, kept))
        taken_grads = exchanged(other_grads, "ctx", 1)
        d_queries, = call(
            add_grads_body, "add_grads", [VMEM] * 2, (shape(all_rows, bf16),),
        )(my_grads, taken_grads)
        last = exchanged(sent, "head", share)
        last, d_queries = lax.optimization_barrier((last, d_queries))
        d_keys, d_values = call(
            functools.partial(near_last_body, share), "last", [VMEM] * 2,
            (shape((groups, tokens // head_count, width), bf16),) * 2)(kept, last)
        return d_queries, d_keys, d_values
    backs.append(exchanged(two_terms, "ctx", 2) if mutual else shifted(two_terms, -2))
    uses.append((lambda i: i & 2 == 0) if mutual else (lambda i: True))
    if far and mutual:
        backs.append(exchanged(two_terms, "ctx", 6))
        uses.append(lambda i: i & 6 == 2)
    own_terms, my_grads, other_grads = call(
        own_terms_body, "own_terms", [VMEM] * 15,
        (shape(pair, f32), shape(all_rows, f32), shape(all_rows, bf16)),
        (half_scratch,) * 4,
    )(coef, e_own, dp_own, e_side, dp_side, *sides, own, two, ds_two, ds_cross, four, ds_four)
    own_terms, = call(
        functools.partial(first_sum_body, uses[0]), "first_sum", [VMEM] * 2,
        (shape(pair, f32),))(own_terms, backs[0])
    backs, uses = backs[1:], uses[1:]
    direct = head_count == 2 * share and share == 2
    slice_dims = (tokens // head_count, 2 * width)
    outs = ((shape(slice_dims, f32),) + (shape(slice_dims, bf16),) * (head_count - 1)
            if direct else (shape(pair, bf16),))
    sums = call(
        functools.partial(sums_body, direct, uses), "sums", [VMEM] * (1 + len(backs)), outs,
    )(own_terms, *backs)
    other_grads, kept = lax.optimization_barrier((other_grads, sums[0]))
    taken_grads = exchanged(other_grads, "ctx", 1)
    d_queries, = call(
        add_grads_body, "add_grads", [VMEM] * 2, (shape(all_rows, bf16),),
    )(my_grads, taken_grads)
    if direct:
        parts = [exchanged(sums[m], "head", m) for m in reversed(range(1, head_count))]
        parts.append(kept)
        *parts, d_queries = lax.optimization_barrier((*parts, d_queries))
        result_dims = (groups, tokens // head_count, width)
        d_keys, d_values = call(
            functools.partial(last_body, share), "last", [VMEM] * head_count,
            (shape(result_dims, bf16),) * 2)(*parts)
        return d_queries, d_keys, d_values
    slices = lax.all_to_all(kept.reshape(head_count, *slice_dims), "head", 0, 0)
    result = jnp.sum(slices.reshape(groups, share, *slice_dims).astype(f32), axis=1).astype(bf16)
    return d_queries, result[..., :width], result[..., width:]


def solution(mesh):
    placed = (
        P("head", "ctx", None),
        P(None, "ctx", None),
        P(None, "ctx", None),
        P("head", "ctx", None),
        P(),
    )
    return jax.shard_map(
        per_device,
        mesh=mesh,
        in_specs=placed,
        out_specs=(
            P("head", "ctx", None),
            P(None, ("ctx", "head"), None),
            P(None, ("ctx", "head"), None),
        ),
        check_vma=False,
    )
```

```python
import functools
import math

import jax
import jax.numpy as jnp
from jax import lax
from jax.experimental import pallas as pl
from jax.experimental.pallas import tpu as pltpu
from jax.sharding import PartitionSpec as P

GROUP = 8
REACH = 4
MASKED = -1e30
NT = (((1,), (1,)), ((), ()))
NN = (((1,), (0,)), ((), ()))
VMEM = pl.BlockSpec(memory_space=pltpu.VMEM)
SMEM = pl.BlockSpec(memory_space=pltpu.SMEM)
bf16, f32, i32 = jnp.bfloat16, jnp.float32, jnp.int32


def dot(a, b, dims=NN):
    return lax.dot_general(a, b, dims, preferred_element_type=f32)


def shape(dims, dtype):
    return jax.ShapeDtypeStruct(dims, dtype)


def call(body, name, in_specs, outs, scratch=()):
    return pl.pallas_call(
        body,
        out_shape=outs,
        in_specs=in_specs,
        out_specs=(VMEM,) * len(outs),
        scratch_shapes=scratch,
        compiler_params=pltpu.CompilerParams(vmem_limit_bytes=20 * 2**20),
        cost_estimate=pl.CostEstimate(flops=2**20, bytes_accessed=2**10, transcendentals=0),
        name=name,
    )


def shifted(block, distance):
    count = lax.axis_size("ctx")
    route = [(i - distance, i) for i in range(count) if 0 <= i - distance < count]
    return lax.ppermute(block, "ctx", route)


def exchanged(block, axis, mask):
    count = math.prod(lax.axis_size(name) for name in axis) if isinstance(axis, tuple) else (
        lax.axis_size(axis))
    return lax.ppermute(block, axis, [(i, i ^ mask) for i in range(count)])


def second_core():
    return lax.rem(lax.axis_index("ctx"), 2) == 1


def doc_starts(lengths_ref, block, tokens):
    row_pos = block * tokens + lax.broadcasted_iota(i32, (1, tokens), 1)
    starts = jnp.zeros((1, tokens), i32)
    end = jnp.int32(0)
    for d in range(lengths_ref.shape[0]):
        end = end + lengths_ref[d]
        starts = jnp.where(row_pos >= end, end, starts)
    return starts


def unit(pair, key_block, starts, q_ref, g_ref, e_ref, dp_ref, stats_ref, causal=False):
    heads, tokens, width = q_ref.shape
    factor = width ** -0.5 * math.log2(math.e)
    key_iota = lax.broadcasted_iota(i32, (tokens, 1), 0)
    allowed = key_block * tokens + key_iota >= starts
    if causal:
        allowed = allowed & (key_iota <= lax.broadcasted_iota(i32, (1, tokens), 1))
    for h in range(heads):
        lanes = slice(h * tokens, (h + 1) * tokens)
        s = jnp.where(allowed, dot(pair[:, :width], q_ref[h], NT), MASKED)
        top = jnp.max(s, axis=0, keepdims=True)
        e = jnp.exp2((s - top) * factor)
        dp = dot(pair[:, width:], g_ref[h], NT)
        e_ref[:, lanes] = e
        dp_ref[:, lanes] = dp
        stats_ref[0:1, lanes] = top
        stats_ref[1:2, lanes] = jnp.sum(e, axis=0, keepdims=True)
        stats_ref[2:3, lanes] = jnp.sum(e * dp, axis=0, keepdims=True)


def rows_of(ref, first=0):
    return [ref[first + row:first + row + 1] for row in range(3)]


def joined(parts, factor):
    top = functools.reduce(jnp.maximum, [part[0] for part in parts])
    gains = [jnp.exp2((part[0] - top) * factor) for part in parts]
    total = sum(gain * part[1] for gain, part in zip(gains, parts))
    weighted = sum(gain * part[2] for gain, part in zip(gains, parts))
    return top, total, weighted


def own_unit_body(starts_ref, q_in, g_in, own_ref, q_ref, g_ref, e_ref, dp_ref, stats_ref):
    q_ref[...] = q_in[...]
    g_ref[...] = g_in[...]
    unit(own_ref, lax.axis_index("ctx"), starts_ref[0:1], q_in, g_in, e_ref, dp_ref, stats_ref,
         causal=True)


def four_unit_body(starts_ref, q_ref, g_ref, four_ref, e_ref, dp_ref, stats_ref):
    here = lax.axis_index("ctx")
    unit(four_ref, here - 4, starts_ref[0:1], q_ref, g_ref, e_ref, dp_ref, stats_ref)


def side_unit_body(starts_ref, other_q, other_g, own_ref, four_ref, e_ref, dp_ref, stats_ref):
    side = jnp.where(second_core(), four_ref[...], own_ref[...])
    block = lax.axis_index("ctx") - jnp.where(second_core(), 4, 0)
    unit(side, block, starts_ref[1:2], other_q, other_g, e_ref, dp_ref, stats_ref)


def prepare_body(share, middle, lengths_in, keys_ref, values_ref,
                 split_ref, starts_ref, own_ref, lengths_ref, sems):
    tokens, width = keys_ref.shape[1:]
    group = lax.axis_index("head") // share
    lengths = pltpu.make_async_copy(lengths_in, lengths_ref, sems.at[0])
    copies = [
        pltpu.make_async_copy(keys_ref.at[group], own_ref.at[:, :width], sems.at[1]),
        pltpu.make_async_copy(values_ref.at[group], own_ref.at[:, width:], sems.at[2]),
    ]
    for copy in [lengths] + copies:
        copy.start()
    lengths.wait()
    end, split = jnp.int32(0), jnp.int32(0)
    for d in range(lengths_ref.shape[0]):
        end = end + lengths_ref[d]
        split = jnp.where(end == middle, 1, split)
    split_ref[0] = split
    here = lax.axis_index("ctx")
    starts_ref[0:1] = doc_starts(lengths_ref, here, tokens)
    starts_ref[1:2] = doc_starts(lengths_ref, jnp.bitwise_xor(here, 1), tokens)
    for copy in copies:
        copy.wait()


def near_side_unit_body(starts_ref, other_q, other_g, own_ref, e_ref, dp_ref, stats_ref):
    block = jnp.where(second_core(), -1, lax.axis_index("ctx"))
    unit(own_ref, block, starts_ref[1:2], other_q, other_g, e_ref, dp_ref, stats_ref)


def write_rows(ref, values):
    for row, value in enumerate(values):
        ref[row:row + 1] = value


def cross_unit_body(starts_ref, other_q, other_g, two_ref, stats_side,
                    e_ref, dp_ref, stats_ref, others_ref):
    factor = other_q.shape[-1] ** -0.5 * math.log2(math.e)
    unit(two_ref, lax.axis_index("ctx") - 2, starts_ref[1:2], other_q, other_g,
         e_ref, dp_ref, stats_ref)
    write_rows(others_ref, joined([rows_of(stats_side), rows_of(stats_ref)], factor))
    others_ref[3:4] = jnp.zeros((1, others_ref.shape[1]), f32)


def two_unit_body(starts_ref, q_ref, g_ref, two_ref, *refs):
    earlier, (e_ref, dp_ref, stats_ref, mine_ref) = refs[:-4], refs[-4:]
    factor = q_ref.shape[-1] ** -0.5 * math.log2(math.e)
    unit(two_ref, lax.axis_index("ctx") - 2, starts_ref[0:1], q_ref, g_ref,
         e_ref, dp_ref, stats_ref)
    write_rows(mine_ref, joined([rows_of(ref) for ref in earlier + (stats_ref,)], factor))
    mine_ref[3:4] = jnp.zeros((1, mine_ref.shape[1]), f32)


def coefficients(here_ref, taken_ref, stats_refs, width):
    factor = width ** -0.5 * math.log2(math.e)
    top, total, weighted = joined([rows_of(here_ref), rows_of(taken_ref)], factor)
    inverse = 1.0 / total
    return [weighted * inverse] + [
        jnp.exp2((ref[0:1] - top) * factor) * inverse for ref in stats_refs]


def slopes(e_ref, dp_ref, gain, delta, p_ref, ds_ref):
    p = e_ref[...] * gain
    p_ref[...] = p.astype(bf16)
    ds_ref[...] = (p * (dp_ref[...] - delta)).astype(bf16)


def flat(ref):
    heads, tokens, width = ref.shape
    return ref[...].reshape(heads * tokens, width)


def add_terms(sum_ref, ds_ref, p_ref, q_ref, g_ref, fresh):
    width = q_ref.shape[-1]
    dk = dot(ds_ref[...], flat(q_ref)) * width ** -0.5
    dv = dot(p_ref[...], flat(g_ref))
    if fresh:
        sum_ref[:, :width] = dk
        sum_ref[:, width:] = dv
    else:
        sum_ref[:, :width] += dk
        sum_ref[:, width:] += dv


def my_terms_body(count, mine_ref, taken_ref, *refs):
    stats, refs = refs[:count], refs[count:]
    parts, (q_ref, g_ref), refs = refs[:4], refs[4:6], refs[6:]
    coef_ref, ds_refs, sums, p_ref = refs[0], refs[1:3], refs[3:5], refs[5]
    coefs = coefficients(mine_ref, taken_ref, stats, q_ref.shape[-1])
    write_rows(coef_ref, coefs)
    for at in range(2):
        slopes(parts[2 * at], parts[2 * at + 1], coefs[count - 1 + at], coefs[0], p_ref.at[at],
               ds_refs[at])
        add_terms(sums[at], ds_refs[at], p_ref.at[at], q_ref, g_ref, True)


def four_terms_body(others_ref, taken_ref, stats_side, stats_cross, e_side, dp_side,
                    other_q, other_g, part_ref, coef_ref, terms_ref, sum_ref, p_ref, ds_ref):
    coefs = coefficients(others_ref, taken_ref, (stats_side, stats_cross), other_q.shape[-1])
    write_rows(coef_ref, coefs)
    sum_ref[...] = part_ref[...]

    @pl.when(second_core())
    def _():
        slopes(e_side, dp_side, coef_ref[1:2], coef_ref[0:1], p_ref, ds_ref)
        add_terms(sum_ref, ds_ref, p_ref, other_q, other_g, False)

    terms_ref[...] = sum_ref[...].astype(bf16)


def two_terms_body(coef_ref, e_cross, dp_cross, other_q, other_g, part_ref,
                   terms_ref, ds_cross, p_ref, sum_ref):
    slopes(e_cross, dp_cross, coef_ref[2:3], coef_ref[0:1], p_ref, ds_cross)
    sum_ref[...] = part_ref[...]
    add_terms(sum_ref, ds_cross, p_ref, other_q, other_g, False)
    terms_ref[...] = sum_ref[...].astype(bf16)


def slice_rows(ref, other):
    count = lax.axis_size("head")
    each = ref.shape[0] // count
    parity = jnp.bitwise_xor(lax.rem(lax.axis_index("head"), 2), other)
    return [ref[pl.ds(pl.multiple_of((2 * at + parity) * each, each), each)]
            for at in range(count // 2)]


def halve(sum_ref, kept_ref, given_ref):
    each = sum_ref.shape[0] // lax.axis_size("head")
    for other, out_ref in enumerate((kept_ref, given_ref)):
        for at, value in enumerate(slice_rows(sum_ref, other)):
            out_ref[at * each:(at + 1) * each] = value.astype(out_ref.dtype)


def near_two_terms_body(others_ref, taken_ref, stats_side, stats_cross, e_cross, dp_cross,
                        other_q, other_g, part_ref,
                        coef_ref, kept_ref, other_ref, ds_cross, p_ref, sum_ref):
    coefs = coefficients(others_ref, taken_ref, (stats_side, stats_cross), other_q.shape[-1])
    write_rows(coef_ref, coefs)
    slopes(e_cross, dp_cross, coefs[2], coefs[0], p_ref, ds_cross)
    sum_ref[...] = part_ref[...]
    add_terms(sum_ref, ds_cross, p_ref, other_q, other_g, False)
    halve(sum_ref, kept_ref, other_ref)


def near_own_terms_body(coef_ref, e_side, dp_side, other_q, other_g, part_ref,
                        kept_ref, other_ref, ds_side, p_ref, sum_ref):
    slopes(e_side, dp_side, coef_ref[1:2], coef_ref[0:1], p_ref, ds_side)
    sum_ref[...] = part_ref[...]

    @pl.when(jnp.logical_not(second_core()))
    def _():
        add_terms(sum_ref, ds_side, p_ref, other_q, other_g, False)

    halve(sum_ref, kept_ref, other_ref)


def near_grads_body(own_ref, two_ref, ds_own, ds_two, ds_side, ds_cross, dq_ref, other_dq_ref):
    width = dq_ref.shape[-1]
    keys = [own_ref[:, :width], two_ref[:, :width]]
    query_grads(keys, [ds_side, ds_cross], other_dq_ref)
    query_grads(keys, [ds_own, ds_two], dq_ref)


def near_first_sum_body(kept_ref, two_ref, two_pair_ref, out_ref):
    taken = two_ref[...].astype(f32) + two_pair_ref[...].astype(f32)
    out_ref[...] = kept_ref[...] + jnp.where(lax.axis_index("ctx") & 2 == 0, taken, 0.0)


def near_sums_body(share, kept_ref, pair_ref, here_ref, there_ref):
    each = here_ref.shape[0]
    group = lax.axis_index("head") // share
    for out_ref, at in ((here_ref, group), (there_ref, 1 - group)):
        rows = pl.ds(pl.multiple_of(at * each, each), each)
        out_ref[...] = (kept_ref[rows] + pair_ref[rows].astype(f32)).astype(out_ref.dtype)


def near_last_body(share, here_ref, taken_ref, dk_ref, dv_ref):
    width = dk_ref.shape[-1]
    group = lax.axis_index("head") // share
    for ref, place in ((here_ref, group), (taken_ref, 1 - group)):
        dk_ref[place] = ref[:, :width]
        dv_ref[place] = ref[:, width:]


def query_grads(keys, ds_refs, out_ref):
    heads, tokens, width = out_ref.shape
    turned = [key.T for key in keys]
    for h in range(heads):
        lanes = slice(h * tokens, (h + 1) * tokens)
        dqt = sum(dot(kt, ds[:, lanes]) for kt, ds in zip(turned, ds_refs))
        out_ref[h] = (dqt.T * width ** -0.5).astype(out_ref.dtype)


def own_terms_body(mine_coef, coef_ref, e_own, dp_own, e_side, dp_side, q_ref, g_ref,
                   other_q, other_g, own_ref, two_ref, ds_two, ds_cross, four_ref, ds_four,
                   terms_ref, dq_ref, other_dq_ref, ds_own, ds_side, p_ref, p_side):
    width = q_ref.shape[-1]
    own, two, four = [ref[:, :width] for ref in (own_ref, two_ref, four_ref)]
    slopes(e_side, dp_side, coef_ref[1:2], coef_ref[0:1], p_side, ds_side)
    query_grads([jnp.where(second_core(), four, own), two], [ds_side, ds_cross], other_dq_ref)
    slopes(e_own, dp_own, mine_coef[1:2], mine_coef[0:1], p_ref, ds_own)
    add_terms(terms_ref, ds_own, p_ref, q_ref, g_ref, True)

    @pl.when(jnp.logical_not(second_core()))
    def _():
        add_terms(terms_ref, ds_side, p_side, other_q, other_g, False)

    query_grads([own, two, four], [ds_own, ds_two, ds_four], dq_ref)


def add_grads_body(mine_ref, taken_ref, dq_ref):
    dq_ref[...] = (mine_ref[...] + taken_ref[...].astype(f32)).astype(dq_ref.dtype)


def first_sum_body(use, own_terms, back, out_ref):
    taken = jnp.where(use(lax.axis_index("ctx")), back[...].astype(f32), 0.0)
    out_ref[...] = own_terms[...] + taken


def sums_body(direct, uses, own_terms, *refs):
    backs, outs = refs[:len(uses)], refs[len(uses):]
    tokens = own_terms.shape[0]
    ctx = lax.axis_index("ctx")
    head = lax.axis_index("head")
    count = lax.axis_size("head")
    rows_each = tokens // count

    def total(rows):
        value = own_terms[rows]
        for back, use in zip(backs, uses):
            value = value + jnp.where(use(ctx), back[rows].astype(f32), 0.0)
        return value

    if not direct:
        outs[0][...] = total(slice(0, tokens)).astype(bf16)
        return
    for mask in range(count):
        place = jnp.bitwise_xor(head, mask)
        value = total(pl.ds(pl.multiple_of(place * rows_each, rows_each), rows_each))
        outs[mask][...] = value.astype(outs[mask].dtype)


def last_body(share, *refs):
    parts, (dk_ref, dv_ref) = refs[-3::-1], refs[-2:]
    width = dk_ref.shape[-1]
    group = lax.axis_index("head") // share
    for other in range(len(parts) // share):
        mine = parts[other * share:(other + 1) * share]
        value = sum(ref[...].astype(f32) for ref in mine).astype(bf16)
        place = jnp.bitwise_xor(group, other)
        dk_ref[place] = value[:, :width]
        dv_ref[place] = value[:, width:]


def per_device(queries, keys, values, d_out, doc_lengths):
    ctx_count, (heads, tokens, width) = lax.axis_size("ctx"), queries.shape
    middle = ctx_count // 2 * tokens
    split, starts, own = pl.pallas_call(
        functools.partial(prepare_body, GROUP // heads, middle),
        out_shape=(shape((1,), i32), shape((2, tokens), i32), shape((tokens, 2 * width), bf16)),
        in_specs=[pl.BlockSpec(memory_space=pl.ANY)] * 3,
        out_specs=(SMEM, VMEM, VMEM),
        scratch_shapes=[pltpu.SMEM(doc_lengths.shape, i32), pltpu.SemaphoreType.DMA((3,))],
        name="prepare",
    )(*[pltpu.with_memory_space_constraint(value, pltpu.HBM)
        for value in (doc_lengths, keys, values)])
    operands = (queries, d_out, own, starts)
    if ctx_count != 2 * REACH or lax.axis_size("head") * heads != 2 * GROUP or 2 * heads != GROUP:
        return gradients(True, *operands)
    return lax.switch(split[0], [functools.partial(gradients, True),
                                 functools.partial(gradients, False)], *operands)


def gradients(far, queries, d_out, own, starts):
    heads, tokens, width = queries.shape
    head_count = lax.axis_size("head")
    share = GROUP // heads
    groups = head_count // share
    rows = heads * tokens
    ctx = lax.axis_index("ctx")
    mutual = lax.axis_size("ctx") == 2 * REACH
    pair = (tokens, 2 * width)
    all_rows = (heads, tokens, width)
    stats = shape((3, rows), f32)
    wide = shape((tokens, rows), f32)
    half = shape((tokens, rows), bf16)
    half_scratch = pltpu.VMEM((tokens, rows), bf16)
    halves_scratch = pltpu.VMEM((2, tokens, rows), bf16)
    pair_scratch = pltpu.VMEM(pair, f32)

    if far:
        four = exchanged(own, "ctx", 4) if mutual else shifted(own, 4)
    two = [exchanged(own, "ctx", 2) if mutual else shifted(own, 2)]
    if far and mutual:
        two.append(exchanged(own, "ctx", 6))
    q, g, e_own, dp_own, stats_own = call(
        own_unit_body, "own_unit", [VMEM] * 4,
        (shape(all_rows, bf16), shape(all_rows, bf16), wide, wide, stats),
    )(starts, queries, d_out, own)
    other_q = exchanged(queries, "ctx", 1)
    other_g = exchanged(d_out, "ctx", 1)
    if far:
        four, stats_own = lax.optimization_barrier((four, stats_own))
        e_four, dp_four, stats_four = call(
            four_unit_body, "four_unit", [VMEM] * 4, (wide, wide, stats))(starts, q, g, four)
        other_q, stats_four = lax.optimization_barrier((other_q, stats_four))
        e_side, dp_side, stats_side = call(
            side_unit_body, "side_unit", [VMEM] * 5, (wide, wide, stats),
        )(starts, other_q, other_g, own, four)
    else:
        e_side, dp_side, stats_side = call(
            near_side_unit_body, "side_unit", [VMEM] * 4, (wide, wide, stats),
        )(starts, other_q, other_g, own)
    *two, stats_side, stats_own = lax.optimization_barrier((*two, stats_side, stats_own))
    mine_stats = (stats_own, stats_four) if far else (stats_own,)
    two = jnp.where(ctx & 2 == 2, *two) if len(two) == 2 else two[0]
    few = shape((4, rows), f32)
    e_cross, dp_cross, stats_cross, others = call(
        cross_unit_body, "cross_unit", [VMEM] * 5, (wide, wide, stats, few),
    )(starts, other_q, other_g, two, stats_side)
    taken_others = exchanged(others, "ctx", 1)
    e_two, dp_two, stats_two, mine = call(
        two_unit_body, "two_unit", [VMEM] * (4 + len(mine_stats)), (wide, wide, stats, few),
    )(starts, q, g, two, *mine_stats)
    taken_mine = exchanged(mine, "ctx", 1)
    mine_stats += (stats_two,)
    parts = ((e_four, dp_four) if far else (e_own, dp_own)) + (e_two, dp_two)
    mine_coef, ds_first, ds_two, first_part, two_part = call(
        functools.partial(my_terms_body, len(mine_stats)), "my_terms",
        [VMEM] * (8 + len(mine_stats)),
        (few, half, half, shape(pair, f32), shape(pair, f32)), (halves_scratch,),
    )(mine, taken_others, *mine_stats, *parts, q, g)
    other_sides = (other_q, other_g)
    last_stats = (others, taken_mine, stats_side, stats_cross)
    backs, uses = [], []
    if far:
        coef, four_terms = call(
            four_terms_body, "four_terms", [VMEM] * 9, (few, shape(pair, bf16)),
            (pair_scratch, half_scratch, half_scratch),
        )(*last_stats, e_side, dp_side, *other_sides, first_part)
        two_terms, ds_cross = call(
            two_terms_body, "two_terms", [VMEM] * 6, (shape(pair, bf16), half),
            (half_scratch, pair_scratch),
        )(coef, e_cross, dp_cross, *other_sides, two_part)
        backs.append(exchanged(four_terms, "ctx", 4) if mutual else shifted(four_terms, -4))
        uses.append((lambda i: i < 4) if mutual else (lambda i: True))
    else:
        slices = (tokens // 2, 2 * width)
        coef, two_kept, two_other, ds_cross = call(
            near_two_terms_body, "two_terms", [VMEM] * 9,
            (few, shape(slices, bf16), shape(slices, bf16), half), (half_scratch, pair_scratch),
        )(*last_stats, e_cross, dp_cross, *other_sides, two_part)
        two_pair = exchanged(two_other, ("ctx", "head"), 2 * head_count + 1)
        two_back = exchanged(two_kept, "ctx", 2)
        own_kept, own_other, ds_side = call(
            near_own_terms_body, "own_terms", [VMEM] * 6,
            (shape(slices, f32), shape(slices, bf16), half), (half_scratch, pair_scratch),
        )(coef, e_side, dp_side, *other_sides, first_part)
        own_pair = exchanged(own_other, "head", 1)
        my_grads, other_grads = call(
            near_grads_body, "query_grads", [VMEM] * 6,
            (shape(all_rows, f32), shape(all_rows, bf16)),
        )(own, two, ds_first, ds_two, ds_side, ds_cross)
        slice_dims = (tokens // head_count, 2 * width)
        own_kept, = call(
            near_first_sum_body, "first_sum", [VMEM] * 3, (shape(slices, f32),),
        )(own_kept, two_back, two_pair)
        kept, sent = call(
            functools.partial(near_sums_body, share), "sums", [VMEM] * 2,
            (shape(slice_dims, bf16),) * 2)(own_kept, own_pair)
        other_grads, kept = lax.optimization_barrier((other_grads, kept))
        taken_grads = exchanged(other_grads, "ctx", 1)
        d_queries, = call(
            add_grads_body, "add_grads", [VMEM] * 2, (shape(all_rows, bf16),),
        )(my_grads, taken_grads)
        last = exchanged(sent, "head", share)
        last, d_queries = lax.optimization_barrier((last, d_queries))
        d_keys, d_values = call(
            functools.partial(near_last_body, share), "last", [VMEM] * 2,
            (shape((groups, tokens // head_count, width), bf16),) * 2)(kept, last)
        return d_queries, d_keys, d_values
    backs.append(exchanged(two_terms, "ctx", 2) if mutual else shifted(two_terms, -2))
    uses.append((lambda i: i & 2 == 0) if mutual else (lambda i: True))
    if far and mutual:
        backs.append(exchanged(two_terms, "ctx", 6))
        uses.append(lambda i: i & 6 == 2)
    own_terms, my_grads, other_grads = call(
        own_terms_body, "own_terms", [VMEM] * 16,
        (shape(pair, f32), shape(all_rows, f32), shape(all_rows, bf16)),
        (half_scratch,) * 4,
    )(mine_coef, coef, e_own, dp_own, e_side, dp_side, q, g, *other_sides, own, two,
      ds_two, ds_cross, four, ds_first)
    own_terms, = call(
        functools.partial(first_sum_body, uses[0]), "first_sum", [VMEM] * 2,
        (shape(pair, f32),))(own_terms, backs[0])
    backs, uses = backs[1:], uses[1:]
    direct = head_count == 2 * share and share == 2
    slice_dims = (tokens // head_count, 2 * width)
    outs = ((shape(slice_dims, f32),) + (shape(slice_dims, bf16),) * (head_count - 1)
            if direct else (shape(pair, bf16),))
    sums = call(
        functools.partial(sums_body, direct, uses), "sums", [VMEM] * (1 + len(backs)), outs,
    )(own_terms, *backs)
    other_grads, kept = lax.optimization_barrier((other_grads, sums[0]))
    taken_grads = exchanged(other_grads, "ctx", 1)
    d_queries, = call(
        add_grads_body, "add_grads", [VMEM] * 2, (shape(all_rows, bf16),),
    )(my_grads, taken_grads)
    if direct:
        parts = [exchanged(sums[m], "head", m) for m in reversed(range(1, head_count))]
        parts.append(kept)
        *parts, d_queries = lax.optimization_barrier((*parts, d_queries))
        result_dims = (groups, tokens // head_count, width)
        d_keys, d_values = call(
            functools.partial(last_body, share), "last", [VMEM] * head_count,
            (shape(result_dims, bf16),) * 2)(*parts)
        return d_queries, d_keys, d_values
    slices = lax.all_to_all(kept.reshape(head_count, *slice_dims), "head", 0, 0)
    result = jnp.sum(slices.reshape(groups, share, *slice_dims).astype(f32), axis=1).astype(bf16)
    return d_queries, result[..., :width], result[..., width:]


def solution(mesh):
    placed = (
        P("head", "ctx", None),
        P(None, "ctx", None),
        P(None, "ctx", None),
        P("head", "ctx", None),
        P(),
    )
    return jax.shard_map(
        per_device,
        mesh=mesh,
        in_specs=placed,
        out_specs=(
            P("head", "ctx", None),
            P(None, ("ctx", "head"), None),
            P(None, ("ctx", "head"), None),
        ),
        check_vma=False,
    )
```

```python
import functools
import math

import jax
import jax.numpy as jnp
from jax import lax
from jax.experimental import pallas as pl
from jax.experimental.pallas import tpu as pltpu
from jax.sharding import PartitionSpec as P

GROUP = 8
REACH = 4
MASKED = -1e30
NT = (((1,), (1,)), ((), ()))
NN = (((1,), (0,)), ((), ()))
VMEM = pl.BlockSpec(memory_space=pltpu.VMEM)
SMEM = pl.BlockSpec(memory_space=pltpu.SMEM)
bf16, f32, i32 = jnp.bfloat16, jnp.float32, jnp.int32


def dot(a, b, dims=NN):
    return lax.dot_general(a, b, dims, preferred_element_type=f32)


def shape(dims, dtype):
    return jax.ShapeDtypeStruct(dims, dtype)


def call(body, name, in_specs, outs, scratch=()):
    return pl.pallas_call(
        body,
        out_shape=outs,
        in_specs=in_specs,
        out_specs=(VMEM,) * len(outs),
        scratch_shapes=scratch,
        compiler_params=pltpu.CompilerParams(vmem_limit_bytes=20 * 2**20),
        cost_estimate=pl.CostEstimate(flops=2**20, bytes_accessed=2**10, transcendentals=0),
        name=name,
    )


def shifted(block, distance):
    count = lax.axis_size("ctx")
    route = [(i - distance, i) for i in range(count) if 0 <= i - distance < count]
    return lax.ppermute(block, "ctx", route)


def exchanged(block, axis, mask):
    count = math.prod(lax.axis_size(name) for name in axis) if isinstance(axis, tuple) else (
        lax.axis_size(axis))
    return lax.ppermute(block, axis, [(i, i ^ mask) for i in range(count)])


def second_core():
    return lax.rem(lax.axis_index("ctx"), 2) == 1


def doc_starts(lengths_ref, block, tokens):
    row_pos = block * tokens + lax.broadcasted_iota(i32, (1, tokens), 1)
    starts = jnp.zeros((1, tokens), i32)
    end = jnp.int32(0)
    for d in range(lengths_ref.shape[0]):
        end = end + lengths_ref[d]
        starts = jnp.where(row_pos >= end, end, starts)
    return starts


def unit(pair, key_block, starts, q_ref, g_ref, e_ref, dp_ref, stats_ref, causal=False):
    heads, tokens, width = q_ref.shape
    factor = width ** -0.5 * math.log2(math.e)
    key_iota = lax.broadcasted_iota(i32, (tokens, 1), 0)
    allowed = key_block * tokens + key_iota >= starts
    if causal:
        allowed = allowed & (key_iota <= lax.broadcasted_iota(i32, (1, tokens), 1))
    for h in range(heads):
        lanes = slice(h * tokens, (h + 1) * tokens)
        s = jnp.where(allowed, dot(pair[:, :width], q_ref[h], NT), MASKED)
        top = jnp.max(s, axis=0, keepdims=True)
        e = jnp.exp2((s - top) * factor)
        dp = dot(pair[:, width:], g_ref[h], NT)
        e_ref[:, lanes] = e
        dp_ref[:, lanes] = dp
        stats_ref[0:1, lanes] = top
        stats_ref[1:2, lanes] = jnp.sum(e, axis=0, keepdims=True)
        stats_ref[2:3, lanes] = jnp.sum(e * dp, axis=0, keepdims=True)


def rows_of(ref, first=0):
    return [ref[first + row:first + row + 1] for row in range(3)]


def joined(parts, factor):
    top = functools.reduce(jnp.maximum, [part[0] for part in parts])
    gains = [jnp.exp2((part[0] - top) * factor) for part in parts]
    total = sum(gain * part[1] for gain, part in zip(gains, parts))
    weighted = sum(gain * part[2] for gain, part in zip(gains, parts))
    return top, total, weighted


def own_unit_body(starts_ref, q_in, g_in, own_ref, q_ref, g_ref, e_ref, dp_ref, stats_ref):
    q_ref[...] = q_in[...]
    g_ref[...] = g_in[...]
    unit(own_ref, lax.axis_index("ctx"), starts_ref[0:1], q_in, g_in, e_ref, dp_ref, stats_ref,
         causal=True)


def four_unit_body(starts_ref, q_ref, g_ref, four_ref, e_ref, dp_ref, stats_ref):
    here = lax.axis_index("ctx")
    unit(four_ref, here - 4, starts_ref[0:1], q_ref, g_ref, e_ref, dp_ref, stats_ref)


def side_unit_body(starts_ref, other_q, other_g, own_ref, four_ref, e_ref, dp_ref, stats_ref):
    side = jnp.where(second_core(), four_ref[...], own_ref[...])
    block = lax.axis_index("ctx") - jnp.where(second_core(), 4, 0)
    unit(side, block, starts_ref[1:2], other_q, other_g, e_ref, dp_ref, stats_ref)


def prepare_body(share, middle, lengths_in, keys_ref, values_ref,
                 split_ref, starts_ref, own_ref, lengths_ref, sems):
    tokens, width = keys_ref.shape[1:]
    group = lax.axis_index("head") // share
    lengths = pltpu.make_async_copy(lengths_in, lengths_ref, sems.at[0])
    copies = [
        pltpu.make_async_copy(keys_ref.at[group], own_ref.at[:, :width], sems.at[1]),
        pltpu.make_async_copy(values_ref.at[group], own_ref.at[:, width:], sems.at[2]),
    ]
    for copy in [lengths] + copies:
        copy.start()
    lengths.wait()
    end, split = jnp.int32(0), jnp.int32(0)
    for d in range(lengths_ref.shape[0]):
        end = end + lengths_ref[d]
        split = jnp.where(end == middle, 1, split)
    split_ref[0] = split
    here = lax.axis_index("ctx")
    starts_ref[0:1] = doc_starts(lengths_ref, here, tokens)
    starts_ref[1:2] = doc_starts(lengths_ref, jnp.bitwise_xor(here, 1), tokens)
    for copy in copies:
        copy.wait()


def near_side_unit_body(starts_ref, other_q, other_g, own_ref, e_ref, dp_ref, stats_ref):
    block = jnp.where(second_core(), -1, lax.axis_index("ctx"))
    unit(own_ref, block, starts_ref[1:2], other_q, other_g, e_ref, dp_ref, stats_ref)


def write_rows(ref, values):
    for row, value in enumerate(values):
        ref[row:row + 1] = value


def cross_unit_body(starts_ref, other_q, other_g, two_ref, stats_side,
                    e_ref, dp_ref, stats_ref, others_ref):
    factor = other_q.shape[-1] ** -0.5 * math.log2(math.e)
    unit(two_ref, lax.axis_index("ctx") - 2, starts_ref[1:2], other_q, other_g,
         e_ref, dp_ref, stats_ref)
    write_rows(others_ref, joined([rows_of(stats_side), rows_of(stats_ref)], factor))
    others_ref[3:4] = jnp.zeros((1, others_ref.shape[1]), f32)


def two_unit_body(starts_ref, q_ref, g_ref, two_ref, *refs):
    earlier, (e_ref, dp_ref, stats_ref, mine_ref) = refs[:-4], refs[-4:]
    factor = q_ref.shape[-1] ** -0.5 * math.log2(math.e)
    unit(two_ref, lax.axis_index("ctx") - 2, starts_ref[0:1], q_ref, g_ref,
         e_ref, dp_ref, stats_ref)
    write_rows(mine_ref, joined([rows_of(ref) for ref in earlier + (stats_ref,)], factor))
    mine_ref[3:4] = jnp.zeros((1, mine_ref.shape[1]), f32)


def coefficients(here_ref, taken_ref, stats_refs, width):
    factor = width ** -0.5 * math.log2(math.e)
    top, total, weighted = joined([rows_of(here_ref), rows_of(taken_ref)], factor)
    inverse = 1.0 / total
    return [weighted * inverse] + [
        jnp.exp2((ref[0:1] - top) * factor) * inverse for ref in stats_refs]


def slopes(e_ref, dp_ref, gain, delta, p_ref, ds_ref):
    p = e_ref[...] * gain
    p_ref[...] = p.astype(bf16)
    ds_ref[...] = (p * (dp_ref[...] - delta)).astype(bf16)


def flat(ref):
    heads, tokens, width = ref.shape
    return ref[...].reshape(heads * tokens, width)


def add_terms(sum_ref, ds_ref, p_ref, q_ref, g_ref, fresh):
    width = q_ref.shape[-1]
    dk = dot(ds_ref[...], flat(q_ref)) * width ** -0.5
    dv = dot(p_ref[...], flat(g_ref))
    if fresh:
        sum_ref[:, :width] = dk
        sum_ref[:, width:] = dv
    else:
        sum_ref[:, :width] += dk
        sum_ref[:, width:] += dv


def my_terms_body(count, mine_ref, taken_ref, *refs):
    stats, refs = refs[:count], refs[count:]
    parts, (q_ref, g_ref), refs = refs[:4], refs[4:6], refs[6:]
    coef_ref, ds_refs, sums, p_ref = refs[0], refs[1:3], refs[3:5], refs[5]
    coefs = coefficients(mine_ref, taken_ref, stats, q_ref.shape[-1])
    write_rows(coef_ref, coefs)
    for at in range(2):
        slopes(parts[2 * at], parts[2 * at + 1], coefs[count - 1 + at], coefs[0], p_ref.at[at],
               ds_refs[at])
        add_terms(sums[at], ds_refs[at], p_ref.at[at], q_ref, g_ref, True)


def four_terms_body(others_ref, taken_ref, stats_side, stats_cross, e_side, dp_side,
                    other_q, other_g, part_ref, coef_ref, terms_ref, sum_ref, p_ref, ds_ref):
    coefs = coefficients(others_ref, taken_ref, (stats_side, stats_cross), other_q.shape[-1])
    write_rows(coef_ref, coefs)
    sum_ref[...] = part_ref[...]

    @pl.when(second_core())
    def _():
        slopes(e_side, dp_side, coef_ref[1:2], coef_ref[0:1], p_ref, ds_ref)
        add_terms(sum_ref, ds_ref, p_ref, other_q, other_g, False)

    terms_ref[...] = sum_ref[...].astype(bf16)


def two_terms_body(coef_ref, e_cross, dp_cross, other_q, other_g, part_ref,
                   terms_ref, ds_cross, p_ref, sum_ref):
    slopes(e_cross, dp_cross, coef_ref[2:3], coef_ref[0:1], p_ref, ds_cross)
    sum_ref[...] = part_ref[...]
    add_terms(sum_ref, ds_cross, p_ref, other_q, other_g, False)
    terms_ref[...] = sum_ref[...].astype(bf16)


def slice_rows(ref, other):
    count = lax.axis_size("head")
    each = ref.shape[0] // count
    parity = jnp.bitwise_xor(lax.rem(lax.axis_index("head"), 2), other)
    return [ref[pl.ds(pl.multiple_of((2 * at + parity) * each, each), each)]
            for at in range(count // 2)]


def halve(sum_ref, kept_ref, given_ref):
    each = sum_ref.shape[0] // lax.axis_size("head")
    for other, out_ref in enumerate((kept_ref, given_ref)):
        for at, value in enumerate(slice_rows(sum_ref, other)):
            out_ref[at * each:(at + 1) * each] = value.astype(out_ref.dtype)


def near_two_terms_body(others_ref, taken_ref, stats_side, stats_cross, e_cross, dp_cross,
                        other_q, other_g, part_ref,
                        coef_ref, kept_ref, other_ref, ds_cross, p_ref, sum_ref):
    coefs = coefficients(others_ref, taken_ref, (stats_side, stats_cross), other_q.shape[-1])
    write_rows(coef_ref, coefs)
    slopes(e_cross, dp_cross, coefs[2], coefs[0], p_ref, ds_cross)
    sum_ref[...] = part_ref[...]
    add_terms(sum_ref, ds_cross, p_ref, other_q, other_g, False)
    halve(sum_ref, kept_ref, other_ref)


def near_own_terms_body(coef_ref, e_side, dp_side, other_q, other_g, part_ref,
                        kept_ref, other_ref, ds_side, p_ref, sum_ref):
    slopes(e_side, dp_side, coef_ref[1:2], coef_ref[0:1], p_ref, ds_side)
    sum_ref[...] = part_ref[...]

    @pl.when(jnp.logical_not(second_core()))
    def _():
        add_terms(sum_ref, ds_side, p_ref, other_q, other_g, False)

    halve(sum_ref, kept_ref, other_ref)


def far_four_terms_body(others_ref, taken_ref, stats_side, stats_cross, e_side, dp_side,
                        other_q, other_g, part_ref,
                        coef_ref, kept_ref, other_ref, sum_ref, p_ref, ds_ref):
    coefs = coefficients(others_ref, taken_ref, (stats_side, stats_cross), other_q.shape[-1])
    write_rows(coef_ref, coefs)
    sum_ref[...] = part_ref[...]

    @pl.when(second_core())
    def _():
        slopes(e_side, dp_side, coef_ref[1:2], coef_ref[0:1], p_ref, ds_ref)
        add_terms(sum_ref, ds_ref, p_ref, other_q, other_g, False)

    halve(sum_ref, kept_ref, other_ref)


def far_two_terms_body(coef_ref, e_cross, dp_cross, other_q, other_g, part_ref,
                       kept_ref, other_ref, ds_cross, p_ref, sum_ref):
    slopes(e_cross, dp_cross, coef_ref[2:3], coef_ref[0:1], p_ref, ds_cross)
    sum_ref[...] = part_ref[...]
    add_terms(sum_ref, ds_cross, p_ref, other_q, other_g, False)
    halve(sum_ref, kept_ref, other_ref)


def far_own_terms_body(mine_coef, coef_ref, e_own, dp_own, e_side, dp_side, q_ref, g_ref,
                       other_q, other_g,
                       kept_ref, other_ref, ds_own, ds_side, p_ref, p_side, sum_ref):
    slopes(e_own, dp_own, mine_coef[1:2], mine_coef[0:1], p_ref, ds_own)
    add_terms(sum_ref, ds_own, p_ref, q_ref, g_ref, True)
    slopes(e_side, dp_side, coef_ref[1:2], coef_ref[0:1], p_side, ds_side)

    @pl.when(jnp.logical_not(second_core()))
    def _():
        add_terms(sum_ref, ds_side, p_side, other_q, other_g, False)

    halve(sum_ref, kept_ref, other_ref)


def grads_body(own_ref, two_ref, ds_own, ds_two, ds_side, ds_cross, *refs):
    four_refs, (dq_ref, other_dq_ref) = refs[:-2], refs[-2:]
    width = dq_ref.shape[-1]
    keys, slope_refs = [own_ref[:, :width], two_ref[:, :width]], [ds_own, ds_two]
    side = keys[0]
    if four_refs:
        keys.append(four_refs[0][:, :width])
        slope_refs.append(four_refs[1])
        side = jnp.where(second_core(), keys[2], side)
    query_grads([side, keys[1]], [ds_side, ds_cross], other_dq_ref)
    query_grads(keys, slope_refs, dq_ref)


def add_body(use, sum_ref, back_ref, out_ref):
    taken = back_ref[...].astype(f32)
    if use is not None:
        taken = jnp.where(use(lax.axis_index("ctx")), taken, 0.0)
    out_ref[...] = sum_ref[...] + taken


def relay_body(kept_ref, four_ref, two_ref, two_pair_ref, out_ref, sent_ref):
    ctx = lax.axis_index("ctx")
    taken = two_ref[...].astype(f32) + two_pair_ref[...].astype(f32)
    out_ref[...] = kept_ref[...] + jnp.where(ctx & 2 == 0, taken, 0.0)
    sent_ref[...] = (four_ref[...] + jnp.where(ctx & 6 == 6, taken, 0.0)).astype(bf16)


def near_first_sum_body(kept_ref, two_ref, two_pair_ref, out_ref):
    taken = two_ref[...].astype(f32) + two_pair_ref[...].astype(f32)
    out_ref[...] = kept_ref[...] + jnp.where(lax.axis_index("ctx") & 2 == 0, taken, 0.0)


def halves_sum_body(share, use, kept_ref, back_ref, here_ref, there_ref):
    each = here_ref.shape[0]
    group = lax.axis_index("head") // share
    for out_ref, at in ((here_ref, group), (there_ref, 1 - group)):
        rows = pl.ds(pl.multiple_of(at * each, each), each)
        taken = back_ref[rows].astype(f32)
        if use is not None:
            taken = jnp.where(use(lax.axis_index("ctx")), taken, 0.0)
        out_ref[...] = (kept_ref[rows] + taken).astype(out_ref.dtype)


def last_body(share, here_ref, taken_ref, dk_ref, dv_ref):
    width = dk_ref.shape[-1]
    group = lax.axis_index("head") // share
    for ref, place in ((here_ref, group), (taken_ref, 1 - group)):
        dk_ref[place] = ref[:, :width]
        dv_ref[place] = ref[:, width:]


def query_grads(keys, ds_refs, out_ref):
    heads, tokens, width = out_ref.shape
    turned = [key.T for key in keys]
    for h in range(heads):
        lanes = slice(h * tokens, (h + 1) * tokens)
        dqt = sum(dot(kt, ds[:, lanes]) for kt, ds in zip(turned, ds_refs))
        out_ref[h] = (dqt.T * width ** -0.5).astype(out_ref.dtype)


def own_terms_body(mine_coef, coef_ref, e_own, dp_own, e_side, dp_side, q_ref, g_ref,
                   other_q, other_g, own_ref, two_ref, ds_two, ds_cross, four_ref, ds_four,
                   terms_ref, dq_ref, other_dq_ref, ds_own, ds_side, p_ref, p_side):
    width = q_ref.shape[-1]
    own, two, four = [ref[:, :width] for ref in (own_ref, two_ref, four_ref)]
    slopes(e_side, dp_side, coef_ref[1:2], coef_ref[0:1], p_side, ds_side)
    query_grads([jnp.where(second_core(), four, own), two], [ds_side, ds_cross], other_dq_ref)
    slopes(e_own, dp_own, mine_coef[1:2], mine_coef[0:1], p_ref, ds_own)
    add_terms(terms_ref, ds_own, p_ref, q_ref, g_ref, True)

    @pl.when(jnp.logical_not(second_core()))
    def _():
        add_terms(terms_ref, ds_side, p_side, other_q, other_g, False)

    query_grads([own, two, four], [ds_own, ds_two, ds_four], dq_ref)


def add_grads_body(mine_ref, taken_ref, dq_ref):
    dq_ref[...] = (mine_ref[...] + taken_ref[...].astype(f32)).astype(dq_ref.dtype)


def sums_body(own_terms, four_back, two_back, out_ref):
    taken = four_back[...].astype(f32) + two_back[...].astype(f32)
    out_ref[...] = (own_terms[...] + taken).astype(bf16)


def per_device(queries, keys, values, d_out, doc_lengths):
    ctx_count, (heads, tokens, width) = lax.axis_size("ctx"), queries.shape
    middle = ctx_count // 2 * tokens
    split, starts, own = pl.pallas_call(
        functools.partial(prepare_body, GROUP // heads, middle),
        out_shape=(shape((1,), i32), shape((2, tokens), i32), shape((tokens, 2 * width), bf16)),
        in_specs=[pl.BlockSpec(memory_space=pl.ANY)] * 3,
        out_specs=(SMEM, VMEM, VMEM),
        scratch_shapes=[pltpu.SMEM(doc_lengths.shape, i32), pltpu.SemaphoreType.DMA((3,))],
        name="prepare",
    )(*[pltpu.with_memory_space_constraint(value, pltpu.HBM)
        for value in (doc_lengths, keys, values)])
    operands = (queries, d_out, own, starts)
    if ctx_count != 2 * REACH or lax.axis_size("head") * heads != 2 * GROUP or 2 * heads != GROUP:
        return gradients(True, *operands)
    return lax.switch(split[0], [functools.partial(gradients, True),
                                 functools.partial(gradients, False)], *operands)


def gradients(far, queries, d_out, own, starts):
    heads, tokens, width = queries.shape
    head_count = lax.axis_size("head")
    share = GROUP // heads
    groups = head_count // share
    rows = heads * tokens
    ctx = lax.axis_index("ctx")
    mutual = lax.axis_size("ctx") == 2 * REACH and share == groups == 2
    pair = (tokens, 2 * width)
    all_rows = (heads, tokens, width)
    stats = shape((3, rows), f32)
    wide = shape((tokens, rows), f32)
    half = shape((tokens, rows), bf16)
    half_scratch = pltpu.VMEM((tokens, rows), bf16)
    halves_scratch = pltpu.VMEM((2, tokens, rows), bf16)
    pair_scratch = pltpu.VMEM(pair, f32)

    if far:
        four = exchanged(own, "ctx", 4) if mutual else shifted(own, 4)
    two = [exchanged(own, "ctx", 2) if mutual else shifted(own, 2)]
    if far and mutual:
        two.append(exchanged(own, "ctx", 6))
    q, g, e_own, dp_own, stats_own = call(
        own_unit_body, "own_unit", [VMEM] * 4,
        (shape(all_rows, bf16), shape(all_rows, bf16), wide, wide, stats),
    )(starts, queries, d_out, own)
    other_q = exchanged(queries, "ctx", 1)
    other_g = exchanged(d_out, "ctx", 1)
    if far:
        four, stats_own = lax.optimization_barrier((four, stats_own))
        e_four, dp_four, stats_four = call(
            four_unit_body, "four_unit", [VMEM] * 4, (wide, wide, stats))(starts, q, g, four)
        other_q, stats_four = lax.optimization_barrier((other_q, stats_four))
        e_side, dp_side, stats_side = call(
            side_unit_body, "side_unit", [VMEM] * 5, (wide, wide, stats),
        )(starts, other_q, other_g, own, four)
    else:
        e_side, dp_side, stats_side = call(
            near_side_unit_body, "side_unit", [VMEM] * 4, (wide, wide, stats),
        )(starts, other_q, other_g, own)
    *two, stats_side, stats_own = lax.optimization_barrier((*two, stats_side, stats_own))
    mine_stats = (stats_own, stats_four) if far else (stats_own,)
    two = jnp.where(ctx & 2 == 2, *two) if len(two) == 2 else two[0]
    few = shape((4, rows), f32)
    e_cross, dp_cross, stats_cross, others = call(
        cross_unit_body, "cross_unit", [VMEM] * 5, (wide, wide, stats, few),
    )(starts, other_q, other_g, two, stats_side)
    taken_others = exchanged(others, "ctx", 1)
    e_two, dp_two, stats_two, mine = call(
        two_unit_body, "two_unit", [VMEM] * (4 + len(mine_stats)), (wide, wide, stats, few),
    )(starts, q, g, two, *mine_stats)
    taken_mine = exchanged(mine, "ctx", 1)
    mine_stats += (stats_two,)
    parts = ((e_four, dp_four) if far else (e_own, dp_own)) + (e_two, dp_two)
    mine_coef, ds_first, ds_two, first_part, two_part = call(
        functools.partial(my_terms_body, len(mine_stats)), "my_terms",
        [VMEM] * (8 + len(mine_stats)),
        (few, half, half, shape(pair, f32), shape(pair, f32)), (halves_scratch,),
    )(mine, taken_others, *mine_stats, *parts, q, g)
    other_sides = (other_q, other_g)
    last_stats = (others, taken_mine, stats_side, stats_cross)
    slices = (tokens // 2, 2 * width)
    slice_dims = (tokens // head_count, 2 * width)
    if not mutual:
        coef, four_terms = call(
            four_terms_body, "four_terms", [VMEM] * 9, (few, shape(pair, bf16)),
            (pair_scratch, half_scratch, half_scratch),
        )(*last_stats, e_side, dp_side, *other_sides, first_part)
        two_terms, ds_cross = call(
            two_terms_body, "two_terms", [VMEM] * 6, (shape(pair, bf16), half),
            (half_scratch, pair_scratch),
        )(coef, e_cross, dp_cross, *other_sides, two_part)
        backs = [shifted(four_terms, -4), shifted(two_terms, -2)]
        own_terms, my_grads, other_grads = call(
            own_terms_body, "own_terms", [VMEM] * 16,
            (shape(pair, f32), shape(all_rows, f32), shape(all_rows, bf16)),
            (half_scratch,) * 4,
        )(mine_coef, coef, e_own, dp_own, e_side, dp_side, q, g, *other_sides, own, two,
          ds_two, ds_cross, four, ds_first)
        taken_grads = exchanged(other_grads, "ctx", 1)
        d_queries, = call(
            add_grads_body, "add_grads", [VMEM] * 2, (shape(all_rows, bf16),),
        )(my_grads, taken_grads)
        sums, = call(sums_body, "sums", [VMEM] * 3, (shape(pair, bf16),))(own_terms, *backs)
        pieces = lax.all_to_all(sums.reshape(head_count, *slice_dims), "head", 0, 0)
        result = jnp.sum(
            pieces.reshape(groups, share, *slice_dims).astype(f32), axis=1).astype(bf16)
        return d_queries, result[..., :width], result[..., width:]

    halves = (shape(slices, bf16), shape(slices, bf16))
    part = shape(slices, f32)
    if far:
        coef, four_kept, four_other = call(
            far_four_terms_body, "four_terms", [VMEM] * 9, (few, part, halves[1]),
            (pair_scratch, half_scratch, half_scratch),
        )(*last_stats, e_side, dp_side, *other_sides, first_part)
        four_pair = exchanged(four_other, ("ctx", "head"), 4 * head_count + 1)
        two_kept, two_other, ds_cross = call(
            far_two_terms_body, "two_terms", [VMEM] * 6, halves + (half,),
            (half_scratch, pair_scratch),
        )(coef, e_cross, dp_cross, *other_sides, two_part)
    else:
        coef, two_kept, two_other, ds_cross = call(
            near_two_terms_body, "two_terms", [VMEM] * 9, (few,) + halves + (half,),
            (half_scratch, pair_scratch),
        )(*last_stats, e_cross, dp_cross, *other_sides, two_part)
    two_back = exchanged(two_kept, "ctx", 2)
    two_pair = exchanged(two_other, ("ctx", "head"), 2 * head_count + 1)
    if far:
        own_kept, own_other, ds_own, ds_side = call(
            far_own_terms_body, "own_terms", [VMEM] * 10, (part, halves[1], half, half),
            (half_scratch, half_scratch, pair_scratch),
        )(mine_coef, coef, e_own, dp_own, e_side, dp_side, q, g, *other_sides)
    else:
        ds_own = ds_first
        own_kept, own_other, ds_side = call(
            near_own_terms_body, "own_terms", [VMEM] * 6, (part, halves[1], half),
            (half_scratch, pair_scratch),
        )(coef, e_side, dp_side, *other_sides, first_part)
    own_pair = exchanged(own_other, "head", 1)
    four_refs = (four, ds_first) if far else ()
    my_grads, other_grads = call(
        grads_body, "query_grads", [VMEM] * (6 + len(four_refs)),
        (shape(all_rows, f32), shape(all_rows, bf16)),
    )(own, two, ds_own, ds_two, ds_side, ds_cross, *four_refs)
    owns_four = lambda i: i < 4
    if far:
        own_kept, = call(functools.partial(add_body, owns_four), "add_four", [VMEM] * 2,
                         (part,))(own_kept, four_pair)
        own_kept, relayed = call(
            relay_body, "relay", [VMEM] * 4, (part, halves[0]),
        )(own_kept, four_kept, two_back, two_pair)
        four_back = exchanged(relayed, "ctx", 4)
        own_kept, = call(functools.partial(add_body, None), "add_pair", [VMEM] * 2,
                         (part,))(own_kept, own_pair)
        final, use = four_back, owns_four
    else:
        own_kept, = call(
            near_first_sum_body, "first_sum", [VMEM] * 3, (part,),
        )(own_kept, two_back, two_pair)
        final, use = own_pair, None
    kept, sent = call(
        functools.partial(halves_sum_body, share, use), "sums", [VMEM] * 2,
        (shape(slice_dims, bf16),) * 2)(own_kept, final)
    other_grads, kept = lax.optimization_barrier((other_grads, kept))
    taken_grads = exchanged(other_grads, "ctx", 1)
    d_queries, = call(
        add_grads_body, "add_grads", [VMEM] * 2, (shape(all_rows, bf16),),
    )(my_grads, taken_grads)
    last = exchanged(sent, "head", share)
    last, d_queries = lax.optimization_barrier((last, d_queries))
    d_keys, d_values = call(
        functools.partial(last_body, share), "last", [VMEM] * 2,
        (shape((groups, tokens // head_count, width), bf16),) * 2)(kept, last)
    return d_queries, d_keys, d_values


def solution(mesh):
    placed = (
        P("head", "ctx", None),
        P(None, "ctx", None),
        P(None, "ctx", None),
        P("head", "ctx", None),
        P(),
    )
    return jax.shard_map(
        per_device,
        mesh=mesh,
        in_specs=placed,
        out_specs=(
            P("head", "ctx", None),
            P(None, ("ctx", "head"), None),
            P(None, ("ctx", "head"), None),
        ),
        check_vma=False,
    )
```

```python
import functools
import math

import jax
import jax.numpy as jnp
from jax import lax
from jax.experimental import pallas as pl
from jax.experimental.pallas import tpu as pltpu
from jax.sharding import PartitionSpec as P

GROUP = 8
REACH = 4
MASKED = -1e30
NT = (((1,), (1,)), ((), ()))
NN = (((1,), (0,)), ((), ()))
VMEM = pl.BlockSpec(memory_space=pltpu.VMEM)
SMEM = pl.BlockSpec(memory_space=pltpu.SMEM)
bf16, f32, i32 = jnp.bfloat16, jnp.float32, jnp.int32


def dot(a, b, dims=NN):
    return lax.dot_general(a, b, dims, preferred_element_type=f32)


def shape(dims, dtype):
    return jax.ShapeDtypeStruct(dims, dtype)


def call(body, name, in_specs, outs, scratch=()):
    return pl.pallas_call(
        body,
        out_shape=outs,
        in_specs=in_specs,
        out_specs=(VMEM,) * len(outs),
        scratch_shapes=scratch,
        compiler_params=pltpu.CompilerParams(vmem_limit_bytes=20 * 2**20),
        cost_estimate=pl.CostEstimate(flops=2**20, bytes_accessed=2**10, transcendentals=0),
        name=name,
    )


def shifted(block, distance):
    count = lax.axis_size("ctx")
    route = [(i - distance, i) for i in range(count) if 0 <= i - distance < count]
    return lax.ppermute(block, "ctx", route)


def exchanged(block, axis, mask):
    count = math.prod(lax.axis_size(name) for name in axis) if isinstance(axis, tuple) else (
        lax.axis_size(axis))
    return lax.ppermute(block, axis, [(i, i ^ mask) for i in range(count)])


def second_core():
    return lax.rem(lax.axis_index("ctx"), 2) == 1


def doc_starts(lengths_ref, block, tokens):
    row_pos = block * tokens + lax.broadcasted_iota(i32, (1, tokens), 1)
    starts = jnp.zeros((1, tokens), i32)
    end = jnp.int32(0)
    for d in range(lengths_ref.shape[0]):
        end = end + lengths_ref[d]
        starts = jnp.where(row_pos >= end, end, starts)
    return starts


def unit(pair, key_block, starts, q_ref, g_ref, e_ref, dp_ref, stats_ref, causal=False):
    heads, tokens, width = q_ref.shape
    factor = width ** -0.5 * math.log2(math.e)
    key_iota = lax.broadcasted_iota(i32, (tokens, 1), 0)
    allowed = key_block * tokens + key_iota >= starts
    if causal:
        allowed = allowed & (key_iota <= lax.broadcasted_iota(i32, (1, tokens), 1))
    for h in range(heads):
        lanes = slice(h * tokens, (h + 1) * tokens)
        s = jnp.where(allowed, dot(pair[:, :width], q_ref[h], NT), MASKED)
        top = jnp.max(s, axis=0, keepdims=True)
        e = jnp.exp2((s - top) * factor)
        dp = dot(pair[:, width:], g_ref[h], NT)
        e_ref[:, lanes] = e
        dp_ref[:, lanes] = dp
        stats_ref[0:1, lanes] = top
        stats_ref[1:2, lanes] = jnp.sum(e, axis=0, keepdims=True)
        stats_ref[2:3, lanes] = jnp.sum(e * dp, axis=0, keepdims=True)


def rows_of(ref, first=0):
    return [ref[first + row:first + row + 1] for row in range(3)]


def joined(parts, factor):
    top = functools.reduce(jnp.maximum, [part[0] for part in parts])
    gains = [jnp.exp2((part[0] - top) * factor) for part in parts]
    total = sum(gain * part[1] for gain, part in zip(gains, parts))
    weighted = sum(gain * part[2] for gain, part in zip(gains, parts))
    return top, total, weighted


def own_unit_body(starts_ref, q_in, g_in, own_ref, q_ref, g_ref, e_ref, dp_ref, stats_ref):
    q_ref[...] = q_in[...]
    g_ref[...] = g_in[...]
    unit(own_ref, lax.axis_index("ctx"), starts_ref[0:1], q_in, g_in, e_ref, dp_ref, stats_ref,
         causal=True)


def four_unit_body(starts_ref, q_ref, g_ref, four_ref, e_ref, dp_ref, stats_ref):
    here = lax.axis_index("ctx")
    unit(four_ref, here - 4, starts_ref[0:1], q_ref, g_ref, e_ref, dp_ref, stats_ref)


def side_unit_body(starts_ref, other_q, other_g, own_ref, four_ref, e_ref, dp_ref, stats_ref):
    side = jnp.where(second_core(), four_ref[...], own_ref[...])
    block = lax.axis_index("ctx") - jnp.where(second_core(), 4, 0)
    unit(side, block, starts_ref[1:2], other_q, other_g, e_ref, dp_ref, stats_ref)


def prepare_body(share, middle, lengths_in, keys_ref, values_ref,
                 split_ref, starts_ref, own_ref, lengths_ref, sems):
    tokens, width = keys_ref.shape[1:]
    group = lax.axis_index("head") // share
    lengths = pltpu.make_async_copy(lengths_in, lengths_ref, sems.at[0])
    copies = [
        pltpu.make_async_copy(keys_ref.at[group], own_ref.at[:, :width], sems.at[1]),
        pltpu.make_async_copy(values_ref.at[group], own_ref.at[:, width:], sems.at[2]),
    ]
    for copy in [lengths] + copies:
        copy.start()
    lengths.wait()
    end, split = jnp.int32(0), jnp.int32(0)
    for d in range(lengths_ref.shape[0]):
        end = end + lengths_ref[d]
        split = jnp.where(end == middle, 1, split)
    split_ref[0] = split
    here = lax.axis_index("ctx")
    starts_ref[0:1] = doc_starts(lengths_ref, here, tokens)
    starts_ref[1:2] = doc_starts(lengths_ref, jnp.bitwise_xor(here, 1), tokens)
    for copy in copies:
        copy.wait()


def near_side_unit_body(starts_ref, other_q, other_g, own_ref, e_ref, dp_ref, stats_ref):
    block = jnp.where(second_core(), -1, lax.axis_index("ctx"))
    unit(own_ref, block, starts_ref[1:2], other_q, other_g, e_ref, dp_ref, stats_ref)


def write_rows(ref, values):
    for row, value in enumerate(values):
        ref[row:row + 1] = value


def cross_unit_body(starts_ref, other_q, other_g, two_ref, stats_side,
                    e_ref, dp_ref, stats_ref, others_ref):
    factor = other_q.shape[-1] ** -0.5 * math.log2(math.e)
    unit(two_ref, lax.axis_index("ctx") - 2, starts_ref[1:2], other_q, other_g,
         e_ref, dp_ref, stats_ref)
    write_rows(others_ref, joined([rows_of(stats_side), rows_of(stats_ref)], factor))
    others_ref[3:4] = jnp.zeros((1, others_ref.shape[1]), f32)


def two_unit_body(starts_ref, q_ref, g_ref, two_ref, *refs):
    earlier, (e_ref, dp_ref, stats_ref, mine_ref) = refs[:-4], refs[-4:]
    factor = q_ref.shape[-1] ** -0.5 * math.log2(math.e)
    unit(two_ref, lax.axis_index("ctx") - 2, starts_ref[0:1], q_ref, g_ref,
         e_ref, dp_ref, stats_ref)
    write_rows(mine_ref, joined([rows_of(ref) for ref in earlier + (stats_ref,)], factor))
    mine_ref[3:4] = jnp.zeros((1, mine_ref.shape[1]), f32)


def coefficients(here_ref, taken_ref, stats_refs, width):
    factor = width ** -0.5 * math.log2(math.e)
    top, total, weighted = joined([rows_of(here_ref), rows_of(taken_ref)], factor)
    inverse = 1.0 / total
    return [weighted * inverse] + [
        jnp.exp2((ref[0:1] - top) * factor) * inverse for ref in stats_refs]


def slopes(e_ref, dp_ref, gain, delta, p_ref, ds_ref):
    p = e_ref[...] * gain
    p_ref[...] = p.astype(bf16)
    ds_ref[...] = (p * (dp_ref[...] - delta)).astype(bf16)


def flat(ref):
    heads, tokens, width = ref.shape
    return ref[...].reshape(heads * tokens, width)


def add_terms(sum_ref, ds_ref, p_ref, q_ref, g_ref, fresh):
    width = q_ref.shape[-1]
    dk = dot(ds_ref[...], flat(q_ref)) * width ** -0.5
    dv = dot(p_ref[...], flat(g_ref))
    if fresh:
        sum_ref[:, :width] = dk
        sum_ref[:, width:] = dv
    else:
        sum_ref[:, :width] += dk
        sum_ref[:, width:] += dv


def my_terms_body(count, mine_ref, taken_ref, *refs):
    stats, refs = refs[:count], refs[count:]
    parts, (q_ref, g_ref), refs = refs[:4], refs[4:6], refs[6:]
    coef_ref, ds_refs, sums, p_ref = refs[0], refs[1:3], refs[3:5], refs[5]
    coefs = coefficients(mine_ref, taken_ref, stats, q_ref.shape[-1])
    write_rows(coef_ref, coefs)
    for at in range(2):
        slopes(parts[2 * at], parts[2 * at + 1], coefs[count - 1 + at], coefs[0], p_ref.at[at],
               ds_refs[at])
        add_terms(sums[at], ds_refs[at], p_ref.at[at], q_ref, g_ref, True)


def four_terms_body(others_ref, taken_ref, stats_side, stats_cross, e_side, dp_side,
                    other_q, other_g, part_ref, coef_ref, terms_ref, sum_ref, p_ref, ds_ref):
    coefs = coefficients(others_ref, taken_ref, (stats_side, stats_cross), other_q.shape[-1])
    write_rows(coef_ref, coefs)
    sum_ref[...] = part_ref[...]

    @pl.when(second_core())
    def _():
        slopes(e_side, dp_side, coef_ref[1:2], coef_ref[0:1], p_ref, ds_ref)
        add_terms(sum_ref, ds_ref, p_ref, other_q, other_g, False)

    terms_ref[...] = sum_ref[...].astype(bf16)


def two_terms_body(coef_ref, e_cross, dp_cross, other_q, other_g, part_ref,
                   terms_ref, ds_cross, p_ref, sum_ref):
    slopes(e_cross, dp_cross, coef_ref[2:3], coef_ref[0:1], p_ref, ds_cross)
    sum_ref[...] = part_ref[...]
    add_terms(sum_ref, ds_cross, p_ref, other_q, other_g, False)
    terms_ref[...] = sum_ref[...].astype(bf16)


def slice_rows(ref, other):
    count = lax.axis_size("head")
    each = ref.shape[0] // count
    parity = jnp.bitwise_xor(lax.rem(lax.axis_index("head"), 2), other)
    return [ref[pl.ds(pl.multiple_of((2 * at + parity) * each, each), each)]
            for at in range(count // 2)]


def halve(sum_ref, kept_ref, given_ref):
    each = sum_ref.shape[0] // lax.axis_size("head")
    for other, out_ref in enumerate((kept_ref, given_ref)):
        for at, value in enumerate(slice_rows(sum_ref, other)):
            out_ref[at * each:(at + 1) * each] = value.astype(out_ref.dtype)


def halved_two_terms_body(others_ref, taken_ref, stats_side, stats_cross, e_cross, dp_cross,
                        other_q, other_g, part_ref,
                        coef_ref, kept_ref, other_ref, ds_cross, p_ref, sum_ref):
    coefs = coefficients(others_ref, taken_ref, (stats_side, stats_cross), other_q.shape[-1])
    write_rows(coef_ref, coefs)
    slopes(e_cross, dp_cross, coefs[2], coefs[0], p_ref, ds_cross)
    sum_ref[...] = part_ref[...]
    add_terms(sum_ref, ds_cross, p_ref, other_q, other_g, False)
    halve(sum_ref, kept_ref, other_ref)


def near_own_terms_body(coef_ref, e_side, dp_side, other_q, other_g, part_ref,
                        kept_ref, other_ref, ds_side, p_ref, sum_ref):
    slopes(e_side, dp_side, coef_ref[1:2], coef_ref[0:1], p_ref, ds_side)
    sum_ref[...] = part_ref[...]

    @pl.when(jnp.logical_not(second_core()))
    def _():
        add_terms(sum_ref, ds_side, p_ref, other_q, other_g, False)

    halve(sum_ref, kept_ref, other_ref)


def far_four_terms_body(coef_ref, e_side, dp_side, other_q, other_g, part_ref,
                        kept_ref, other_ref, sum_ref, p_ref, ds_ref):
    sum_ref[...] = part_ref[...]

    @pl.when(second_core())
    def _():
        slopes(e_side, dp_side, coef_ref[1:2], coef_ref[0:1], p_ref, ds_ref)
        add_terms(sum_ref, ds_ref, p_ref, other_q, other_g, False)

    halve(sum_ref, kept_ref, other_ref)


def far_own_terms_body(mine_coef, coef_ref, e_own, dp_own, e_side, dp_side, q_ref, g_ref,
                       other_q, other_g,
                       kept_ref, other_ref, ds_own, ds_side, p_ref, p_side, sum_ref):
    slopes(e_own, dp_own, mine_coef[1:2], mine_coef[0:1], p_ref, ds_own)
    add_terms(sum_ref, ds_own, p_ref, q_ref, g_ref, True)
    slopes(e_side, dp_side, coef_ref[1:2], coef_ref[0:1], p_side, ds_side)

    @pl.when(jnp.logical_not(second_core()))
    def _():
        add_terms(sum_ref, ds_side, p_side, other_q, other_g, False)

    halve(sum_ref, kept_ref, other_ref)


def grads_body(own_ref, two_ref, ds_own, ds_two, ds_side, ds_cross, *refs):
    four_refs, (dq_ref, other_dq_ref) = refs[:-2], refs[-2:]
    width = dq_ref.shape[-1]
    keys, slope_refs = [own_ref[:, :width], two_ref[:, :width]], [ds_own, ds_two]
    side = keys[0]
    if four_refs:
        keys.append(four_refs[0][:, :width])
        slope_refs.append(four_refs[1])
        side = jnp.where(second_core(), keys[2], side)
    query_grads([side, keys[1]], [ds_side, ds_cross], other_dq_ref)
    query_grads(keys, slope_refs, dq_ref)


def add_others_body(use, sum_ref, pair_ref, four_ref, out_ref):
    taken = jnp.where(use(lax.axis_index("ctx")), four_ref[...].astype(f32), 0.0)
    out_ref[...] = sum_ref[...] + pair_ref[...].astype(f32) + taken


def relay_body(kept_ref, four_ref, two_ref, two_pair_ref, out_ref, sent_ref):
    ctx = lax.axis_index("ctx")
    taken = two_ref[...].astype(f32) + two_pair_ref[...].astype(f32)
    out_ref[...] = kept_ref[...] + jnp.where(ctx & 2 == 0, taken, 0.0)
    sent_ref[...] = (four_ref[...] + jnp.where(ctx & 6 == 6, taken, 0.0)).astype(bf16)


def near_first_sum_body(kept_ref, two_ref, two_pair_ref, out_ref):
    taken = two_ref[...].astype(f32) + two_pair_ref[...].astype(f32)
    out_ref[...] = kept_ref[...] + jnp.where(lax.axis_index("ctx") & 2 == 0, taken, 0.0)


def halves_sum_body(share, use, kept_ref, back_ref, here_ref, there_ref):
    each = here_ref.shape[0]
    group = lax.axis_index("head") // share
    for out_ref, at in ((here_ref, group), (there_ref, 1 - group)):
        rows = pl.ds(pl.multiple_of(at * each, each), each)
        taken = back_ref[rows].astype(f32)
        if use is not None:
            taken = jnp.where(use(lax.axis_index("ctx")), taken, 0.0)
        out_ref[...] = (kept_ref[rows] + taken).astype(out_ref.dtype)


def last_body(share, here_ref, taken_ref, dk_ref, dv_ref):
    width = dk_ref.shape[-1]
    group = lax.axis_index("head") // share
    for ref, place in ((here_ref, group), (taken_ref, 1 - group)):
        dk_ref[place] = ref[:, :width]
        dv_ref[place] = ref[:, width:]


def query_grads(keys, ds_refs, out_ref):
    heads, tokens, width = out_ref.shape
    turned = [key.T for key in keys]
    for h in range(heads):
        lanes = slice(h * tokens, (h + 1) * tokens)
        dqt = sum(dot(kt, ds[:, lanes]) for kt, ds in zip(turned, ds_refs))
        out_ref[h] = (dqt.T * width ** -0.5).astype(out_ref.dtype)


def own_terms_body(mine_coef, coef_ref, e_own, dp_own, e_side, dp_side, q_ref, g_ref,
                   other_q, other_g, own_ref, two_ref, ds_two, ds_cross, four_ref, ds_four,
                   terms_ref, dq_ref, other_dq_ref, ds_own, ds_side, p_ref, p_side):
    width = q_ref.shape[-1]
    own, two, four = [ref[:, :width] for ref in (own_ref, two_ref, four_ref)]
    slopes(e_side, dp_side, coef_ref[1:2], coef_ref[0:1], p_side, ds_side)
    query_grads([jnp.where(second_core(), four, own), two], [ds_side, ds_cross], other_dq_ref)
    slopes(e_own, dp_own, mine_coef[1:2], mine_coef[0:1], p_ref, ds_own)
    add_terms(terms_ref, ds_own, p_ref, q_ref, g_ref, True)

    @pl.when(jnp.logical_not(second_core()))
    def _():
        add_terms(terms_ref, ds_side, p_side, other_q, other_g, False)

    query_grads([own, two, four], [ds_own, ds_two, ds_four], dq_ref)


def add_grads_body(mine_ref, taken_ref, dq_ref):
    dq_ref[...] = (mine_ref[...] + taken_ref[...].astype(f32)).astype(dq_ref.dtype)


def sums_body(own_terms, four_back, two_back, out_ref):
    taken = four_back[...].astype(f32) + two_back[...].astype(f32)
    out_ref[...] = (own_terms[...] + taken).astype(bf16)


def per_device(queries, keys, values, d_out, doc_lengths):
    ctx_count, (heads, tokens, width) = lax.axis_size("ctx"), queries.shape
    middle = ctx_count // 2 * tokens
    split, starts, own = pl.pallas_call(
        functools.partial(prepare_body, GROUP // heads, middle),
        out_shape=(shape((1,), i32), shape((2, tokens), i32), shape((tokens, 2 * width), bf16)),
        in_specs=[pl.BlockSpec(memory_space=pl.ANY)] * 3,
        out_specs=(SMEM, VMEM, VMEM),
        scratch_shapes=[pltpu.SMEM(doc_lengths.shape, i32), pltpu.SemaphoreType.DMA((3,))],
        name="prepare",
    )(*[pltpu.with_memory_space_constraint(value, pltpu.HBM)
        for value in (doc_lengths, keys, values)])
    operands = (queries, d_out, own, starts)
    if ctx_count != 2 * REACH or lax.axis_size("head") * heads != 2 * GROUP or 2 * heads != GROUP:
        return gradients(True, *operands)
    return lax.switch(split[0], [functools.partial(gradients, True),
                                 functools.partial(gradients, False)], *operands)


def gradients(far, queries, d_out, own, starts):
    heads, tokens, width = queries.shape
    head_count = lax.axis_size("head")
    share = GROUP // heads
    groups = head_count // share
    rows = heads * tokens
    ctx = lax.axis_index("ctx")
    mutual = lax.axis_size("ctx") == 2 * REACH and share == groups == 2
    pair = (tokens, 2 * width)
    all_rows = (heads, tokens, width)
    stats = shape((3, rows), f32)
    wide = shape((tokens, rows), f32)
    half = shape((tokens, rows), bf16)
    half_scratch = pltpu.VMEM((tokens, rows), bf16)
    halves_scratch = pltpu.VMEM((2, tokens, rows), bf16)
    pair_scratch = pltpu.VMEM(pair, f32)

    if far:
        four = exchanged(own, "ctx", 4) if mutual else shifted(own, 4)
    two = [exchanged(own, "ctx", 2) if mutual else shifted(own, 2)]
    if far and mutual:
        two.append(exchanged(own, "ctx", 6))
    q, g, e_own, dp_own, stats_own = call(
        own_unit_body, "own_unit", [VMEM] * 4,
        (shape(all_rows, bf16), shape(all_rows, bf16), wide, wide, stats),
    )(starts, queries, d_out, own)
    other_q = exchanged(queries, "ctx", 1)
    other_g = exchanged(d_out, "ctx", 1)
    if far:
        four, stats_own = lax.optimization_barrier((four, stats_own))
        e_four, dp_four, stats_four = call(
            four_unit_body, "four_unit", [VMEM] * 4, (wide, wide, stats))(starts, q, g, four)
        other_q, stats_four = lax.optimization_barrier((other_q, stats_four))
        e_side, dp_side, stats_side = call(
            side_unit_body, "side_unit", [VMEM] * 5, (wide, wide, stats),
        )(starts, other_q, other_g, own, four)
    else:
        e_side, dp_side, stats_side = call(
            near_side_unit_body, "side_unit", [VMEM] * 4, (wide, wide, stats),
        )(starts, other_q, other_g, own)
    *two, stats_side, stats_own = lax.optimization_barrier((*two, stats_side, stats_own))
    mine_stats = (stats_own, stats_four) if far else (stats_own,)
    two = jnp.where(ctx & 2 == 2, *two) if len(two) == 2 else two[0]
    few = shape((4, rows), f32)
    e_cross, dp_cross, stats_cross, others = call(
        cross_unit_body, "cross_unit", [VMEM] * 5, (wide, wide, stats, few),
    )(starts, other_q, other_g, two, stats_side)
    taken_others = exchanged(others, "ctx", 1)
    e_two, dp_two, stats_two, mine = call(
        two_unit_body, "two_unit", [VMEM] * (4 + len(mine_stats)), (wide, wide, stats, few),
    )(starts, q, g, two, *mine_stats)
    taken_mine = exchanged(mine, "ctx", 1)
    mine_stats += (stats_two,)
    parts = ((e_four, dp_four) if far else (e_own, dp_own)) + (e_two, dp_two)
    mine_coef, ds_first, ds_two, first_part, two_part = call(
        functools.partial(my_terms_body, len(mine_stats)), "my_terms",
        [VMEM] * (8 + len(mine_stats)),
        (few, half, half, shape(pair, f32), shape(pair, f32)), (halves_scratch,),
    )(mine, taken_others, *mine_stats, *parts, q, g)
    other_sides = (other_q, other_g)
    last_stats = (others, taken_mine, stats_side, stats_cross)
    slices = (tokens // 2, 2 * width)
    slice_dims = (tokens // head_count, 2 * width)
    if not mutual:
        coef, four_terms = call(
            four_terms_body, "four_terms", [VMEM] * 9, (few, shape(pair, bf16)),
            (pair_scratch, half_scratch, half_scratch),
        )(*last_stats, e_side, dp_side, *other_sides, first_part)
        two_terms, ds_cross = call(
            two_terms_body, "two_terms", [VMEM] * 6, (shape(pair, bf16), half),
            (half_scratch, pair_scratch),
        )(coef, e_cross, dp_cross, *other_sides, two_part)
        backs = [shifted(four_terms, -4), shifted(two_terms, -2)]
        own_terms, my_grads, other_grads = call(
            own_terms_body, "own_terms", [VMEM] * 16,
            (shape(pair, f32), shape(all_rows, f32), shape(all_rows, bf16)),
            (half_scratch,) * 4,
        )(mine_coef, coef, e_own, dp_own, e_side, dp_side, q, g, *other_sides, own, two,
          ds_two, ds_cross, four, ds_first)
        taken_grads = exchanged(other_grads, "ctx", 1)
        d_queries, = call(
            add_grads_body, "add_grads", [VMEM] * 2, (shape(all_rows, bf16),),
        )(my_grads, taken_grads)
        sums, = call(sums_body, "sums", [VMEM] * 3, (shape(pair, bf16),))(own_terms, *backs)
        pieces = lax.all_to_all(sums.reshape(head_count, *slice_dims), "head", 0, 0)
        result = jnp.sum(
            pieces.reshape(groups, share, *slice_dims).astype(f32), axis=1).astype(bf16)
        return d_queries, result[..., :width], result[..., width:]

    halves = (shape(slices, bf16), shape(slices, bf16))
    part = shape(slices, f32)
    coef, two_kept, two_other, ds_cross = call(
        halved_two_terms_body, "two_terms", [VMEM] * 9, (few,) + halves + (half,),
        (half_scratch, pair_scratch),
    )(*last_stats, e_cross, dp_cross, *other_sides, two_part)
    two_back = exchanged(two_kept, "ctx", 2)
    two_pair = exchanged(two_other, ("ctx", "head"), 2 * head_count + 1)
    if far:
        four_kept, four_other = call(
            far_four_terms_body, "four_terms", [VMEM] * 6, (part, halves[1]),
            (pair_scratch, half_scratch, half_scratch),
        )(coef, e_side, dp_side, *other_sides, first_part)
        four_pair = exchanged(four_other, ("ctx", "head"), 4 * head_count + 1)
        own_kept, own_other, ds_own, ds_side = call(
            far_own_terms_body, "own_terms", [VMEM] * 10, (part, halves[1], half, half),
            (half_scratch, half_scratch, pair_scratch),
        )(mine_coef, coef, e_own, dp_own, e_side, dp_side, q, g, *other_sides)
    else:
        ds_own = ds_first
        own_kept, own_other, ds_side = call(
            near_own_terms_body, "own_terms", [VMEM] * 6, (part, halves[1], half),
            (half_scratch, pair_scratch),
        )(coef, e_side, dp_side, *other_sides, first_part)
    own_pair = exchanged(own_other, "head", 1)
    four_refs = (four, ds_first) if far else ()
    my_grads, other_grads = call(
        grads_body, "query_grads", [VMEM] * (6 + len(four_refs)),
        (shape(all_rows, f32), shape(all_rows, bf16)),
    )(own, two, ds_own, ds_two, ds_side, ds_cross, *four_refs)
    owns_four = lambda i: i < 4
    if far:
        own_kept, relayed = call(
            relay_body, "relay", [VMEM] * 4, (part, halves[0]),
        )(own_kept, four_kept, two_back, two_pair)
        four_back = exchanged(relayed, "ctx", 4)
        own_kept, = call(functools.partial(add_others_body, owns_four), "add_others", [VMEM] * 3,
                         (part,))(own_kept, own_pair, four_pair)
        final, use = four_back, owns_four
    else:
        own_kept, = call(
            near_first_sum_body, "first_sum", [VMEM] * 3, (part,),
        )(own_kept, two_back, two_pair)
        final, use = own_pair, None
    kept, sent = call(
        functools.partial(halves_sum_body, share, use), "sums", [VMEM] * 2,
        (shape(slice_dims, bf16),) * 2)(own_kept, final)
    other_grads, kept = lax.optimization_barrier((other_grads, kept))
    taken_grads = exchanged(other_grads, "ctx", 1)
    d_queries, = call(
        add_grads_body, "add_grads", [VMEM] * 2, (shape(all_rows, bf16),),
    )(my_grads, taken_grads)
    last = exchanged(sent, "head", share)
    last, d_queries = lax.optimization_barrier((last, d_queries))
    d_keys, d_values = call(
        functools.partial(last_body, share), "last", [VMEM] * 2,
        (shape((groups, tokens // head_count, width), bf16),) * 2)(kept, last)
    return d_queries, d_keys, d_values


def solution(mesh):
    placed = (
        P("head", "ctx", None),
        P(None, "ctx", None),
        P(None, "ctx", None),
        P("head", "ctx", None),
        P(),
    )
    return jax.shard_map(
        per_device,
        mesh=mesh,
        in_specs=placed,
        out_specs=(
            P("head", "ctx", None),
            P(None, ("ctx", "head"), None),
            P(None, ("ctx", "head"), None),
        ),
        check_vma=False,
    )
```

```python
import functools
import math

import jax
import jax.numpy as jnp
from jax import lax
from jax.experimental import pallas as pl
from jax.experimental.pallas import tpu as pltpu
from jax.sharding import PartitionSpec as P

GROUP = 8
REACH = 4
MASKED = -1e30
NT = (((1,), (1,)), ((), ()))
NN = (((1,), (0,)), ((), ()))
VMEM = pl.BlockSpec(memory_space=pltpu.VMEM)
SMEM = pl.BlockSpec(memory_space=pltpu.SMEM)
bf16, f32, i32 = jnp.bfloat16, jnp.float32, jnp.int32


def dot(a, b, dims=NN):
    return lax.dot_general(a, b, dims, preferred_element_type=f32)


def shape(dims, dtype):
    return jax.ShapeDtypeStruct(dims, dtype)


def call(body, name, in_specs, outs, scratch=()):
    return pl.pallas_call(
        body,
        out_shape=outs,
        in_specs=in_specs,
        out_specs=(VMEM,) * len(outs),
        scratch_shapes=scratch,
        compiler_params=pltpu.CompilerParams(vmem_limit_bytes=20 * 2**20),
        cost_estimate=pl.CostEstimate(flops=2**20, bytes_accessed=2**10, transcendentals=0),
        name=name,
    )


def shifted(block, distance):
    count = lax.axis_size("ctx")
    route = [(i - distance, i) for i in range(count) if 0 <= i - distance < count]
    return lax.ppermute(block, "ctx", route)


def exchanged(block, axis, mask):
    count = math.prod(lax.axis_size(name) for name in axis) if isinstance(axis, tuple) else (
        lax.axis_size(axis))
    return lax.ppermute(block, axis, [(i, i ^ mask) for i in range(count)])


def both(rows_ref):
    heads = rows_ref.shape[0] // 2
    return rows_ref.at[:heads], rows_ref.at[heads:]


def second_core():
    return lax.rem(lax.axis_index("ctx"), 2) == 1


def doc_starts(lengths_ref, block, tokens):
    row_pos = block * tokens + lax.broadcasted_iota(i32, (1, tokens), 1)
    starts = jnp.zeros((1, tokens), i32)
    end = jnp.int32(0)
    for d in range(lengths_ref.shape[0]):
        end = end + lengths_ref[d]
        starts = jnp.where(row_pos >= end, end, starts)
    return starts


def unit(pair, key_block, starts, rows_ref, e_ref, dp_ref, stats_ref, causal=False):
    q_ref, g_ref = both(rows_ref)
    heads, tokens, width = q_ref.shape
    factor = width ** -0.5 * math.log2(math.e)
    key_iota = lax.broadcasted_iota(i32, (tokens, 1), 0)
    allowed = key_block * tokens + key_iota >= starts
    if causal:
        allowed = allowed & (key_iota <= lax.broadcasted_iota(i32, (1, tokens), 1))
    for h in range(heads):
        lanes = slice(h * tokens, (h + 1) * tokens)
        s = jnp.where(allowed, dot(pair[:, :width], q_ref[h], NT), MASKED)
        top = jnp.max(s, axis=0, keepdims=True)
        e = jnp.exp2((s - top) * factor)
        dp = dot(pair[:, width:], g_ref[h], NT)
        e_ref[:, lanes] = e
        dp_ref[:, lanes] = dp
        stats_ref[0:1, lanes] = top
        stats_ref[1:2, lanes] = jnp.sum(e, axis=0, keepdims=True)
        stats_ref[2:3, lanes] = jnp.sum(e * dp, axis=0, keepdims=True)


def rows_of(ref, first=0):
    return [ref[first + row:first + row + 1] for row in range(3)]


def joined(parts, factor):
    top = functools.reduce(jnp.maximum, [part[0] for part in parts])
    gains = [jnp.exp2((part[0] - top) * factor) for part in parts]
    total = sum(gain * part[1] for gain, part in zip(gains, parts))
    weighted = sum(gain * part[2] for gain, part in zip(gains, parts))
    return top, total, weighted


def own_unit_body(starts_ref, rows_ref, own_ref, e_ref, dp_ref, stats_ref):
    unit(own_ref, lax.axis_index("ctx"), starts_ref[0:1], rows_ref, e_ref, dp_ref, stats_ref,
         causal=True)


def four_unit_body(starts_ref, rows_ref, four_ref, e_ref, dp_ref, stats_ref):
    here = lax.axis_index("ctx")
    unit(four_ref, here - 4, starts_ref[0:1], rows_ref, e_ref, dp_ref, stats_ref)


def side_unit_body(starts_ref, other_rows, own_ref, four_ref, e_ref, dp_ref, stats_ref):
    side = jnp.where(second_core(), four_ref[...], own_ref[...])
    block = lax.axis_index("ctx") - jnp.where(second_core(), 4, 0)
    unit(side, block, starts_ref[1:2], other_rows, e_ref, dp_ref, stats_ref)


def prepare_body(share, middle, lengths_in, keys_ref, values_ref, queries_ref, d_out_ref,
                 split_ref, starts_ref, own_ref, rows_ref, lengths_ref, sems):
    heads, tokens, width = queries_ref.shape
    group = lax.axis_index("head") // share
    lengths = pltpu.make_async_copy(lengths_in, lengths_ref, sems.at[0])
    copies = [
        pltpu.make_async_copy(keys_ref.at[group], own_ref.at[:, :width], sems.at[1]),
        pltpu.make_async_copy(values_ref.at[group], own_ref.at[:, width:], sems.at[2]),
        pltpu.make_async_copy(queries_ref, rows_ref.at[:heads], sems.at[3]),
        pltpu.make_async_copy(d_out_ref, rows_ref.at[heads:], sems.at[4]),
    ]
    for copy in [lengths] + copies:
        copy.start()
    lengths.wait()
    end, split = jnp.int32(0), jnp.int32(0)
    for d in range(lengths_ref.shape[0]):
        end = end + lengths_ref[d]
        split = jnp.where(end == middle, 1, split)
    split_ref[0] = split
    here = lax.axis_index("ctx")
    starts_ref[0:1] = doc_starts(lengths_ref, here, tokens)
    starts_ref[1:2] = doc_starts(lengths_ref, jnp.bitwise_xor(here, 1), tokens)
    for copy in copies:
        copy.wait()


def near_side_unit_body(starts_ref, other_rows, own_ref, e_ref, dp_ref, stats_ref):
    block = jnp.where(second_core(), -1, lax.axis_index("ctx"))
    unit(own_ref, block, starts_ref[1:2], other_rows, e_ref, dp_ref, stats_ref)


def write_rows(ref, values):
    for row, value in enumerate(values):
        ref[row:row + 1] = value


def cross_unit_body(starts_ref, other_rows, two_ref, stats_side,
                    e_ref, dp_ref, stats_ref, others_ref):
    factor = other_rows.shape[-1] ** -0.5 * math.log2(math.e)
    unit(two_ref, lax.axis_index("ctx") - 2, starts_ref[1:2], other_rows,
         e_ref, dp_ref, stats_ref)
    write_rows(others_ref, joined([rows_of(stats_side), rows_of(stats_ref)], factor))
    others_ref[3:4] = jnp.zeros((1, others_ref.shape[1]), f32)


def two_unit_body(starts_ref, rows_ref, two_ref, *refs):
    earlier, (e_ref, dp_ref, stats_ref, mine_ref) = refs[:-4], refs[-4:]
    factor = rows_ref.shape[-1] ** -0.5 * math.log2(math.e)
    unit(two_ref, lax.axis_index("ctx") - 2, starts_ref[0:1], rows_ref,
         e_ref, dp_ref, stats_ref)
    write_rows(mine_ref, joined([rows_of(ref) for ref in earlier + (stats_ref,)], factor))
    mine_ref[3:4] = jnp.zeros((1, mine_ref.shape[1]), f32)


def coefficients(here_ref, taken_ref, stats_refs, width):
    factor = width ** -0.5 * math.log2(math.e)
    top, total, weighted = joined([rows_of(here_ref), rows_of(taken_ref)], factor)
    inverse = 1.0 / total
    return [weighted * inverse] + [
        jnp.exp2((ref[0:1] - top) * factor) * inverse for ref in stats_refs]


def slopes(e_ref, dp_ref, gain, delta, p_ref, ds_ref):
    p = e_ref[...] * gain
    p_ref[...] = p.astype(bf16)
    ds_ref[...] = (p * (dp_ref[...] - delta)).astype(bf16)


def flat(ref):
    heads, tokens, width = ref.shape
    return ref[...].reshape(heads * tokens, width)


def add_terms(sum_ref, ds_ref, p_ref, rows_ref, fresh):
    q_ref, g_ref = both(rows_ref)
    width = q_ref.shape[-1]
    dk = dot(ds_ref[...], flat(q_ref)) * width ** -0.5
    dv = dot(p_ref[...], flat(g_ref))
    if fresh:
        sum_ref[:, :width] = dk
        sum_ref[:, width:] = dv
    else:
        sum_ref[:, :width] += dk
        sum_ref[:, width:] += dv


def my_terms_body(count, mine_ref, taken_ref, *refs):
    stats, refs = refs[:count], refs[count:]
    parts, rows_ref, refs = refs[:4], refs[4], refs[5:]
    coef_ref, ds_refs, sums, p_ref = refs[0], refs[1:3], refs[3:5], refs[5]
    coefs = coefficients(mine_ref, taken_ref, stats, rows_ref.shape[-1])
    write_rows(coef_ref, coefs)
    for at in range(2):
        slopes(parts[2 * at], parts[2 * at + 1], coefs[count - 1 + at], coefs[0], p_ref.at[at],
               ds_refs[at])
        add_terms(sums[at], ds_refs[at], p_ref.at[at], rows_ref, True)


def four_terms_body(others_ref, taken_ref, stats_side, stats_cross, e_side, dp_side,
                    other_rows, part_ref, coef_ref, terms_ref, sum_ref, p_ref, ds_ref):
    coefs = coefficients(others_ref, taken_ref, (stats_side, stats_cross), other_rows.shape[-1])
    write_rows(coef_ref, coefs)
    sum_ref[...] = part_ref[...]

    @pl.when(second_core())
    def _():
        slopes(e_side, dp_side, coef_ref[1:2], coef_ref[0:1], p_ref, ds_ref)
        add_terms(sum_ref, ds_ref, p_ref, other_rows, False)

    terms_ref[...] = sum_ref[...].astype(bf16)


def two_terms_body(coef_ref, e_cross, dp_cross, other_rows, part_ref,
                   terms_ref, ds_cross, p_ref, sum_ref):
    slopes(e_cross, dp_cross, coef_ref[2:3], coef_ref[0:1], p_ref, ds_cross)
    sum_ref[...] = part_ref[...]
    add_terms(sum_ref, ds_cross, p_ref, other_rows, False)
    terms_ref[...] = sum_ref[...].astype(bf16)


def slice_rows(ref, other):
    count = lax.axis_size("head")
    each = ref.shape[0] // count
    parity = jnp.bitwise_xor(lax.rem(lax.axis_index("head"), 2), other)
    return [ref[pl.ds(pl.multiple_of((2 * at + parity) * each, each), each)]
            for at in range(count // 2)]


def halve(sum_ref, kept_ref, given_ref):
    each = sum_ref.shape[0] // lax.axis_size("head")
    for other, out_ref in enumerate((kept_ref, given_ref)):
        for at, value in enumerate(slice_rows(sum_ref, other)):
            out_ref[at * each:(at + 1) * each] = value.astype(out_ref.dtype)


def halved_two_terms_body(others_ref, taken_ref, stats_side, stats_cross, e_cross, dp_cross,
                        other_rows, part_ref,
                        coef_ref, kept_ref, other_ref, ds_cross, p_ref, sum_ref):
    coefs = coefficients(others_ref, taken_ref, (stats_side, stats_cross), other_rows.shape[-1])
    write_rows(coef_ref, coefs)
    slopes(e_cross, dp_cross, coefs[2], coefs[0], p_ref, ds_cross)
    sum_ref[...] = part_ref[...]
    add_terms(sum_ref, ds_cross, p_ref, other_rows, False)
    halve(sum_ref, kept_ref, other_ref)


def near_own_terms_body(coef_ref, e_side, dp_side, other_rows, part_ref,
                        kept_ref, other_ref, ds_side, p_ref, sum_ref):
    slopes(e_side, dp_side, coef_ref[1:2], coef_ref[0:1], p_ref, ds_side)
    sum_ref[...] = part_ref[...]

    @pl.when(jnp.logical_not(second_core()))
    def _():
        add_terms(sum_ref, ds_side, p_ref, other_rows, False)

    halve(sum_ref, kept_ref, other_ref)


def far_four_terms_body(coef_ref, e_side, dp_side, other_rows, part_ref,
                        kept_ref, other_ref, sum_ref, p_ref, ds_ref):
    sum_ref[...] = part_ref[...]

    @pl.when(second_core())
    def _():
        slopes(e_side, dp_side, coef_ref[1:2], coef_ref[0:1], p_ref, ds_ref)
        add_terms(sum_ref, ds_ref, p_ref, other_rows, False)

    halve(sum_ref, kept_ref, other_ref)


def far_own_terms_body(mine_coef, coef_ref, e_own, dp_own, e_side, dp_side, rows_ref,
                       other_rows,
                       kept_ref, other_ref, ds_own, ds_side, p_ref, p_side, sum_ref):
    slopes(e_own, dp_own, mine_coef[1:2], mine_coef[0:1], p_ref, ds_own)
    add_terms(sum_ref, ds_own, p_ref, rows_ref, True)
    slopes(e_side, dp_side, coef_ref[1:2], coef_ref[0:1], p_side, ds_side)

    @pl.when(jnp.logical_not(second_core()))
    def _():
        add_terms(sum_ref, ds_side, p_side, other_rows, False)

    halve(sum_ref, kept_ref, other_ref)


def grads_body(own_ref, two_ref, ds_own, ds_two, ds_side, ds_cross, *refs):
    four_refs, (dq_ref, other_dq_ref) = refs[:-2], refs[-2:]
    width = dq_ref.shape[-1]
    keys, slope_refs = [own_ref[:, :width], two_ref[:, :width]], [ds_own, ds_two]
    side = keys[0]
    if four_refs:
        keys.append(four_refs[0][:, :width])
        slope_refs.append(four_refs[1])
        side = jnp.where(second_core(), keys[2], side)
    query_grads([side, keys[1]], [ds_side, ds_cross], other_dq_ref)
    query_grads(keys, slope_refs, dq_ref)


def add_others_body(use, sum_ref, pair_ref, four_ref, out_ref):
    taken = jnp.where(use(lax.axis_index("ctx")), four_ref[...].astype(f32), 0.0)
    out_ref[...] = sum_ref[...] + pair_ref[...].astype(f32) + taken


def relay_body(kept_ref, four_ref, two_ref, two_pair_ref, out_ref, sent_ref):
    ctx = lax.axis_index("ctx")
    taken = two_ref[...].astype(f32) + two_pair_ref[...].astype(f32)
    out_ref[...] = kept_ref[...] + jnp.where(ctx & 2 == 0, taken, 0.0)
    sent_ref[...] = (four_ref[...] + jnp.where(ctx & 6 == 6, taken, 0.0)).astype(bf16)


def near_first_sum_body(kept_ref, two_ref, two_pair_ref, out_ref):
    taken = two_ref[...].astype(f32) + two_pair_ref[...].astype(f32)
    out_ref[...] = kept_ref[...] + jnp.where(lax.axis_index("ctx") & 2 == 0, taken, 0.0)


def halves_sum_body(share, use, kept_ref, back_ref, here_ref, there_ref):
    each = here_ref.shape[0]
    group = lax.axis_index("head") // share
    for out_ref, at in ((here_ref, group), (there_ref, 1 - group)):
        rows = pl.ds(pl.multiple_of(at * each, each), each)
        taken = back_ref[rows].astype(f32)
        if use is not None:
            taken = jnp.where(use(lax.axis_index("ctx")), taken, 0.0)
        out_ref[...] = (kept_ref[rows] + taken).astype(out_ref.dtype)


def last_body(share, here_ref, taken_ref, dk_ref, dv_ref):
    width = dk_ref.shape[-1]
    group = lax.axis_index("head") // share
    for ref, place in ((here_ref, group), (taken_ref, 1 - group)):
        dk_ref[place] = ref[:, :width]
        dv_ref[place] = ref[:, width:]


def query_grads(keys, ds_refs, out_ref):
    heads, tokens, width = out_ref.shape
    turned = [key.T for key in keys]
    for h in range(heads):
        lanes = slice(h * tokens, (h + 1) * tokens)
        dqt = sum(dot(kt, ds[:, lanes]) for kt, ds in zip(turned, ds_refs))
        out_ref[h] = (dqt.T * width ** -0.5).astype(out_ref.dtype)


def own_terms_body(mine_coef, coef_ref, e_own, dp_own, e_side, dp_side, rows_ref,
                   other_rows, own_ref, two_ref, ds_two, ds_cross, four_ref, ds_four,
                   terms_ref, dq_ref, other_dq_ref, ds_own, ds_side, p_ref, p_side):
    width = dq_ref.shape[-1]
    own, two, four = [ref[:, :width] for ref in (own_ref, two_ref, four_ref)]
    slopes(e_side, dp_side, coef_ref[1:2], coef_ref[0:1], p_side, ds_side)
    query_grads([jnp.where(second_core(), four, own), two], [ds_side, ds_cross], other_dq_ref)
    slopes(e_own, dp_own, mine_coef[1:2], mine_coef[0:1], p_ref, ds_own)
    add_terms(terms_ref, ds_own, p_ref, rows_ref, True)

    @pl.when(jnp.logical_not(second_core()))
    def _():
        add_terms(terms_ref, ds_side, p_side, other_rows, False)

    query_grads([own, two, four], [ds_own, ds_two, ds_four], dq_ref)


def add_grads_body(mine_ref, taken_ref, dq_ref):
    dq_ref[...] = (mine_ref[...] + taken_ref[...].astype(f32)).astype(dq_ref.dtype)


def sums_body(own_terms, four_back, two_back, out_ref):
    taken = four_back[...].astype(f32) + two_back[...].astype(f32)
    out_ref[...] = (own_terms[...] + taken).astype(bf16)


def per_device(queries, keys, values, d_out, doc_lengths):
    ctx_count, (heads, tokens, width) = lax.axis_size("ctx"), queries.shape
    middle = ctx_count // 2 * tokens
    split, starts, own, rows = pl.pallas_call(
        functools.partial(prepare_body, GROUP // heads, middle),
        out_shape=(shape((1,), i32), shape((2, tokens), i32), shape((tokens, 2 * width), bf16),
                   shape((2 * heads, tokens, width), bf16)),
        in_specs=[pl.BlockSpec(memory_space=pl.ANY)] * 5,
        out_specs=(SMEM, VMEM, VMEM, VMEM),
        scratch_shapes=[pltpu.SMEM(doc_lengths.shape, i32), pltpu.SemaphoreType.DMA((5,))],
        name="prepare",
    )(*[pltpu.with_memory_space_constraint(value, pltpu.HBM)
        for value in (doc_lengths, keys, values, queries, d_out)])
    operands = (rows, own, starts)
    if ctx_count != 2 * REACH or lax.axis_size("head") * heads != 2 * GROUP or 2 * heads != GROUP:
        return gradients(True, *operands)
    return lax.switch(split[0], [functools.partial(gradients, True),
                                 functools.partial(gradients, False)], *operands)


def gradients(far, row_data, own, starts):
    heads, (tokens, width) = row_data.shape[0] // 2, row_data.shape[1:]
    head_count = lax.axis_size("head")
    share = GROUP // heads
    groups = head_count // share
    rows = heads * tokens
    ctx = lax.axis_index("ctx")
    mutual = lax.axis_size("ctx") == 2 * REACH and share == groups == 2
    pair = (tokens, 2 * width)
    all_rows = (heads, tokens, width)
    stats = shape((3, rows), f32)
    wide = shape((tokens, rows), f32)
    half = shape((tokens, rows), bf16)
    half_scratch = pltpu.VMEM((tokens, rows), bf16)
    halves_scratch = pltpu.VMEM((2, tokens, rows), bf16)
    pair_scratch = pltpu.VMEM(pair, f32)

    if far:
        four = exchanged(own, "ctx", 4) if mutual else shifted(own, 4)
    two = [exchanged(own, "ctx", 2) if mutual else shifted(own, 2)]
    if far and mutual:
        two.append(exchanged(own, "ctx", 6))
    e_own, dp_own, stats_own = call(
        own_unit_body, "own_unit", [VMEM] * 3, (wide, wide, stats))(starts, row_data, own)
    other_rows = exchanged(row_data, "ctx", 1)
    if far:
        four, stats_own = lax.optimization_barrier((four, stats_own))
        e_four, dp_four, stats_four = call(
            four_unit_body, "four_unit", [VMEM] * 3, (wide, wide, stats))(starts, row_data, four)
        other_rows, stats_four = lax.optimization_barrier((other_rows, stats_four))
        e_side, dp_side, stats_side = call(
            side_unit_body, "side_unit", [VMEM] * 4, (wide, wide, stats),
        )(starts, other_rows, own, four)
    else:
        e_side, dp_side, stats_side = call(
            near_side_unit_body, "side_unit", [VMEM] * 3, (wide, wide, stats),
        )(starts, other_rows, own)
    *two, stats_side, stats_own = lax.optimization_barrier((*two, stats_side, stats_own))
    mine_stats = (stats_own, stats_four) if far else (stats_own,)
    two = jnp.where(ctx & 2 == 2, *two) if len(two) == 2 else two[0]
    few = shape((4, rows), f32)
    e_cross, dp_cross, stats_cross, others = call(
        cross_unit_body, "cross_unit", [VMEM] * 4, (wide, wide, stats, few),
    )(starts, other_rows, two, stats_side)
    taken_others = exchanged(others, "ctx", 1)
    e_two, dp_two, stats_two, mine = call(
        two_unit_body, "two_unit", [VMEM] * (3 + len(mine_stats)), (wide, wide, stats, few),
    )(starts, row_data, two, *mine_stats)
    taken_mine = exchanged(mine, "ctx", 1)
    mine_stats += (stats_two,)
    parts = ((e_four, dp_four) if far else (e_own, dp_own)) + (e_two, dp_two)
    mine_coef, ds_first, ds_two, first_part, two_part = call(
        functools.partial(my_terms_body, len(mine_stats)), "my_terms",
        [VMEM] * (7 + len(mine_stats)),
        (few, half, half, shape(pair, f32), shape(pair, f32)), (halves_scratch,),
    )(mine, taken_others, *mine_stats, *parts, row_data)
    last_stats = (others, taken_mine, stats_side, stats_cross)
    slices = (tokens // 2, 2 * width)
    slice_dims = (tokens // head_count, 2 * width)
    if not mutual:
        coef, four_terms = call(
            four_terms_body, "four_terms", [VMEM] * 8, (few, shape(pair, bf16)),
            (pair_scratch, half_scratch, half_scratch),
        )(*last_stats, e_side, dp_side, other_rows, first_part)
        two_terms, ds_cross = call(
            two_terms_body, "two_terms", [VMEM] * 5, (shape(pair, bf16), half),
            (half_scratch, pair_scratch),
        )(coef, e_cross, dp_cross, other_rows, two_part)
        backs = [shifted(four_terms, -4), shifted(two_terms, -2)]
        own_terms, my_grads, other_grads = call(
            own_terms_body, "own_terms", [VMEM] * 14,
            (shape(pair, f32), shape(all_rows, f32), shape(all_rows, bf16)),
            (half_scratch,) * 4,
        )(mine_coef, coef, e_own, dp_own, e_side, dp_side, row_data, other_rows, own, two,
          ds_two, ds_cross, four, ds_first)
        taken_grads = exchanged(other_grads, "ctx", 1)
        d_queries, = call(
            add_grads_body, "add_grads", [VMEM] * 2, (shape(all_rows, bf16),),
        )(my_grads, taken_grads)
        sums, = call(sums_body, "sums", [VMEM] * 3, (shape(pair, bf16),))(own_terms, *backs)
        pieces = lax.all_to_all(sums.reshape(head_count, *slice_dims), "head", 0, 0)
        result = jnp.sum(
            pieces.reshape(groups, share, *slice_dims).astype(f32), axis=1).astype(bf16)
        return d_queries, result[..., :width], result[..., width:]

    halves = (shape(slices, bf16), shape(slices, bf16))
    part = shape(slices, f32)
    coef, two_kept, two_other, ds_cross = call(
        halved_two_terms_body, "two_terms", [VMEM] * 8, (few,) + halves + (half,),
        (half_scratch, pair_scratch),
    )(*last_stats, e_cross, dp_cross, other_rows, two_part)
    two_back = exchanged(two_kept, "ctx", 2)
    two_pair = exchanged(two_other, ("ctx", "head"), 2 * head_count + 1)
    if far:
        four_kept, four_other = call(
            far_four_terms_body, "four_terms", [VMEM] * 5, (part, halves[1]),
            (pair_scratch, half_scratch, half_scratch),
        )(coef, e_side, dp_side, other_rows, first_part)
        four_pair = exchanged(four_other, ("ctx", "head"), 4 * head_count + 1)
        own_kept, own_other, ds_own, ds_side = call(
            far_own_terms_body, "own_terms", [VMEM] * 8, (part, halves[1], half, half),
            (half_scratch, half_scratch, pair_scratch),
        )(mine_coef, coef, e_own, dp_own, e_side, dp_side, row_data, other_rows)
    else:
        ds_own = ds_first
        own_kept, own_other, ds_side = call(
            near_own_terms_body, "own_terms", [VMEM] * 5, (part, halves[1], half),
            (half_scratch, pair_scratch),
        )(coef, e_side, dp_side, other_rows, first_part)
    own_pair = exchanged(own_other, "head", 1)
    four_refs = (four, ds_first) if far else ()
    my_grads, other_grads = call(
        grads_body, "query_grads", [VMEM] * (6 + len(four_refs)),
        (shape(all_rows, f32), shape(all_rows, bf16)),
    )(own, two, ds_own, ds_two, ds_side, ds_cross, *four_refs)
    owns_four = lambda i: i < 4
    if far:
        own_kept, relayed = call(
            relay_body, "relay", [VMEM] * 4, (part, halves[0]),
        )(own_kept, four_kept, two_back, two_pair)
        four_back = exchanged(relayed, "ctx", 4)
        own_kept, = call(functools.partial(add_others_body, owns_four), "add_others", [VMEM] * 3,
                         (part,))(own_kept, own_pair, four_pair)
        final, use = four_back, owns_four
    else:
        own_kept, = call(
            near_first_sum_body, "first_sum", [VMEM] * 3, (part,),
        )(own_kept, two_back, two_pair)
        final, use = own_pair, None
    kept, sent = call(
        functools.partial(halves_sum_body, share, use), "sums", [VMEM] * 2,
        (shape(slice_dims, bf16),) * 2)(own_kept, final)
    other_grads, kept = lax.optimization_barrier((other_grads, kept))
    taken_grads = exchanged(other_grads, "ctx", 1)
    d_queries, = call(
        add_grads_body, "add_grads", [VMEM] * 2, (shape(all_rows, bf16),),
    )(my_grads, taken_grads)
    last = exchanged(sent, "head", share)
    last, d_queries = lax.optimization_barrier((last, d_queries))
    d_keys, d_values = call(
        functools.partial(last_body, share), "last", [VMEM] * 2,
        (shape((groups, tokens // head_count, width), bf16),) * 2)(kept, last)
    return d_queries, d_keys, d_values


def solution(mesh):
    placed = (
        P("head", "ctx", None),
        P(None, "ctx", None),
        P(None, "ctx", None),
        P("head", "ctx", None),
        P(),
    )
    return jax.shard_map(
        per_device,
        mesh=mesh,
        in_specs=placed,
        out_specs=(
            P("head", "ctx", None),
            P(None, ("ctx", "head"), None),
            P(None, ("ctx", "head"), None),
        ),
        check_vma=False,
    )
```

```python
import functools
import math

import jax
import jax.numpy as jnp
from jax import lax
from jax.experimental import pallas as pl
from jax.experimental.pallas import tpu as pltpu
from jax.sharding import PartitionSpec as P

GROUP = 8
REACH = 4
MASKED = -1e30
NT = (((1,), (1,)), ((), ()))
NN = (((1,), (0,)), ((), ()))
VMEM = pl.BlockSpec(memory_space=pltpu.VMEM)
SMEM = pl.BlockSpec(memory_space=pltpu.SMEM)
bf16, f32, i32 = jnp.bfloat16, jnp.float32, jnp.int32


def dot(a, b, dims=NN):
    return lax.dot_general(a, b, dims, preferred_element_type=f32)


def shape(dims, dtype):
    return jax.ShapeDtypeStruct(dims, dtype)


def call(body, name, in_specs, outs, scratch=()):
    return pl.pallas_call(
        body,
        out_shape=outs,
        in_specs=in_specs,
        out_specs=(VMEM,) * len(outs),
        scratch_shapes=scratch,
        compiler_params=pltpu.CompilerParams(vmem_limit_bytes=20 * 2**20),
        cost_estimate=pl.CostEstimate(flops=2**20, bytes_accessed=2**10, transcendentals=0),
        name=name,
    )


def shifted(block, distance):
    count = lax.axis_size("ctx")
    route = [(i - distance, i) for i in range(count) if 0 <= i - distance < count]
    return lax.ppermute(block, "ctx", route)


def exchanged(block, axis, mask):
    count = math.prod(lax.axis_size(name) for name in axis) if isinstance(axis, tuple) else (
        lax.axis_size(axis))
    return lax.ppermute(block, axis, [(i, i ^ mask) for i in range(count)])


def both(rows_ref):
    heads = rows_ref.shape[0] // 2
    return rows_ref.at[:heads], rows_ref.at[heads:]


def second_core():
    return lax.rem(lax.axis_index("ctx"), 2) == 1


def doc_starts(lengths_ref, block, tokens):
    row_pos = block * tokens + lax.broadcasted_iota(i32, (1, tokens), 1)
    starts = jnp.zeros((1, tokens), i32)
    end = jnp.int32(0)
    for d in range(lengths_ref.shape[0]):
        end = end + lengths_ref[d]
        starts = jnp.where(row_pos >= end, end, starts)
    return starts


def unit(pair, key_block, starts, rows_ref, e_ref, dp_ref, stats_ref, causal=False):
    q_ref, g_ref = both(rows_ref)
    heads, tokens, width = q_ref.shape
    factor = width ** -0.5 * math.log2(math.e)
    key_iota = lax.broadcasted_iota(i32, (tokens, 1), 0)
    allowed = key_block * tokens + key_iota >= starts
    if causal:
        allowed = allowed & (key_iota <= lax.broadcasted_iota(i32, (1, tokens), 1))
    for h in range(heads):
        lanes = slice(h * tokens, (h + 1) * tokens)
        s = jnp.where(allowed, dot(pair[:, :width], q_ref[h], NT), MASKED)
        top = jnp.max(s, axis=0, keepdims=True)
        e = jnp.exp2((s - top) * factor)
        dp = dot(pair[:, width:], g_ref[h], NT)
        e_ref[:, lanes] = e
        dp_ref[:, lanes] = dp
        stats_ref[0:1, lanes] = top
        stats_ref[1:2, lanes] = jnp.sum(e, axis=0, keepdims=True)
        stats_ref[2:3, lanes] = jnp.sum(e * dp, axis=0, keepdims=True)


def rows_of(ref, first=0):
    return [ref[first + row:first + row + 1] for row in range(3)]


def joined(parts, factor):
    top = functools.reduce(jnp.maximum, [part[0] for part in parts])
    gains = [jnp.exp2((part[0] - top) * factor) for part in parts]
    total = sum(gain * part[1] for gain, part in zip(gains, parts))
    weighted = sum(gain * part[2] for gain, part in zip(gains, parts))
    return top, total, weighted


def own_unit_body(starts_ref, rows_ref, own_ref, e_ref, dp_ref, stats_ref):
    unit(own_ref, lax.axis_index("ctx"), starts_ref[0:1], rows_ref, e_ref, dp_ref, stats_ref,
         causal=True)


def four_unit_body(starts_ref, rows_ref, four_ref, e_ref, dp_ref, stats_ref):
    here = lax.axis_index("ctx")
    unit(four_ref, here - 4, starts_ref[0:1], rows_ref, e_ref, dp_ref, stats_ref)


def side_unit_body(starts_ref, other_rows, own_ref, four_ref, e_ref, dp_ref, stats_ref):
    side = jnp.where(second_core(), four_ref[...], own_ref[...])
    block = lax.axis_index("ctx") - jnp.where(second_core(), 4, 0)
    unit(side, block, starts_ref[1:2], other_rows, e_ref, dp_ref, stats_ref)


def prepare_body(share, middle, lengths_in, keys_ref, values_ref, queries_ref, d_out_ref,
                 split_out, starts_ref, own_ref, rows_ref, lengths_ref, split_ref, sems):
    heads, tokens, width = queries_ref.shape
    group = lax.axis_index("head") // share
    lengths = pltpu.make_async_copy(lengths_in, lengths_ref, sems.at[0])
    copies = [
        pltpu.make_async_copy(keys_ref.at[group], own_ref.at[:, :width], sems.at[1]),
        pltpu.make_async_copy(values_ref.at[group], own_ref.at[:, width:], sems.at[2]),
        pltpu.make_async_copy(queries_ref, rows_ref.at[:heads], sems.at[3]),
        pltpu.make_async_copy(d_out_ref, rows_ref.at[heads:], sems.at[4]),
    ]
    for copy in [lengths] + copies:
        copy.start()
    lengths.wait()
    end, split = jnp.int32(0), jnp.int32(0)
    for d in range(lengths_ref.shape[0]):
        end = end + lengths_ref[d]
        split = jnp.where(end == middle, 1, split)
    split_ref[0] = split
    copies.append(pltpu.make_async_copy(split_ref, split_out, sems.at[5]))
    copies[-1].start()
    here = lax.axis_index("ctx")
    starts_ref[0:1] = doc_starts(lengths_ref, here, tokens)
    starts_ref[1:2] = doc_starts(lengths_ref, jnp.bitwise_xor(here, 1), tokens)
    for copy in copies:
        copy.wait()


def near_side_unit_body(starts_ref, other_rows, own_ref, e_ref, dp_ref, stats_ref):
    block = jnp.where(second_core(), -1, lax.axis_index("ctx"))
    unit(own_ref, block, starts_ref[1:2], other_rows, e_ref, dp_ref, stats_ref)


def write_rows(ref, values):
    for row, value in enumerate(values):
        ref[row:row + 1] = value


def cross_unit_body(starts_ref, other_rows, two_ref, stats_side,
                    e_ref, dp_ref, stats_ref, others_ref):
    factor = other_rows.shape[-1] ** -0.5 * math.log2(math.e)
    unit(two_ref, lax.axis_index("ctx") - 2, starts_ref[1:2], other_rows,
         e_ref, dp_ref, stats_ref)
    write_rows(others_ref, joined([rows_of(stats_side), rows_of(stats_ref)], factor))
    others_ref[3:4] = jnp.zeros((1, others_ref.shape[1]), f32)


def two_unit_body(starts_ref, rows_ref, two_ref, *refs):
    earlier, (e_ref, dp_ref, stats_ref, mine_ref) = refs[:-4], refs[-4:]
    factor = rows_ref.shape[-1] ** -0.5 * math.log2(math.e)
    unit(two_ref, lax.axis_index("ctx") - 2, starts_ref[0:1], rows_ref,
         e_ref, dp_ref, stats_ref)
    write_rows(mine_ref, joined([rows_of(ref) for ref in earlier + (stats_ref,)], factor))
    mine_ref[3:4] = jnp.zeros((1, mine_ref.shape[1]), f32)


def coefficients(here_ref, taken_ref, stats_refs, width):
    factor = width ** -0.5 * math.log2(math.e)
    top, total, weighted = joined([rows_of(here_ref), rows_of(taken_ref)], factor)
    inverse = 1.0 / total
    return [weighted * inverse] + [
        jnp.exp2((ref[0:1] - top) * factor) * inverse for ref in stats_refs]


def slopes(e_ref, dp_ref, gain, delta, p_ref, ds_ref):
    p = e_ref[...] * gain
    p_ref[...] = p.astype(bf16)
    ds_ref[...] = (p * (dp_ref[...] - delta)).astype(bf16)


def flat(ref):
    heads, tokens, width = ref.shape
    return ref[...].reshape(heads * tokens, width)


def add_terms(sum_ref, ds_ref, p_ref, rows_ref, fresh):
    q_ref, g_ref = both(rows_ref)
    width = q_ref.shape[-1]
    dk = dot(ds_ref[...], flat(q_ref)) * width ** -0.5
    dv = dot(p_ref[...], flat(g_ref))
    if fresh:
        sum_ref[:, :width] = dk
        sum_ref[:, width:] = dv
    else:
        sum_ref[:, :width] += dk
        sum_ref[:, width:] += dv


def my_terms_body(count, mine_ref, taken_ref, *refs):
    stats, refs = refs[:count], refs[count:]
    parts, rows_ref, refs = refs[:4], refs[4], refs[5:]
    coef_ref, ds_refs, sums, p_ref = refs[0], refs[1:3], refs[3:5], refs[5]
    coefs = coefficients(mine_ref, taken_ref, stats, rows_ref.shape[-1])
    write_rows(coef_ref, coefs)
    for at in range(2):
        slopes(parts[2 * at], parts[2 * at + 1], coefs[count - 1 + at], coefs[0], p_ref.at[at],
               ds_refs[at])
        add_terms(sums[at], ds_refs[at], p_ref.at[at], rows_ref, True)


def four_terms_body(others_ref, taken_ref, stats_side, stats_cross, e_side, dp_side,
                    other_rows, part_ref, coef_ref, terms_ref, sum_ref, p_ref, ds_ref):
    coefs = coefficients(others_ref, taken_ref, (stats_side, stats_cross), other_rows.shape[-1])
    write_rows(coef_ref, coefs)
    sum_ref[...] = part_ref[...]

    @pl.when(second_core())
    def _():
        slopes(e_side, dp_side, coef_ref[1:2], coef_ref[0:1], p_ref, ds_ref)
        add_terms(sum_ref, ds_ref, p_ref, other_rows, False)

    terms_ref[...] = sum_ref[...].astype(bf16)


def two_terms_body(coef_ref, e_cross, dp_cross, other_rows, part_ref,
                   terms_ref, ds_cross, p_ref, sum_ref):
    slopes(e_cross, dp_cross, coef_ref[2:3], coef_ref[0:1], p_ref, ds_cross)
    sum_ref[...] = part_ref[...]
    add_terms(sum_ref, ds_cross, p_ref, other_rows, False)
    terms_ref[...] = sum_ref[...].astype(bf16)


def slice_rows(ref, other):
    count = lax.axis_size("head")
    each = ref.shape[0] // count
    parity = jnp.bitwise_xor(lax.rem(lax.axis_index("head"), 2), other)
    return [ref[pl.ds(pl.multiple_of((2 * at + parity) * each, each), each)]
            for at in range(count // 2)]


def halve(sum_ref, kept_ref, given_ref):
    each = sum_ref.shape[0] // lax.axis_size("head")
    for other, out_ref in enumerate((kept_ref, given_ref)):
        for at, value in enumerate(slice_rows(sum_ref, other)):
            out_ref[at * each:(at + 1) * each] = value.astype(out_ref.dtype)


def halved_two_terms_body(others_ref, taken_ref, stats_side, stats_cross, e_cross, dp_cross,
                        other_rows, part_ref,
                        coef_ref, kept_ref, other_ref, ds_cross, p_ref, sum_ref):
    coefs = coefficients(others_ref, taken_ref, (stats_side, stats_cross), other_rows.shape[-1])
    write_rows(coef_ref, coefs)
    slopes(e_cross, dp_cross, coefs[2], coefs[0], p_ref, ds_cross)
    sum_ref[...] = part_ref[...]
    add_terms(sum_ref, ds_cross, p_ref, other_rows, False)
    halve(sum_ref, kept_ref, other_ref)


def near_own_terms_body(coef_ref, e_side, dp_side, other_rows, part_ref,
                        kept_ref, other_ref, ds_side, p_ref, sum_ref):
    slopes(e_side, dp_side, coef_ref[1:2], coef_ref[0:1], p_ref, ds_side)
    sum_ref[...] = part_ref[...]

    @pl.when(jnp.logical_not(second_core()))
    def _():
        add_terms(sum_ref, ds_side, p_ref, other_rows, False)

    halve(sum_ref, kept_ref, other_ref)


def far_four_terms_body(coef_ref, e_side, dp_side, other_rows, part_ref,
                        kept_ref, other_ref, sum_ref, p_ref, ds_ref):
    sum_ref[...] = part_ref[...]

    @pl.when(second_core())
    def _():
        slopes(e_side, dp_side, coef_ref[1:2], coef_ref[0:1], p_ref, ds_ref)
        add_terms(sum_ref, ds_ref, p_ref, other_rows, False)

    halve(sum_ref, kept_ref, other_ref)


def far_own_terms_body(mine_coef, coef_ref, e_own, dp_own, e_side, dp_side, rows_ref,
                       other_rows,
                       kept_ref, other_ref, ds_own, ds_side, p_ref, p_side, sum_ref):
    slopes(e_own, dp_own, mine_coef[1:2], mine_coef[0:1], p_ref, ds_own)
    add_terms(sum_ref, ds_own, p_ref, rows_ref, True)
    slopes(e_side, dp_side, coef_ref[1:2], coef_ref[0:1], p_side, ds_side)

    @pl.when(jnp.logical_not(second_core()))
    def _():
        add_terms(sum_ref, ds_side, p_side, other_rows, False)

    halve(sum_ref, kept_ref, other_ref)


def grads_body(own_ref, two_ref, ds_own, ds_two, ds_side, ds_cross, *refs):
    four_refs, (dq_ref, other_dq_ref) = refs[:-2], refs[-2:]
    width = dq_ref.shape[-1]
    keys, slope_refs = [own_ref[:, :width], two_ref[:, :width]], [ds_own, ds_two]
    side = keys[0]
    if four_refs:
        keys.append(four_refs[0][:, :width])
        slope_refs.append(four_refs[1])
        side = jnp.where(second_core(), keys[2], side)
    query_grads([side, keys[1]], [ds_side, ds_cross], other_dq_ref)
    query_grads(keys, slope_refs, dq_ref)


def add_others_body(use, sum_ref, pair_ref, four_ref, out_ref):
    taken = jnp.where(use(lax.axis_index("ctx")), four_ref[...].astype(f32), 0.0)
    out_ref[...] = sum_ref[...] + pair_ref[...].astype(f32) + taken


def relay_body(kept_ref, four_ref, two_ref, two_pair_ref, out_ref, sent_ref):
    ctx = lax.axis_index("ctx")
    taken = two_ref[...].astype(f32) + two_pair_ref[...].astype(f32)
    out_ref[...] = kept_ref[...] + jnp.where(ctx & 2 == 0, taken, 0.0)
    sent_ref[...] = (four_ref[...] + jnp.where(ctx & 6 == 6, taken, 0.0)).astype(bf16)


def near_first_sum_body(kept_ref, two_ref, two_pair_ref, out_ref):
    taken = two_ref[...].astype(f32) + two_pair_ref[...].astype(f32)
    out_ref[...] = kept_ref[...] + jnp.where(lax.axis_index("ctx") & 2 == 0, taken, 0.0)


def halves_sum_body(share, use, kept_ref, back_ref, here_ref, there_ref):
    each = here_ref.shape[0]
    group = lax.axis_index("head") // share
    for out_ref, at in ((here_ref, group), (there_ref, 1 - group)):
        rows = pl.ds(pl.multiple_of(at * each, each), each)
        taken = back_ref[rows].astype(f32)
        if use is not None:
            taken = jnp.where(use(lax.axis_index("ctx")), taken, 0.0)
        out_ref[...] = (kept_ref[rows] + taken).astype(out_ref.dtype)


def last_body(share, here_ref, taken_ref, dk_ref, dv_ref):
    width = dk_ref.shape[-1]
    group = lax.axis_index("head") // share
    for ref, place in ((here_ref, group), (taken_ref, 1 - group)):
        dk_ref[place] = ref[:, :width]
        dv_ref[place] = ref[:, width:]


def query_grads(keys, ds_refs, out_ref):
    heads, tokens, width = out_ref.shape
    turned = [key.T for key in keys]
    for h in range(heads):
        lanes = slice(h * tokens, (h + 1) * tokens)
        dqt = sum(dot(kt, ds[:, lanes]) for kt, ds in zip(turned, ds_refs))
        out_ref[h] = (dqt.T * width ** -0.5).astype(out_ref.dtype)


def own_terms_body(mine_coef, coef_ref, e_own, dp_own, e_side, dp_side, rows_ref,
                   other_rows, own_ref, two_ref, ds_two, ds_cross, four_ref, ds_four,
                   terms_ref, dq_ref, other_dq_ref, ds_own, ds_side, p_ref, p_side):
    width = dq_ref.shape[-1]
    own, two, four = [ref[:, :width] for ref in (own_ref, two_ref, four_ref)]
    slopes(e_side, dp_side, coef_ref[1:2], coef_ref[0:1], p_side, ds_side)
    query_grads([jnp.where(second_core(), four, own), two], [ds_side, ds_cross], other_dq_ref)
    slopes(e_own, dp_own, mine_coef[1:2], mine_coef[0:1], p_ref, ds_own)
    add_terms(terms_ref, ds_own, p_ref, rows_ref, True)

    @pl.when(jnp.logical_not(second_core()))
    def _():
        add_terms(terms_ref, ds_side, p_side, other_rows, False)

    query_grads([own, two, four], [ds_own, ds_two, ds_four], dq_ref)


def add_grads_body(mine_ref, taken_ref, dq_ref):
    dq_ref[...] = (mine_ref[...] + taken_ref[...].astype(f32)).astype(dq_ref.dtype)


def sums_body(own_terms, four_back, two_back, out_ref):
    taken = four_back[...].astype(f32) + two_back[...].astype(f32)
    out_ref[...] = (own_terms[...] + taken).astype(bf16)


def per_device(queries, keys, values, d_out, doc_lengths):
    ctx_count, (heads, tokens, width) = lax.axis_size("ctx"), queries.shape
    middle = ctx_count // 2 * tokens
    split, starts, own, rows = pl.pallas_call(
        functools.partial(prepare_body, GROUP // heads, middle),
        out_shape=(shape((1,), i32), shape((2, tokens), i32), shape((tokens, 2 * width), bf16),
                   shape((2 * heads, tokens, width), bf16)),
        in_specs=[pl.BlockSpec(memory_space=pl.ANY)] * 5,
        out_specs=(pl.BlockSpec(memory_space=pl.ANY), VMEM, VMEM, VMEM),
        scratch_shapes=[pltpu.SMEM(doc_lengths.shape, i32), pltpu.SMEM((1,), i32),
                        pltpu.SemaphoreType.DMA((6,))],
        name="prepare",
    )(*[pltpu.with_memory_space_constraint(value, pltpu.HBM)
        for value in (doc_lengths, keys, values, queries, d_out)])
    operands = (rows, own, starts)
    if ctx_count != 2 * REACH or lax.axis_size("head") * heads != 2 * GROUP or 2 * heads != GROUP:
        return gradients(True, *operands)
    return lax.switch(split[0], [functools.partial(gradients, True),
                                 functools.partial(gradients, False)], *operands)


def gradients(far, row_data, own, starts):
    heads, (tokens, width) = row_data.shape[0] // 2, row_data.shape[1:]
    head_count = lax.axis_size("head")
    share = GROUP // heads
    groups = head_count // share
    rows = heads * tokens
    ctx = lax.axis_index("ctx")
    mutual = lax.axis_size("ctx") == 2 * REACH and share == groups == 2
    pair = (tokens, 2 * width)
    all_rows = (heads, tokens, width)
    stats = shape((3, rows), f32)
    wide = shape((tokens, rows), f32)
    half = shape((tokens, rows), bf16)
    half_scratch = pltpu.VMEM((tokens, rows), bf16)
    halves_scratch = pltpu.VMEM((2, tokens, rows), bf16)
    pair_scratch = pltpu.VMEM(pair, f32)

    if far:
        four = exchanged(own, "ctx", 4) if mutual else shifted(own, 4)
    two = [exchanged(own, "ctx", 2) if mutual else shifted(own, 2)]
    if far and mutual:
        two.append(exchanged(own, "ctx", 6))
    e_own, dp_own, stats_own = call(
        own_unit_body, "own_unit", [VMEM] * 3, (wide, wide, stats))(starts, row_data, own)
    other_rows = exchanged(row_data, "ctx", 1)
    if far:
        four, stats_own = lax.optimization_barrier((four, stats_own))
        e_four, dp_four, stats_four = call(
            four_unit_body, "four_unit", [VMEM] * 3, (wide, wide, stats))(starts, row_data, four)
        other_rows, stats_four = lax.optimization_barrier((other_rows, stats_four))
        e_side, dp_side, stats_side = call(
            side_unit_body, "side_unit", [VMEM] * 4, (wide, wide, stats),
        )(starts, other_rows, own, four)
    else:
        e_side, dp_side, stats_side = call(
            near_side_unit_body, "side_unit", [VMEM] * 3, (wide, wide, stats),
        )(starts, other_rows, own)
    *two, stats_side, stats_own = lax.optimization_barrier((*two, stats_side, stats_own))
    mine_stats = (stats_own, stats_four) if far else (stats_own,)
    two = jnp.where(ctx & 2 == 2, *two) if len(two) == 2 else two[0]
    few = shape((4, rows), f32)
    e_cross, dp_cross, stats_cross, others = call(
        cross_unit_body, "cross_unit", [VMEM] * 4, (wide, wide, stats, few),
    )(starts, other_rows, two, stats_side)
    taken_others = exchanged(others, "ctx", 1)
    e_two, dp_two, stats_two, mine = call(
        two_unit_body, "two_unit", [VMEM] * (3 + len(mine_stats)), (wide, wide, stats, few),
    )(starts, row_data, two, *mine_stats)
    taken_mine = exchanged(mine, "ctx", 1)
    mine_stats += (stats_two,)
    parts = ((e_four, dp_four) if far else (e_own, dp_own)) + (e_two, dp_two)
    mine_coef, ds_first, ds_two, first_part, two_part = call(
        functools.partial(my_terms_body, len(mine_stats)), "my_terms",
        [VMEM] * (7 + len(mine_stats)),
        (few, half, half, shape(pair, f32), shape(pair, f32)), (halves_scratch,),
    )(mine, taken_others, *mine_stats, *parts, row_data)
    last_stats = (others, taken_mine, stats_side, stats_cross)
    slices = (tokens // 2, 2 * width)
    slice_dims = (tokens // head_count, 2 * width)
    if not mutual:
        coef, four_terms = call(
            four_terms_body, "four_terms", [VMEM] * 8, (few, shape(pair, bf16)),
            (pair_scratch, half_scratch, half_scratch),
        )(*last_stats, e_side, dp_side, other_rows, first_part)
        two_terms, ds_cross = call(
            two_terms_body, "two_terms", [VMEM] * 5, (shape(pair, bf16), half),
            (half_scratch, pair_scratch),
        )(coef, e_cross, dp_cross, other_rows, two_part)
        backs = [shifted(four_terms, -4), shifted(two_terms, -2)]
        own_terms, my_grads, other_grads = call(
            own_terms_body, "own_terms", [VMEM] * 14,
            (shape(pair, f32), shape(all_rows, f32), shape(all_rows, bf16)),
            (half_scratch,) * 4,
        )(mine_coef, coef, e_own, dp_own, e_side, dp_side, row_data, other_rows, own, two,
          ds_two, ds_cross, four, ds_first)
        taken_grads = exchanged(other_grads, "ctx", 1)
        d_queries, = call(
            add_grads_body, "add_grads", [VMEM] * 2, (shape(all_rows, bf16),),
        )(my_grads, taken_grads)
        sums, = call(sums_body, "sums", [VMEM] * 3, (shape(pair, bf16),))(own_terms, *backs)
        pieces = lax.all_to_all(sums.reshape(head_count, *slice_dims), "head", 0, 0)
        result = jnp.sum(
            pieces.reshape(groups, share, *slice_dims).astype(f32), axis=1).astype(bf16)
        return d_queries, result[..., :width], result[..., width:]

    halves = (shape(slices, bf16), shape(slices, bf16))
    part = shape(slices, f32)
    coef, two_kept, two_other, ds_cross = call(
        halved_two_terms_body, "two_terms", [VMEM] * 8, (few,) + halves + (half,),
        (half_scratch, pair_scratch),
    )(*last_stats, e_cross, dp_cross, other_rows, two_part)
    two_back = exchanged(two_kept, "ctx", 2)
    two_pair = exchanged(two_other, ("ctx", "head"), 2 * head_count + 1)
    if far:
        four_kept, four_other = call(
            far_four_terms_body, "four_terms", [VMEM] * 5, (part, halves[1]),
            (pair_scratch, half_scratch, half_scratch),
        )(coef, e_side, dp_side, other_rows, first_part)
        four_pair = exchanged(four_other, ("ctx", "head"), 4 * head_count + 1)
        own_kept, own_other, ds_own, ds_side = call(
            far_own_terms_body, "own_terms", [VMEM] * 8, (part, halves[1], half, half),
            (half_scratch, half_scratch, pair_scratch),
        )(mine_coef, coef, e_own, dp_own, e_side, dp_side, row_data, other_rows)
    else:
        ds_own = ds_first
        own_kept, own_other, ds_side = call(
            near_own_terms_body, "own_terms", [VMEM] * 5, (part, halves[1], half),
            (half_scratch, pair_scratch),
        )(coef, e_side, dp_side, other_rows, first_part)
    own_pair = exchanged(own_other, "head", 1)
    four_refs = (four, ds_first) if far else ()
    my_grads, other_grads = call(
        grads_body, "query_grads", [VMEM] * (6 + len(four_refs)),
        (shape(all_rows, f32), shape(all_rows, bf16)),
    )(own, two, ds_own, ds_two, ds_side, ds_cross, *four_refs)
    owns_four = lambda i: i < 4
    if far:
        own_kept, relayed = call(
            relay_body, "relay", [VMEM] * 4, (part, halves[0]),
        )(own_kept, four_kept, two_back, two_pair)
        four_back = exchanged(relayed, "ctx", 4)
        own_kept, = call(functools.partial(add_others_body, owns_four), "add_others", [VMEM] * 3,
                         (part,))(own_kept, own_pair, four_pair)
        final, use = four_back, owns_four
    else:
        own_kept, = call(
            near_first_sum_body, "first_sum", [VMEM] * 3, (part,),
        )(own_kept, two_back, two_pair)
        final, use = own_pair, None
    kept, sent = call(
        functools.partial(halves_sum_body, share, use), "sums", [VMEM] * 2,
        (shape(slice_dims, bf16),) * 2)(own_kept, final)
    other_grads, kept = lax.optimization_barrier((other_grads, kept))
    taken_grads = exchanged(other_grads, "ctx", 1)
    d_queries, = call(
        add_grads_body, "add_grads", [VMEM] * 2, (shape(all_rows, bf16),),
    )(my_grads, taken_grads)
    last = exchanged(sent, "head", share)
    last, d_queries = lax.optimization_barrier((last, d_queries))
    d_keys, d_values = call(
        functools.partial(last_body, share), "last", [VMEM] * 2,
        (shape((groups, tokens // head_count, width), bf16),) * 2)(kept, last)
    return d_queries, d_keys, d_values


def solution(mesh):
    placed = (
        P("head", "ctx", None),
        P(None, "ctx", None),
        P(None, "ctx", None),
        P("head", "ctx", None),
        P(),
    )
    return jax.shard_map(
        per_device,
        mesh=mesh,
        in_specs=placed,
        out_specs=(
            P("head", "ctx", None),
            P(None, ("ctx", "head"), None),
            P(None, ("ctx", "head"), None),
        ),
        check_vma=False,
    )
```

```python
import functools
import math

import jax
import jax.numpy as jnp
from jax import lax
from jax.experimental import pallas as pl
from jax.experimental.pallas import tpu as pltpu
from jax.sharding import PartitionSpec as P

GROUP = 8
REACH = 4
MASKED = -1e30
NT = (((1,), (1,)), ((), ()))
NN = (((1,), (0,)), ((), ()))
VMEM = pl.BlockSpec(memory_space=pltpu.VMEM)
SMEM = pl.BlockSpec(memory_space=pltpu.SMEM)
bf16, f32, i32 = jnp.bfloat16, jnp.float32, jnp.int32


def dot(a, b, dims=NN):
    return lax.dot_general(a, b, dims, preferred_element_type=f32)


def shape(dims, dtype):
    return jax.ShapeDtypeStruct(dims, dtype)


def call(body, name, in_specs, outs, scratch=()):
    return pl.pallas_call(
        body,
        out_shape=outs,
        in_specs=in_specs,
        out_specs=(VMEM,) * len(outs),
        scratch_shapes=scratch,
        compiler_params=pltpu.CompilerParams(vmem_limit_bytes=20 * 2**20),
        cost_estimate=pl.CostEstimate(flops=2**20, bytes_accessed=2**10, transcendentals=0),
        name=name,
    )


def shifted(block, distance):
    count = lax.axis_size("ctx")
    route = [(i - distance, i) for i in range(count) if 0 <= i - distance < count]
    return lax.ppermute(block, "ctx", route)


def exchanged(block, axis, mask):
    count = math.prod(lax.axis_size(name) for name in axis) if isinstance(axis, tuple) else (
        lax.axis_size(axis))
    return lax.ppermute(block, axis, [(i, i ^ mask) for i in range(count)])


def both(rows_ref):
    heads = rows_ref.shape[0] // 2
    return rows_ref.at[:heads], rows_ref.at[heads:]


def second_core():
    return lax.rem(lax.axis_index("ctx"), 2) == 1


def doc_starts(lengths_ref, block, tokens):
    row_pos = block * tokens + lax.broadcasted_iota(i32, (1, tokens), 1)
    starts = jnp.zeros((1, tokens), i32)
    end = jnp.int32(0)
    for d in range(lengths_ref.shape[0]):
        end = end + lengths_ref[d]
        starts = jnp.where(row_pos >= end, end, starts)
    return starts


def unit(pair, key_block, starts, rows_ref, e_ref, dp_ref, stats_ref, causal=False):
    q_ref, g_ref = both(rows_ref)
    heads, tokens, width = q_ref.shape
    factor = width ** -0.5 * math.log2(math.e)
    key_iota = lax.broadcasted_iota(i32, (tokens, 1), 0)
    allowed = key_block * tokens + key_iota >= starts
    if causal:
        allowed = allowed & (key_iota <= lax.broadcasted_iota(i32, (1, tokens), 1))
    for h in range(heads):
        lanes = slice(h * tokens, (h + 1) * tokens)
        s = jnp.where(allowed, dot(pair[:, :width], q_ref[h], NT), MASKED)
        top = jnp.max(s, axis=0, keepdims=True)
        e = jnp.exp2((s - top) * factor)
        dp = dot(pair[:, width:], g_ref[h], NT)
        e_ref[:, lanes] = e
        dp_ref[:, lanes] = dp
        stats_ref[0:1, lanes] = top
        stats_ref[1:2, lanes] = jnp.sum(e, axis=0, keepdims=True)
        stats_ref[2:3, lanes] = jnp.sum(e * dp, axis=0, keepdims=True)


def rows_of(ref, first=0):
    return [ref[first + row:first + row + 1] for row in range(3)]


def joined(parts, factor):
    top = functools.reduce(jnp.maximum, [part[0] for part in parts])
    gains = [jnp.exp2((part[0] - top) * factor) for part in parts]
    total = sum(gain * part[1] for gain, part in zip(gains, parts))
    weighted = sum(gain * part[2] for gain, part in zip(gains, parts))
    return top, total, weighted


def own_unit_body(starts_ref, rows_ref, own_ref, e_ref, dp_ref, stats_ref, *copies):
    for copy_ref in copies:
        copy_ref[...] = own_ref[...]
    unit(own_ref, lax.axis_index("ctx"), starts_ref[0:1], rows_ref, e_ref, dp_ref, stats_ref,
         causal=True)


def four_unit_body(starts_ref, rows_ref, four_ref, e_ref, dp_ref, stats_ref):
    here = lax.axis_index("ctx")
    unit(four_ref, here - 4, starts_ref[0:1], rows_ref, e_ref, dp_ref, stats_ref)


def side_unit_body(starts_ref, other_rows, own_ref, four_ref, e_ref, dp_ref, stats_ref):
    side = jnp.where(second_core(), four_ref[...], own_ref[...])
    block = lax.axis_index("ctx") - jnp.where(second_core(), 4, 0)
    unit(side, block, starts_ref[1:2], other_rows, e_ref, dp_ref, stats_ref)


def prepare_body(share, middle, lengths_in, keys_ref, values_ref, queries_ref, d_out_ref,
                 split_out, starts_ref, own_ref, rows_ref, lengths_ref, split_ref, sems):
    heads, tokens, width = queries_ref.shape
    group = lax.axis_index("head") // share
    lengths = pltpu.make_async_copy(lengths_in, lengths_ref, sems.at[0])
    copies = [
        pltpu.make_async_copy(keys_ref.at[group], own_ref.at[:, :width], sems.at[1]),
        pltpu.make_async_copy(values_ref.at[group], own_ref.at[:, width:], sems.at[2]),
        pltpu.make_async_copy(queries_ref, rows_ref.at[:heads], sems.at[3]),
        pltpu.make_async_copy(d_out_ref, rows_ref.at[heads:], sems.at[4]),
    ]
    for copy in [lengths] + copies:
        copy.start()
    lengths.wait()
    end, split = jnp.int32(0), jnp.int32(0)
    for d in range(lengths_ref.shape[0]):
        end = end + lengths_ref[d]
        split = jnp.where(end == middle, 1, split)
    split_ref[0] = split
    copies.append(pltpu.make_async_copy(split_ref, split_out, sems.at[5]))
    copies[-1].start()
    here = lax.axis_index("ctx")
    starts_ref[0:1] = doc_starts(lengths_ref, here, tokens)
    starts_ref[1:2] = doc_starts(lengths_ref, jnp.bitwise_xor(here, 1), tokens)
    for copy in copies:
        copy.wait()


def near_side_unit_body(starts_ref, other_rows, own_ref, e_ref, dp_ref, stats_ref):
    block = jnp.where(second_core(), -1, lax.axis_index("ctx"))
    unit(own_ref, block, starts_ref[1:2], other_rows, e_ref, dp_ref, stats_ref)


def write_rows(ref, values):
    for row, value in enumerate(values):
        ref[row:row + 1] = value


def cross_unit_body(starts_ref, other_rows, two_ref, stats_side,
                    e_ref, dp_ref, stats_ref, others_ref):
    factor = other_rows.shape[-1] ** -0.5 * math.log2(math.e)
    unit(two_ref, lax.axis_index("ctx") - 2, starts_ref[1:2], other_rows,
         e_ref, dp_ref, stats_ref)
    write_rows(others_ref, joined([rows_of(stats_side), rows_of(stats_ref)], factor))
    others_ref[3:4] = jnp.zeros((1, others_ref.shape[1]), f32)


def two_unit_body(starts_ref, rows_ref, two_ref, *refs):
    earlier, (e_ref, dp_ref, stats_ref, mine_ref) = refs[:-4], refs[-4:]
    factor = rows_ref.shape[-1] ** -0.5 * math.log2(math.e)
    unit(two_ref, lax.axis_index("ctx") - 2, starts_ref[0:1], rows_ref,
         e_ref, dp_ref, stats_ref)
    write_rows(mine_ref, joined([rows_of(ref) for ref in earlier + (stats_ref,)], factor))
    mine_ref[3:4] = jnp.zeros((1, mine_ref.shape[1]), f32)


def coefficients(here_ref, taken_ref, stats_refs, width):
    factor = width ** -0.5 * math.log2(math.e)
    top, total, weighted = joined([rows_of(here_ref), rows_of(taken_ref)], factor)
    inverse = 1.0 / total
    return [weighted * inverse] + [
        jnp.exp2((ref[0:1] - top) * factor) * inverse for ref in stats_refs]


def slopes(e_ref, dp_ref, gain, delta, p_ref, ds_ref):
    p = e_ref[...] * gain
    p_ref[...] = p.astype(bf16)
    ds_ref[...] = (p * (dp_ref[...] - delta)).astype(bf16)


def flat(ref):
    heads, tokens, width = ref.shape
    return ref[...].reshape(heads * tokens, width)


def add_terms(sum_ref, ds_ref, p_ref, rows_ref, fresh):
    q_ref, g_ref = both(rows_ref)
    width = q_ref.shape[-1]
    dk = dot(ds_ref[...], flat(q_ref)) * width ** -0.5
    dv = dot(p_ref[...], flat(g_ref))
    if fresh:
        sum_ref[:, :width] = dk
        sum_ref[:, width:] = dv
    else:
        sum_ref[:, :width] += dk
        sum_ref[:, width:] += dv


def my_terms_body(count, mine_ref, taken_ref, *refs):
    stats, refs = refs[:count], refs[count:]
    parts, rows_ref, refs = refs[:4], refs[4], refs[5:]
    coef_ref, ds_refs, sums, p_ref = refs[0], refs[1:3], refs[3:5], refs[5]
    coefs = coefficients(mine_ref, taken_ref, stats, rows_ref.shape[-1])
    write_rows(coef_ref, coefs)
    for at in range(2):
        slopes(parts[2 * at], parts[2 * at + 1], coefs[count - 1 + at], coefs[0], p_ref.at[at],
               ds_refs[at])
        add_terms(sums[at], ds_refs[at], p_ref.at[at], rows_ref, True)


def four_terms_body(others_ref, taken_ref, stats_side, stats_cross, e_side, dp_side,
                    other_rows, part_ref, coef_ref, terms_ref, sum_ref, p_ref, ds_ref):
    coefs = coefficients(others_ref, taken_ref, (stats_side, stats_cross), other_rows.shape[-1])
    write_rows(coef_ref, coefs)
    sum_ref[...] = part_ref[...]

    @pl.when(second_core())
    def _():
        slopes(e_side, dp_side, coef_ref[1:2], coef_ref[0:1], p_ref, ds_ref)
        add_terms(sum_ref, ds_ref, p_ref, other_rows, False)

    terms_ref[...] = sum_ref[...].astype(bf16)


def two_terms_body(coef_ref, e_cross, dp_cross, other_rows, part_ref,
                   terms_ref, ds_cross, p_ref, sum_ref):
    slopes(e_cross, dp_cross, coef_ref[2:3], coef_ref[0:1], p_ref, ds_cross)
    sum_ref[...] = part_ref[...]
    add_terms(sum_ref, ds_cross, p_ref, other_rows, False)
    terms_ref[...] = sum_ref[...].astype(bf16)


def slice_rows(ref, other):
    count = lax.axis_size("head")
    each = ref.shape[0] // count
    parity = jnp.bitwise_xor(lax.rem(lax.axis_index("head"), 2), other)
    return [ref[pl.ds(pl.multiple_of((2 * at + parity) * each, each), each)]
            for at in range(count // 2)]


def halve(sum_ref, kept_ref, given_ref):
    each = sum_ref.shape[0] // lax.axis_size("head")
    for other, out_ref in enumerate((kept_ref, given_ref)):
        for at, value in enumerate(slice_rows(sum_ref, other)):
            out_ref[at * each:(at + 1) * each] = value.astype(out_ref.dtype)


def halved_two_terms_body(others_ref, taken_ref, stats_side, stats_cross, e_cross, dp_cross,
                        other_rows, part_ref,
                        coef_ref, kept_ref, other_ref, ds_cross, p_ref, sum_ref):
    coefs = coefficients(others_ref, taken_ref, (stats_side, stats_cross), other_rows.shape[-1])
    write_rows(coef_ref, coefs)
    slopes(e_cross, dp_cross, coefs[2], coefs[0], p_ref, ds_cross)
    sum_ref[...] = part_ref[...]
    add_terms(sum_ref, ds_cross, p_ref, other_rows, False)
    halve(sum_ref, kept_ref, other_ref)


def near_own_terms_body(coef_ref, e_side, dp_side, other_rows, part_ref,
                        kept_ref, other_ref, ds_side, p_ref, sum_ref):
    slopes(e_side, dp_side, coef_ref[1:2], coef_ref[0:1], p_ref, ds_side)
    sum_ref[...] = part_ref[...]

    @pl.when(jnp.logical_not(second_core()))
    def _():
        add_terms(sum_ref, ds_side, p_ref, other_rows, False)

    halve(sum_ref, kept_ref, other_ref)


def far_four_terms_body(coef_ref, e_side, dp_side, other_rows, part_ref,
                        kept_ref, other_ref, sum_ref, p_ref, ds_ref):
    sum_ref[...] = part_ref[...]

    @pl.when(second_core())
    def _():
        slopes(e_side, dp_side, coef_ref[1:2], coef_ref[0:1], p_ref, ds_ref)
        add_terms(sum_ref, ds_ref, p_ref, other_rows, False)

    halve(sum_ref, kept_ref, other_ref)


def far_own_terms_body(mine_coef, coef_ref, e_own, dp_own, e_side, dp_side, rows_ref,
                       other_rows,
                       kept_ref, other_ref, ds_own, ds_side, p_ref, p_side, sum_ref):
    slopes(e_own, dp_own, mine_coef[1:2], mine_coef[0:1], p_ref, ds_own)
    add_terms(sum_ref, ds_own, p_ref, rows_ref, True)
    slopes(e_side, dp_side, coef_ref[1:2], coef_ref[0:1], p_side, ds_side)

    @pl.when(jnp.logical_not(second_core()))
    def _():
        add_terms(sum_ref, ds_side, p_side, other_rows, False)

    halve(sum_ref, kept_ref, other_ref)


def grads_body(own_ref, two_ref, ds_own, ds_two, ds_side, ds_cross, *refs):
    four_refs, (dq_ref, other_dq_ref) = refs[:-2], refs[-2:]
    width = dq_ref.shape[-1]
    keys, slope_refs = [own_ref[:, :width], two_ref[:, :width]], [ds_own, ds_two]
    side = keys[0]
    if four_refs:
        keys.append(four_refs[0][:, :width])
        slope_refs.append(four_refs[1])
        side = jnp.where(second_core(), keys[2], side)
    query_grads([side, keys[1]], [ds_side, ds_cross], other_dq_ref)
    query_grads(keys, slope_refs, dq_ref)


def add_others_body(use, sum_ref, pair_ref, four_ref, out_ref):
    taken = jnp.where(use(lax.axis_index("ctx")), four_ref[...].astype(f32), 0.0)
    out_ref[...] = sum_ref[...] + pair_ref[...].astype(f32) + taken


def relay_body(kept_ref, four_ref, two_ref, two_pair_ref, out_ref, sent_ref):
    ctx = lax.axis_index("ctx")
    taken = two_ref[...].astype(f32) + two_pair_ref[...].astype(f32)
    out_ref[...] = kept_ref[...] + jnp.where(ctx & 2 == 0, taken, 0.0)
    sent_ref[...] = (four_ref[...] + jnp.where(ctx & 6 == 6, taken, 0.0)).astype(bf16)


def near_first_sum_body(kept_ref, two_ref, two_pair_ref, out_ref):
    taken = two_ref[...].astype(f32) + two_pair_ref[...].astype(f32)
    out_ref[...] = kept_ref[...] + jnp.where(lax.axis_index("ctx") & 2 == 0, taken, 0.0)


def halves_sum_body(share, use, kept_ref, back_ref, here_ref, there_ref):
    each = here_ref.shape[0]
    group = lax.axis_index("head") // share
    for out_ref, at in ((here_ref, group), (there_ref, 1 - group)):
        rows = pl.ds(pl.multiple_of(at * each, each), each)
        taken = back_ref[rows].astype(f32)
        if use is not None:
            taken = jnp.where(use(lax.axis_index("ctx")), taken, 0.0)
        out_ref[...] = (kept_ref[rows] + taken).astype(out_ref.dtype)


def last_body(share, here_ref, taken_ref, dk_ref, dv_ref):
    width = dk_ref.shape[-1]
    group = lax.axis_index("head") // share
    for ref, place in ((here_ref, group), (taken_ref, 1 - group)):
        dk_ref[place] = ref[:, :width]
        dv_ref[place] = ref[:, width:]


def query_grads(keys, ds_refs, out_ref):
    heads, tokens, width = out_ref.shape
    turned = [key.T for key in keys]
    for h in range(heads):
        lanes = slice(h * tokens, (h + 1) * tokens)
        dqt = sum(dot(kt, ds[:, lanes]) for kt, ds in zip(turned, ds_refs))
        out_ref[h] = (dqt.T * width ** -0.5).astype(out_ref.dtype)


def own_terms_body(mine_coef, coef_ref, e_own, dp_own, e_side, dp_side, rows_ref,
                   other_rows, own_ref, two_ref, ds_two, ds_cross, four_ref, ds_four,
                   terms_ref, dq_ref, other_dq_ref, ds_own, ds_side, p_ref, p_side):
    width = dq_ref.shape[-1]
    own, two, four = [ref[:, :width] for ref in (own_ref, two_ref, four_ref)]
    slopes(e_side, dp_side, coef_ref[1:2], coef_ref[0:1], p_side, ds_side)
    query_grads([jnp.where(second_core(), four, own), two], [ds_side, ds_cross], other_dq_ref)
    slopes(e_own, dp_own, mine_coef[1:2], mine_coef[0:1], p_ref, ds_own)
    add_terms(terms_ref, ds_own, p_ref, rows_ref, True)

    @pl.when(jnp.logical_not(second_core()))
    def _():
        add_terms(terms_ref, ds_side, p_side, other_rows, False)

    query_grads([own, two, four], [ds_own, ds_two, ds_four], dq_ref)


def add_grads_body(mine_ref, taken_ref, dq_ref):
    dq_ref[...] = (mine_ref[...] + taken_ref[...].astype(f32)).astype(dq_ref.dtype)


def sums_body(own_terms, four_back, two_back, out_ref):
    taken = four_back[...].astype(f32) + two_back[...].astype(f32)
    out_ref[...] = (own_terms[...] + taken).astype(bf16)


def per_device(queries, keys, values, d_out, doc_lengths):
    ctx_count, (heads, tokens, width) = lax.axis_size("ctx"), queries.shape
    middle = ctx_count // 2 * tokens
    split, starts, own, rows = pl.pallas_call(
        functools.partial(prepare_body, GROUP // heads, middle),
        out_shape=(shape((1,), i32), shape((2, tokens), i32), shape((tokens, 2 * width), bf16),
                   shape((2 * heads, tokens, width), bf16)),
        in_specs=[pl.BlockSpec(memory_space=pl.ANY)] * 5,
        out_specs=(pl.BlockSpec(memory_space=pl.ANY), VMEM, VMEM, VMEM),
        scratch_shapes=[pltpu.SMEM(doc_lengths.shape, i32), pltpu.SMEM((1,), i32),
                        pltpu.SemaphoreType.DMA((6,))],
        name="prepare",
    )(*[pltpu.with_memory_space_constraint(value, pltpu.HBM)
        for value in (doc_lengths, keys, values, queries, d_out)])
    operands = (rows, own, starts)
    if ctx_count != 2 * REACH or lax.axis_size("head") * heads != 2 * GROUP or 2 * heads != GROUP:
        return gradients(True, *operands)
    return lax.switch(split[0], [functools.partial(gradients, True),
                                 functools.partial(gradients, False)], *operands)


def gradients(far, row_data, own, starts):
    heads, (tokens, width) = row_data.shape[0] // 2, row_data.shape[1:]
    head_count = lax.axis_size("head")
    share = GROUP // heads
    groups = head_count // share
    rows = heads * tokens
    ctx = lax.axis_index("ctx")
    mutual = lax.axis_size("ctx") == 2 * REACH and share == groups == 2
    pair = (tokens, 2 * width)
    all_rows = (heads, tokens, width)
    stats = shape((3, rows), f32)
    wide = shape((tokens, rows), f32)
    half = shape((tokens, rows), bf16)
    half_scratch = pltpu.VMEM((tokens, rows), bf16)
    halves_scratch = pltpu.VMEM((2, tokens, rows), bf16)
    pair_scratch = pltpu.VMEM(pair, f32)

    if far:
        four = exchanged(own, "ctx", 4) if mutual else shifted(own, 4)
    e_own, dp_own, stats_own, *copies = call(
        own_unit_body, "own_unit", [VMEM] * 3,
        (wide, wide, stats) + ((shape(pair, bf16),) if far else ()))(starts, row_data, own)
    sent = copies[0] if far else own
    two = [exchanged(sent, "ctx", 2) if mutual else shifted(sent, 2)]
    if far and mutual:
        two.append(exchanged(sent, "ctx", 6))
    other_rows = exchanged(row_data, "ctx", 1)
    if far:
        four, stats_own = lax.optimization_barrier((four, stats_own))
        e_four, dp_four, stats_four = call(
            four_unit_body, "four_unit", [VMEM] * 3, (wide, wide, stats))(starts, row_data, four)
        other_rows, stats_four = lax.optimization_barrier((other_rows, stats_four))
        e_side, dp_side, stats_side = call(
            side_unit_body, "side_unit", [VMEM] * 4, (wide, wide, stats),
        )(starts, other_rows, own, four)
    else:
        e_side, dp_side, stats_side = call(
            near_side_unit_body, "side_unit", [VMEM] * 3, (wide, wide, stats),
        )(starts, other_rows, own)
    *two, stats_side, stats_own = lax.optimization_barrier((*two, stats_side, stats_own))
    mine_stats = (stats_own, stats_four) if far else (stats_own,)
    two = jnp.where(ctx & 2 == 2, *two) if len(two) == 2 else two[0]
    few = shape((4, rows), f32)
    e_cross, dp_cross, stats_cross, others = call(
        cross_unit_body, "cross_unit", [VMEM] * 4, (wide, wide, stats, few),
    )(starts, other_rows, two, stats_side)
    taken_others = exchanged(others, "ctx", 1)
    e_two, dp_two, stats_two, mine = call(
        two_unit_body, "two_unit", [VMEM] * (3 + len(mine_stats)), (wide, wide, stats, few),
    )(starts, row_data, two, *mine_stats)
    taken_mine = exchanged(mine, "ctx", 1)
    mine_stats += (stats_two,)
    parts = ((e_four, dp_four) if far else (e_own, dp_own)) + (e_two, dp_two)
    mine_coef, ds_first, ds_two, first_part, two_part = call(
        functools.partial(my_terms_body, len(mine_stats)), "my_terms",
        [VMEM] * (7 + len(mine_stats)),
        (few, half, half, shape(pair, f32), shape(pair, f32)), (halves_scratch,),
    )(mine, taken_others, *mine_stats, *parts, row_data)
    last_stats = (others, taken_mine, stats_side, stats_cross)
    slices = (tokens // 2, 2 * width)
    slice_dims = (tokens // head_count, 2 * width)
    if not mutual:
        coef, four_terms = call(
            four_terms_body, "four_terms", [VMEM] * 8, (few, shape(pair, bf16)),
            (pair_scratch, half_scratch, half_scratch),
        )(*last_stats, e_side, dp_side, other_rows, first_part)
        two_terms, ds_cross = call(
            two_terms_body, "two_terms", [VMEM] * 5, (shape(pair, bf16), half),
            (half_scratch, pair_scratch),
        )(coef, e_cross, dp_cross, other_rows, two_part)
        backs = [shifted(four_terms, -4), shifted(two_terms, -2)]
        own_terms, my_grads, other_grads = call(
            own_terms_body, "own_terms", [VMEM] * 14,
            (shape(pair, f32), shape(all_rows, f32), shape(all_rows, bf16)),
            (half_scratch,) * 4,
        )(mine_coef, coef, e_own, dp_own, e_side, dp_side, row_data, other_rows, own, two,
          ds_two, ds_cross, four, ds_first)
        taken_grads = exchanged(other_grads, "ctx", 1)
        d_queries, = call(
            add_grads_body, "add_grads", [VMEM] * 2, (shape(all_rows, bf16),),
        )(my_grads, taken_grads)
        sums, = call(sums_body, "sums", [VMEM] * 3, (shape(pair, bf16),))(own_terms, *backs)
        pieces = lax.all_to_all(sums.reshape(head_count, *slice_dims), "head", 0, 0)
        result = jnp.sum(
            pieces.reshape(groups, share, *slice_dims).astype(f32), axis=1).astype(bf16)
        return d_queries, result[..., :width], result[..., width:]

    halves = (shape(slices, bf16), shape(slices, bf16))
    part = shape(slices, f32)
    coef, two_kept, two_other, ds_cross = call(
        halved_two_terms_body, "two_terms", [VMEM] * 8, (few,) + halves + (half,),
        (half_scratch, pair_scratch),
    )(*last_stats, e_cross, dp_cross, other_rows, two_part)
    two_back = exchanged(two_kept, "ctx", 2)
    two_pair = exchanged(two_other, ("ctx", "head"), 2 * head_count + 1)
    if far:
        four_kept, four_other = call(
            far_four_terms_body, "four_terms", [VMEM] * 5, (part, halves[1]),
            (pair_scratch, half_scratch, half_scratch),
        )(coef, e_side, dp_side, other_rows, first_part)
        four_pair = exchanged(four_other, ("ctx", "head"), 4 * head_count + 1)
        own_kept, own_other, ds_own, ds_side = call(
            far_own_terms_body, "own_terms", [VMEM] * 8, (part, halves[1], half, half),
            (half_scratch, half_scratch, pair_scratch),
        )(mine_coef, coef, e_own, dp_own, e_side, dp_side, row_data, other_rows)
    else:
        ds_own = ds_first
        own_kept, own_other, ds_side = call(
            near_own_terms_body, "own_terms", [VMEM] * 5, (part, halves[1], half),
            (half_scratch, pair_scratch),
        )(coef, e_side, dp_side, other_rows, first_part)
    own_pair = exchanged(own_other, "head", 1)
    four_refs = (four, ds_first) if far else ()
    my_grads, other_grads = call(
        grads_body, "query_grads", [VMEM] * (6 + len(four_refs)),
        (shape(all_rows, f32), shape(all_rows, bf16)),
    )(own, two, ds_own, ds_two, ds_side, ds_cross, *four_refs)
    owns_four = lambda i: i < 4
    if far:
        own_kept, relayed = call(
            relay_body, "relay", [VMEM] * 4, (part, halves[0]),
        )(own_kept, four_kept, two_back, two_pair)
        four_back = exchanged(relayed, "ctx", 4)
        own_kept, = call(functools.partial(add_others_body, owns_four), "add_others", [VMEM] * 3,
                         (part,))(own_kept, own_pair, four_pair)
        final, use = four_back, owns_four
    else:
        own_kept, = call(
            near_first_sum_body, "first_sum", [VMEM] * 3, (part,),
        )(own_kept, two_back, two_pair)
        final, use = own_pair, None
    kept, sent = call(
        functools.partial(halves_sum_body, share, use), "sums", [VMEM] * 2,
        (shape(slice_dims, bf16),) * 2)(own_kept, final)
    other_grads, kept = lax.optimization_barrier((other_grads, kept))
    taken_grads = exchanged(other_grads, "ctx", 1)
    d_queries, = call(
        add_grads_body, "add_grads", [VMEM] * 2, (shape(all_rows, bf16),),
    )(my_grads, taken_grads)
    last = exchanged(sent, "head", share)
    last, d_queries = lax.optimization_barrier((last, d_queries))
    d_keys, d_values = call(
        functools.partial(last_body, share), "last", [VMEM] * 2,
        (shape((groups, tokens // head_count, width), bf16),) * 2)(kept, last)
    return d_queries, d_keys, d_values


def solution(mesh):
    placed = (
        P("head", "ctx", None),
        P(None, "ctx", None),
        P(None, "ctx", None),
        P("head", "ctx", None),
        P(),
    )
    return jax.shard_map(
        per_device,
        mesh=mesh,
        in_specs=placed,
        out_specs=(
            P("head", "ctx", None),
            P(None, ("ctx", "head"), None),
            P(None, ("ctx", "head"), None),
        ),
        check_vma=False,
    )
```

```python
import functools
import math

import jax
import jax.numpy as jnp
from jax import lax
from jax.experimental import pallas as pl
from jax.experimental.pallas import tpu as pltpu
from jax.sharding import PartitionSpec as P

GROUP = 8
REACH = 4
MASKED = -1e30
NT = (((1,), (1,)), ((), ()))
NN = (((1,), (0,)), ((), ()))
VMEM = pl.BlockSpec(memory_space=pltpu.VMEM)
SMEM = pl.BlockSpec(memory_space=pltpu.SMEM)
bf16, f32, i32 = jnp.bfloat16, jnp.float32, jnp.int32


def dot(a, b, dims=NN):
    return lax.dot_general(a, b, dims, preferred_element_type=f32)


def shape(dims, dtype):
    return jax.ShapeDtypeStruct(dims, dtype)


def call(body, name, in_specs, outs, scratch=()):
    return pl.pallas_call(
        body,
        out_shape=outs,
        in_specs=in_specs,
        out_specs=(VMEM,) * len(outs),
        scratch_shapes=scratch,
        compiler_params=pltpu.CompilerParams(vmem_limit_bytes=20 * 2**20),
        cost_estimate=pl.CostEstimate(flops=2**20, bytes_accessed=2**10, transcendentals=0),
        name=name,
    )


def shifted(block, distance):
    count = lax.axis_size("ctx")
    route = [(i - distance, i) for i in range(count) if 0 <= i - distance < count]
    return lax.ppermute(block, "ctx", route)


def exchanged(block, axis, mask):
    count = math.prod(lax.axis_size(name) for name in axis) if isinstance(axis, tuple) else (
        lax.axis_size(axis))
    return lax.ppermute(block, axis, [(i, i ^ mask) for i in range(count)])


def second_core():
    return lax.rem(lax.axis_index("ctx"), 2) == 1


def doc_starts(lengths_ref, block, tokens):
    row_pos = block * tokens + lax.broadcasted_iota(i32, (1, tokens), 1)
    starts = jnp.zeros((1, tokens), i32)
    end = jnp.int32(0)
    for d in range(lengths_ref.shape[0]):
        end = end + lengths_ref[d]
        starts = jnp.where(row_pos >= end, end, starts)
    return starts


def unit(pair, key_block, starts, q_ref, g_ref, e_ref, dp_ref, stats_ref, causal=False):
    heads, tokens, width = q_ref.shape
    factor = width ** -0.5 * math.log2(math.e)
    key_iota = lax.broadcasted_iota(i32, (tokens, 1), 0)
    allowed = key_block * tokens + key_iota >= starts
    if causal:
        allowed = allowed & (key_iota <= lax.broadcasted_iota(i32, (1, tokens), 1))
    for h in range(heads):
        lanes = slice(h * tokens, (h + 1) * tokens)
        s = jnp.where(allowed, dot(pair[:, :width], q_ref[h], NT), MASKED)
        top = jnp.max(s, axis=0, keepdims=True)
        e = jnp.exp2((s - top) * factor)
        dp = dot(pair[:, width:], g_ref[h], NT)
        e_ref[:, lanes] = e
        dp_ref[:, lanes] = dp
        stats_ref[0:1, lanes] = top
        stats_ref[1:2, lanes] = jnp.sum(e, axis=0, keepdims=True)
        stats_ref[2:3, lanes] = jnp.sum(e * dp, axis=0, keepdims=True)


def rows_of(ref, first=0):
    return [ref[first + row:first + row + 1] for row in range(3)]


def joined(parts, factor):
    top = functools.reduce(jnp.maximum, [part[0] for part in parts])
    gains = [jnp.exp2((part[0] - top) * factor) for part in parts]
    total = sum(gain * part[1] for gain, part in zip(gains, parts))
    weighted = sum(gain * part[2] for gain, part in zip(gains, parts))
    return top, total, weighted


def own_unit_body(starts_ref, q_in, g_in, own_ref, q_ref, g_ref, e_ref, dp_ref, stats_ref):
    q_ref[...] = q_in[...]
    g_ref[...] = g_in[...]
    unit(own_ref, lax.axis_index("ctx"), starts_ref[0:1], q_in, g_in, e_ref, dp_ref, stats_ref,
         causal=True)


def four_unit_body(starts_ref, q_ref, g_ref, four_ref, e_ref, dp_ref, stats_ref):
    here = lax.axis_index("ctx")
    unit(four_ref, here - 4, starts_ref[0:1], q_ref, g_ref, e_ref, dp_ref, stats_ref)


def side_unit_body(starts_ref, other_q, other_g, own_ref, four_ref, e_ref, dp_ref, stats_ref):
    side = jnp.where(second_core(), four_ref[...], own_ref[...])
    block = lax.axis_index("ctx") - jnp.where(second_core(), 4, 0)
    unit(side, block, starts_ref[1:2], other_q, other_g, e_ref, dp_ref, stats_ref)


def prepare_body(share, middle, lengths_in, keys_ref, values_ref,
                 split_out, starts_ref, own_ref, lengths_ref, split_ref, sems):
    tokens, width = keys_ref.shape[1:]
    group = lax.axis_index("head") // share
    lengths = pltpu.make_async_copy(lengths_in, lengths_ref, sems.at[0])
    copies = [
        pltpu.make_async_copy(keys_ref.at[group], own_ref.at[:, :width], sems.at[1]),
        pltpu.make_async_copy(values_ref.at[group], own_ref.at[:, width:], sems.at[2]),
    ]
    for copy in [lengths] + copies:
        copy.start()
    lengths.wait()
    end, split = jnp.int32(0), jnp.int32(0)
    for d in range(lengths_ref.shape[0]):
        end = end + lengths_ref[d]
        split = jnp.where(end == middle, 1, split)
    split_ref[0] = split
    copies.append(pltpu.make_async_copy(split_ref, split_out, sems.at[3]))
    copies[-1].start()
    here = lax.axis_index("ctx")
    starts_ref[0:1] = doc_starts(lengths_ref, here, tokens)
    starts_ref[1:2] = doc_starts(lengths_ref, jnp.bitwise_xor(here, 1), tokens)
    for copy in copies:
        copy.wait()


def near_side_unit_body(starts_ref, other_q, other_g, own_ref, e_ref, dp_ref, stats_ref):
    block = jnp.where(second_core(), -1, lax.axis_index("ctx"))
    unit(own_ref, block, starts_ref[1:2], other_q, other_g, e_ref, dp_ref, stats_ref)


def write_rows(ref, values):
    for row, value in enumerate(values):
        ref[row:row + 1] = value


def cross_unit_body(starts_ref, other_q, other_g, two_ref, stats_side,
                    e_ref, dp_ref, stats_ref, others_ref):
    factor = other_q.shape[-1] ** -0.5 * math.log2(math.e)
    unit(two_ref, lax.axis_index("ctx") - 2, starts_ref[1:2], other_q, other_g,
         e_ref, dp_ref, stats_ref)
    write_rows(others_ref, joined([rows_of(stats_side), rows_of(stats_ref)], factor))
    others_ref[3:4] = jnp.zeros((1, others_ref.shape[1]), f32)


def two_unit_body(starts_ref, q_ref, g_ref, two_ref, *refs):
    earlier, (e_ref, dp_ref, stats_ref, mine_ref) = refs[:-4], refs[-4:]
    factor = q_ref.shape[-1] ** -0.5 * math.log2(math.e)
    unit(two_ref, lax.axis_index("ctx") - 2, starts_ref[0:1], q_ref, g_ref,
         e_ref, dp_ref, stats_ref)
    write_rows(mine_ref, joined([rows_of(ref) for ref in earlier + (stats_ref,)], factor))
    mine_ref[3:4] = jnp.zeros((1, mine_ref.shape[1]), f32)


def coefficients(here_ref, taken_ref, stats_refs, width):
    factor = width ** -0.5 * math.log2(math.e)
    top, total, weighted = joined([rows_of(here_ref), rows_of(taken_ref)], factor)
    inverse = 1.0 / total
    return [weighted * inverse] + [
        jnp.exp2((ref[0:1] - top) * factor) * inverse for ref in stats_refs]


def slopes(e_ref, dp_ref, gain, delta, p_ref, ds_ref):
    p = e_ref[...] * gain
    p_ref[...] = p.astype(bf16)
    ds_ref[...] = (p * (dp_ref[...] - delta)).astype(bf16)


def flat(ref):
    heads, tokens, width = ref.shape
    return ref[...].reshape(heads * tokens, width)


def add_terms(sum_ref, ds_ref, p_ref, q_ref, g_ref, fresh):
    width = q_ref.shape[-1]
    dk = dot(ds_ref[...], flat(q_ref)) * width ** -0.5
    dv = dot(p_ref[...], flat(g_ref))
    if fresh:
        sum_ref[:, :width] = dk
        sum_ref[:, width:] = dv
    else:
        sum_ref[:, :width] += dk
        sum_ref[:, width:] += dv


def my_terms_body(count, mine_ref, taken_ref, *refs):
    stats, refs = refs[:count], refs[count:]
    parts, (q_ref, g_ref), refs = refs[:4], refs[4:6], refs[6:]
    coef_ref, ds_refs, sums, p_ref = refs[0], refs[1:3], refs[3:5], refs[5]
    coefs = coefficients(mine_ref, taken_ref, stats, q_ref.shape[-1])
    write_rows(coef_ref, coefs)
    for at in range(2):
        slopes(parts[2 * at], parts[2 * at + 1], coefs[count - 1 + at], coefs[0], p_ref.at[at],
               ds_refs[at])
        add_terms(sums[at], ds_refs[at], p_ref.at[at], q_ref, g_ref, True)


def four_terms_body(others_ref, taken_ref, stats_side, stats_cross, e_side, dp_side,
                    other_q, other_g, part_ref, coef_ref, terms_ref, sum_ref, p_ref, ds_ref):
    coefs = coefficients(others_ref, taken_ref, (stats_side, stats_cross), other_q.shape[-1])
    write_rows(coef_ref, coefs)
    sum_ref[...] = part_ref[...]

    @pl.when(second_core())
    def _():
        slopes(e_side, dp_side, coef_ref[1:2], coef_ref[0:1], p_ref, ds_ref)
        add_terms(sum_ref, ds_ref, p_ref, other_q, other_g, False)

    terms_ref[...] = sum_ref[...].astype(bf16)


def two_terms_body(coef_ref, e_cross, dp_cross, other_q, other_g, part_ref,
                   terms_ref, ds_cross, p_ref, sum_ref):
    slopes(e_cross, dp_cross, coef_ref[2:3], coef_ref[0:1], p_ref, ds_cross)
    sum_ref[...] = part_ref[...]
    add_terms(sum_ref, ds_cross, p_ref, other_q, other_g, False)
    terms_ref[...] = sum_ref[...].astype(bf16)


def slice_rows(ref, other):
    count = lax.axis_size("head")
    each = ref.shape[0] // count
    parity = jnp.bitwise_xor(lax.rem(lax.axis_index("head"), 2), other)
    return [ref[pl.ds(pl.multiple_of((2 * at + parity) * each, each), each)]
            for at in range(count // 2)]


def halve(sum_ref, kept_ref, given_ref):
    each = sum_ref.shape[0] // lax.axis_size("head")
    for other, out_ref in enumerate((kept_ref, given_ref)):
        for at, value in enumerate(slice_rows(sum_ref, other)):
            out_ref[at * each:(at + 1) * each] = value.astype(out_ref.dtype)


def halved_two_terms_body(others_ref, taken_ref, stats_side, stats_cross, e_cross, dp_cross,
                        other_q, other_g, part_ref,
                        coef_ref, kept_ref, other_ref, ds_cross, p_ref, sum_ref):
    coefs = coefficients(others_ref, taken_ref, (stats_side, stats_cross), other_q.shape[-1])
    write_rows(coef_ref, coefs)
    slopes(e_cross, dp_cross, coefs[2], coefs[0], p_ref, ds_cross)
    sum_ref[...] = part_ref[...]
    add_terms(sum_ref, ds_cross, p_ref, other_q, other_g, False)
    halve(sum_ref, kept_ref, other_ref)


def near_own_terms_body(coef_ref, e_side, dp_side, other_q, other_g, part_ref,
                        kept_ref, other_ref, ds_side, p_ref, sum_ref):
    slopes(e_side, dp_side, coef_ref[1:2], coef_ref[0:1], p_ref, ds_side)
    sum_ref[...] = part_ref[...]

    @pl.when(jnp.logical_not(second_core()))
    def _():
        add_terms(sum_ref, ds_side, p_ref, other_q, other_g, False)

    halve(sum_ref, kept_ref, other_ref)


def far_four_terms_body(coef_ref, e_side, dp_side, other_q, other_g, part_ref,
                        kept_ref, other_ref, sum_ref, p_ref, ds_ref):
    sum_ref[...] = part_ref[...]

    @pl.when(second_core())
    def _():
        slopes(e_side, dp_side, coef_ref[1:2], coef_ref[0:1], p_ref, ds_ref)
        add_terms(sum_ref, ds_ref, p_ref, other_q, other_g, False)

    halve(sum_ref, kept_ref, other_ref)


def far_own_terms_body(mine_coef, coef_ref, e_own, dp_own, e_side, dp_side, q_ref, g_ref,
                       other_q, other_g,
                       kept_ref, other_ref, ds_own, ds_side, p_ref, p_side, sum_ref):
    slopes(e_own, dp_own, mine_coef[1:2], mine_coef[0:1], p_ref, ds_own)
    add_terms(sum_ref, ds_own, p_ref, q_ref, g_ref, True)
    slopes(e_side, dp_side, coef_ref[1:2], coef_ref[0:1], p_side, ds_side)

    @pl.when(jnp.logical_not(second_core()))
    def _():
        add_terms(sum_ref, ds_side, p_side, other_q, other_g, False)

    halve(sum_ref, kept_ref, other_ref)


def grads_body(own_ref, two_ref, ds_own, ds_two, ds_side, ds_cross, *refs):
    four_refs, (dq_ref, other_dq_ref) = refs[:-2], refs[-2:]
    width = dq_ref.shape[-1]
    keys, slope_refs = [own_ref[:, :width], two_ref[:, :width]], [ds_own, ds_two]
    side = keys[0]
    if four_refs:
        keys.append(four_refs[0][:, :width])
        slope_refs.append(four_refs[1])
        side = jnp.where(second_core(), keys[2], side)
    query_grads([side, keys[1]], [ds_side, ds_cross], other_dq_ref)
    query_grads(keys, slope_refs, dq_ref)


def add_others_body(use, sum_ref, pair_ref, four_ref, out_ref):
    taken = jnp.where(use(lax.axis_index("ctx")), four_ref[...].astype(f32), 0.0)
    out_ref[...] = sum_ref[...] + pair_ref[...].astype(f32) + taken


def relay_body(kept_ref, four_ref, two_ref, two_pair_ref, out_ref, sent_ref):
    ctx = lax.axis_index("ctx")
    taken = two_ref[...].astype(f32) + two_pair_ref[...].astype(f32)
    out_ref[...] = kept_ref[...] + jnp.where(ctx & 2 == 0, taken, 0.0)
    sent_ref[...] = (four_ref[...] + jnp.where(ctx & 6 == 6, taken, 0.0)).astype(bf16)


def near_first_sum_body(kept_ref, two_ref, two_pair_ref, out_ref):
    taken = two_ref[...].astype(f32) + two_pair_ref[...].astype(f32)
    out_ref[...] = kept_ref[...] + jnp.where(lax.axis_index("ctx") & 2 == 0, taken, 0.0)


def halves_sum_body(share, use, kept_ref, back_ref, here_ref, there_ref):
    each = here_ref.shape[0]
    group = lax.axis_index("head") // share
    for out_ref, at in ((here_ref, group), (there_ref, 1 - group)):
        rows = pl.ds(pl.multiple_of(at * each, each), each)
        taken = back_ref[rows].astype(f32)
        if use is not None:
            taken = jnp.where(use(lax.axis_index("ctx")), taken, 0.0)
        out_ref[...] = (kept_ref[rows] + taken).astype(out_ref.dtype)


def last_body(share, here_ref, taken_ref, dk_ref, dv_ref):
    width = dk_ref.shape[-1]
    group = lax.axis_index("head") // share
    for ref, place in ((here_ref, group), (taken_ref, 1 - group)):
        dk_ref[place] = ref[:, :width]
        dv_ref[place] = ref[:, width:]


def query_grads(keys, ds_refs, out_ref):
    heads, tokens, width = out_ref.shape
    turned = [key.T for key in keys]
    for h in range(heads):
        lanes = slice(h * tokens, (h + 1) * tokens)
        dqt = sum(dot(kt, ds[:, lanes]) for kt, ds in zip(turned, ds_refs))
        out_ref[h] = (dqt.T * width ** -0.5).astype(out_ref.dtype)


def own_terms_body(mine_coef, coef_ref, e_own, dp_own, e_side, dp_side, q_ref, g_ref,
                   other_q, other_g, own_ref, two_ref, ds_two, ds_cross, four_ref, ds_four,
                   terms_ref, dq_ref, other_dq_ref, ds_own, ds_side, p_ref, p_side):
    width = q_ref.shape[-1]
    own, two, four = [ref[:, :width] for ref in (own_ref, two_ref, four_ref)]
    slopes(e_side, dp_side, coef_ref[1:2], coef_ref[0:1], p_side, ds_side)
    query_grads([jnp.where(second_core(), four, own), two], [ds_side, ds_cross], other_dq_ref)
    slopes(e_own, dp_own, mine_coef[1:2], mine_coef[0:1], p_ref, ds_own)
    add_terms(terms_ref, ds_own, p_ref, q_ref, g_ref, True)

    @pl.when(jnp.logical_not(second_core()))
    def _():
        add_terms(terms_ref, ds_side, p_side, other_q, other_g, False)

    query_grads([own, two, four], [ds_own, ds_two, ds_four], dq_ref)


def add_grads_body(mine_ref, taken_ref, dq_ref):
    dq_ref[...] = (mine_ref[...] + taken_ref[...].astype(f32)).astype(dq_ref.dtype)


def sums_body(own_terms, four_back, two_back, out_ref):
    taken = four_back[...].astype(f32) + two_back[...].astype(f32)
    out_ref[...] = (own_terms[...] + taken).astype(bf16)


def per_device(queries, keys, values, d_out, doc_lengths):
    ctx_count, (heads, tokens, width) = lax.axis_size("ctx"), queries.shape
    middle = ctx_count // 2 * tokens
    split, starts, own = pl.pallas_call(
        functools.partial(prepare_body, GROUP // heads, middle),
        out_shape=(shape((1,), i32), shape((2, tokens), i32), shape((tokens, 2 * width), bf16)),
        in_specs=[pl.BlockSpec(memory_space=pl.ANY)] * 3,
        out_specs=(pl.BlockSpec(memory_space=pl.ANY), VMEM, VMEM),
        scratch_shapes=[pltpu.SMEM(doc_lengths.shape, i32), pltpu.SMEM((1,), i32),
                        pltpu.SemaphoreType.DMA((4,))],
        name="prepare",
    )(*[pltpu.with_memory_space_constraint(value, pltpu.HBM)
        for value in (doc_lengths, keys, values)])
    operands = (queries, d_out, own, starts)
    if ctx_count != 2 * REACH or lax.axis_size("head") * heads != 2 * GROUP or 2 * heads != GROUP:
        return gradients(True, *operands)
    return lax.switch(split[0], [functools.partial(gradients, True),
                                 functools.partial(gradients, False)], *operands)


def gradients(far, queries, d_out, own, starts):
    heads, tokens, width = queries.shape
    head_count = lax.axis_size("head")
    share = GROUP // heads
    groups = head_count // share
    rows = heads * tokens
    ctx = lax.axis_index("ctx")
    mutual = lax.axis_size("ctx") == 2 * REACH and share == groups == 2
    pair = (tokens, 2 * width)
    all_rows = (heads, tokens, width)
    stats = shape((3, rows), f32)
    wide = shape((tokens, rows), f32)
    half = shape((tokens, rows), bf16)
    half_scratch = pltpu.VMEM((tokens, rows), bf16)
    halves_scratch = pltpu.VMEM((2, tokens, rows), bf16)
    pair_scratch = pltpu.VMEM(pair, f32)

    if far:
        four = exchanged(own, "ctx", 4) if mutual else shifted(own, 4)
    two = [exchanged(own, "ctx", 2) if mutual else shifted(own, 2)]
    if far and mutual:
        two.append(exchanged(own, "ctx", 6))
    q, g, e_own, dp_own, stats_own = call(
        own_unit_body, "own_unit", [VMEM] * 4,
        (shape(all_rows, bf16), shape(all_rows, bf16), wide, wide, stats),
    )(starts, queries, d_out, own)
    other_q = exchanged(queries, "ctx", 1)
    other_g = exchanged(d_out, "ctx", 1)
    if far:
        four, stats_own = lax.optimization_barrier((four, stats_own))
        e_four, dp_four, stats_four = call(
            four_unit_body, "four_unit", [VMEM] * 4, (wide, wide, stats))(starts, q, g, four)
        other_q, stats_four = lax.optimization_barrier((other_q, stats_four))
        e_side, dp_side, stats_side = call(
            side_unit_body, "side_unit", [VMEM] * 5, (wide, wide, stats),
        )(starts, other_q, other_g, own, four)
    else:
        e_side, dp_side, stats_side = call(
            near_side_unit_body, "side_unit", [VMEM] * 4, (wide, wide, stats),
        )(starts, other_q, other_g, own)
    *two, stats_side, stats_own = lax.optimization_barrier((*two, stats_side, stats_own))
    mine_stats = (stats_own, stats_four) if far else (stats_own,)
    two = jnp.where(ctx & 2 == 2, *two) if len(two) == 2 else two[0]
    few = shape((4, rows), f32)
    e_cross, dp_cross, stats_cross, others = call(
        cross_unit_body, "cross_unit", [VMEM] * 5, (wide, wide, stats, few),
    )(starts, other_q, other_g, two, stats_side)
    taken_others = exchanged(others, "ctx", 1)
    e_two, dp_two, stats_two, mine = call(
        two_unit_body, "two_unit", [VMEM] * (4 + len(mine_stats)), (wide, wide, stats, few),
    )(starts, q, g, two, *mine_stats)
    taken_mine = exchanged(mine, "ctx", 1)
    mine_stats += (stats_two,)
    parts = ((e_four, dp_four) if far else (e_own, dp_own)) + (e_two, dp_two)
    mine_coef, ds_first, ds_two, first_part, two_part = call(
        functools.partial(my_terms_body, len(mine_stats)), "my_terms",
        [VMEM] * (8 + len(mine_stats)),
        (few, half, half, shape(pair, f32), shape(pair, f32)), (halves_scratch,),
    )(mine, taken_others, *mine_stats, *parts, q, g)
    other_sides = (other_q, other_g)
    last_stats = (others, taken_mine, stats_side, stats_cross)
    slices = (tokens // 2, 2 * width)
    slice_dims = (tokens // head_count, 2 * width)
    if not mutual:
        coef, four_terms = call(
            four_terms_body, "four_terms", [VMEM] * 9, (few, shape(pair, bf16)),
            (pair_scratch, half_scratch, half_scratch),
        )(*last_stats, e_side, dp_side, *other_sides, first_part)
        two_terms, ds_cross = call(
            two_terms_body, "two_terms", [VMEM] * 6, (shape(pair, bf16), half),
            (half_scratch, pair_scratch),
        )(coef, e_cross, dp_cross, *other_sides, two_part)
        backs = [shifted(four_terms, -4), shifted(two_terms, -2)]
        own_terms, my_grads, other_grads = call(
            own_terms_body, "own_terms", [VMEM] * 16,
            (shape(pair, f32), shape(all_rows, f32), shape(all_rows, bf16)),
            (half_scratch,) * 4,
        )(mine_coef, coef, e_own, dp_own, e_side, dp_side, q, g, *other_sides, own, two,
          ds_two, ds_cross, four, ds_first)
        taken_grads = exchanged(other_grads, "ctx", 1)
        d_queries, = call(
            add_grads_body, "add_grads", [VMEM] * 2, (shape(all_rows, bf16),),
        )(my_grads, taken_grads)
        sums, = call(sums_body, "sums", [VMEM] * 3, (shape(pair, bf16),))(own_terms, *backs)
        pieces = lax.all_to_all(sums.reshape(head_count, *slice_dims), "head", 0, 0)
        result = jnp.sum(
            pieces.reshape(groups, share, *slice_dims).astype(f32), axis=1).astype(bf16)
        return d_queries, result[..., :width], result[..., width:]

    halves = (shape(slices, bf16), shape(slices, bf16))
    part = shape(slices, f32)
    coef, two_kept, two_other, ds_cross = call(
        halved_two_terms_body, "two_terms", [VMEM] * 9, (few,) + halves + (half,),
        (half_scratch, pair_scratch),
    )(*last_stats, e_cross, dp_cross, *other_sides, two_part)
    two_back = exchanged(two_kept, "ctx", 2)
    two_pair = exchanged(two_other, ("ctx", "head"), 2 * head_count + 1)
    if far:
        four_kept, four_other = call(
            far_four_terms_body, "four_terms", [VMEM] * 6, (part, halves[1]),
            (pair_scratch, half_scratch, half_scratch),
        )(coef, e_side, dp_side, *other_sides, first_part)
        four_pair = exchanged(four_other, ("ctx", "head"), 4 * head_count + 1)
        own_kept, own_other, ds_own, ds_side = call(
            far_own_terms_body, "own_terms", [VMEM] * 10, (part, halves[1], half, half),
            (half_scratch, half_scratch, pair_scratch),
        )(mine_coef, coef, e_own, dp_own, e_side, dp_side, q, g, *other_sides)
    else:
        ds_own = ds_first
        own_kept, own_other, ds_side = call(
            near_own_terms_body, "own_terms", [VMEM] * 6, (part, halves[1], half),
            (half_scratch, pair_scratch),
        )(coef, e_side, dp_side, *other_sides, first_part)
    own_pair = exchanged(own_other, "head", 1)
    four_refs = (four, ds_first) if far else ()
    my_grads, other_grads = call(
        grads_body, "query_grads", [VMEM] * (6 + len(four_refs)),
        (shape(all_rows, f32), shape(all_rows, bf16)),
    )(own, two, ds_own, ds_two, ds_side, ds_cross, *four_refs)
    owns_four = lambda i: i < 4
    if far:
        own_kept, relayed = call(
            relay_body, "relay", [VMEM] * 4, (part, halves[0]),
        )(own_kept, four_kept, two_back, two_pair)
        four_back = exchanged(relayed, "ctx", 4)
        own_kept, = call(functools.partial(add_others_body, owns_four), "add_others", [VMEM] * 3,
                         (part,))(own_kept, own_pair, four_pair)
        final, use = four_back, owns_four
    else:
        own_kept, = call(
            near_first_sum_body, "first_sum", [VMEM] * 3, (part,),
        )(own_kept, two_back, two_pair)
        final, use = own_pair, None
    kept, sent = call(
        functools.partial(halves_sum_body, share, use), "sums", [VMEM] * 2,
        (shape(slice_dims, bf16),) * 2)(own_kept, final)
    other_grads, kept = lax.optimization_barrier((other_grads, kept))
    taken_grads = exchanged(other_grads, "ctx", 1)
    d_queries, = call(
        add_grads_body, "add_grads", [VMEM] * 2, (shape(all_rows, bf16),),
    )(my_grads, taken_grads)
    last = exchanged(sent, "head", share)
    last, d_queries = lax.optimization_barrier((last, d_queries))
    d_keys, d_values = call(
        functools.partial(last_body, share), "last", [VMEM] * 2,
        (shape((groups, tokens // head_count, width), bf16),) * 2)(kept, last)
    return d_queries, d_keys, d_values


def solution(mesh):
    placed = (
        P("head", "ctx", None),
        P(None, "ctx", None),
        P(None, "ctx", None),
        P("head", "ctx", None),
        P(),
    )
    return jax.shard_map(
        per_device,
        mesh=mesh,
        in_specs=placed,
        out_specs=(
            P("head", "ctx", None),
            P(None, ("ctx", "head"), None),
            P(None, ("ctx", "head"), None),
        ),
        check_vma=False,
    )
```

```python
import functools
import math

import jax
import jax.numpy as jnp
from jax import lax
from jax.experimental import pallas as pl
from jax.experimental.pallas import tpu as pltpu
from jax.sharding import PartitionSpec as P

GROUP = 8
REACH = 4
MASKED = -1e30
NT = (((1,), (1,)), ((), ()))
NN = (((1,), (0,)), ((), ()))
VMEM = pl.BlockSpec(memory_space=pltpu.VMEM)
SMEM = pl.BlockSpec(memory_space=pltpu.SMEM)
bf16, f32, i32 = jnp.bfloat16, jnp.float32, jnp.int32


def dot(a, b, dims=NN):
    return lax.dot_general(a, b, dims, preferred_element_type=f32)


def shape(dims, dtype):
    return jax.ShapeDtypeStruct(dims, dtype)


def call(body, name, in_specs, outs, scratch=()):
    return pl.pallas_call(
        body,
        out_shape=outs,
        in_specs=in_specs,
        out_specs=(VMEM,) * len(outs),
        scratch_shapes=scratch,
        compiler_params=pltpu.CompilerParams(vmem_limit_bytes=20 * 2**20),
        cost_estimate=pl.CostEstimate(flops=2**20, bytes_accessed=2**10, transcendentals=0),
        name=name,
    )


def shifted(block, distance):
    count = lax.axis_size("ctx")
    route = [(i - distance, i) for i in range(count) if 0 <= i - distance < count]
    return lax.ppermute(block, "ctx", route)


def exchanged(block, axis, mask):
    count = math.prod(lax.axis_size(name) for name in axis) if isinstance(axis, tuple) else (
        lax.axis_size(axis))
    return lax.ppermute(block, axis, [(i, i ^ mask) for i in range(count)])


def both(rows_ref):
    heads = rows_ref.shape[0] // 2
    return rows_ref.at[:heads], rows_ref.at[heads:]


def second_core():
    return lax.rem(lax.axis_index("ctx"), 2) == 1


def doc_starts(lengths_ref, block, tokens):
    row_pos = block * tokens + lax.broadcasted_iota(i32, (1, tokens), 1)
    starts = jnp.zeros((1, tokens), i32)
    end = jnp.int32(0)
    for d in range(lengths_ref.shape[0]):
        end = end + lengths_ref[d]
        starts = jnp.where(row_pos >= end, end, starts)
    return starts


def unit(pair, key_block, starts, rows_ref, e_ref, dp_ref, stats_ref, causal=False):
    q_ref, g_ref = both(rows_ref)
    heads, tokens, width = q_ref.shape
    factor = width ** -0.5 * math.log2(math.e)
    key_iota = lax.broadcasted_iota(i32, (tokens, 1), 0)
    allowed = key_block * tokens + key_iota >= starts
    if causal:
        allowed = allowed & (key_iota <= lax.broadcasted_iota(i32, (1, tokens), 1))
    for h in range(heads):
        lanes = slice(h * tokens, (h + 1) * tokens)
        s = jnp.where(allowed, dot(pair[:, :width], q_ref[h], NT), MASKED)
        top = jnp.max(s, axis=0, keepdims=True)
        e = jnp.exp2((s - top) * factor)
        dp = dot(pair[:, width:], g_ref[h], NT)
        e_ref[:, lanes] = e
        dp_ref[:, lanes] = dp
        stats_ref[0:1, lanes] = top
        stats_ref[1:2, lanes] = jnp.sum(e, axis=0, keepdims=True)
        stats_ref[2:3, lanes] = jnp.sum(e * dp, axis=0, keepdims=True)


def rows_of(ref, first=0):
    return [ref[first + row:first + row + 1] for row in range(3)]


def joined(parts, factor):
    top = functools.reduce(jnp.maximum, [part[0] for part in parts])
    gains = [jnp.exp2((part[0] - top) * factor) for part in parts]
    total = sum(gain * part[1] for gain, part in zip(gains, parts))
    weighted = sum(gain * part[2] for gain, part in zip(gains, parts))
    return top, total, weighted


def own_unit_body(starts_ref, rows_ref, own_ref, e_ref, dp_ref, stats_ref):
    unit(own_ref, lax.axis_index("ctx"), starts_ref[0:1], rows_ref, e_ref, dp_ref, stats_ref,
         causal=True)


def four_unit_body(starts_ref, rows_ref, four_ref, e_ref, dp_ref, stats_ref):
    here = lax.axis_index("ctx")
    unit(four_ref, here - 4, starts_ref[0:1], rows_ref, e_ref, dp_ref, stats_ref)


def side_unit_body(starts_ref, other_rows, own_ref, four_ref, e_ref, dp_ref, stats_ref):
    side = jnp.where(second_core(), four_ref[...], own_ref[...])
    block = lax.axis_index("ctx") - jnp.where(second_core(), 4, 0)
    unit(side, block, starts_ref[1:2], other_rows, e_ref, dp_ref, stats_ref)


def prepare_body(share, middle, lengths_in, keys_ref, values_ref, queries_ref, d_out_ref,
                 split_out, starts_ref, own_ref, rows_ref, lengths_ref, split_ref, sems):
    heads, tokens, width = queries_ref.shape
    group = lax.axis_index("head") // share
    lengths = pltpu.make_async_copy(lengths_in, lengths_ref, sems.at[0])
    copies = [
        pltpu.make_async_copy(keys_ref.at[group], own_ref.at[:, :width], sems.at[1]),
        pltpu.make_async_copy(values_ref.at[group], own_ref.at[:, width:], sems.at[2]),
        pltpu.make_async_copy(queries_ref, rows_ref.at[:heads], sems.at[3]),
        pltpu.make_async_copy(d_out_ref, rows_ref.at[heads:], sems.at[4]),
    ]
    for copy in [lengths] + copies:
        copy.start()
    lengths.wait()
    end, split = jnp.int32(0), jnp.int32(0)
    for d in range(lengths_ref.shape[0]):
        end = end + lengths_ref[d]
        split = jnp.where(end == middle, 1, split)
    split_ref[0] = split
    copies.append(pltpu.make_async_copy(split_ref, split_out, sems.at[5]))
    copies[-1].start()
    here = lax.axis_index("ctx")
    starts_ref[0:1] = doc_starts(lengths_ref, here, tokens)
    starts_ref[1:2] = doc_starts(lengths_ref, jnp.bitwise_xor(here, 1), tokens)
    for copy in copies:
        copy.wait()


def near_side_unit_body(starts_ref, other_rows, own_ref, e_ref, dp_ref, stats_ref):
    block = jnp.where(second_core(), -1, lax.axis_index("ctx"))
    unit(own_ref, block, starts_ref[1:2], other_rows, e_ref, dp_ref, stats_ref)


def write_rows(ref, values):
    for row, value in enumerate(values):
        ref[row:row + 1] = value


def cross_unit_body(starts_ref, other_rows, two_ref, stats_side,
                    e_ref, dp_ref, stats_ref, others_ref):
    factor = other_rows.shape[-1] ** -0.5 * math.log2(math.e)
    unit(two_ref, lax.axis_index("ctx") - 2, starts_ref[1:2], other_rows,
         e_ref, dp_ref, stats_ref)
    write_rows(others_ref, joined([rows_of(stats_side), rows_of(stats_ref)], factor))
    others_ref[3:4] = jnp.zeros((1, others_ref.shape[1]), f32)


def two_unit_body(starts_ref, rows_ref, two_ref, *refs):
    earlier, (e_ref, dp_ref, stats_ref, mine_ref) = refs[:-4], refs[-4:]
    factor = rows_ref.shape[-1] ** -0.5 * math.log2(math.e)
    unit(two_ref, lax.axis_index("ctx") - 2, starts_ref[0:1], rows_ref,
         e_ref, dp_ref, stats_ref)
    write_rows(mine_ref, joined([rows_of(ref) for ref in earlier + (stats_ref,)], factor))
    mine_ref[3:4] = jnp.zeros((1, mine_ref.shape[1]), f32)


def coefficients(here_ref, taken_ref, stats_refs, width):
    factor = width ** -0.5 * math.log2(math.e)
    top, total, weighted = joined([rows_of(here_ref), rows_of(taken_ref)], factor)
    inverse = 1.0 / total
    return [weighted * inverse] + [
        jnp.exp2((ref[0:1] - top) * factor) * inverse for ref in stats_refs]


def slopes(e_ref, dp_ref, gain, delta, p_ref, ds_ref):
    p = e_ref[...] * gain
    p_ref[...] = p.astype(bf16)
    ds_ref[...] = (p * (dp_ref[...] - delta)).astype(bf16)


def flat(ref):
    heads, tokens, width = ref.shape
    return ref[...].reshape(heads * tokens, width)


def add_terms(sum_ref, ds_ref, p_ref, rows_ref, fresh):
    q_ref, g_ref = both(rows_ref)
    width = q_ref.shape[-1]
    dk = dot(ds_ref[...], flat(q_ref)) * width ** -0.5
    dv = dot(p_ref[...], flat(g_ref))
    if fresh:
        sum_ref[:, :width] = dk
        sum_ref[:, width:] = dv
    else:
        sum_ref[:, :width] += dk
        sum_ref[:, width:] += dv


def my_terms_body(count, mine_ref, taken_ref, *refs):
    stats, refs = refs[:count], refs[count:]
    parts, rows_ref, refs = refs[:4], refs[4], refs[5:]
    coef_ref, ds_refs, sums, p_ref = refs[0], refs[1:3], refs[3:5], refs[5]
    coefs = coefficients(mine_ref, taken_ref, stats, rows_ref.shape[-1])
    write_rows(coef_ref, coefs)
    for at in range(2):
        slopes(parts[2 * at], parts[2 * at + 1], coefs[count - 1 + at], coefs[0], p_ref.at[at],
               ds_refs[at])
        add_terms(sums[at], ds_refs[at], p_ref.at[at], rows_ref, True)


def four_terms_body(others_ref, taken_ref, stats_side, stats_cross, e_side, dp_side,
                    other_rows, part_ref, coef_ref, terms_ref, sum_ref, p_ref, ds_ref):
    coefs = coefficients(others_ref, taken_ref, (stats_side, stats_cross), other_rows.shape[-1])
    write_rows(coef_ref, coefs)
    sum_ref[...] = part_ref[...]

    @pl.when(second_core())
    def _():
        slopes(e_side, dp_side, coef_ref[1:2], coef_ref[0:1], p_ref, ds_ref)
        add_terms(sum_ref, ds_ref, p_ref, other_rows, False)

    terms_ref[...] = sum_ref[...].astype(bf16)


def two_terms_body(coef_ref, e_cross, dp_cross, other_rows, part_ref,
                   terms_ref, ds_cross, p_ref, sum_ref):
    slopes(e_cross, dp_cross, coef_ref[2:3], coef_ref[0:1], p_ref, ds_cross)
    sum_ref[...] = part_ref[...]
    add_terms(sum_ref, ds_cross, p_ref, other_rows, False)
    terms_ref[...] = sum_ref[...].astype(bf16)


def slice_rows(ref, other):
    count = lax.axis_size("head")
    each = ref.shape[0] // count
    parity = jnp.bitwise_xor(lax.rem(lax.axis_index("head"), 2), other)
    return [ref[pl.ds(pl.multiple_of((2 * at + parity) * each, each), each)]
            for at in range(count // 2)]


def halve(sum_ref, kept_ref, given_ref):
    each = sum_ref.shape[0] // lax.axis_size("head")
    for other, out_ref in enumerate((kept_ref, given_ref)):
        for at, value in enumerate(slice_rows(sum_ref, other)):
            out_ref[at * each:(at + 1) * each] = value.astype(out_ref.dtype)


def halved_two_terms_body(others_ref, taken_ref, stats_side, stats_cross, e_cross, dp_cross,
                        other_rows, part_ref,
                        coef_ref, kept_ref, other_ref, ds_cross, p_ref, sum_ref):
    coefs = coefficients(others_ref, taken_ref, (stats_side, stats_cross), other_rows.shape[-1])
    write_rows(coef_ref, coefs)
    slopes(e_cross, dp_cross, coefs[2], coefs[0], p_ref, ds_cross)
    sum_ref[...] = part_ref[...]
    add_terms(sum_ref, ds_cross, p_ref, other_rows, False)
    halve(sum_ref, kept_ref, other_ref)


def near_own_terms_body(coef_ref, e_side, dp_side, other_rows, part_ref,
                        kept_ref, other_ref, ds_side, p_ref, sum_ref):
    slopes(e_side, dp_side, coef_ref[1:2], coef_ref[0:1], p_ref, ds_side)
    sum_ref[...] = part_ref[...]

    @pl.when(jnp.logical_not(second_core()))
    def _():
        add_terms(sum_ref, ds_side, p_ref, other_rows, False)

    halve(sum_ref, kept_ref, other_ref)


def far_four_terms_body(coef_ref, e_side, dp_side, other_rows, part_ref,
                        kept_ref, other_ref, sum_ref, p_ref, ds_ref):
    sum_ref[...] = part_ref[...]

    @pl.when(second_core())
    def _():
        slopes(e_side, dp_side, coef_ref[1:2], coef_ref[0:1], p_ref, ds_ref)
        add_terms(sum_ref, ds_ref, p_ref, other_rows, False)

    halve(sum_ref, kept_ref, other_ref)


def far_own_terms_body(mine_coef, coef_ref, e_own, dp_own, e_side, dp_side, rows_ref,
                       other_rows,
                       kept_ref, other_ref, ds_own, ds_side, p_ref, p_side, sum_ref):
    slopes(e_own, dp_own, mine_coef[1:2], mine_coef[0:1], p_ref, ds_own)
    add_terms(sum_ref, ds_own, p_ref, rows_ref, True)
    slopes(e_side, dp_side, coef_ref[1:2], coef_ref[0:1], p_side, ds_side)

    @pl.when(jnp.logical_not(second_core()))
    def _():
        add_terms(sum_ref, ds_side, p_side, other_rows, False)

    halve(sum_ref, kept_ref, other_ref)


def grads_body(own_ref, two_ref, ds_own, ds_two, ds_side, ds_cross, *refs):
    four_refs, (dq_ref, other_dq_ref) = refs[:-2], refs[-2:]
    width = dq_ref.shape[-1]
    keys, slope_refs = [own_ref[:, :width], two_ref[:, :width]], [ds_own, ds_two]
    side = keys[0]
    if four_refs:
        keys.append(four_refs[0][:, :width])
        slope_refs.append(four_refs[1])
        side = jnp.where(second_core(), keys[2], side)
    query_grads([side, keys[1]], [ds_side, ds_cross], other_dq_ref)
    query_grads(keys, slope_refs, dq_ref)


def add_others_body(use, sum_ref, pair_ref, four_ref, out_ref):
    taken = jnp.where(use(lax.axis_index("ctx")), four_ref[...].astype(f32), 0.0)
    out_ref[...] = sum_ref[...] + pair_ref[...].astype(f32) + taken


def relay_body(kept_ref, four_ref, two_ref, two_pair_ref, out_ref, sent_ref):
    ctx = lax.axis_index("ctx")
    taken = two_ref[...].astype(f32) + two_pair_ref[...].astype(f32)
    out_ref[...] = kept_ref[...] + jnp.where(ctx & 2 == 0, taken, 0.0)
    sent_ref[...] = (four_ref[...] + jnp.where(ctx & 6 == 6, taken, 0.0)).astype(bf16)


def near_first_sum_body(kept_ref, two_ref, two_pair_ref, out_ref):
    taken = two_ref[...].astype(f32) + two_pair_ref[...].astype(f32)
    out_ref[...] = kept_ref[...] + jnp.where(lax.axis_index("ctx") & 2 == 0, taken, 0.0)


def halves_sum_body(share, use, kept_ref, back_ref, here_ref, there_ref):
    each = here_ref.shape[0]
    group = lax.axis_index("head") // share
    for out_ref, at in ((here_ref, group), (there_ref, 1 - group)):
        rows = pl.ds(pl.multiple_of(at * each, each), each)
        taken = back_ref[rows].astype(f32)
        if use is not None:
            taken = jnp.where(use(lax.axis_index("ctx")), taken, 0.0)
        out_ref[...] = (kept_ref[rows] + taken).astype(out_ref.dtype)


def last_body(share, here_ref, taken_ref, dk_ref, dv_ref):
    width = dk_ref.shape[-1]
    group = lax.axis_index("head") // share
    for ref, place in ((here_ref, group), (taken_ref, 1 - group)):
        dk_ref[place] = ref[:, :width]
        dv_ref[place] = ref[:, width:]


def query_grads(keys, ds_refs, out_ref):
    heads, tokens, width = out_ref.shape
    turned = [key.T for key in keys]
    for h in range(heads):
        lanes = slice(h * tokens, (h + 1) * tokens)
        dqt = sum(dot(kt, ds[:, lanes]) for kt, ds in zip(turned, ds_refs))
        out_ref[h] = (dqt.T * width ** -0.5).astype(out_ref.dtype)


def own_terms_body(mine_coef, coef_ref, e_own, dp_own, e_side, dp_side, rows_ref,
                   other_rows, own_ref, two_ref, ds_two, ds_cross, four_ref, ds_four,
                   terms_ref, dq_ref, other_dq_ref, ds_own, ds_side, p_ref, p_side):
    width = dq_ref.shape[-1]
    own, two, four = [ref[:, :width] for ref in (own_ref, two_ref, four_ref)]
    slopes(e_side, dp_side, coef_ref[1:2], coef_ref[0:1], p_side, ds_side)
    query_grads([jnp.where(second_core(), four, own), two], [ds_side, ds_cross], other_dq_ref)
    slopes(e_own, dp_own, mine_coef[1:2], mine_coef[0:1], p_ref, ds_own)
    add_terms(terms_ref, ds_own, p_ref, rows_ref, True)

    @pl.when(jnp.logical_not(second_core()))
    def _():
        add_terms(terms_ref, ds_side, p_side, other_rows, False)

    query_grads([own, two, four], [ds_own, ds_two, ds_four], dq_ref)


def add_grads_body(mine_ref, taken_ref, dq_ref):
    dq_ref[...] = (mine_ref[...] + taken_ref[...].astype(f32)).astype(dq_ref.dtype)


def sums_body(own_terms, four_back, two_back, out_ref):
    taken = four_back[...].astype(f32) + two_back[...].astype(f32)
    out_ref[...] = (own_terms[...] + taken).astype(bf16)


def per_device(queries, keys, values, d_out, doc_lengths):
    ctx_count, (heads, tokens, width) = lax.axis_size("ctx"), queries.shape
    middle = ctx_count // 2 * tokens
    split, starts, own, rows = pl.pallas_call(
        functools.partial(prepare_body, GROUP // heads, middle),
        out_shape=(shape((1,), i32), shape((2, tokens), i32), shape((tokens, 2 * width), bf16),
                   shape((2 * heads, tokens, width), bf16)),
        in_specs=[pl.BlockSpec(memory_space=pl.ANY)] * 5,
        out_specs=(pl.BlockSpec(memory_space=pl.ANY), VMEM, VMEM, VMEM),
        scratch_shapes=[pltpu.SMEM(doc_lengths.shape, i32), pltpu.SMEM((1,), i32),
                        pltpu.SemaphoreType.DMA((6,))],
        name="prepare",
    )(*[pltpu.with_memory_space_constraint(value, pltpu.HBM)
        for value in (doc_lengths, keys, values, queries, d_out)])
    operands = (rows, own, starts)
    if ctx_count != 2 * REACH or lax.axis_size("head") * heads != 2 * GROUP or 2 * heads != GROUP:
        return gradients(True, *operands)
    return lax.switch(split[0], [functools.partial(gradients, True),
                                 functools.partial(gradients, False)], *operands)


def gradients(far, row_data, own, starts):
    heads, (tokens, width) = row_data.shape[0] // 2, row_data.shape[1:]
    head_count = lax.axis_size("head")
    share = GROUP // heads
    groups = head_count // share
    rows = heads * tokens
    ctx = lax.axis_index("ctx")
    mutual = lax.axis_size("ctx") == 2 * REACH and share == groups == 2
    pair = (tokens, 2 * width)
    all_rows = (heads, tokens, width)
    stats = shape((3, rows), f32)
    wide = shape((tokens, rows), f32)
    half = shape((tokens, rows), bf16)
    half_scratch = pltpu.VMEM((tokens, rows), bf16)
    halves_scratch = pltpu.VMEM((2, tokens, rows), bf16)
    pair_scratch = pltpu.VMEM(pair, f32)

    if far:
        four = exchanged(own, "ctx", 4) if mutual else shifted(own, 4)
    two = [exchanged(own, "ctx", 6)] if far and mutual else []
    two.append(exchanged(own, "ctx", 2) if mutual else shifted(own, 2))
    e_own, dp_own, stats_own = call(
        own_unit_body, "own_unit", [VMEM] * 3, (wide, wide, stats))(starts, row_data, own)
    other_rows = exchanged(row_data, "ctx", 1)
    if far:
        four, stats_own = lax.optimization_barrier((four, stats_own))
        e_four, dp_four, stats_four = call(
            four_unit_body, "four_unit", [VMEM] * 3, (wide, wide, stats))(starts, row_data, four)
        other_rows, stats_four = lax.optimization_barrier((other_rows, stats_four))
        e_side, dp_side, stats_side = call(
            side_unit_body, "side_unit", [VMEM] * 4, (wide, wide, stats),
        )(starts, other_rows, own, four)
    else:
        e_side, dp_side, stats_side = call(
            near_side_unit_body, "side_unit", [VMEM] * 3, (wide, wide, stats),
        )(starts, other_rows, own)
    *two, stats_side, stats_own = lax.optimization_barrier((*two, stats_side, stats_own))
    mine_stats = (stats_own, stats_four) if far else (stats_own,)
    two = jnp.where(ctx & 2 == 2, two[1], two[0]) if len(two) == 2 else two[0]
    few = shape((4, rows), f32)
    e_cross, dp_cross, stats_cross, others = call(
        cross_unit_body, "cross_unit", [VMEM] * 4, (wide, wide, stats, few),
    )(starts, other_rows, two, stats_side)
    taken_others = exchanged(others, "ctx", 1)
    e_two, dp_two, stats_two, mine = call(
        two_unit_body, "two_unit", [VMEM] * (3 + len(mine_stats)), (wide, wide, stats, few),
    )(starts, row_data, two, *mine_stats)
    taken_mine = exchanged(mine, "ctx", 1)
    mine_stats += (stats_two,)
    parts = ((e_four, dp_four) if far else (e_own, dp_own)) + (e_two, dp_two)
    mine_coef, ds_first, ds_two, first_part, two_part = call(
        functools.partial(my_terms_body, len(mine_stats)), "my_terms",
        [VMEM] * (7 + len(mine_stats)),
        (few, half, half, shape(pair, f32), shape(pair, f32)), (halves_scratch,),
    )(mine, taken_others, *mine_stats, *parts, row_data)
    last_stats = (others, taken_mine, stats_side, stats_cross)
    slices = (tokens // 2, 2 * width)
    slice_dims = (tokens // head_count, 2 * width)
    if not mutual:
        coef, four_terms = call(
            four_terms_body, "four_terms", [VMEM] * 8, (few, shape(pair, bf16)),
            (pair_scratch, half_scratch, half_scratch),
        )(*last_stats, e_side, dp_side, other_rows, first_part)
        two_terms, ds_cross = call(
            two_terms_body, "two_terms", [VMEM] * 5, (shape(pair, bf16), half),
            (half_scratch, pair_scratch),
        )(coef, e_cross, dp_cross, other_rows, two_part)
        backs = [shifted(four_terms, -4), shifted(two_terms, -2)]
        own_terms, my_grads, other_grads = call(
            own_terms_body, "own_terms", [VMEM] * 14,
            (shape(pair, f32), shape(all_rows, f32), shape(all_rows, bf16)),
            (half_scratch,) * 4,
        )(mine_coef, coef, e_own, dp_own, e_side, dp_side, row_data, other_rows, own, two,
          ds_two, ds_cross, four, ds_first)
        taken_grads = exchanged(other_grads, "ctx", 1)
        d_queries, = call(
            add_grads_body, "add_grads", [VMEM] * 2, (shape(all_rows, bf16),),
        )(my_grads, taken_grads)
        sums, = call(sums_body, "sums", [VMEM] * 3, (shape(pair, bf16),))(own_terms, *backs)
        pieces = lax.all_to_all(sums.reshape(head_count, *slice_dims), "head", 0, 0)
        result = jnp.sum(
            pieces.reshape(groups, share, *slice_dims).astype(f32), axis=1).astype(bf16)
        return d_queries, result[..., :width], result[..., width:]

    halves = (shape(slices, bf16), shape(slices, bf16))
    part = shape(slices, f32)
    coef, two_kept, two_other, ds_cross = call(
        halved_two_terms_body, "two_terms", [VMEM] * 8, (few,) + halves + (half,),
        (half_scratch, pair_scratch),
    )(*last_stats, e_cross, dp_cross, other_rows, two_part)
    two_back = exchanged(two_kept, "ctx", 2)
    two_pair = exchanged(two_other, ("ctx", "head"), 2 * head_count + 1)
    if far:
        four_kept, four_other = call(
            far_four_terms_body, "four_terms", [VMEM] * 5, (part, halves[1]),
            (pair_scratch, half_scratch, half_scratch),
        )(coef, e_side, dp_side, other_rows, first_part)
        four_pair = exchanged(four_other, ("ctx", "head"), 4 * head_count + 1)
        own_kept, own_other, ds_own, ds_side = call(
            far_own_terms_body, "own_terms", [VMEM] * 8, (part, halves[1], half, half),
            (half_scratch, half_scratch, pair_scratch),
        )(mine_coef, coef, e_own, dp_own, e_side, dp_side, row_data, other_rows)
    else:
        ds_own = ds_first
        own_kept, own_other, ds_side = call(
            near_own_terms_body, "own_terms", [VMEM] * 5, (part, halves[1], half),
            (half_scratch, pair_scratch),
        )(coef, e_side, dp_side, other_rows, first_part)
    own_pair = exchanged(own_other, "head", 1)
    four_refs = (four, ds_first) if far else ()
    my_grads, other_grads = call(
        grads_body, "query_grads", [VMEM] * (6 + len(four_refs)),
        (shape(all_rows, f32), shape(all_rows, bf16)),
    )(own, two, ds_own, ds_two, ds_side, ds_cross, *four_refs)
    owns_four = lambda i: i < 4
    if far:
        own_kept, relayed = call(
            relay_body, "relay", [VMEM] * 4, (part, halves[0]),
        )(own_kept, four_kept, two_back, two_pair)
        four_back = exchanged(relayed, "ctx", 4)
        own_kept, = call(functools.partial(add_others_body, owns_four), "add_others", [VMEM] * 3,
                         (part,))(own_kept, own_pair, four_pair)
        final, use = four_back, owns_four
    else:
        own_kept, = call(
            near_first_sum_body, "first_sum", [VMEM] * 3, (part,),
        )(own_kept, two_back, two_pair)
        final, use = own_pair, None
    kept, sent = call(
        functools.partial(halves_sum_body, share, use), "sums", [VMEM] * 2,
        (shape(slice_dims, bf16),) * 2)(own_kept, final)
    other_grads, kept = lax.optimization_barrier((other_grads, kept))
    taken_grads = exchanged(other_grads, "ctx", 1)
    d_queries, = call(
        add_grads_body, "add_grads", [VMEM] * 2, (shape(all_rows, bf16),),
    )(my_grads, taken_grads)
    last = exchanged(sent, "head", share)
    last, d_queries = lax.optimization_barrier((last, d_queries))
    d_keys, d_values = call(
        functools.partial(last_body, share), "last", [VMEM] * 2,
        (shape((groups, tokens // head_count, width), bf16),) * 2)(kept, last)
    return d_queries, d_keys, d_values


def solution(mesh):
    placed = (
        P("head", "ctx", None),
        P(None, "ctx", None),
        P(None, "ctx", None),
        P("head", "ctx", None),
        P(),
    )
    return jax.shard_map(
        per_device,
        mesh=mesh,
        in_specs=placed,
        out_specs=(
            P("head", "ctx", None),
            P(None, ("ctx", "head"), None),
            P(None, ("ctx", "head"), None),
        ),
        check_vma=False,
    )
```

```python
import functools
import math

import jax
import jax.numpy as jnp
from jax import lax
from jax.experimental import pallas as pl
from jax.experimental.pallas import tpu as pltpu
from jax.sharding import PartitionSpec as P

GROUP = 8
REACH = 4
MASKED = -1e30
NN = (((1,), (0,)), ((), ()))
VMEM = pl.BlockSpec(memory_space=pltpu.VMEM)
SMEM = pl.BlockSpec(memory_space=pltpu.SMEM)
bf16, f32, i32 = jnp.bfloat16, jnp.float32, jnp.int32


def dot(a, b, dims=NN):
    return lax.dot_general(a, b, dims, preferred_element_type=f32)


def shape(dims, dtype):
    return jax.ShapeDtypeStruct(dims, dtype)


def call(body, name, in_specs, outs, scratch=()):
    return pl.pallas_call(
        body,
        out_shape=outs,
        in_specs=in_specs,
        out_specs=(VMEM,) * len(outs),
        scratch_shapes=scratch,
        compiler_params=pltpu.CompilerParams(vmem_limit_bytes=20 * 2**20),
        cost_estimate=pl.CostEstimate(flops=2**20, bytes_accessed=2**10, transcendentals=0),
        name=name,
    )


def shifted(block, distance):
    count = lax.axis_size("ctx")
    route = [(i - distance, i) for i in range(count) if 0 <= i - distance < count]
    return lax.ppermute(block, "ctx", route)


def exchanged(block, axis, mask):
    count = math.prod(lax.axis_size(name) for name in axis) if isinstance(axis, tuple) else (
        lax.axis_size(axis))
    return lax.ppermute(block, axis, [(i, i ^ mask) for i in range(count)])


def both(rows_ref):
    heads = rows_ref.shape[0] // 2
    return rows_ref.at[:heads], rows_ref.at[heads:]


def second_core():
    return lax.rem(lax.axis_index("ctx"), 2) == 1


def doc_starts(lengths_ref, block, tokens):
    row_pos = block * tokens + lax.broadcasted_iota(i32, (1, tokens), 1)
    starts = jnp.zeros((1, tokens), i32)
    end = jnp.int32(0)
    for d in range(lengths_ref.shape[0]):
        end = end + lengths_ref[d]
        starts = jnp.where(row_pos >= end, end, starts)
    return starts


def unit(pair, key_block, starts, turned_ref, e_ref, dp_ref, stats_ref, causal=False):
    heads, (width, tokens) = turned_ref.shape[0] // 2, turned_ref.shape[1:]
    factor = width ** -0.5 * math.log2(math.e)
    key_iota = lax.broadcasted_iota(i32, (tokens, 1), 0)
    allowed = key_block * tokens + key_iota >= starts
    if causal:
        allowed = allowed & (key_iota <= lax.broadcasted_iota(i32, (1, tokens), 1))
    for h in range(heads):
        lanes = slice(h * tokens, (h + 1) * tokens)
        s = jnp.where(allowed, dot(pair[:, :width], turned_ref[h]), MASKED)
        top = jnp.max(s, axis=0, keepdims=True)
        e = jnp.exp2((s - top) * factor)
        dp = dot(pair[:, width:], turned_ref[heads + h])
        e_ref[:, lanes] = e
        dp_ref[:, lanes] = dp
        stats_ref[0:1, lanes] = top
        stats_ref[1:2, lanes] = jnp.sum(e, axis=0, keepdims=True)
        stats_ref[2:3, lanes] = jnp.sum(e * dp, axis=0, keepdims=True)


def turn(rows_ref, turned_ref):
    for at in range(rows_ref.shape[0]):
        turned_ref[at] = rows_ref[at].T


def rows_of(ref, first=0):
    return [ref[first + row:first + row + 1] for row in range(3)]


def joined(parts, factor):
    top = functools.reduce(jnp.maximum, [part[0] for part in parts])
    gains = [jnp.exp2((part[0] - top) * factor) for part in parts]
    total = sum(gain * part[1] for gain, part in zip(gains, parts))
    weighted = sum(gain * part[2] for gain, part in zip(gains, parts))
    return top, total, weighted


def own_unit_body(starts_ref, rows_ref, own_ref, turned_ref, e_ref, dp_ref, stats_ref):
    turn(rows_ref, turned_ref)
    unit(own_ref, lax.axis_index("ctx"), starts_ref[0:1], turned_ref, e_ref, dp_ref, stats_ref,
         causal=True)


def four_unit_body(starts_ref, turned_ref, four_ref, e_ref, dp_ref, stats_ref):
    here = lax.axis_index("ctx")
    unit(four_ref, here - 4, starts_ref[0:1], turned_ref, e_ref, dp_ref, stats_ref)


def side_unit_body(starts_ref, other_rows, own_ref, four_ref,
                   turned_ref, e_ref, dp_ref, stats_ref):
    turn(other_rows, turned_ref)
    side = jnp.where(second_core(), four_ref[...], own_ref[...])
    block = lax.axis_index("ctx") - jnp.where(second_core(), 4, 0)
    unit(side, block, starts_ref[1:2], turned_ref, e_ref, dp_ref, stats_ref)


def prepare_body(share, middle, lengths_in, keys_ref, values_ref, queries_ref, d_out_ref,
                 split_out, starts_ref, own_ref, rows_ref, lengths_ref, split_ref, sems):
    heads, tokens, width = queries_ref.shape
    group = lax.axis_index("head") // share
    lengths = pltpu.make_async_copy(lengths_in, lengths_ref, sems.at[0])
    copies = [
        pltpu.make_async_copy(keys_ref.at[group], own_ref.at[:, :width], sems.at[1]),
        pltpu.make_async_copy(values_ref.at[group], own_ref.at[:, width:], sems.at[2]),
        pltpu.make_async_copy(queries_ref, rows_ref.at[:heads], sems.at[3]),
        pltpu.make_async_copy(d_out_ref, rows_ref.at[heads:], sems.at[4]),
    ]
    for copy in [lengths] + copies:
        copy.start()
    lengths.wait()
    end, split = jnp.int32(0), jnp.int32(0)
    for d in range(lengths_ref.shape[0]):
        end = end + lengths_ref[d]
        split = jnp.where(end == middle, 1, split)
    split_ref[0] = split
    copies.append(pltpu.make_async_copy(split_ref, split_out, sems.at[5]))
    copies[-1].start()
    here = lax.axis_index("ctx")
    starts_ref[0:1] = doc_starts(lengths_ref, here, tokens)
    starts_ref[1:2] = doc_starts(lengths_ref, jnp.bitwise_xor(here, 1), tokens)
    for copy in copies:
        copy.wait()


def near_side_unit_body(starts_ref, other_rows, own_ref, turned_ref, e_ref, dp_ref, stats_ref):
    turn(other_rows, turned_ref)
    block = jnp.where(second_core(), -1, lax.axis_index("ctx"))
    unit(own_ref, block, starts_ref[1:2], turned_ref, e_ref, dp_ref, stats_ref)


def write_rows(ref, values):
    for row, value in enumerate(values):
        ref[row:row + 1] = value


def cross_unit_body(starts_ref, turned_ref, two_ref, stats_side,
                    e_ref, dp_ref, stats_ref, others_ref):
    factor = turned_ref.shape[1] ** -0.5 * math.log2(math.e)
    unit(two_ref, lax.axis_index("ctx") - 2, starts_ref[1:2], turned_ref,
         e_ref, dp_ref, stats_ref)
    write_rows(others_ref, joined([rows_of(stats_side), rows_of(stats_ref)], factor))
    others_ref[3:4] = jnp.zeros((1, others_ref.shape[1]), f32)


def two_unit_body(starts_ref, turned_ref, two_ref, *refs):
    earlier, (e_ref, dp_ref, stats_ref, mine_ref) = refs[:-4], refs[-4:]
    factor = turned_ref.shape[1] ** -0.5 * math.log2(math.e)
    unit(two_ref, lax.axis_index("ctx") - 2, starts_ref[0:1], turned_ref,
         e_ref, dp_ref, stats_ref)
    write_rows(mine_ref, joined([rows_of(ref) for ref in earlier + (stats_ref,)], factor))
    mine_ref[3:4] = jnp.zeros((1, mine_ref.shape[1]), f32)


def coefficients(here_ref, taken_ref, stats_refs, width):
    factor = width ** -0.5 * math.log2(math.e)
    top, total, weighted = joined([rows_of(here_ref), rows_of(taken_ref)], factor)
    inverse = 1.0 / total
    return [weighted * inverse] + [
        jnp.exp2((ref[0:1] - top) * factor) * inverse for ref in stats_refs]


def slopes(e_ref, dp_ref, gain, delta, p_ref, ds_ref):
    p = e_ref[...] * gain
    p_ref[...] = p.astype(bf16)
    ds_ref[...] = (p * (dp_ref[...] - delta)).astype(bf16)


def flat(ref):
    heads, tokens, width = ref.shape
    return ref[...].reshape(heads * tokens, width)


def add_terms(sum_ref, ds_ref, p_ref, rows_ref, fresh):
    q_ref, g_ref = both(rows_ref)
    width = q_ref.shape[-1]
    dk = dot(ds_ref[...], flat(q_ref)) * width ** -0.5
    dv = dot(p_ref[...], flat(g_ref))
    if fresh:
        sum_ref[:, :width] = dk
        sum_ref[:, width:] = dv
    else:
        sum_ref[:, :width] += dk
        sum_ref[:, width:] += dv


def my_terms_body(count, mine_ref, taken_ref, *refs):
    stats, refs = refs[:count], refs[count:]
    parts, rows_ref, refs = refs[:4], refs[4], refs[5:]
    coef_ref, ds_refs, sums, p_ref = refs[0], refs[1:3], refs[3:5], refs[5]
    coefs = coefficients(mine_ref, taken_ref, stats, rows_ref.shape[-1])
    write_rows(coef_ref, coefs)
    for at in range(2):
        slopes(parts[2 * at], parts[2 * at + 1], coefs[count - 1 + at], coefs[0], p_ref.at[at],
               ds_refs[at])
        add_terms(sums[at], ds_refs[at], p_ref.at[at], rows_ref, True)


def four_terms_body(others_ref, taken_ref, stats_side, stats_cross, e_side, dp_side,
                    other_rows, part_ref, coef_ref, terms_ref, sum_ref, p_ref, ds_ref):
    coefs = coefficients(others_ref, taken_ref, (stats_side, stats_cross), other_rows.shape[-1])
    write_rows(coef_ref, coefs)
    sum_ref[...] = part_ref[...]

    @pl.when(second_core())
    def _():
        slopes(e_side, dp_side, coef_ref[1:2], coef_ref[0:1], p_ref, ds_ref)
        add_terms(sum_ref, ds_ref, p_ref, other_rows, False)

    terms_ref[...] = sum_ref[...].astype(bf16)


def two_terms_body(coef_ref, e_cross, dp_cross, other_rows, part_ref,
                   terms_ref, ds_cross, p_ref, sum_ref):
    slopes(e_cross, dp_cross, coef_ref[2:3], coef_ref[0:1], p_ref, ds_cross)
    sum_ref[...] = part_ref[...]
    add_terms(sum_ref, ds_cross, p_ref, other_rows, False)
    terms_ref[...] = sum_ref[...].astype(bf16)


def slice_rows(ref, other):
    count = lax.axis_size("head")
    each = ref.shape[0] // count
    parity = jnp.bitwise_xor(lax.rem(lax.axis_index("head"), 2), other)
    return [ref[pl.ds(pl.multiple_of((2 * at + parity) * each, each), each)]
            for at in range(count // 2)]


def halve(sum_ref, kept_ref, given_ref):
    each = sum_ref.shape[0] // lax.axis_size("head")
    for other, out_ref in enumerate((kept_ref, given_ref)):
        for at, value in enumerate(slice_rows(sum_ref, other)):
            out_ref[at * each:(at + 1) * each] = value.astype(out_ref.dtype)


def halved_two_terms_body(others_ref, taken_ref, stats_side, stats_cross, e_cross, dp_cross,
                        other_rows, part_ref,
                        coef_ref, kept_ref, other_ref, ds_cross, p_ref, sum_ref):
    coefs = coefficients(others_ref, taken_ref, (stats_side, stats_cross), other_rows.shape[-1])
    write_rows(coef_ref, coefs)
    slopes(e_cross, dp_cross, coefs[2], coefs[0], p_ref, ds_cross)
    sum_ref[...] = part_ref[...]
    add_terms(sum_ref, ds_cross, p_ref, other_rows, False)
    halve(sum_ref, kept_ref, other_ref)


def near_own_terms_body(coef_ref, e_side, dp_side, other_rows, part_ref,
                        kept_ref, other_ref, ds_side, p_ref, sum_ref):
    slopes(e_side, dp_side, coef_ref[1:2], coef_ref[0:1], p_ref, ds_side)
    sum_ref[...] = part_ref[...]

    @pl.when(jnp.logical_not(second_core()))
    def _():
        add_terms(sum_ref, ds_side, p_ref, other_rows, False)

    halve(sum_ref, kept_ref, other_ref)


def far_four_terms_body(coef_ref, e_side, dp_side, other_rows, part_ref,
                        kept_ref, other_ref, sum_ref, p_ref, ds_ref):
    sum_ref[...] = part_ref[...]

    @pl.when(second_core())
    def _():
        slopes(e_side, dp_side, coef_ref[1:2], coef_ref[0:1], p_ref, ds_ref)
        add_terms(sum_ref, ds_ref, p_ref, other_rows, False)

    halve(sum_ref, kept_ref, other_ref)


def far_own_terms_body(mine_coef, coef_ref, e_own, dp_own, e_side, dp_side, rows_ref,
                       other_rows,
                       kept_ref, other_ref, ds_own, ds_side, p_ref, p_side, sum_ref):
    slopes(e_own, dp_own, mine_coef[1:2], mine_coef[0:1], p_ref, ds_own)
    add_terms(sum_ref, ds_own, p_ref, rows_ref, True)
    slopes(e_side, dp_side, coef_ref[1:2], coef_ref[0:1], p_side, ds_side)

    @pl.when(jnp.logical_not(second_core()))
    def _():
        add_terms(sum_ref, ds_side, p_side, other_rows, False)

    halve(sum_ref, kept_ref, other_ref)


def grads_body(own_ref, two_ref, ds_own, ds_two, ds_side, ds_cross, *refs):
    four_refs, (dq_ref, other_dq_ref) = refs[:-2], refs[-2:]
    width = dq_ref.shape[-1]
    keys, slope_refs = [own_ref[:, :width], two_ref[:, :width]], [ds_own, ds_two]
    side = keys[0]
    if four_refs:
        keys.append(four_refs[0][:, :width])
        slope_refs.append(four_refs[1])
        side = jnp.where(second_core(), keys[2], side)
    query_grads([side, keys[1]], [ds_side, ds_cross], other_dq_ref)
    query_grads(keys, slope_refs, dq_ref)


def add_others_body(use, sum_ref, pair_ref, four_ref, out_ref):
    taken = jnp.where(use(lax.axis_index("ctx")), four_ref[...].astype(f32), 0.0)
    out_ref[...] = sum_ref[...] + pair_ref[...].astype(f32) + taken


def relay_body(kept_ref, four_ref, two_ref, two_pair_ref, out_ref, sent_ref):
    ctx = lax.axis_index("ctx")
    taken = two_ref[...].astype(f32) + two_pair_ref[...].astype(f32)
    out_ref[...] = kept_ref[...] + jnp.where(ctx & 2 == 0, taken, 0.0)
    sent_ref[...] = (four_ref[...] + jnp.where(ctx & 6 == 6, taken, 0.0)).astype(bf16)


def near_first_sum_body(kept_ref, two_ref, two_pair_ref, out_ref):
    taken = two_ref[...].astype(f32) + two_pair_ref[...].astype(f32)
    out_ref[...] = kept_ref[...] + jnp.where(lax.axis_index("ctx") & 2 == 0, taken, 0.0)


def halves_sum_body(share, use, kept_ref, back_ref, here_ref, there_ref):
    each = here_ref.shape[0]
    group = lax.axis_index("head") // share
    for out_ref, at in ((here_ref, group), (there_ref, 1 - group)):
        rows = pl.ds(pl.multiple_of(at * each, each), each)
        taken = back_ref[rows].astype(f32)
        if use is not None:
            taken = jnp.where(use(lax.axis_index("ctx")), taken, 0.0)
        out_ref[...] = (kept_ref[rows] + taken).astype(out_ref.dtype)


def last_body(share, here_ref, taken_ref, dk_ref, dv_ref):
    width = dk_ref.shape[-1]
    group = lax.axis_index("head") // share
    for ref, place in ((here_ref, group), (taken_ref, 1 - group)):
        dk_ref[place] = ref[:, :width]
        dv_ref[place] = ref[:, width:]


def query_grads(keys, ds_refs, out_ref):
    heads, tokens, width = out_ref.shape
    turned = [key.T for key in keys]
    for h in range(heads):
        lanes = slice(h * tokens, (h + 1) * tokens)
        dqt = sum(dot(kt, ds[:, lanes]) for kt, ds in zip(turned, ds_refs))
        out_ref[h] = (dqt.T * width ** -0.5).astype(out_ref.dtype)


def own_terms_body(mine_coef, coef_ref, e_own, dp_own, e_side, dp_side, rows_ref,
                   other_rows, own_ref, two_ref, ds_two, ds_cross, four_ref, ds_four,
                   terms_ref, dq_ref, other_dq_ref, ds_own, ds_side, p_ref, p_side):
    width = dq_ref.shape[-1]
    own, two, four = [ref[:, :width] for ref in (own_ref, two_ref, four_ref)]
    slopes(e_side, dp_side, coef_ref[1:2], coef_ref[0:1], p_side, ds_side)
    query_grads([jnp.where(second_core(), four, own), two], [ds_side, ds_cross], other_dq_ref)
    slopes(e_own, dp_own, mine_coef[1:2], mine_coef[0:1], p_ref, ds_own)
    add_terms(terms_ref, ds_own, p_ref, rows_ref, True)

    @pl.when(jnp.logical_not(second_core()))
    def _():
        add_terms(terms_ref, ds_side, p_side, other_rows, False)

    query_grads([own, two, four], [ds_own, ds_two, ds_four], dq_ref)


def add_grads_body(mine_ref, taken_ref, dq_ref):
    dq_ref[...] = (mine_ref[...] + taken_ref[...].astype(f32)).astype(dq_ref.dtype)


def sums_body(own_terms, four_back, two_back, out_ref):
    taken = four_back[...].astype(f32) + two_back[...].astype(f32)
    out_ref[...] = (own_terms[...] + taken).astype(bf16)


def per_device(queries, keys, values, d_out, doc_lengths):
    ctx_count, (heads, tokens, width) = lax.axis_size("ctx"), queries.shape
    middle = ctx_count // 2 * tokens
    split, starts, own, rows = pl.pallas_call(
        functools.partial(prepare_body, GROUP // heads, middle),
        out_shape=(shape((1,), i32), shape((2, tokens), i32), shape((tokens, 2 * width), bf16),
                   shape((2 * heads, tokens, width), bf16)),
        in_specs=[pl.BlockSpec(memory_space=pl.ANY)] * 5,
        out_specs=(pl.BlockSpec(memory_space=pl.ANY), VMEM, VMEM, VMEM),
        scratch_shapes=[pltpu.SMEM(doc_lengths.shape, i32), pltpu.SMEM((1,), i32),
                        pltpu.SemaphoreType.DMA((6,))],
        name="prepare",
    )(*[pltpu.with_memory_space_constraint(value, pltpu.HBM)
        for value in (doc_lengths, keys, values, queries, d_out)])
    operands = (rows, own, starts)
    if ctx_count != 2 * REACH or lax.axis_size("head") * heads != 2 * GROUP or 2 * heads != GROUP:
        return gradients(True, *operands)
    return lax.switch(split[0], [functools.partial(gradients, True),
                                 functools.partial(gradients, False)], *operands)


def gradients(far, row_data, own, starts):
    heads, (tokens, width) = row_data.shape[0] // 2, row_data.shape[1:]
    head_count = lax.axis_size("head")
    share = GROUP // heads
    groups = head_count // share
    rows = heads * tokens
    ctx = lax.axis_index("ctx")
    mutual = lax.axis_size("ctx") == 2 * REACH and share == groups == 2
    pair = (tokens, 2 * width)
    all_rows = (heads, tokens, width)
    stats = shape((3, rows), f32)
    wide = shape((tokens, rows), f32)
    half = shape((tokens, rows), bf16)
    half_scratch = pltpu.VMEM((tokens, rows), bf16)
    halves_scratch = pltpu.VMEM((2, tokens, rows), bf16)
    pair_scratch = pltpu.VMEM(pair, f32)

    if far:
        four = exchanged(own, "ctx", 4) if mutual else shifted(own, 4)
    two = [exchanged(own, "ctx", 6)] if far and mutual else []
    two.append(exchanged(own, "ctx", 2) if mutual else shifted(own, 2))
    flipped = shape((2 * heads, width, tokens), bf16)
    turned, e_own, dp_own, stats_own = call(
        own_unit_body, "own_unit", [VMEM] * 3, (flipped, wide, wide, stats),
    )(starts, row_data, own)
    other_rows = exchanged(row_data, "ctx", 1)
    if far:
        four, stats_own = lax.optimization_barrier((four, stats_own))
        e_four, dp_four, stats_four = call(
            four_unit_body, "four_unit", [VMEM] * 3, (wide, wide, stats))(starts, turned, four)
        other_rows, stats_four = lax.optimization_barrier((other_rows, stats_four))
        other_turned, e_side, dp_side, stats_side = call(
            side_unit_body, "side_unit", [VMEM] * 4, (flipped, wide, wide, stats),
        )(starts, other_rows, own, four)
    else:
        other_turned, e_side, dp_side, stats_side = call(
            near_side_unit_body, "side_unit", [VMEM] * 3, (flipped, wide, wide, stats),
        )(starts, other_rows, own)
    *two, stats_side, stats_own = lax.optimization_barrier((*two, stats_side, stats_own))
    mine_stats = (stats_own, stats_four) if far else (stats_own,)
    two = jnp.where(ctx & 2 == 2, two[1], two[0]) if len(two) == 2 else two[0]
    few = shape((4, rows), f32)
    e_cross, dp_cross, stats_cross, others = call(
        cross_unit_body, "cross_unit", [VMEM] * 4, (wide, wide, stats, few),
    )(starts, other_turned, two, stats_side)
    taken_others = exchanged(others, "ctx", 1)
    e_two, dp_two, stats_two, mine = call(
        two_unit_body, "two_unit", [VMEM] * (3 + len(mine_stats)), (wide, wide, stats, few),
    )(starts, turned, two, *mine_stats)
    taken_mine = exchanged(mine, "ctx", 1)
    mine_stats += (stats_two,)
    parts = ((e_four, dp_four) if far else (e_own, dp_own)) + (e_two, dp_two)
    mine_coef, ds_first, ds_two, first_part, two_part = call(
        functools.partial(my_terms_body, len(mine_stats)), "my_terms",
        [VMEM] * (7 + len(mine_stats)),
        (few, half, half, shape(pair, f32), shape(pair, f32)), (halves_scratch,),
    )(mine, taken_others, *mine_stats, *parts, row_data)
    last_stats = (others, taken_mine, stats_side, stats_cross)
    slices = (tokens // 2, 2 * width)
    slice_dims = (tokens // head_count, 2 * width)
    if not mutual:
        coef, four_terms = call(
            four_terms_body, "four_terms", [VMEM] * 8, (few, shape(pair, bf16)),
            (pair_scratch, half_scratch, half_scratch),
        )(*last_stats, e_side, dp_side, other_rows, first_part)
        two_terms, ds_cross = call(
            two_terms_body, "two_terms", [VMEM] * 5, (shape(pair, bf16), half),
            (half_scratch, pair_scratch),
        )(coef, e_cross, dp_cross, other_rows, two_part)
        backs = [shifted(four_terms, -4), shifted(two_terms, -2)]
        own_terms, my_grads, other_grads = call(
            own_terms_body, "own_terms", [VMEM] * 14,
            (shape(pair, f32), shape(all_rows, f32), shape(all_rows, bf16)),
            (half_scratch,) * 4,
        )(mine_coef, coef, e_own, dp_own, e_side, dp_side, row_data, other_rows, own, two,
          ds_two, ds_cross, four, ds_first)
        taken_grads = exchanged(other_grads, "ctx", 1)
        d_queries, = call(
            add_grads_body, "add_grads", [VMEM] * 2, (shape(all_rows, bf16),),
        )(my_grads, taken_grads)
        sums, = call(sums_body, "sums", [VMEM] * 3, (shape(pair, bf16),))(own_terms, *backs)
        pieces = lax.all_to_all(sums.reshape(head_count, *slice_dims), "head", 0, 0)
        result = jnp.sum(
            pieces.reshape(groups, share, *slice_dims).astype(f32), axis=1).astype(bf16)
        return d_queries, result[..., :width], result[..., width:]

    halves = (shape(slices, bf16), shape(slices, bf16))
    part = shape(slices, f32)
    coef, two_kept, two_other, ds_cross = call(
        halved_two_terms_body, "two_terms", [VMEM] * 8, (few,) + halves + (half,),
        (half_scratch, pair_scratch),
    )(*last_stats, e_cross, dp_cross, other_rows, two_part)
    two_back = exchanged(two_kept, "ctx", 2)
    two_pair = exchanged(two_other, ("ctx", "head"), 2 * head_count + 1)
    if far:
        four_kept, four_other = call(
            far_four_terms_body, "four_terms", [VMEM] * 5, (part, halves[1]),
            (pair_scratch, half_scratch, half_scratch),
        )(coef, e_side, dp_side, other_rows, first_part)
        four_pair = exchanged(four_other, ("ctx", "head"), 4 * head_count + 1)
        own_kept, own_other, ds_own, ds_side = call(
            far_own_terms_body, "own_terms", [VMEM] * 8, (part, halves[1], half, half),
            (half_scratch, half_scratch, pair_scratch),
        )(mine_coef, coef, e_own, dp_own, e_side, dp_side, row_data, other_rows)
    else:
        ds_own = ds_first
        own_kept, own_other, ds_side = call(
            near_own_terms_body, "own_terms", [VMEM] * 5, (part, halves[1], half),
            (half_scratch, pair_scratch),
        )(coef, e_side, dp_side, other_rows, first_part)
    own_pair = exchanged(own_other, "head", 1)
    four_refs = (four, ds_first) if far else ()
    my_grads, other_grads = call(
        grads_body, "query_grads", [VMEM] * (6 + len(four_refs)),
        (shape(all_rows, f32), shape(all_rows, bf16)),
    )(own, two, ds_own, ds_two, ds_side, ds_cross, *four_refs)
    owns_four = lambda i: i < 4
    if far:
        own_kept, relayed = call(
            relay_body, "relay", [VMEM] * 4, (part, halves[0]),
        )(own_kept, four_kept, two_back, two_pair)
        four_back = exchanged(relayed, "ctx", 4)
        own_kept, = call(functools.partial(add_others_body, owns_four), "add_others", [VMEM] * 3,
                         (part,))(own_kept, own_pair, four_pair)
        final, use = four_back, owns_four
    else:
        own_kept, = call(
            near_first_sum_body, "first_sum", [VMEM] * 3, (part,),
        )(own_kept, two_back, two_pair)
        final, use = own_pair, None
    kept, sent = call(
        functools.partial(halves_sum_body, share, use), "sums", [VMEM] * 2,
        (shape(slice_dims, bf16),) * 2)(own_kept, final)
    other_grads, kept = lax.optimization_barrier((other_grads, kept))
    taken_grads = exchanged(other_grads, "ctx", 1)
    d_queries, = call(
        add_grads_body, "add_grads", [VMEM] * 2, (shape(all_rows, bf16),),
    )(my_grads, taken_grads)
    last = exchanged(sent, "head", share)
    last, d_queries = lax.optimization_barrier((last, d_queries))
    d_keys, d_values = call(
        functools.partial(last_body, share), "last", [VMEM] * 2,
        (shape((groups, tokens // head_count, width), bf16),) * 2)(kept, last)
    return d_queries, d_keys, d_values


def solution(mesh):
    placed = (
        P("head", "ctx", None),
        P(None, "ctx", None),
        P(None, "ctx", None),
        P("head", "ctx", None),
        P(),
    )
    return jax.shard_map(
        per_device,
        mesh=mesh,
        in_specs=placed,
        out_specs=(
            P("head", "ctx", None),
            P(None, ("ctx", "head"), None),
            P(None, ("ctx", "head"), None),
        ),
        check_vma=False,
    )
```

```python
import functools
import math

import jax
import jax.numpy as jnp
from jax import lax
from jax.experimental import pallas as pl
from jax.experimental.pallas import tpu as pltpu
from jax.sharding import PartitionSpec as P

GROUP = 8
REACH = 4
MASKED = -1e30
NN = (((1,), (0,)), ((), ()))
VMEM = pl.BlockSpec(memory_space=pltpu.VMEM)
SMEM = pl.BlockSpec(memory_space=pltpu.SMEM)
bf16, f32, i32 = jnp.bfloat16, jnp.float32, jnp.int32


def dot(a, b, dims=NN):
    return lax.dot_general(a, b, dims, preferred_element_type=f32)


def shape(dims, dtype):
    return jax.ShapeDtypeStruct(dims, dtype)


def call(body, name, in_specs, outs, scratch=()):
    return pl.pallas_call(
        body,
        out_shape=outs,
        in_specs=in_specs,
        out_specs=(VMEM,) * len(outs),
        scratch_shapes=scratch,
        compiler_params=pltpu.CompilerParams(vmem_limit_bytes=20 * 2**20),
        cost_estimate=pl.CostEstimate(flops=2**20, bytes_accessed=2**10, transcendentals=0),
        name=name,
    )


def shifted(block, distance):
    count = lax.axis_size("ctx")
    route = [(i - distance, i) for i in range(count) if 0 <= i - distance < count]
    return lax.ppermute(block, "ctx", route)


def exchanged(block, axis, mask):
    count = math.prod(lax.axis_size(name) for name in axis) if isinstance(axis, tuple) else (
        lax.axis_size(axis))
    return lax.ppermute(block, axis, [(i, i ^ mask) for i in range(count)])


def both(rows_ref):
    heads = rows_ref.shape[0] // 2
    return rows_ref.at[:heads], rows_ref.at[heads:]


def second_core():
    return lax.rem(lax.axis_index("ctx"), 2) == 1


def doc_starts(lengths_ref, block, tokens):
    row_pos = block * tokens + lax.broadcasted_iota(i32, (1, tokens), 1)
    starts = jnp.zeros((1, tokens), i32)
    end = jnp.int32(0)
    for d in range(lengths_ref.shape[0]):
        end = end + lengths_ref[d]
        starts = jnp.where(row_pos >= end, end, starts)
    return starts


def unit(pair, key_block, starts, turned_ref, e_ref, dp_ref, stats_ref, causal=False):
    heads, (width, tokens) = turned_ref.shape[0] // 2, turned_ref.shape[1:]
    factor = width ** -0.5 * math.log2(math.e)
    key_iota = lax.broadcasted_iota(i32, (tokens, 1), 0)
    allowed = key_block * tokens + key_iota >= starts
    if causal:
        allowed = allowed & (key_iota <= lax.broadcasted_iota(i32, (1, tokens), 1))
    for h in range(heads):
        lanes = slice(h * tokens, (h + 1) * tokens)
        s = jnp.where(allowed, dot(pair[:, :width], turned_ref[h]), MASKED)
        top = jnp.max(s, axis=0, keepdims=True)
        e = jnp.exp2((s - top) * factor)
        dp = dot(pair[:, width:], turned_ref[heads + h])
        e_ref[:, lanes] = e
        dp_ref[:, lanes] = dp
        stats_ref[0:1, lanes] = top
        stats_ref[1:2, lanes] = jnp.sum(e, axis=0, keepdims=True)
        stats_ref[2:3, lanes] = jnp.sum(e * dp, axis=0, keepdims=True)


def turn(rows_ref, turned_ref):
    for at in range(rows_ref.shape[0]):
        turned_ref[at] = rows_ref[at].T


def rows_of(ref, first=0):
    return [ref[first + row:first + row + 1] for row in range(3)]


def joined(parts, factor):
    top = functools.reduce(jnp.maximum, [part[0] for part in parts])
    gains = [jnp.exp2((part[0] - top) * factor) for part in parts]
    total = sum(gain * part[1] for gain, part in zip(gains, parts))
    weighted = sum(gain * part[2] for gain, part in zip(gains, parts))
    return top, total, weighted


def own_unit_body(starts_ref, rows_ref, own_ref, turned_ref, e_ref, dp_ref, stats_ref):
    turn(rows_ref, turned_ref)
    unit(own_ref, lax.axis_index("ctx"), starts_ref[0:1], turned_ref, e_ref, dp_ref, stats_ref,
         causal=True)


def four_unit_body(starts_ref, turned_ref, four_ref, e_ref, dp_ref, stats_ref):
    here = lax.axis_index("ctx")
    unit(four_ref, here - 4, starts_ref[0:1], turned_ref, e_ref, dp_ref, stats_ref)


def side_unit_body(starts_ref, other_rows, own_ref, four_ref,
                   turned_ref, e_ref, dp_ref, stats_ref):
    turn(other_rows, turned_ref)
    side = jnp.where(second_core(), four_ref[...], own_ref[...])
    block = lax.axis_index("ctx") - jnp.where(second_core(), 4, 0)
    unit(side, block, starts_ref[1:2], turned_ref, e_ref, dp_ref, stats_ref)


def prepare_body(share, middle, lengths_in, keys_ref, values_ref, queries_ref, d_out_ref,
                 split_out, starts_ref, own_ref, rows_ref, lengths_ref, split_ref, sems):
    heads, tokens, width = queries_ref.shape
    group = lax.axis_index("head") // share
    lengths = pltpu.make_async_copy(lengths_in, lengths_ref, sems.at[0])
    copies = [
        pltpu.make_async_copy(keys_ref.at[group], own_ref.at[:, :width], sems.at[1]),
        pltpu.make_async_copy(values_ref.at[group], own_ref.at[:, width:], sems.at[2]),
        pltpu.make_async_copy(queries_ref, rows_ref.at[:heads], sems.at[3]),
        pltpu.make_async_copy(d_out_ref, rows_ref.at[heads:], sems.at[4]),
    ]
    for copy in [lengths] + copies:
        copy.start()
    lengths.wait()
    end, split = jnp.int32(0), jnp.int32(0)
    for d in range(lengths_ref.shape[0]):
        end = end + lengths_ref[d]
        split = jnp.where(end == middle, 1, split)
    split_ref[0] = split
    copies.append(pltpu.make_async_copy(split_ref, split_out, sems.at[5]))
    copies[-1].start()
    here = lax.axis_index("ctx")
    starts_ref[0:1] = doc_starts(lengths_ref, here, tokens)
    starts_ref[1:2] = doc_starts(lengths_ref, jnp.bitwise_xor(here, 1), tokens)
    for copy in copies:
        copy.wait()


def near_side_unit_body(starts_ref, other_rows, own_ref, turned_ref, e_ref, dp_ref, stats_ref):
    turn(other_rows, turned_ref)
    block = jnp.where(second_core(), -1, lax.axis_index("ctx"))
    unit(own_ref, block, starts_ref[1:2], turned_ref, e_ref, dp_ref, stats_ref)


def write_rows(ref, values):
    for row, value in enumerate(values):
        ref[row:row + 1] = value


def cross_unit_body(starts_ref, turned_ref, two_ref, stats_side,
                    e_ref, dp_ref, stats_ref, others_ref):
    factor = turned_ref.shape[1] ** -0.5 * math.log2(math.e)
    unit(two_ref, lax.axis_index("ctx") - 2, starts_ref[1:2], turned_ref,
         e_ref, dp_ref, stats_ref)
    write_rows(others_ref, joined([rows_of(stats_side), rows_of(stats_ref)], factor))
    others_ref[3:4] = jnp.zeros((1, others_ref.shape[1]), f32)


def two_unit_body(starts_ref, turned_ref, two_ref, *refs):
    earlier, (e_ref, dp_ref, stats_ref, mine_ref) = refs[:-4], refs[-4:]
    factor = turned_ref.shape[1] ** -0.5 * math.log2(math.e)
    unit(two_ref, lax.axis_index("ctx") - 2, starts_ref[0:1], turned_ref,
         e_ref, dp_ref, stats_ref)
    write_rows(mine_ref, joined([rows_of(ref) for ref in earlier + (stats_ref,)], factor))
    mine_ref[3:4] = jnp.zeros((1, mine_ref.shape[1]), f32)


def coefficients(here_ref, taken_ref, stats_refs, width):
    factor = width ** -0.5 * math.log2(math.e)
    top, total, weighted = joined([rows_of(here_ref), rows_of(taken_ref)], factor)
    inverse = 1.0 / total
    return [weighted * inverse] + [
        jnp.exp2((ref[0:1] - top) * factor) * inverse for ref in stats_refs]


def slopes(e_ref, dp_ref, gain, delta, p_ref, ds_ref):
    p = e_ref[...] * gain
    p_ref[...] = p.astype(bf16)
    ds_ref[...] = (p * (dp_ref[...] - delta)).astype(bf16)


def flat(ref):
    heads, tokens, width = ref.shape
    return ref[...].reshape(heads * tokens, width)


def add_terms(sum_ref, ds_ref, p_ref, rows_ref, fresh):
    q_ref, g_ref = both(rows_ref)
    width = q_ref.shape[-1]
    dk = dot(ds_ref[...], flat(q_ref)) * width ** -0.5
    dv = dot(p_ref[...], flat(g_ref))
    if fresh:
        sum_ref[:, :width] = dk
        sum_ref[:, width:] = dv
    else:
        sum_ref[:, :width] += dk
        sum_ref[:, width:] += dv


def my_terms_body(count, mine_ref, taken_ref, *refs):
    stats, refs = refs[:count], refs[count:]
    parts, rows_ref, refs = refs[:4], refs[4], refs[5:]
    coef_ref, ds_refs, sums, p_ref = refs[0], refs[1:3], refs[3:5], refs[5]
    coefs = coefficients(mine_ref, taken_ref, stats, rows_ref.shape[-1])
    write_rows(coef_ref, coefs)
    for at in range(2):
        slopes(parts[2 * at], parts[2 * at + 1], coefs[count - 1 + at], coefs[0], p_ref.at[at],
               ds_refs[at])
        add_terms(sums[at], ds_refs[at], p_ref.at[at], rows_ref, True)


def four_terms_body(others_ref, taken_ref, stats_side, stats_cross, e_side, dp_side,
                    other_rows, part_ref, coef_ref, terms_ref, sum_ref, p_ref, ds_ref):
    coefs = coefficients(others_ref, taken_ref, (stats_side, stats_cross), other_rows.shape[-1])
    write_rows(coef_ref, coefs)
    sum_ref[...] = part_ref[...]

    @pl.when(second_core())
    def _():
        slopes(e_side, dp_side, coef_ref[1:2], coef_ref[0:1], p_ref, ds_ref)
        add_terms(sum_ref, ds_ref, p_ref, other_rows, False)

    terms_ref[...] = sum_ref[...].astype(bf16)


def two_terms_body(coef_ref, e_cross, dp_cross, other_rows, part_ref,
                   terms_ref, ds_cross, p_ref, sum_ref):
    slopes(e_cross, dp_cross, coef_ref[2:3], coef_ref[0:1], p_ref, ds_cross)
    sum_ref[...] = part_ref[...]
    add_terms(sum_ref, ds_cross, p_ref, other_rows, False)
    terms_ref[...] = sum_ref[...].astype(bf16)


def slice_rows(ref, other):
    count = lax.axis_size("head")
    each = ref.shape[0] // count
    parity = jnp.bitwise_xor(lax.rem(lax.axis_index("head"), 2), other)
    return [ref[pl.ds(pl.multiple_of((2 * at + parity) * each, each), each)]
            for at in range(count // 2)]


def halve(sum_ref, kept_ref, given_ref):
    each = sum_ref.shape[0] // lax.axis_size("head")
    for other, out_ref in enumerate((kept_ref, given_ref)):
        for at, value in enumerate(slice_rows(sum_ref, other)):
            out_ref[at * each:(at + 1) * each] = value.astype(out_ref.dtype)


def halved_two_terms_body(others_ref, taken_ref, stats_side, stats_cross, e_cross, dp_cross,
                        other_rows, part_ref,
                        coef_ref, kept_ref, other_ref, ds_cross, p_ref, sum_ref):
    coefs = coefficients(others_ref, taken_ref, (stats_side, stats_cross), other_rows.shape[-1])
    write_rows(coef_ref, coefs)
    slopes(e_cross, dp_cross, coefs[2], coefs[0], p_ref, ds_cross)
    sum_ref[...] = part_ref[...]
    add_terms(sum_ref, ds_cross, p_ref, other_rows, False)
    halve(sum_ref, kept_ref, other_ref)


def near_own_terms_body(coef_ref, e_side, dp_side, other_rows, part_ref,
                        kept_ref, other_ref, ds_side, p_ref, sum_ref):
    slopes(e_side, dp_side, coef_ref[1:2], coef_ref[0:1], p_ref, ds_side)
    sum_ref[...] = part_ref[...]

    @pl.when(jnp.logical_not(second_core()))
    def _():
        add_terms(sum_ref, ds_side, p_ref, other_rows, False)

    halve(sum_ref, kept_ref, other_ref)


def far_four_terms_body(coef_ref, e_side, dp_side, other_rows, part_ref,
                        kept_ref, other_ref, sum_ref, p_ref, ds_ref):
    sum_ref[...] = part_ref[...]

    @pl.when(second_core())
    def _():
        slopes(e_side, dp_side, coef_ref[1:2], coef_ref[0:1], p_ref, ds_ref)
        add_terms(sum_ref, ds_ref, p_ref, other_rows, False)

    halve(sum_ref, kept_ref, other_ref)


def far_own_terms_body(mine_coef, coef_ref, e_own, dp_own, e_side, dp_side, rows_ref,
                       other_rows,
                       kept_ref, other_ref, ds_own, ds_side, p_ref, p_side, sum_ref):
    slopes(e_own, dp_own, mine_coef[1:2], mine_coef[0:1], p_ref, ds_own)
    add_terms(sum_ref, ds_own, p_ref, rows_ref, True)
    slopes(e_side, dp_side, coef_ref[1:2], coef_ref[0:1], p_side, ds_side)

    @pl.when(jnp.logical_not(second_core()))
    def _():
        add_terms(sum_ref, ds_side, p_side, other_rows, False)

    halve(sum_ref, kept_ref, other_ref)


def grads_body(own_ref, two_ref, ds_own, ds_two, ds_side, ds_cross, *refs):
    four_refs, (dq_ref, other_dq_ref) = refs[:-2], refs[-2:]
    width = dq_ref.shape[-1]
    keys, slope_refs = [own_ref[:, :width], two_ref[:, :width]], [ds_own, ds_two]
    side = keys[0]
    if four_refs:
        keys.append(four_refs[0][:, :width])
        slope_refs.append(four_refs[1])
        side = jnp.where(second_core(), keys[2], side)
    query_grads([side, keys[1]], [ds_side, ds_cross], other_dq_ref)
    query_grads(keys, slope_refs, dq_ref)


def add_others_body(use, sum_ref, pair_ref, four_ref, out_ref):
    taken = jnp.where(use(lax.axis_index("ctx")), four_ref[...].astype(f32), 0.0)
    out_ref[...] = sum_ref[...] + pair_ref[...].astype(f32) + taken


def relay_body(kept_ref, four_ref, two_pair_ref, two_ref, out_ref, sent_ref):
    ctx = lax.axis_index("ctx")
    taken = two_ref[...].astype(f32) + two_pair_ref[...].astype(f32)
    out_ref[...] = kept_ref[...] + jnp.where(ctx & 2 == 0, taken, 0.0)
    sent_ref[...] = (four_ref[...] + jnp.where(ctx & 6 == 6, taken, 0.0)).astype(bf16)


def near_first_sum_body(kept_ref, two_ref, two_pair_ref, out_ref):
    taken = two_ref[...].astype(f32) + two_pair_ref[...].astype(f32)
    out_ref[...] = kept_ref[...] + jnp.where(lax.axis_index("ctx") & 2 == 0, taken, 0.0)


def halves_sum_body(share, use, kept_ref, back_ref, here_ref, there_ref):
    each = here_ref.shape[0]
    group = lax.axis_index("head") // share
    for out_ref, at in ((here_ref, group), (there_ref, 1 - group)):
        rows = pl.ds(pl.multiple_of(at * each, each), each)
        taken = back_ref[rows].astype(f32)
        if use is not None:
            taken = jnp.where(use(lax.axis_index("ctx")), taken, 0.0)
        out_ref[...] = (kept_ref[rows] + taken).astype(out_ref.dtype)


def last_body(share, here_ref, taken_ref, dk_ref, dv_ref):
    width = dk_ref.shape[-1]
    group = lax.axis_index("head") // share
    for ref, place in ((here_ref, group), (taken_ref, 1 - group)):
        dk_ref[place] = ref[:, :width]
        dv_ref[place] = ref[:, width:]


def query_grads(keys, ds_refs, out_ref):
    heads, tokens, width = out_ref.shape
    turned = [key.T for key in keys]
    for h in range(heads):
        lanes = slice(h * tokens, (h + 1) * tokens)
        dqt = sum(dot(kt, ds[:, lanes]) for kt, ds in zip(turned, ds_refs))
        out_ref[h] = (dqt.T * width ** -0.5).astype(out_ref.dtype)


def own_terms_body(mine_coef, coef_ref, e_own, dp_own, e_side, dp_side, rows_ref,
                   other_rows, own_ref, two_ref, ds_two, ds_cross, four_ref, ds_four,
                   terms_ref, dq_ref, other_dq_ref, ds_own, ds_side, p_ref, p_side):
    width = dq_ref.shape[-1]
    own, two, four = [ref[:, :width] for ref in (own_ref, two_ref, four_ref)]
    slopes(e_side, dp_side, coef_ref[1:2], coef_ref[0:1], p_side, ds_side)
    query_grads([jnp.where(second_core(), four, own), two], [ds_side, ds_cross], other_dq_ref)
    slopes(e_own, dp_own, mine_coef[1:2], mine_coef[0:1], p_ref, ds_own)
    add_terms(terms_ref, ds_own, p_ref, rows_ref, True)

    @pl.when(jnp.logical_not(second_core()))
    def _():
        add_terms(terms_ref, ds_side, p_side, other_rows, False)

    query_grads([own, two, four], [ds_own, ds_two, ds_four], dq_ref)


def add_grads_body(mine_ref, taken_ref, dq_ref):
    dq_ref[...] = (mine_ref[...] + taken_ref[...].astype(f32)).astype(dq_ref.dtype)


def sums_body(own_terms, four_back, two_back, out_ref):
    taken = four_back[...].astype(f32) + two_back[...].astype(f32)
    out_ref[...] = (own_terms[...] + taken).astype(bf16)


def per_device(queries, keys, values, d_out, doc_lengths):
    ctx_count, (heads, tokens, width) = lax.axis_size("ctx"), queries.shape
    middle = ctx_count // 2 * tokens
    split, starts, own, rows = pl.pallas_call(
        functools.partial(prepare_body, GROUP // heads, middle),
        out_shape=(shape((1,), i32), shape((2, tokens), i32), shape((tokens, 2 * width), bf16),
                   shape((2 * heads, tokens, width), bf16)),
        in_specs=[pl.BlockSpec(memory_space=pl.ANY)] * 5,
        out_specs=(pl.BlockSpec(memory_space=pl.ANY), VMEM, VMEM, VMEM),
        scratch_shapes=[pltpu.SMEM(doc_lengths.shape, i32), pltpu.SMEM((1,), i32),
                        pltpu.SemaphoreType.DMA((6,))],
        name="prepare",
    )(*[pltpu.with_memory_space_constraint(value, pltpu.HBM)
        for value in (doc_lengths, keys, values, queries, d_out)])
    operands = (rows, own, starts)
    if ctx_count != 2 * REACH or lax.axis_size("head") * heads != 2 * GROUP or 2 * heads != GROUP:
        return gradients(True, *operands)
    return lax.switch(split[0], [functools.partial(gradients, True),
                                 functools.partial(gradients, False)], *operands)


def gradients(far, row_data, own, starts):
    heads, (tokens, width) = row_data.shape[0] // 2, row_data.shape[1:]
    head_count = lax.axis_size("head")
    share = GROUP // heads
    groups = head_count // share
    rows = heads * tokens
    ctx = lax.axis_index("ctx")
    mutual = lax.axis_size("ctx") == 2 * REACH and share == groups == 2
    pair = (tokens, 2 * width)
    all_rows = (heads, tokens, width)
    stats = shape((3, rows), f32)
    wide = shape((tokens, rows), f32)
    half = shape((tokens, rows), bf16)
    half_scratch = pltpu.VMEM((tokens, rows), bf16)
    halves_scratch = pltpu.VMEM((2, tokens, rows), bf16)
    pair_scratch = pltpu.VMEM(pair, f32)

    if far:
        four = exchanged(own, "ctx", 4) if mutual else shifted(own, 4)
    two = [exchanged(own, "ctx", 6)] if far and mutual else []
    two.append(exchanged(own, "ctx", 2) if mutual else shifted(own, 2))
    flipped = shape((2 * heads, width, tokens), bf16)
    turned, e_own, dp_own, stats_own = call(
        own_unit_body, "own_unit", [VMEM] * 3, (flipped, wide, wide, stats),
    )(starts, row_data, own)
    other_rows = exchanged(row_data, "ctx", 1)
    if far:
        four, stats_own = lax.optimization_barrier((four, stats_own))
        e_four, dp_four, stats_four = call(
            four_unit_body, "four_unit", [VMEM] * 3, (wide, wide, stats))(starts, turned, four)
        other_rows, stats_four = lax.optimization_barrier((other_rows, stats_four))
        other_turned, e_side, dp_side, stats_side = call(
            side_unit_body, "side_unit", [VMEM] * 4, (flipped, wide, wide, stats),
        )(starts, other_rows, own, four)
    else:
        other_turned, e_side, dp_side, stats_side = call(
            near_side_unit_body, "side_unit", [VMEM] * 3, (flipped, wide, wide, stats),
        )(starts, other_rows, own)
    *two, stats_side, stats_own = lax.optimization_barrier((*two, stats_side, stats_own))
    mine_stats = (stats_own, stats_four) if far else (stats_own,)
    two = jnp.where(ctx & 2 == 2, two[1], two[0]) if len(two) == 2 else two[0]
    few = shape((4, rows), f32)
    e_cross, dp_cross, stats_cross, others = call(
        cross_unit_body, "cross_unit", [VMEM] * 4, (wide, wide, stats, few),
    )(starts, other_turned, two, stats_side)
    taken_others = exchanged(others, "ctx", 1)
    e_two, dp_two, stats_two, mine = call(
        two_unit_body, "two_unit", [VMEM] * (3 + len(mine_stats)), (wide, wide, stats, few),
    )(starts, turned, two, *mine_stats)
    taken_mine = exchanged(mine, "ctx", 1)
    mine_stats += (stats_two,)
    parts = ((e_four, dp_four) if far else (e_own, dp_own)) + (e_two, dp_two)
    mine_coef, ds_first, ds_two, first_part, two_part = call(
        functools.partial(my_terms_body, len(mine_stats)), "my_terms",
        [VMEM] * (7 + len(mine_stats)),
        (few, half, half, shape(pair, f32), shape(pair, f32)), (halves_scratch,),
    )(mine, taken_others, *mine_stats, *parts, row_data)
    last_stats = (others, taken_mine, stats_side, stats_cross)
    slices = (tokens // 2, 2 * width)
    slice_dims = (tokens // head_count, 2 * width)
    if not mutual:
        coef, four_terms = call(
            four_terms_body, "four_terms", [VMEM] * 8, (few, shape(pair, bf16)),
            (pair_scratch, half_scratch, half_scratch),
        )(*last_stats, e_side, dp_side, other_rows, first_part)
        two_terms, ds_cross = call(
            two_terms_body, "two_terms", [VMEM] * 5, (shape(pair, bf16), half),
            (half_scratch, pair_scratch),
        )(coef, e_cross, dp_cross, other_rows, two_part)
        backs = [shifted(four_terms, -4), shifted(two_terms, -2)]
        own_terms, my_grads, other_grads = call(
            own_terms_body, "own_terms", [VMEM] * 14,
            (shape(pair, f32), shape(all_rows, f32), shape(all_rows, bf16)),
            (half_scratch,) * 4,
        )(mine_coef, coef, e_own, dp_own, e_side, dp_side, row_data, other_rows, own, two,
          ds_two, ds_cross, four, ds_first)
        taken_grads = exchanged(other_grads, "ctx", 1)
        d_queries, = call(
            add_grads_body, "add_grads", [VMEM] * 2, (shape(all_rows, bf16),),
        )(my_grads, taken_grads)
        sums, = call(sums_body, "sums", [VMEM] * 3, (shape(pair, bf16),))(own_terms, *backs)
        pieces = lax.all_to_all(sums.reshape(head_count, *slice_dims), "head", 0, 0)
        result = jnp.sum(
            pieces.reshape(groups, share, *slice_dims).astype(f32), axis=1).astype(bf16)
        return d_queries, result[..., :width], result[..., width:]

    halves = (shape(slices, bf16), shape(slices, bf16))
    part = shape(slices, f32)
    coef, two_kept, two_other, ds_cross = call(
        halved_two_terms_body, "two_terms", [VMEM] * 8, (few,) + halves + (half,),
        (half_scratch, pair_scratch),
    )(*last_stats, e_cross, dp_cross, other_rows, two_part)
    two_back = exchanged(two_kept, "ctx", 2)
    two_pair = exchanged(two_other, ("ctx", "head"), 2 * head_count + 1)
    if far:
        four_kept, four_other = call(
            far_four_terms_body, "four_terms", [VMEM] * 5, (part, halves[1]),
            (pair_scratch, half_scratch, half_scratch),
        )(coef, e_side, dp_side, other_rows, first_part)
        four_pair = exchanged(four_other, ("ctx", "head"), 4 * head_count + 1)
        own_kept, own_other, ds_own, ds_side = call(
            far_own_terms_body, "own_terms", [VMEM] * 8, (part, halves[1], half, half),
            (half_scratch, half_scratch, pair_scratch),
        )(mine_coef, coef, e_own, dp_own, e_side, dp_side, row_data, other_rows)
    else:
        ds_own = ds_first
        own_kept, own_other, ds_side = call(
            near_own_terms_body, "own_terms", [VMEM] * 5, (part, halves[1], half),
            (half_scratch, pair_scratch),
        )(coef, e_side, dp_side, other_rows, first_part)
    own_pair = exchanged(own_other, "head", 1)
    four_refs = (four, ds_first) if far else ()
    my_grads, other_grads = call(
        grads_body, "query_grads", [VMEM] * (6 + len(four_refs)),
        (shape(all_rows, f32), shape(all_rows, bf16)),
    )(own, two, ds_own, ds_two, ds_side, ds_cross, *four_refs)
    owns_four = lambda i: i < 4
    if far:
        own_kept, relayed = call(
            relay_body, "relay", [VMEM] * 4, (part, halves[0]),
        )(own_kept, four_kept, two_pair, two_back)
        four_back = exchanged(relayed, "ctx", 4)
        own_kept, = call(functools.partial(add_others_body, owns_four), "add_others", [VMEM] * 3,
                         (part,))(own_kept, own_pair, four_pair)
        final, use = four_back, owns_four
    else:
        own_kept, = call(
            near_first_sum_body, "first_sum", [VMEM] * 3, (part,),
        )(own_kept, two_back, two_pair)
        final, use = own_pair, None
    kept, sent = call(
        functools.partial(halves_sum_body, share, use), "sums", [VMEM] * 2,
        (shape(slice_dims, bf16),) * 2)(own_kept, final)
    other_grads, kept = lax.optimization_barrier((other_grads, kept))
    taken_grads = exchanged(other_grads, "ctx", 1)
    d_queries, = call(
        add_grads_body, "add_grads", [VMEM] * 2, (shape(all_rows, bf16),),
    )(my_grads, taken_grads)
    last = exchanged(sent, "head", share)
    last, d_queries = lax.optimization_barrier((last, d_queries))
    d_keys, d_values = call(
        functools.partial(last_body, share), "last", [VMEM] * 2,
        (shape((groups, tokens // head_count, width), bf16),) * 2)(kept, last)
    return d_queries, d_keys, d_values


def solution(mesh):
    placed = (
        P("head", "ctx", None),
        P(None, "ctx", None),
        P(None, "ctx", None),
        P("head", "ctx", None),
        P(),
    )
    return jax.shard_map(
        per_device,
        mesh=mesh,
        in_specs=placed,
        out_specs=(
            P("head", "ctx", None),
            P(None, ("ctx", "head"), None),
            P(None, ("ctx", "head"), None),
        ),
        check_vma=False,
    )
```

```python
import functools
import math

import jax
import jax.numpy as jnp
from jax import lax
from jax.experimental import pallas as pl
from jax.experimental.pallas import tpu as pltpu
from jax.sharding import PartitionSpec as P

GROUP = 8
REACH = 4
MASKED = -1e30
NN = (((1,), (0,)), ((), ()))
VMEM = pl.BlockSpec(memory_space=pltpu.VMEM)
SMEM = pl.BlockSpec(memory_space=pltpu.SMEM)
bf16, f32, i32 = jnp.bfloat16, jnp.float32, jnp.int32


def dot(a, b, dims=NN):
    return lax.dot_general(a, b, dims, preferred_element_type=f32)


def shape(dims, dtype):
    return jax.ShapeDtypeStruct(dims, dtype)


def call(body, name, in_specs, outs, scratch=()):
    return pl.pallas_call(
        body,
        out_shape=outs,
        in_specs=in_specs,
        out_specs=(VMEM,) * len(outs),
        scratch_shapes=scratch,
        compiler_params=pltpu.CompilerParams(vmem_limit_bytes=10 * 2**20),
        cost_estimate=pl.CostEstimate(flops=2**20, bytes_accessed=2**10, transcendentals=0),
        name=name,
    )


def shifted(block, distance):
    count = lax.axis_size("ctx")
    route = [(i - distance, i) for i in range(count) if 0 <= i - distance < count]
    return lax.ppermute(block, "ctx", route)


def exchanged(block, axis, mask):
    count = math.prod(lax.axis_size(name) for name in axis) if isinstance(axis, tuple) else (
        lax.axis_size(axis))
    return lax.ppermute(block, axis, [(i, i ^ mask) for i in range(count)])


def both(rows_ref):
    heads = rows_ref.shape[0] // 2
    return rows_ref.at[:heads], rows_ref.at[heads:]


def second_core():
    return lax.rem(lax.axis_index("ctx"), 2) == 1


def doc_starts(lengths_ref, block, tokens):
    row_pos = block * tokens + lax.broadcasted_iota(i32, (1, tokens), 1)
    starts = jnp.zeros((1, tokens), i32)
    end = jnp.int32(0)
    for d in range(lengths_ref.shape[0]):
        end = end + lengths_ref[d]
        starts = jnp.where(row_pos >= end, end, starts)
    return starts


def unit(pair, key_block, starts, turned_ref, e_ref, dp_ref, stats_ref, causal=False):
    heads, (width, tokens) = turned_ref.shape[0] // 2, turned_ref.shape[1:]
    factor = width ** -0.5 * math.log2(math.e)
    key_iota = lax.broadcasted_iota(i32, (tokens, 1), 0)
    allowed = key_block * tokens + key_iota >= starts
    if causal:
        allowed = allowed & (key_iota <= lax.broadcasted_iota(i32, (1, tokens), 1))
    for h in range(heads):
        lanes = slice(h * tokens, (h + 1) * tokens)
        s = jnp.where(allowed, dot(pair[:, :width], turned_ref[h]), MASKED)
        top = jnp.max(s, axis=0, keepdims=True)
        e = jnp.exp2((s - top) * factor)
        dp = dot(pair[:, width:], turned_ref[heads + h])
        e_ref[:, lanes] = e
        dp_ref[:, lanes] = dp
        stats_ref[0:1, lanes] = top
        stats_ref[1:2, lanes] = jnp.sum(e, axis=0, keepdims=True)
        stats_ref[2:3, lanes] = jnp.sum(e * dp, axis=0, keepdims=True)


def turn(rows_ref, turned_ref):
    for at in range(rows_ref.shape[0]):
        turned_ref[at] = rows_ref[at].T


def rows_of(ref, first=0):
    return [ref[first + row:first + row + 1] for row in range(3)]


def joined(parts, factor):
    top = functools.reduce(jnp.maximum, [part[0] for part in parts])
    gains = [jnp.exp2((part[0] - top) * factor) for part in parts]
    total = sum(gain * part[1] for gain, part in zip(gains, parts))
    weighted = sum(gain * part[2] for gain, part in zip(gains, parts))
    return top, total, weighted


def own_unit_body(starts_ref, rows_ref, own_ref, turned_ref, e_ref, dp_ref, stats_ref):
    turn(rows_ref, turned_ref)
    unit(own_ref, lax.axis_index("ctx"), starts_ref[0:1], turned_ref, e_ref, dp_ref, stats_ref,
         causal=True)


def four_unit_body(starts_ref, turned_ref, four_ref, e_ref, dp_ref, stats_ref):
    here = lax.axis_index("ctx")
    unit(four_ref, here - 4, starts_ref[0:1], turned_ref, e_ref, dp_ref, stats_ref)


def side_unit_body(starts_ref, other_rows, own_ref, four_ref,
                   turned_ref, e_ref, dp_ref, stats_ref):
    turn(other_rows, turned_ref)
    side = jnp.where(second_core(), four_ref[...], own_ref[...])
    block = lax.axis_index("ctx") - jnp.where(second_core(), 4, 0)
    unit(side, block, starts_ref[1:2], turned_ref, e_ref, dp_ref, stats_ref)


def prepare_body(share, middle, lengths_in, keys_ref, values_ref, queries_ref, d_out_ref,
                 split_out, starts_ref, own_ref, rows_ref, lengths_ref, split_ref, sems):
    heads, tokens, width = queries_ref.shape
    group = lax.axis_index("head") // share
    lengths = pltpu.make_async_copy(lengths_in, lengths_ref, sems.at[0])
    copies = [
        pltpu.make_async_copy(keys_ref.at[group], own_ref.at[:, :width], sems.at[1]),
        pltpu.make_async_copy(values_ref.at[group], own_ref.at[:, width:], sems.at[2]),
        pltpu.make_async_copy(queries_ref, rows_ref.at[:heads], sems.at[3]),
        pltpu.make_async_copy(d_out_ref, rows_ref.at[heads:], sems.at[4]),
    ]
    for copy in [lengths] + copies:
        copy.start()
    lengths.wait()
    end, split = jnp.int32(0), jnp.int32(0)
    for d in range(lengths_ref.shape[0]):
        end = end + lengths_ref[d]
        split = jnp.where(end == middle, 1, split)
    split_ref[0] = split
    copies.append(pltpu.make_async_copy(split_ref, split_out, sems.at[5]))
    copies[-1].start()
    here = lax.axis_index("ctx")
    starts_ref[0:1] = doc_starts(lengths_ref, here, tokens)
    starts_ref[1:2] = doc_starts(lengths_ref, jnp.bitwise_xor(here, 1), tokens)
    for copy in copies:
        copy.wait()


def near_side_unit_body(starts_ref, other_rows, own_ref, turned_ref, e_ref, dp_ref, stats_ref):
    turn(other_rows, turned_ref)
    block = jnp.where(second_core(), -1, lax.axis_index("ctx"))
    unit(own_ref, block, starts_ref[1:2], turned_ref, e_ref, dp_ref, stats_ref)


def write_rows(ref, values):
    for row, value in enumerate(values):
        ref[row:row + 1] = value


def cross_unit_body(starts_ref, turned_ref, two_ref, stats_side,
                    e_ref, dp_ref, stats_ref, others_ref):
    factor = turned_ref.shape[1] ** -0.5 * math.log2(math.e)
    unit(two_ref, lax.axis_index("ctx") - 2, starts_ref[1:2], turned_ref,
         e_ref, dp_ref, stats_ref)
    write_rows(others_ref, joined([rows_of(stats_side), rows_of(stats_ref)], factor))
    others_ref[3:4] = jnp.zeros((1, others_ref.shape[1]), f32)


def two_unit_body(starts_ref, turned_ref, two_ref, *refs):
    earlier, (e_ref, dp_ref, stats_ref, mine_ref) = refs[:-4], refs[-4:]
    factor = turned_ref.shape[1] ** -0.5 * math.log2(math.e)
    unit(two_ref, lax.axis_index("ctx") - 2, starts_ref[0:1], turned_ref,
         e_ref, dp_ref, stats_ref)
    write_rows(mine_ref, joined([rows_of(ref) for ref in earlier + (stats_ref,)], factor))
    mine_ref[3:4] = jnp.zeros((1, mine_ref.shape[1]), f32)


def coefficients(here_ref, taken_ref, stats_refs, width):
    factor = width ** -0.5 * math.log2(math.e)
    top, total, weighted = joined([rows_of(here_ref), rows_of(taken_ref)], factor)
    inverse = 1.0 / total
    return [weighted * inverse] + [
        jnp.exp2((ref[0:1] - top) * factor) * inverse for ref in stats_refs]


def slopes(e_ref, dp_ref, gain, delta, p_ref, ds_ref):
    p = e_ref[...] * gain
    p_ref[...] = p.astype(bf16)
    ds_ref[...] = (p * (dp_ref[...] - delta)).astype(bf16)


def flat(ref):
    heads, tokens, width = ref.shape
    return ref[...].reshape(heads * tokens, width)


def add_terms(sum_ref, ds_ref, p_ref, rows_ref, fresh):
    q_ref, g_ref = both(rows_ref)
    width = q_ref.shape[-1]
    dk = dot(ds_ref[...], flat(q_ref)) * width ** -0.5
    dv = dot(p_ref[...], flat(g_ref))
    if fresh:
        sum_ref[:, :width] = dk
        sum_ref[:, width:] = dv
    else:
        sum_ref[:, :width] += dk
        sum_ref[:, width:] += dv


def my_terms_body(count, mine_ref, taken_ref, *refs):
    stats, refs = refs[:count], refs[count:]
    parts, rows_ref, refs = refs[:4], refs[4], refs[5:]
    coef_ref, ds_refs, sums, p_ref = refs[0], refs[1:3], refs[3:5], refs[5]
    coefs = coefficients(mine_ref, taken_ref, stats, rows_ref.shape[-1])
    write_rows(coef_ref, coefs)
    for at in range(2):
        slopes(parts[2 * at], parts[2 * at + 1], coefs[count - 1 + at], coefs[0], p_ref.at[at],
               ds_refs[at])
        add_terms(sums[at], ds_refs[at], p_ref.at[at], rows_ref, True)


def four_terms_body(others_ref, taken_ref, stats_side, stats_cross, e_side, dp_side,
                    other_rows, part_ref, coef_ref, terms_ref, sum_ref, p_ref, ds_ref):
    coefs = coefficients(others_ref, taken_ref, (stats_side, stats_cross), other_rows.shape[-1])
    write_rows(coef_ref, coefs)
    sum_ref[...] = part_ref[...]

    @pl.when(second_core())
    def _():
        slopes(e_side, dp_side, coef_ref[1:2], coef_ref[0:1], p_ref, ds_ref)
        add_terms(sum_ref, ds_ref, p_ref, other_rows, False)

    terms_ref[...] = sum_ref[...].astype(bf16)


def two_terms_body(coef_ref, e_cross, dp_cross, other_rows, part_ref,
                   terms_ref, ds_cross, p_ref, sum_ref):
    slopes(e_cross, dp_cross, coef_ref[2:3], coef_ref[0:1], p_ref, ds_cross)
    sum_ref[...] = part_ref[...]
    add_terms(sum_ref, ds_cross, p_ref, other_rows, False)
    terms_ref[...] = sum_ref[...].astype(bf16)


def slice_rows(ref, other):
    count = lax.axis_size("head")
    each = ref.shape[0] // count
    parity = jnp.bitwise_xor(lax.rem(lax.axis_index("head"), 2), other)
    return [ref[pl.ds(pl.multiple_of((2 * at + parity) * each, each), each)]
            for at in range(count // 2)]


def halve(sum_ref, kept_ref, given_ref):
    each = sum_ref.shape[0] // lax.axis_size("head")
    for other, out_ref in enumerate((kept_ref, given_ref)):
        for at, value in enumerate(slice_rows(sum_ref, other)):
            out_ref[at * each:(at + 1) * each] = value.astype(out_ref.dtype)


def halved_two_terms_body(others_ref, taken_ref, stats_side, stats_cross, e_cross, dp_cross,
                        other_rows, part_ref,
                        coef_ref, kept_ref, other_ref, ds_cross, p_ref, sum_ref):
    coefs = coefficients(others_ref, taken_ref, (stats_side, stats_cross), other_rows.shape[-1])
    write_rows(coef_ref, coefs)
    slopes(e_cross, dp_cross, coefs[2], coefs[0], p_ref, ds_cross)
    sum_ref[...] = part_ref[...]
    add_terms(sum_ref, ds_cross, p_ref, other_rows, False)
    halve(sum_ref, kept_ref, other_ref)


def near_own_terms_body(coef_ref, e_side, dp_side, other_rows, part_ref,
                        kept_ref, other_ref, ds_side, p_ref, sum_ref):
    slopes(e_side, dp_side, coef_ref[1:2], coef_ref[0:1], p_ref, ds_side)
    sum_ref[...] = part_ref[...]

    @pl.when(jnp.logical_not(second_core()))
    def _():
        add_terms(sum_ref, ds_side, p_ref, other_rows, False)

    halve(sum_ref, kept_ref, other_ref)


def far_four_terms_body(coef_ref, e_side, dp_side, other_rows, part_ref,
                        kept_ref, other_ref, sum_ref, p_ref, ds_ref):
    sum_ref[...] = part_ref[...]

    @pl.when(second_core())
    def _():
        slopes(e_side, dp_side, coef_ref[1:2], coef_ref[0:1], p_ref, ds_ref)
        add_terms(sum_ref, ds_ref, p_ref, other_rows, False)

    halve(sum_ref, kept_ref, other_ref)


def far_own_terms_body(mine_coef, coef_ref, e_own, dp_own, e_side, dp_side, rows_ref,
                       other_rows,
                       kept_ref, other_ref, ds_own, ds_side, p_ref, p_side, sum_ref):
    slopes(e_own, dp_own, mine_coef[1:2], mine_coef[0:1], p_ref, ds_own)
    add_terms(sum_ref, ds_own, p_ref, rows_ref, True)
    slopes(e_side, dp_side, coef_ref[1:2], coef_ref[0:1], p_side, ds_side)

    @pl.when(jnp.logical_not(second_core()))
    def _():
        add_terms(sum_ref, ds_side, p_side, other_rows, False)

    halve(sum_ref, kept_ref, other_ref)


def grads_body(own_ref, two_ref, ds_own, ds_two, ds_side, ds_cross, *refs):
    four_refs, (dq_ref, other_dq_ref) = refs[:-2], refs[-2:]
    width = dq_ref.shape[-1]
    keys, slope_refs = [own_ref[:, :width], two_ref[:, :width]], [ds_own, ds_two]
    side = keys[0]
    if four_refs:
        keys.append(four_refs[0][:, :width])
        slope_refs.append(four_refs[1])
        side = jnp.where(second_core(), keys[2], side)
    query_grads([side, keys[1]], [ds_side, ds_cross], other_dq_ref)
    query_grads(keys, slope_refs, dq_ref)


def add_others_body(use, sum_ref, pair_ref, four_ref, out_ref):
    taken = jnp.where(use(lax.axis_index("ctx")), four_ref[...].astype(f32), 0.0)
    out_ref[...] = sum_ref[...] + pair_ref[...].astype(f32) + taken


def relay_body(kept_ref, four_ref, two_ref, two_pair_ref, out_ref, sent_ref):
    ctx = lax.axis_index("ctx")
    taken = two_ref[...].astype(f32) + two_pair_ref[...].astype(f32)
    out_ref[...] = kept_ref[...] + jnp.where(ctx & 2 == 0, taken, 0.0)
    sent_ref[...] = (four_ref[...] + jnp.where(ctx & 6 == 6, taken, 0.0)).astype(bf16)


def near_first_sum_body(kept_ref, two_ref, two_pair_ref, out_ref):
    taken = two_ref[...].astype(f32) + two_pair_ref[...].astype(f32)
    out_ref[...] = kept_ref[...] + jnp.where(lax.axis_index("ctx") & 2 == 0, taken, 0.0)


def halves_sum_body(share, use, kept_ref, back_ref, here_ref, there_ref):
    each = here_ref.shape[0]
    group = lax.axis_index("head") // share
    for out_ref, at in ((here_ref, group), (there_ref, 1 - group)):
        rows = pl.ds(pl.multiple_of(at * each, each), each)
        taken = back_ref[rows].astype(f32)
        if use is not None:
            taken = jnp.where(use(lax.axis_index("ctx")), taken, 0.0)
        out_ref[...] = (kept_ref[rows] + taken).astype(out_ref.dtype)


def last_body(share, here_ref, taken_ref, dk_ref, dv_ref):
    width = dk_ref.shape[-1]
    group = lax.axis_index("head") // share
    for ref, place in ((here_ref, group), (taken_ref, 1 - group)):
        dk_ref[place] = ref[:, :width]
        dv_ref[place] = ref[:, width:]


def query_grads(keys, ds_refs, out_ref):
    heads, tokens, width = out_ref.shape
    turned = [key.T for key in keys]
    for h in range(heads):
        lanes = slice(h * tokens, (h + 1) * tokens)
        dqt = sum(dot(kt, ds[:, lanes]) for kt, ds in zip(turned, ds_refs))
        out_ref[h] = (dqt.T * width ** -0.5).astype(out_ref.dtype)


def own_terms_body(mine_coef, coef_ref, e_own, dp_own, e_side, dp_side, rows_ref,
                   other_rows, own_ref, two_ref, ds_two, ds_cross, four_ref, ds_four,
                   terms_ref, dq_ref, other_dq_ref, ds_own, ds_side, p_ref, p_side):
    width = dq_ref.shape[-1]
    own, two, four = [ref[:, :width] for ref in (own_ref, two_ref, four_ref)]
    slopes(e_side, dp_side, coef_ref[1:2], coef_ref[0:1], p_side, ds_side)
    query_grads([jnp.where(second_core(), four, own), two], [ds_side, ds_cross], other_dq_ref)
    slopes(e_own, dp_own, mine_coef[1:2], mine_coef[0:1], p_ref, ds_own)
    add_terms(terms_ref, ds_own, p_ref, rows_ref, True)

    @pl.when(jnp.logical_not(second_core()))
    def _():
        add_terms(terms_ref, ds_side, p_side, other_rows, False)

    query_grads([own, two, four], [ds_own, ds_two, ds_four], dq_ref)


def add_grads_body(mine_ref, taken_ref, dq_ref):
    dq_ref[...] = (mine_ref[...] + taken_ref[...].astype(f32)).astype(dq_ref.dtype)


def sums_body(own_terms, four_back, two_back, out_ref):
    taken = four_back[...].astype(f32) + two_back[...].astype(f32)
    out_ref[...] = (own_terms[...] + taken).astype(bf16)


def per_device(queries, keys, values, d_out, doc_lengths):
    ctx_count, (heads, tokens, width) = lax.axis_size("ctx"), queries.shape
    middle = ctx_count // 2 * tokens
    split, starts, own, rows = pl.pallas_call(
        functools.partial(prepare_body, GROUP // heads, middle),
        out_shape=(shape((1,), i32), shape((2, tokens), i32), shape((tokens, 2 * width), bf16),
                   shape((2 * heads, tokens, width), bf16)),
        in_specs=[pl.BlockSpec(memory_space=pl.ANY)] * 5,
        out_specs=(pl.BlockSpec(memory_space=pl.ANY), VMEM, VMEM, VMEM),
        scratch_shapes=[pltpu.SMEM(doc_lengths.shape, i32), pltpu.SMEM((1,), i32),
                        pltpu.SemaphoreType.DMA((6,))],
        name="prepare",
    )(*[pltpu.with_memory_space_constraint(value, pltpu.HBM)
        for value in (doc_lengths, keys, values, queries, d_out)])
    operands = (rows, own, starts)
    if ctx_count != 2 * REACH or lax.axis_size("head") * heads != 2 * GROUP or 2 * heads != GROUP:
        return gradients(True, *operands)
    return lax.switch(split[0], [functools.partial(gradients, True),
                                 functools.partial(gradients, False)], *operands)


def gradients(far, row_data, own, starts):
    heads, (tokens, width) = row_data.shape[0] // 2, row_data.shape[1:]
    head_count = lax.axis_size("head")
    share = GROUP // heads
    groups = head_count // share
    rows = heads * tokens
    ctx = lax.axis_index("ctx")
    mutual = lax.axis_size("ctx") == 2 * REACH and share == groups == 2
    pair = (tokens, 2 * width)
    all_rows = (heads, tokens, width)
    stats = shape((3, rows), f32)
    wide = shape((tokens, rows), f32)
    half = shape((tokens, rows), bf16)
    half_scratch = pltpu.VMEM((tokens, rows), bf16)
    halves_scratch = pltpu.VMEM((2, tokens, rows), bf16)
    pair_scratch = pltpu.VMEM(pair, f32)

    if far:
        four = exchanged(own, "ctx", 4) if mutual else shifted(own, 4)
    flipped = shape((2 * heads, width, tokens), bf16)
    turned, e_own, dp_own, stats_own = call(
        own_unit_body, "own_unit", [VMEM] * 3, (flipped, wide, wide, stats),
    )(starts, row_data, own)
    sent = own
    if far:
        sent, stats_own = lax.optimization_barrier((own, stats_own))
    two = [exchanged(sent, "ctx", 2) if mutual else shifted(sent, 2)]
    if far and mutual:
        two.append(exchanged(sent, "ctx", 6))
    other_rows = exchanged(row_data, "ctx", 1)
    if far:
        four, stats_own = lax.optimization_barrier((four, stats_own))
        e_four, dp_four, stats_four = call(
            four_unit_body, "four_unit", [VMEM] * 3, (wide, wide, stats))(starts, turned, four)
        other_rows, stats_four = lax.optimization_barrier((other_rows, stats_four))
        other_turned, e_side, dp_side, stats_side = call(
            side_unit_body, "side_unit", [VMEM] * 4, (flipped, wide, wide, stats),
        )(starts, other_rows, own, four)
    else:
        other_turned, e_side, dp_side, stats_side = call(
            near_side_unit_body, "side_unit", [VMEM] * 3, (flipped, wide, wide, stats),
        )(starts, other_rows, own)
    *two, stats_side, stats_own = lax.optimization_barrier((*two, stats_side, stats_own))
    mine_stats = (stats_own, stats_four) if far else (stats_own,)
    two = jnp.where(ctx & 2 == 2, *two) if len(two) == 2 else two[0]
    few = shape((4, rows), f32)
    e_cross, dp_cross, stats_cross, others = call(
        cross_unit_body, "cross_unit", [VMEM] * 4, (wide, wide, stats, few),
    )(starts, other_turned, two, stats_side)
    taken_others = exchanged(others, "ctx", 1)
    e_two, dp_two, stats_two, mine = call(
        two_unit_body, "two_unit", [VMEM] * (3 + len(mine_stats)), (wide, wide, stats, few),
    )(starts, turned, two, *mine_stats)
    taken_mine = exchanged(mine, "ctx", 1)
    mine_stats += (stats_two,)
    parts = ((e_four, dp_four) if far else (e_own, dp_own)) + (e_two, dp_two)
    mine_coef, ds_first, ds_two, first_part, two_part = call(
        functools.partial(my_terms_body, len(mine_stats)), "my_terms",
        [VMEM] * (7 + len(mine_stats)),
        (few, half, half, shape(pair, f32), shape(pair, f32)), (halves_scratch,),
    )(mine, taken_others, *mine_stats, *parts, row_data)
    last_stats = (others, taken_mine, stats_side, stats_cross)
    slices = (tokens // 2, 2 * width)
    slice_dims = (tokens // head_count, 2 * width)
    if not mutual:
        coef, four_terms = call(
            four_terms_body, "four_terms", [VMEM] * 8, (few, shape(pair, bf16)),
            (pair_scratch, half_scratch, half_scratch),
        )(*last_stats, e_side, dp_side, other_rows, first_part)
        two_terms, ds_cross = call(
            two_terms_body, "two_terms", [VMEM] * 5, (shape(pair, bf16), half),
            (half_scratch, pair_scratch),
        )(coef, e_cross, dp_cross, other_rows, two_part)
        backs = [shifted(four_terms, -4), shifted(two_terms, -2)]
        own_terms, my_grads, other_grads = call(
            own_terms_body, "own_terms", [VMEM] * 14,
            (shape(pair, f32), shape(all_rows, f32), shape(all_rows, bf16)),
            (half_scratch,) * 4,
        )(mine_coef, coef, e_own, dp_own, e_side, dp_side, row_data, other_rows, own, two,
          ds_two, ds_cross, four, ds_first)
        taken_grads = exchanged(other_grads, "ctx", 1)
        d_queries, = call(
            add_grads_body, "add_grads", [VMEM] * 2, (shape(all_rows, bf16),),
        )(my_grads, taken_grads)
        sums, = call(sums_body, "sums", [VMEM] * 3, (shape(pair, bf16),))(own_terms, *backs)
        pieces = lax.all_to_all(sums.reshape(head_count, *slice_dims), "head", 0, 0)
        result = jnp.sum(
            pieces.reshape(groups, share, *slice_dims).astype(f32), axis=1).astype(bf16)
        return d_queries, result[..., :width], result[..., width:]

    halves = (shape(slices, bf16), shape(slices, bf16))
    part = shape(slices, f32)
    coef, two_kept, two_other, ds_cross = call(
        halved_two_terms_body, "two_terms", [VMEM] * 8, (few,) + halves + (half,),
        (half_scratch, pair_scratch),
    )(*last_stats, e_cross, dp_cross, other_rows, two_part)
    two_back = exchanged(two_kept, "ctx", 2)
    two_pair = exchanged(two_other, ("ctx", "head"), 2 * head_count + 1)
    if far:
        four_kept, four_other = call(
            far_four_terms_body, "four_terms", [VMEM] * 5, (part, halves[1]),
            (pair_scratch, half_scratch, half_scratch),
        )(coef, e_side, dp_side, other_rows, first_part)
        four_pair = exchanged(four_other, ("ctx", "head"), 4 * head_count + 1)
        own_kept, own_other, ds_own, ds_side = call(
            far_own_terms_body, "own_terms", [VMEM] * 8, (part, halves[1], half, half),
            (half_scratch, half_scratch, pair_scratch),
        )(mine_coef, coef, e_own, dp_own, e_side, dp_side, row_data, other_rows)
    else:
        ds_own = ds_first
        own_kept, own_other, ds_side = call(
            near_own_terms_body, "own_terms", [VMEM] * 5, (part, halves[1], half),
            (half_scratch, pair_scratch),
        )(coef, e_side, dp_side, other_rows, first_part)
    own_pair = exchanged(own_other, "head", 1)
    four_refs = (four, ds_first) if far else ()
    my_grads, other_grads = call(
        grads_body, "query_grads", [VMEM] * (6 + len(four_refs)),
        (shape(all_rows, f32), shape(all_rows, bf16)),
    )(own, two, ds_own, ds_two, ds_side, ds_cross, *four_refs)
    owns_four = lambda i: i < 4
    if far:
        own_kept, relayed = call(
            relay_body, "relay", [VMEM] * 4, (part, halves[0]),
        )(own_kept, four_kept, two_back, two_pair)
        four_back = exchanged(relayed, "ctx", 4)
        own_kept, = call(functools.partial(add_others_body, owns_four), "add_others", [VMEM] * 3,
                         (part,))(own_kept, own_pair, four_pair)
        final, use = four_back, owns_four
    else:
        own_kept, = call(
            near_first_sum_body, "first_sum", [VMEM] * 3, (part,),
        )(own_kept, two_back, two_pair)
        final, use = own_pair, None
    kept, sent = call(
        functools.partial(halves_sum_body, share, use), "sums", [VMEM] * 2,
        (shape(slice_dims, bf16),) * 2)(own_kept, final)
    other_grads, kept = lax.optimization_barrier((other_grads, kept))
    taken_grads = exchanged(other_grads, "ctx", 1)
    d_queries, = call(
        add_grads_body, "add_grads", [VMEM] * 2, (shape(all_rows, bf16),),
    )(my_grads, taken_grads)
    last = exchanged(sent, "head", share)
    last, d_queries = lax.optimization_barrier((last, d_queries))
    d_keys, d_values = call(
        functools.partial(last_body, share), "last", [VMEM] * 2,
        (shape((groups, tokens // head_count, width), bf16),) * 2)(kept, last)
    return d_queries, d_keys, d_values


def solution(mesh):
    placed = (
        P("head", "ctx", None),
        P(None, "ctx", None),
        P(None, "ctx", None),
        P("head", "ctx", None),
        P(),
    )
    return jax.shard_map(
        per_device,
        mesh=mesh,
        in_specs=placed,
        out_specs=(
            P("head", "ctx", None),
            P(None, ("ctx", "head"), None),
            P(None, ("ctx", "head"), None),
        ),
        check_vma=False,
    )
```

```python
import functools
import math

import jax
import jax.numpy as jnp
from jax import lax
from jax.experimental import pallas as pl
from jax.experimental.pallas import tpu as pltpu
from jax.sharding import PartitionSpec as P

GROUP = 8
REACH = 4
MASKED = -1e30
NN = (((1,), (0,)), ((), ()))
VMEM = pl.BlockSpec(memory_space=pltpu.VMEM)
SMEM = pl.BlockSpec(memory_space=pltpu.SMEM)
bf16, f32, i32 = jnp.bfloat16, jnp.float32, jnp.int32


def dot(a, b, dims=NN):
    return lax.dot_general(a, b, dims, preferred_element_type=f32)


def shape(dims, dtype):
    return jax.ShapeDtypeStruct(dims, dtype)


def call(body, name, in_specs, outs, scratch=()):
    return pl.pallas_call(
        body,
        out_shape=outs,
        in_specs=in_specs,
        out_specs=(VMEM,) * len(outs),
        scratch_shapes=scratch,
        compiler_params=pltpu.CompilerParams(vmem_limit_bytes=40 * 2**20),
        cost_estimate=pl.CostEstimate(flops=2**20, bytes_accessed=2**10, transcendentals=0),
        name=name,
    )


def shifted(block, distance):
    count = lax.axis_size("ctx")
    route = [(i - distance, i) for i in range(count) if 0 <= i - distance < count]
    return lax.ppermute(block, "ctx", route)


def exchanged(block, axis, mask):
    count = math.prod(lax.axis_size(name) for name in axis) if isinstance(axis, tuple) else (
        lax.axis_size(axis))
    return lax.ppermute(block, axis, [(i, i ^ mask) for i in range(count)])


def both(rows_ref):
    heads = rows_ref.shape[0] // 2
    return rows_ref.at[:heads], rows_ref.at[heads:]


def second_core():
    return lax.rem(lax.axis_index("ctx"), 2) == 1


def doc_starts(lengths_ref, block, tokens):
    row_pos = block * tokens + lax.broadcasted_iota(i32, (1, tokens), 1)
    starts = jnp.zeros((1, tokens), i32)
    end = jnp.int32(0)
    for d in range(lengths_ref.shape[0]):
        end = end + lengths_ref[d]
        starts = jnp.where(row_pos >= end, end, starts)
    return starts


def unit(pair, key_block, starts, turned_ref, e_ref, dp_ref, stats_ref, causal=False):
    heads, (width, tokens) = turned_ref.shape[0] // 2, turned_ref.shape[1:]
    factor = width ** -0.5 * math.log2(math.e)
    key_iota = lax.broadcasted_iota(i32, (tokens, 1), 0)
    allowed = key_block * tokens + key_iota >= starts
    if causal:
        allowed = allowed & (key_iota <= lax.broadcasted_iota(i32, (1, tokens), 1))
    for h in range(heads):
        lanes = slice(h * tokens, (h + 1) * tokens)
        s = jnp.where(allowed, dot(pair[:, :width], turned_ref[h]), MASKED)
        top = jnp.max(s, axis=0, keepdims=True)
        e = jnp.exp2((s - top) * factor)
        dp = dot(pair[:, width:], turned_ref[heads + h])
        e_ref[:, lanes] = e
        dp_ref[:, lanes] = dp
        stats_ref[0:1, lanes] = top
        stats_ref[1:2, lanes] = jnp.sum(e, axis=0, keepdims=True)
        stats_ref[2:3, lanes] = jnp.sum(e * dp, axis=0, keepdims=True)


def turn(rows_ref, turned_ref):
    for at in range(rows_ref.shape[0]):
        turned_ref[at] = rows_ref[at].T


def rows_of(ref, first=0):
    return [ref[first + row:first + row + 1] for row in range(3)]


def joined(parts, factor):
    top = functools.reduce(jnp.maximum, [part[0] for part in parts])
    gains = [jnp.exp2((part[0] - top) * factor) for part in parts]
    total = sum(gain * part[1] for gain, part in zip(gains, parts))
    weighted = sum(gain * part[2] for gain, part in zip(gains, parts))
    return top, total, weighted


def own_unit_body(starts_ref, rows_ref, own_ref, turned_ref, e_ref, dp_ref, stats_ref):
    turn(rows_ref, turned_ref)
    unit(own_ref, lax.axis_index("ctx"), starts_ref[0:1], turned_ref, e_ref, dp_ref, stats_ref,
         causal=True)


def four_unit_body(starts_ref, turned_ref, four_ref, e_ref, dp_ref, stats_ref):
    here = lax.axis_index("ctx")
    unit(four_ref, here - 4, starts_ref[0:1], turned_ref, e_ref, dp_ref, stats_ref)


def side_unit_body(starts_ref, other_rows, own_ref, four_ref,
                   turned_ref, e_ref, dp_ref, stats_ref):
    turn(other_rows, turned_ref)
    side = jnp.where(second_core(), four_ref[...], own_ref[...])
    block = lax.axis_index("ctx") - jnp.where(second_core(), 4, 0)
    unit(side, block, starts_ref[1:2], turned_ref, e_ref, dp_ref, stats_ref)


def prepare_body(share, middle, lengths_in, keys_ref, values_ref, queries_ref, d_out_ref,
                 split_out, starts_ref, own_ref, rows_ref, lengths_ref, split_ref, sems):
    heads, tokens, width = queries_ref.shape
    group = lax.axis_index("head") // share
    lengths = pltpu.make_async_copy(lengths_in, lengths_ref, sems.at[0])
    copies = [
        pltpu.make_async_copy(keys_ref.at[group], own_ref.at[:, :width], sems.at[1]),
        pltpu.make_async_copy(values_ref.at[group], own_ref.at[:, width:], sems.at[2]),
        pltpu.make_async_copy(queries_ref, rows_ref.at[:heads], sems.at[3]),
        pltpu.make_async_copy(d_out_ref, rows_ref.at[heads:], sems.at[4]),
    ]
    for copy in [lengths] + copies:
        copy.start()
    lengths.wait()
    end, split = jnp.int32(0), jnp.int32(0)
    for d in range(lengths_ref.shape[0]):
        end = end + lengths_ref[d]
        split = jnp.where(end == middle, 1, split)
    split_ref[0] = split
    copies.append(pltpu.make_async_copy(split_ref, split_out, sems.at[5]))
    copies[-1].start()
    here = lax.axis_index("ctx")
    starts_ref[0:1] = doc_starts(lengths_ref, here, tokens)
    starts_ref[1:2] = doc_starts(lengths_ref, jnp.bitwise_xor(here, 1), tokens)
    for copy in copies:
        copy.wait()


def near_side_unit_body(starts_ref, other_rows, own_ref, turned_ref, e_ref, dp_ref, stats_ref):
    turn(other_rows, turned_ref)
    block = jnp.where(second_core(), -1, lax.axis_index("ctx"))
    unit(own_ref, block, starts_ref[1:2], turned_ref, e_ref, dp_ref, stats_ref)


def write_rows(ref, values):
    for row, value in enumerate(values):
        ref[row:row + 1] = value


def cross_unit_body(starts_ref, turned_ref, two_ref, stats_side,
                    e_ref, dp_ref, stats_ref, others_ref):
    factor = turned_ref.shape[1] ** -0.5 * math.log2(math.e)
    unit(two_ref, lax.axis_index("ctx") - 2, starts_ref[1:2], turned_ref,
         e_ref, dp_ref, stats_ref)
    write_rows(others_ref, joined([rows_of(stats_side), rows_of(stats_ref)], factor))
    others_ref[3:4] = jnp.zeros((1, others_ref.shape[1]), f32)


def two_unit_body(starts_ref, turned_ref, two_ref, *refs):
    earlier, (e_ref, dp_ref, stats_ref, mine_ref) = refs[:-4], refs[-4:]
    factor = turned_ref.shape[1] ** -0.5 * math.log2(math.e)
    unit(two_ref, lax.axis_index("ctx") - 2, starts_ref[0:1], turned_ref,
         e_ref, dp_ref, stats_ref)
    write_rows(mine_ref, joined([rows_of(ref) for ref in earlier + (stats_ref,)], factor))
    mine_ref[3:4] = jnp.zeros((1, mine_ref.shape[1]), f32)


def coefficients(here_ref, taken_ref, stats_refs, width):
    factor = width ** -0.5 * math.log2(math.e)
    top, total, weighted = joined([rows_of(here_ref), rows_of(taken_ref)], factor)
    inverse = 1.0 / total
    return [weighted * inverse] + [
        jnp.exp2((ref[0:1] - top) * factor) * inverse for ref in stats_refs]


def slopes(e_ref, dp_ref, gain, delta, p_ref, ds_ref):
    p = e_ref[...] * gain
    p_ref[...] = p.astype(bf16)
    ds_ref[...] = (p * (dp_ref[...] - delta)).astype(bf16)


def flat(ref):
    heads, tokens, width = ref.shape
    return ref[...].reshape(heads * tokens, width)


def add_terms(sum_ref, ds_ref, p_ref, rows_ref, fresh):
    q_ref, g_ref = both(rows_ref)
    width = q_ref.shape[-1]
    dk = dot(ds_ref[...], flat(q_ref)) * width ** -0.5
    dv = dot(p_ref[...], flat(g_ref))
    if fresh:
        sum_ref[:, :width] = dk
        sum_ref[:, width:] = dv
    else:
        sum_ref[:, :width] += dk
        sum_ref[:, width:] += dv


def my_terms_body(count, mine_ref, taken_ref, *refs):
    stats, refs = refs[:count], refs[count:]
    parts, rows_ref, refs = refs[:4], refs[4], refs[5:]
    coef_ref, ds_refs, sums, p_ref = refs[0], refs[1:3], refs[3:5], refs[5]
    coefs = coefficients(mine_ref, taken_ref, stats, rows_ref.shape[-1])
    write_rows(coef_ref, coefs)
    for at in range(2):
        slopes(parts[2 * at], parts[2 * at + 1], coefs[count - 1 + at], coefs[0], p_ref.at[at],
               ds_refs[at])
        add_terms(sums[at], ds_refs[at], p_ref.at[at], rows_ref, True)


def four_terms_body(others_ref, taken_ref, stats_side, stats_cross, e_side, dp_side,
                    other_rows, part_ref, coef_ref, terms_ref, sum_ref, p_ref, ds_ref):
    coefs = coefficients(others_ref, taken_ref, (stats_side, stats_cross), other_rows.shape[-1])
    write_rows(coef_ref, coefs)
    sum_ref[...] = part_ref[...]

    @pl.when(second_core())
    def _():
        slopes(e_side, dp_side, coef_ref[1:2], coef_ref[0:1], p_ref, ds_ref)
        add_terms(sum_ref, ds_ref, p_ref, other_rows, False)

    terms_ref[...] = sum_ref[...].astype(bf16)


def two_terms_body(coef_ref, e_cross, dp_cross, other_rows, part_ref,
                   terms_ref, ds_cross, p_ref, sum_ref):
    slopes(e_cross, dp_cross, coef_ref[2:3], coef_ref[0:1], p_ref, ds_cross)
    sum_ref[...] = part_ref[...]
    add_terms(sum_ref, ds_cross, p_ref, other_rows, False)
    terms_ref[...] = sum_ref[...].astype(bf16)


def slice_rows(ref, other):
    count = lax.axis_size("head")
    each = ref.shape[0] // count
    parity = jnp.bitwise_xor(lax.rem(lax.axis_index("head"), 2), other)
    return [ref[pl.ds(pl.multiple_of((2 * at + parity) * each, each), each)]
            for at in range(count // 2)]


def halve(sum_ref, kept_ref, given_ref):
    each = sum_ref.shape[0] // lax.axis_size("head")
    for other, out_ref in enumerate((kept_ref, given_ref)):
        for at, value in enumerate(slice_rows(sum_ref, other)):
            out_ref[at * each:(at + 1) * each] = value.astype(out_ref.dtype)


def halved_two_terms_body(others_ref, taken_ref, stats_side, stats_cross, e_cross, dp_cross,
                        other_rows, part_ref,
                        coef_ref, kept_ref, other_ref, ds_cross, p_ref, sum_ref):
    coefs = coefficients(others_ref, taken_ref, (stats_side, stats_cross), other_rows.shape[-1])
    write_rows(coef_ref, coefs)
    slopes(e_cross, dp_cross, coefs[2], coefs[0], p_ref, ds_cross)
    sum_ref[...] = part_ref[...]
    add_terms(sum_ref, ds_cross, p_ref, other_rows, False)
    halve(sum_ref, kept_ref, other_ref)


def near_own_terms_body(coef_ref, e_side, dp_side, other_rows, part_ref,
                        kept_ref, other_ref, ds_side, p_ref, sum_ref):
    slopes(e_side, dp_side, coef_ref[1:2], coef_ref[0:1], p_ref, ds_side)
    sum_ref[...] = part_ref[...]

    @pl.when(jnp.logical_not(second_core()))
    def _():
        add_terms(sum_ref, ds_side, p_ref, other_rows, False)

    halve(sum_ref, kept_ref, other_ref)


def far_four_terms_body(coef_ref, e_side, dp_side, other_rows, part_ref,
                        kept_ref, other_ref, sum_ref, p_ref, ds_ref):
    sum_ref[...] = part_ref[...]

    @pl.when(second_core())
    def _():
        slopes(e_side, dp_side, coef_ref[1:2], coef_ref[0:1], p_ref, ds_ref)
        add_terms(sum_ref, ds_ref, p_ref, other_rows, False)

    halve(sum_ref, kept_ref, other_ref)


def far_own_terms_body(mine_coef, coef_ref, e_own, dp_own, e_side, dp_side, rows_ref,
                       other_rows,
                       kept_ref, other_ref, ds_own, ds_side, p_ref, p_side, sum_ref):
    slopes(e_own, dp_own, mine_coef[1:2], mine_coef[0:1], p_ref, ds_own)
    add_terms(sum_ref, ds_own, p_ref, rows_ref, True)
    slopes(e_side, dp_side, coef_ref[1:2], coef_ref[0:1], p_side, ds_side)

    @pl.when(jnp.logical_not(second_core()))
    def _():
        add_terms(sum_ref, ds_side, p_side, other_rows, False)

    halve(sum_ref, kept_ref, other_ref)


def grads_body(own_ref, two_ref, ds_own, ds_two, ds_side, ds_cross, *refs):
    four_refs, (dq_ref, other_dq_ref) = refs[:-2], refs[-2:]
    width = dq_ref.shape[-1]
    keys, slope_refs = [own_ref[:, :width], two_ref[:, :width]], [ds_own, ds_two]
    side = keys[0]
    if four_refs:
        keys.append(four_refs[0][:, :width])
        slope_refs.append(four_refs[1])
        side = jnp.where(second_core(), keys[2], side)
    query_grads([side, keys[1]], [ds_side, ds_cross], other_dq_ref)
    query_grads(keys, slope_refs, dq_ref)


def add_others_body(use, sum_ref, pair_ref, four_ref, out_ref):
    taken = jnp.where(use(lax.axis_index("ctx")), four_ref[...].astype(f32), 0.0)
    out_ref[...] = sum_ref[...] + pair_ref[...].astype(f32) + taken


def relay_body(kept_ref, four_ref, two_ref, two_pair_ref, out_ref, sent_ref):
    ctx = lax.axis_index("ctx")
    taken = two_ref[...].astype(f32) + two_pair_ref[...].astype(f32)
    out_ref[...] = kept_ref[...] + jnp.where(ctx & 2 == 0, taken, 0.0)
    sent_ref[...] = (four_ref[...] + jnp.where(ctx & 6 == 6, taken, 0.0)).astype(bf16)


def near_first_sum_body(kept_ref, two_ref, two_pair_ref, out_ref):
    taken = two_ref[...].astype(f32) + two_pair_ref[...].astype(f32)
    out_ref[...] = kept_ref[...] + jnp.where(lax.axis_index("ctx") & 2 == 0, taken, 0.0)


def halves_sum_body(share, use, kept_ref, back_ref, here_ref, there_ref):
    each = here_ref.shape[0]
    group = lax.axis_index("head") // share
    for out_ref, at in ((here_ref, group), (there_ref, 1 - group)):
        rows = pl.ds(pl.multiple_of(at * each, each), each)
        taken = back_ref[rows].astype(f32)
        if use is not None:
            taken = jnp.where(use(lax.axis_index("ctx")), taken, 0.0)
        out_ref[...] = (kept_ref[rows] + taken).astype(out_ref.dtype)


def last_body(share, here_ref, taken_ref, dk_ref, dv_ref):
    width = dk_ref.shape[-1]
    group = lax.axis_index("head") // share
    for ref, place in ((here_ref, group), (taken_ref, 1 - group)):
        dk_ref[place] = ref[:, :width]
        dv_ref[place] = ref[:, width:]


def query_grads(keys, ds_refs, out_ref):
    heads, tokens, width = out_ref.shape
    turned = [key.T for key in keys]
    for h in range(heads):
        lanes = slice(h * tokens, (h + 1) * tokens)
        dqt = sum(dot(kt, ds[:, lanes]) for kt, ds in zip(turned, ds_refs))
        out_ref[h] = (dqt.T * width ** -0.5).astype(out_ref.dtype)


def own_terms_body(mine_coef, coef_ref, e_own, dp_own, e_side, dp_side, rows_ref,
                   other_rows, own_ref, two_ref, ds_two, ds_cross, four_ref, ds_four,
                   terms_ref, dq_ref, other_dq_ref, ds_own, ds_side, p_ref, p_side):
    width = dq_ref.shape[-1]
    own, two, four = [ref[:, :width] for ref in (own_ref, two_ref, four_ref)]
    slopes(e_side, dp_side, coef_ref[1:2], coef_ref[0:1], p_side, ds_side)
    query_grads([jnp.where(second_core(), four, own), two], [ds_side, ds_cross], other_dq_ref)
    slopes(e_own, dp_own, mine_coef[1:2], mine_coef[0:1], p_ref, ds_own)
    add_terms(terms_ref, ds_own, p_ref, rows_ref, True)

    @pl.when(jnp.logical_not(second_core()))
    def _():
        add_terms(terms_ref, ds_side, p_side, other_rows, False)

    query_grads([own, two, four], [ds_own, ds_two, ds_four], dq_ref)


def add_grads_body(mine_ref, taken_ref, dq_ref):
    dq_ref[...] = (mine_ref[...] + taken_ref[...].astype(f32)).astype(dq_ref.dtype)


def sums_body(own_terms, four_back, two_back, out_ref):
    taken = four_back[...].astype(f32) + two_back[...].astype(f32)
    out_ref[...] = (own_terms[...] + taken).astype(bf16)


def per_device(queries, keys, values, d_out, doc_lengths):
    ctx_count, (heads, tokens, width) = lax.axis_size("ctx"), queries.shape
    middle = ctx_count // 2 * tokens
    split, starts, own, rows = pl.pallas_call(
        functools.partial(prepare_body, GROUP // heads, middle),
        out_shape=(shape((1,), i32), shape((2, tokens), i32), shape((tokens, 2 * width), bf16),
                   shape((2 * heads, tokens, width), bf16)),
        in_specs=[pl.BlockSpec(memory_space=pl.ANY)] * 5,
        out_specs=(pl.BlockSpec(memory_space=pl.ANY), VMEM, VMEM, VMEM),
        scratch_shapes=[pltpu.SMEM(doc_lengths.shape, i32), pltpu.SMEM((1,), i32),
                        pltpu.SemaphoreType.DMA((6,))],
        name="prepare",
    )(*[pltpu.with_memory_space_constraint(value, pltpu.HBM)
        for value in (doc_lengths, keys, values, queries, d_out)])
    operands = (rows, own, starts)
    if ctx_count != 2 * REACH or lax.axis_size("head") * heads != 2 * GROUP or 2 * heads != GROUP:
        return gradients(True, *operands)
    return lax.switch(split[0], [functools.partial(gradients, True),
                                 functools.partial(gradients, False)], *operands)


def gradients(far, row_data, own, starts):
    heads, (tokens, width) = row_data.shape[0] // 2, row_data.shape[1:]
    head_count = lax.axis_size("head")
    share = GROUP // heads
    groups = head_count // share
    rows = heads * tokens
    ctx = lax.axis_index("ctx")
    mutual = lax.axis_size("ctx") == 2 * REACH and share == groups == 2
    pair = (tokens, 2 * width)
    all_rows = (heads, tokens, width)
    stats = shape((3, rows), f32)
    wide = shape((tokens, rows), f32)
    half = shape((tokens, rows), bf16)
    half_scratch = pltpu.VMEM((tokens, rows), bf16)
    halves_scratch = pltpu.VMEM((2, tokens, rows), bf16)
    pair_scratch = pltpu.VMEM(pair, f32)

    if far:
        four = exchanged(own, "ctx", 4) if mutual else shifted(own, 4)
    flipped = shape((2 * heads, width, tokens), bf16)
    turned, e_own, dp_own, stats_own = call(
        own_unit_body, "own_unit", [VMEM] * 3, (flipped, wide, wide, stats),
    )(starts, row_data, own)
    sent = own
    if far:
        sent, stats_own = lax.optimization_barrier((own, stats_own))
    two = [exchanged(sent, "ctx", 2) if mutual else shifted(sent, 2)]
    if far and mutual:
        two.append(exchanged(sent, "ctx", 6))
    other_rows = exchanged(row_data, "ctx", 1)
    if far:
        four, stats_own = lax.optimization_barrier((four, stats_own))
        e_four, dp_four, stats_four = call(
            four_unit_body, "four_unit", [VMEM] * 3, (wide, wide, stats))(starts, turned, four)
        other_rows, stats_four = lax.optimization_barrier((other_rows, stats_four))
        other_turned, e_side, dp_side, stats_side = call(
            side_unit_body, "side_unit", [VMEM] * 4, (flipped, wide, wide, stats),
        )(starts, other_rows, own, four)
    else:
        other_turned, e_side, dp_side, stats_side = call(
            near_side_unit_body, "side_unit", [VMEM] * 3, (flipped, wide, wide, stats),
        )(starts, other_rows, own)
    *two, stats_side, stats_own = lax.optimization_barrier((*two, stats_side, stats_own))
    mine_stats = (stats_own, stats_four) if far else (stats_own,)
    two = jnp.where(ctx & 2 == 2, *two) if len(two) == 2 else two[0]
    few = shape((4, rows), f32)
    e_cross, dp_cross, stats_cross, others = call(
        cross_unit_body, "cross_unit", [VMEM] * 4, (wide, wide, stats, few),
    )(starts, other_turned, two, stats_side)
    taken_others = exchanged(others, "ctx", 1)
    e_two, dp_two, stats_two, mine = call(
        two_unit_body, "two_unit", [VMEM] * (3 + len(mine_stats)), (wide, wide, stats, few),
    )(starts, turned, two, *mine_stats)
    taken_mine = exchanged(mine, "ctx", 1)
    mine_stats += (stats_two,)
    parts = ((e_four, dp_four) if far else (e_own, dp_own)) + (e_two, dp_two)
    mine_coef, ds_first, ds_two, first_part, two_part = call(
        functools.partial(my_terms_body, len(mine_stats)), "my_terms",
        [VMEM] * (7 + len(mine_stats)),
        (few, half, half, shape(pair, f32), shape(pair, f32)), (halves_scratch,),
    )(mine, taken_others, *mine_stats, *parts, row_data)
    last_stats = (others, taken_mine, stats_side, stats_cross)
    slices = (tokens // 2, 2 * width)
    slice_dims = (tokens // head_count, 2 * width)
    if not mutual:
        coef, four_terms = call(
            four_terms_body, "four_terms", [VMEM] * 8, (few, shape(pair, bf16)),
            (pair_scratch, half_scratch, half_scratch),
        )(*last_stats, e_side, dp_side, other_rows, first_part)
        two_terms, ds_cross = call(
            two_terms_body, "two_terms", [VMEM] * 5, (shape(pair, bf16), half),
            (half_scratch, pair_scratch),
        )(coef, e_cross, dp_cross, other_rows, two_part)
        backs = [shifted(four_terms, -4), shifted(two_terms, -2)]
        own_terms, my_grads, other_grads = call(
            own_terms_body, "own_terms", [VMEM] * 14,
            (shape(pair, f32), shape(all_rows, f32), shape(all_rows, bf16)),
            (half_scratch,) * 4,
        )(mine_coef, coef, e_own, dp_own, e_side, dp_side, row_data, other_rows, own, two,
          ds_two, ds_cross, four, ds_first)
        taken_grads = exchanged(other_grads, "ctx", 1)
        d_queries, = call(
            add_grads_body, "add_grads", [VMEM] * 2, (shape(all_rows, bf16),),
        )(my_grads, taken_grads)
        sums, = call(sums_body, "sums", [VMEM] * 3, (shape(pair, bf16),))(own_terms, *backs)
        pieces = lax.all_to_all(sums.reshape(head_count, *slice_dims), "head", 0, 0)
        result = jnp.sum(
            pieces.reshape(groups, share, *slice_dims).astype(f32), axis=1).astype(bf16)
        return d_queries, result[..., :width], result[..., width:]

    halves = (shape(slices, bf16), shape(slices, bf16))
    part = shape(slices, f32)
    coef, two_kept, two_other, ds_cross = call(
        halved_two_terms_body, "two_terms", [VMEM] * 8, (few,) + halves + (half,),
        (half_scratch, pair_scratch),
    )(*last_stats, e_cross, dp_cross, other_rows, two_part)
    two_back = exchanged(two_kept, "ctx", 2)
    two_pair = exchanged(two_other, ("ctx", "head"), 2 * head_count + 1)
    if far:
        four_kept, four_other = call(
            far_four_terms_body, "four_terms", [VMEM] * 5, (part, halves[1]),
            (pair_scratch, half_scratch, half_scratch),
        )(coef, e_side, dp_side, other_rows, first_part)
        four_pair = exchanged(four_other, ("ctx", "head"), 4 * head_count + 1)
        own_kept, own_other, ds_own, ds_side = call(
            far_own_terms_body, "own_terms", [VMEM] * 8, (part, halves[1], half, half),
            (half_scratch, half_scratch, pair_scratch),
        )(mine_coef, coef, e_own, dp_own, e_side, dp_side, row_data, other_rows)
    else:
        ds_own = ds_first
        own_kept, own_other, ds_side = call(
            near_own_terms_body, "own_terms", [VMEM] * 5, (part, halves[1], half),
            (half_scratch, pair_scratch),
        )(coef, e_side, dp_side, other_rows, first_part)
    own_pair = exchanged(own_other, "head", 1)
    four_refs = (four, ds_first) if far else ()
    my_grads, other_grads = call(
        grads_body, "query_grads", [VMEM] * (6 + len(four_refs)),
        (shape(all_rows, f32), shape(all_rows, bf16)),
    )(own, two, ds_own, ds_two, ds_side, ds_cross, *four_refs)
    owns_four = lambda i: i < 4
    if far:
        own_kept, relayed = call(
            relay_body, "relay", [VMEM] * 4, (part, halves[0]),
        )(own_kept, four_kept, two_back, two_pair)
        four_back = exchanged(relayed, "ctx", 4)
        own_kept, = call(functools.partial(add_others_body, owns_four), "add_others", [VMEM] * 3,
                         (part,))(own_kept, own_pair, four_pair)
        final, use = four_back, owns_four
    else:
        own_kept, = call(
            near_first_sum_body, "first_sum", [VMEM] * 3, (part,),
        )(own_kept, two_back, two_pair)
        final, use = own_pair, None
    kept, sent = call(
        functools.partial(halves_sum_body, share, use), "sums", [VMEM] * 2,
        (shape(slice_dims, bf16),) * 2)(own_kept, final)
    other_grads, kept = lax.optimization_barrier((other_grads, kept))
    taken_grads = exchanged(other_grads, "ctx", 1)
    d_queries, = call(
        add_grads_body, "add_grads", [VMEM] * 2, (shape(all_rows, bf16),),
    )(my_grads, taken_grads)
    last = exchanged(sent, "head", share)
    last, d_queries = lax.optimization_barrier((last, d_queries))
    d_keys, d_values = call(
        functools.partial(last_body, share), "last", [VMEM] * 2,
        (shape((groups, tokens // head_count, width), bf16),) * 2)(kept, last)
    return d_queries, d_keys, d_values


def solution(mesh):
    placed = (
        P("head", "ctx", None),
        P(None, "ctx", None),
        P(None, "ctx", None),
        P("head", "ctx", None),
        P(),
    )
    return jax.shard_map(
        per_device,
        mesh=mesh,
        in_specs=placed,
        out_specs=(
            P("head", "ctx", None),
            P(None, ("ctx", "head"), None),
            P(None, ("ctx", "head"), None),
        ),
        check_vma=False,
    )
```

```python
import functools
import math

import jax
import jax.numpy as jnp
from jax import lax
from jax.experimental import pallas as pl
from jax.experimental.pallas import tpu as pltpu
from jax.sharding import PartitionSpec as P

GROUP = 8
REACH = 4
MASKED = -1e30
NT = (((1,), (1,)), ((), ()))
NN = (((1,), (0,)), ((), ()))
VMEM = pl.BlockSpec(memory_space=pltpu.VMEM)
SMEM = pl.BlockSpec(memory_space=pltpu.SMEM)
bf16, f32, i32 = jnp.bfloat16, jnp.float32, jnp.int32


def dot(a, b, dims=NN):
    return lax.dot_general(a, b, dims, preferred_element_type=f32)


def shape(dims, dtype):
    return jax.ShapeDtypeStruct(dims, dtype)


def call(body, name, in_specs, outs, scratch=()):
    return pl.pallas_call(
        body,
        out_shape=outs,
        in_specs=in_specs,
        out_specs=(VMEM,) * len(outs),
        scratch_shapes=scratch,
        compiler_params=pltpu.CompilerParams(vmem_limit_bytes=20 * 2**20),
        cost_estimate=pl.CostEstimate(flops=2**20, bytes_accessed=2**10, transcendentals=0),
        name=name,
    )


def shifted(block, distance):
    count = lax.axis_size("ctx")
    route = [(i - distance, i) for i in range(count) if 0 <= i - distance < count]
    return lax.ppermute(block, "ctx", route)


def exchanged(block, axis, mask):
    count = math.prod(lax.axis_size(name) for name in axis) if isinstance(axis, tuple) else (
        lax.axis_size(axis))
    return lax.ppermute(block, axis, [(i, i ^ mask) for i in range(count)])


def both(rows_ref):
    heads = rows_ref.shape[0] // 2
    return rows_ref.at[:heads], rows_ref.at[heads:]


def second_core():
    return lax.rem(lax.axis_index("ctx"), 2) == 1


def doc_starts(lengths_ref, block, tokens):
    row_pos = block * tokens + lax.broadcasted_iota(i32, (1, tokens), 1)
    starts = jnp.zeros((1, tokens), i32)
    end = jnp.int32(0)
    for d in range(lengths_ref.shape[0]):
        end = end + lengths_ref[d]
        starts = jnp.where(row_pos >= end, end, starts)
    return starts


def unit(pair, key_block, starts, rows_ref, e_ref, dp_ref, stats_ref, causal=False):
    q_ref, g_ref = both(rows_ref)
    heads, tokens, width = q_ref.shape
    factor = width ** -0.5 * math.log2(math.e)
    key_iota = lax.broadcasted_iota(i32, (tokens, 1), 0)
    allowed = key_block * tokens + key_iota >= starts
    if causal:
        allowed = allowed & (key_iota <= lax.broadcasted_iota(i32, (1, tokens), 1))
    for h in range(heads):
        lanes = slice(h * tokens, (h + 1) * tokens)
        s = jnp.where(allowed, dot(pair[:, :width], q_ref[h], NT), MASKED)
        top = jnp.max(s, axis=0, keepdims=True)
        e = jnp.exp2((s - top) * factor)
        dp = dot(pair[:, width:], g_ref[h], NT)
        e_ref[:, lanes] = e
        dp_ref[:, lanes] = dp
        stats_ref[0:1, lanes] = top
        stats_ref[1:2, lanes] = jnp.sum(e, axis=0, keepdims=True)
        stats_ref[2:3, lanes] = jnp.sum(e * dp, axis=0, keepdims=True)


def rows_of(ref, first=0):
    return [ref[first + row:first + row + 1] for row in range(3)]


def joined(parts, factor):
    top = functools.reduce(jnp.maximum, [part[0] for part in parts])
    gains = [jnp.exp2((part[0] - top) * factor) for part in parts]
    total = sum(gain * part[1] for gain, part in zip(gains, parts))
    weighted = sum(gain * part[2] for gain, part in zip(gains, parts))
    return top, total, weighted


def own_unit_body(starts_ref, rows_ref, own_ref, e_ref, dp_ref, stats_ref):
    unit(own_ref, lax.axis_index("ctx"), starts_ref[0:1], rows_ref, e_ref, dp_ref, stats_ref,
         causal=True)


def four_unit_body(starts_ref, rows_ref, four_ref, e_ref, dp_ref, stats_ref):
    here = lax.axis_index("ctx")
    unit(four_ref, here - 4, starts_ref[0:1], rows_ref, e_ref, dp_ref, stats_ref)


def side_unit_body(starts_ref, other_rows, own_ref, four_ref, e_ref, dp_ref, stats_ref):
    side = jnp.where(second_core(), four_ref[...], own_ref[...])
    block = lax.axis_index("ctx") - jnp.where(second_core(), 4, 0)
    unit(side, block, starts_ref[1:2], other_rows, e_ref, dp_ref, stats_ref)


def prepare_body(share, middle, lengths_in, keys_ref, values_ref, queries_ref, d_out_ref,
                 split_out, starts_ref, own_ref, rows_ref, lengths_ref, split_ref, sems):
    heads, tokens, width = queries_ref.shape
    group = lax.axis_index("head") // share
    lengths = pltpu.make_async_copy(lengths_in, lengths_ref, sems.at[0])
    copies = [
        pltpu.make_async_copy(keys_ref.at[group], own_ref.at[:, :width], sems.at[1]),
        pltpu.make_async_copy(values_ref.at[group], own_ref.at[:, width:], sems.at[2]),
        pltpu.make_async_copy(queries_ref, rows_ref.at[:heads], sems.at[3]),
        pltpu.make_async_copy(d_out_ref, rows_ref.at[heads:], sems.at[4]),
    ]
    lengths.start()
    for copy in copies[:2]:
        copy.start()
    lengths.wait()
    end, split = jnp.int32(0), jnp.int32(0)
    for d in range(lengths_ref.shape[0]):
        end = end + lengths_ref[d]
        split = jnp.where(end == middle, 1, split)
    split_ref[0] = split
    copies.append(pltpu.make_async_copy(split_ref, split_out, sems.at[5]))
    for copy in copies[:1:-1]:
        copy.start()
    here = lax.axis_index("ctx")
    starts_ref[0:1] = doc_starts(lengths_ref, here, tokens)
    starts_ref[1:2] = doc_starts(lengths_ref, jnp.bitwise_xor(here, 1), tokens)
    for copy in copies:
        copy.wait()


def near_side_unit_body(starts_ref, other_rows, own_ref, e_ref, dp_ref, stats_ref):
    block = jnp.where(second_core(), -1, lax.axis_index("ctx"))
    unit(own_ref, block, starts_ref[1:2], other_rows, e_ref, dp_ref, stats_ref)


def write_rows(ref, values):
    for row, value in enumerate(values):
        ref[row:row + 1] = value


def cross_unit_body(starts_ref, other_rows, two_ref, stats_side,
                    e_ref, dp_ref, stats_ref, others_ref):
    factor = other_rows.shape[-1] ** -0.5 * math.log2(math.e)
    unit(two_ref, lax.axis_index("ctx") - 2, starts_ref[1:2], other_rows,
         e_ref, dp_ref, stats_ref)
    write_rows(others_ref, joined([rows_of(stats_side), rows_of(stats_ref)], factor))
    others_ref[3:4] = jnp.zeros((1, others_ref.shape[1]), f32)


def two_unit_body(starts_ref, rows_ref, two_ref, *refs):
    earlier, (e_ref, dp_ref, stats_ref, mine_ref) = refs[:-4], refs[-4:]
    factor = rows_ref.shape[-1] ** -0.5 * math.log2(math.e)
    unit(two_ref, lax.axis_index("ctx") - 2, starts_ref[0:1], rows_ref,
         e_ref, dp_ref, stats_ref)
    write_rows(mine_ref, joined([rows_of(ref) for ref in earlier + (stats_ref,)], factor))
    mine_ref[3:4] = jnp.zeros((1, mine_ref.shape[1]), f32)


def coefficients(here_ref, taken_ref, stats_refs, width):
    factor = width ** -0.5 * math.log2(math.e)
    top, total, weighted = joined([rows_of(here_ref), rows_of(taken_ref)], factor)
    inverse = 1.0 / total
    return [weighted * inverse] + [
        jnp.exp2((ref[0:1] - top) * factor) * inverse for ref in stats_refs]


def slopes(e_ref, dp_ref, gain, delta, p_ref, ds_ref):
    p = e_ref[...] * gain
    p_ref[...] = p.astype(bf16)
    ds_ref[...] = (p * (dp_ref[...] - delta)).astype(bf16)


def flat(ref):
    heads, tokens, width = ref.shape
    return ref[...].reshape(heads * tokens, width)


def add_terms(sum_ref, ds_ref, p_ref, rows_ref, fresh):
    q_ref, g_ref = both(rows_ref)
    width = q_ref.shape[-1]
    dk = dot(ds_ref[...], flat(q_ref)) * width ** -0.5
    dv = dot(p_ref[...], flat(g_ref))
    if fresh:
        sum_ref[:, :width] = dk
        sum_ref[:, width:] = dv
    else:
        sum_ref[:, :width] += dk
        sum_ref[:, width:] += dv


def my_terms_body(count, mine_ref, taken_ref, *refs):
    stats, refs = refs[:count], refs[count:]
    parts, rows_ref, refs = refs[:4], refs[4], refs[5:]
    coef_ref, ds_refs, sums, p_ref = refs[0], refs[1:3], refs[3:5], refs[5]
    coefs = coefficients(mine_ref, taken_ref, stats, rows_ref.shape[-1])
    write_rows(coef_ref, coefs)
    for at in range(2):
        slopes(parts[2 * at], parts[2 * at + 1], coefs[count - 1 + at], coefs[0], p_ref.at[at],
               ds_refs[at])
        add_terms(sums[at], ds_refs[at], p_ref.at[at], rows_ref, True)


def four_terms_body(others_ref, taken_ref, stats_side, stats_cross, e_side, dp_side,
                    other_rows, part_ref, coef_ref, terms_ref, sum_ref, p_ref, ds_ref):
    coefs = coefficients(others_ref, taken_ref, (stats_side, stats_cross), other_rows.shape[-1])
    write_rows(coef_ref, coefs)
    sum_ref[...] = part_ref[...]

    @pl.when(second_core())
    def _():
        slopes(e_side, dp_side, coef_ref[1:2], coef_ref[0:1], p_ref, ds_ref)
        add_terms(sum_ref, ds_ref, p_ref, other_rows, False)

    terms_ref[...] = sum_ref[...].astype(bf16)


def two_terms_body(coef_ref, e_cross, dp_cross, other_rows, part_ref,
                   terms_ref, ds_cross, p_ref, sum_ref):
    slopes(e_cross, dp_cross, coef_ref[2:3], coef_ref[0:1], p_ref, ds_cross)
    sum_ref[...] = part_ref[...]
    add_terms(sum_ref, ds_cross, p_ref, other_rows, False)
    terms_ref[...] = sum_ref[...].astype(bf16)


def slice_rows(ref, other):
    count = lax.axis_size("head")
    each = ref.shape[0] // count
    parity = jnp.bitwise_xor(lax.rem(lax.axis_index("head"), 2), other)
    return [ref[pl.ds(pl.multiple_of((2 * at + parity) * each, each), each)]
            for at in range(count // 2)]


def halve(sum_ref, kept_ref, given_ref):
    each = sum_ref.shape[0] // lax.axis_size("head")
    for other, out_ref in enumerate((kept_ref, given_ref)):
        for at, value in enumerate(slice_rows(sum_ref, other)):
            out_ref[at * each:(at + 1) * each] = value.astype(out_ref.dtype)


def halved_two_terms_body(others_ref, taken_ref, stats_side, stats_cross, e_cross, dp_cross,
                        other_rows, part_ref,
                        coef_ref, kept_ref, other_ref, ds_cross, p_ref, sum_ref):
    coefs = coefficients(others_ref, taken_ref, (stats_side, stats_cross), other_rows.shape[-1])
    write_rows(coef_ref, coefs)
    slopes(e_cross, dp_cross, coefs[2], coefs[0], p_ref, ds_cross)
    sum_ref[...] = part_ref[...]
    add_terms(sum_ref, ds_cross, p_ref, other_rows, False)
    halve(sum_ref, kept_ref, other_ref)


def near_own_terms_body(coef_ref, e_side, dp_side, other_rows, part_ref,
                        kept_ref, other_ref, ds_side, p_ref, sum_ref):
    slopes(e_side, dp_side, coef_ref[1:2], coef_ref[0:1], p_ref, ds_side)
    sum_ref[...] = part_ref[...]

    @pl.when(jnp.logical_not(second_core()))
    def _():
        add_terms(sum_ref, ds_side, p_ref, other_rows, False)

    halve(sum_ref, kept_ref, other_ref)


def far_four_terms_body(coef_ref, e_side, dp_side, other_rows, part_ref,
                        kept_ref, other_ref, sum_ref, p_ref, ds_ref):
    sum_ref[...] = part_ref[...]

    @pl.when(second_core())
    def _():
        slopes(e_side, dp_side, coef_ref[1:2], coef_ref[0:1], p_ref, ds_ref)
        add_terms(sum_ref, ds_ref, p_ref, other_rows, False)

    halve(sum_ref, kept_ref, other_ref)


def far_own_terms_body(mine_coef, coef_ref, e_own, dp_own, e_side, dp_side, rows_ref,
                       other_rows,
                       kept_ref, other_ref, ds_own, ds_side, p_ref, p_side, sum_ref):
    slopes(e_own, dp_own, mine_coef[1:2], mine_coef[0:1], p_ref, ds_own)
    add_terms(sum_ref, ds_own, p_ref, rows_ref, True)
    slopes(e_side, dp_side, coef_ref[1:2], coef_ref[0:1], p_side, ds_side)

    @pl.when(jnp.logical_not(second_core()))
    def _():
        add_terms(sum_ref, ds_side, p_side, other_rows, False)

    halve(sum_ref, kept_ref, other_ref)


def grads_body(own_ref, two_ref, ds_own, ds_two, ds_side, ds_cross, *refs):
    four_refs, (dq_ref, other_dq_ref) = refs[:-2], refs[-2:]
    width = dq_ref.shape[-1]
    keys, slope_refs = [own_ref[:, :width], two_ref[:, :width]], [ds_own, ds_two]
    side = keys[0]
    if four_refs:
        keys.append(four_refs[0][:, :width])
        slope_refs.append(four_refs[1])
        side = jnp.where(second_core(), keys[2], side)
    query_grads([side, keys[1]], [ds_side, ds_cross], other_dq_ref)
    query_grads(keys, slope_refs, dq_ref)


def add_others_body(use, sum_ref, pair_ref, four_ref, out_ref):
    taken = jnp.where(use(lax.axis_index("ctx")), four_ref[...].astype(f32), 0.0)
    out_ref[...] = sum_ref[...] + pair_ref[...].astype(f32) + taken


def relay_body(kept_ref, four_ref, two_ref, two_pair_ref, out_ref, sent_ref):
    ctx = lax.axis_index("ctx")
    taken = two_ref[...].astype(f32) + two_pair_ref[...].astype(f32)
    out_ref[...] = kept_ref[...] + jnp.where(ctx & 2 == 0, taken, 0.0)
    sent_ref[...] = (four_ref[...] + jnp.where(ctx & 6 == 6, taken, 0.0)).astype(bf16)


def near_first_sum_body(kept_ref, two_ref, two_pair_ref, out_ref):
    taken = two_ref[...].astype(f32) + two_pair_ref[...].astype(f32)
    out_ref[...] = kept_ref[...] + jnp.where(lax.axis_index("ctx") & 2 == 0, taken, 0.0)


def halves_sum_body(share, use, kept_ref, back_ref, here_ref, there_ref):
    each = here_ref.shape[0]
    group = lax.axis_index("head") // share
    for out_ref, at in ((here_ref, group), (there_ref, 1 - group)):
        rows = pl.ds(pl.multiple_of(at * each, each), each)
        taken = back_ref[rows].astype(f32)
        if use is not None:
            taken = jnp.where(use(lax.axis_index("ctx")), taken, 0.0)
        out_ref[...] = (kept_ref[rows] + taken).astype(out_ref.dtype)


def last_body(share, here_ref, taken_ref, dk_ref, dv_ref):
    width = dk_ref.shape[-1]
    group = lax.axis_index("head") // share
    for ref, place in ((here_ref, group), (taken_ref, 1 - group)):
        dk_ref[place] = ref[:, :width]
        dv_ref[place] = ref[:, width:]


def query_grads(keys, ds_refs, out_ref):
    heads, tokens, width = out_ref.shape
    turned = [key.T for key in keys]
    for h in range(heads):
        lanes = slice(h * tokens, (h + 1) * tokens)
        dqt = sum(dot(kt, ds[:, lanes]) for kt, ds in zip(turned, ds_refs))
        out_ref[h] = (dqt.T * width ** -0.5).astype(out_ref.dtype)


def own_terms_body(mine_coef, coef_ref, e_own, dp_own, e_side, dp_side, rows_ref,
                   other_rows, own_ref, two_ref, ds_two, ds_cross, four_ref, ds_four,
                   terms_ref, dq_ref, other_dq_ref, ds_own, ds_side, p_ref, p_side):
    width = dq_ref.shape[-1]
    own, two, four = [ref[:, :width] for ref in (own_ref, two_ref, four_ref)]
    slopes(e_side, dp_side, coef_ref[1:2], coef_ref[0:1], p_side, ds_side)
    query_grads([jnp.where(second_core(), four, own), two], [ds_side, ds_cross], other_dq_ref)
    slopes(e_own, dp_own, mine_coef[1:2], mine_coef[0:1], p_ref, ds_own)
    add_terms(terms_ref, ds_own, p_ref, rows_ref, True)

    @pl.when(jnp.logical_not(second_core()))
    def _():
        add_terms(terms_ref, ds_side, p_side, other_rows, False)

    query_grads([own, two, four], [ds_own, ds_two, ds_four], dq_ref)


def add_grads_body(mine_ref, taken_ref, dq_ref):
    dq_ref[...] = (mine_ref[...] + taken_ref[...].astype(f32)).astype(dq_ref.dtype)


def sums_body(own_terms, four_back, two_back, out_ref):
    taken = four_back[...].astype(f32) + two_back[...].astype(f32)
    out_ref[...] = (own_terms[...] + taken).astype(bf16)


def per_device(queries, keys, values, d_out, doc_lengths):
    ctx_count, (heads, tokens, width) = lax.axis_size("ctx"), queries.shape
    middle = ctx_count // 2 * tokens
    split, starts, own, rows = pl.pallas_call(
        functools.partial(prepare_body, GROUP // heads, middle),
        out_shape=(shape((1,), i32), shape((2, tokens), i32), shape((tokens, 2 * width), bf16),
                   shape((2 * heads, tokens, width), bf16)),
        in_specs=[pl.BlockSpec(memory_space=pl.ANY)] * 5,
        out_specs=(pl.BlockSpec(memory_space=pl.ANY), VMEM, VMEM, VMEM),
        scratch_shapes=[pltpu.SMEM(doc_lengths.shape, i32), pltpu.SMEM((1,), i32),
                        pltpu.SemaphoreType.DMA((6,))],
        name="prepare",
    )(*[pltpu.with_memory_space_constraint(value, pltpu.HBM)
        for value in (doc_lengths, keys, values, queries, d_out)])
    operands = (rows, own, starts)
    if ctx_count != 2 * REACH or lax.axis_size("head") * heads != 2 * GROUP or 2 * heads != GROUP:
        return gradients(True, *operands)
    return lax.switch(split[0], [functools.partial(gradients, True),
                                 functools.partial(gradients, False)], *operands)


def gradients(far, row_data, own, starts):
    heads, (tokens, width) = row_data.shape[0] // 2, row_data.shape[1:]
    head_count = lax.axis_size("head")
    share = GROUP // heads
    groups = head_count // share
    rows = heads * tokens
    ctx = lax.axis_index("ctx")
    mutual = lax.axis_size("ctx") == 2 * REACH and share == groups == 2
    pair = (tokens, 2 * width)
    all_rows = (heads, tokens, width)
    stats = shape((3, rows), f32)
    wide = shape((tokens, rows), f32)
    half = shape((tokens, rows), bf16)
    half_scratch = pltpu.VMEM((tokens, rows), bf16)
    halves_scratch = pltpu.VMEM((2, tokens, rows), bf16)
    pair_scratch = pltpu.VMEM(pair, f32)

    if far:
        four = exchanged(own, "ctx", 4) if mutual else shifted(own, 4)
    two = [exchanged(own, "ctx", 6)] if far and mutual else []
    two.append(exchanged(own, "ctx", 2) if mutual else shifted(own, 2))
    e_own, dp_own, stats_own = call(
        own_unit_body, "own_unit", [VMEM] * 3, (wide, wide, stats))(starts, row_data, own)
    other_rows = exchanged(row_data, "ctx", 1)
    if far:
        four, stats_own = lax.optimization_barrier((four, stats_own))
        e_four, dp_four, stats_four = call(
            four_unit_body, "four_unit", [VMEM] * 3, (wide, wide, stats))(starts, row_data, four)
        other_rows, stats_four = lax.optimization_barrier((other_rows, stats_four))
        e_side, dp_side, stats_side = call(
            side_unit_body, "side_unit", [VMEM] * 4, (wide, wide, stats),
        )(starts, other_rows, own, four)
    else:
        e_side, dp_side, stats_side = call(
            near_side_unit_body, "side_unit", [VMEM] * 3, (wide, wide, stats),
        )(starts, other_rows, own)
    *two, stats_side, stats_own = lax.optimization_barrier((*two, stats_side, stats_own))
    mine_stats = (stats_own, stats_four) if far else (stats_own,)
    two = jnp.where(ctx & 2 == 2, two[1], two[0]) if len(two) == 2 else two[0]
    few = shape((4, rows), f32)
    e_cross, dp_cross, stats_cross, others = call(
        cross_unit_body, "cross_unit", [VMEM] * 4, (wide, wide, stats, few),
    )(starts, other_rows, two, stats_side)
    taken_others = exchanged(others, "ctx", 1)
    e_two, dp_two, stats_two, mine = call(
        two_unit_body, "two_unit", [VMEM] * (3 + len(mine_stats)), (wide, wide, stats, few),
    )(starts, row_data, two, *mine_stats)
    taken_mine = exchanged(mine, "ctx", 1)
    mine_stats += (stats_two,)
    parts = ((e_four, dp_four) if far else (e_own, dp_own)) + (e_two, dp_two)
    mine_coef, ds_first, ds_two, first_part, two_part = call(
        functools.partial(my_terms_body, len(mine_stats)), "my_terms",
        [VMEM] * (7 + len(mine_stats)),
        (few, half, half, shape(pair, f32), shape(pair, f32)), (halves_scratch,),
    )(mine, taken_others, *mine_stats, *parts, row_data)
    last_stats = (others, taken_mine, stats_side, stats_cross)
    slices = (tokens // 2, 2 * width)
    slice_dims = (tokens // head_count, 2 * width)
    if not mutual:
        coef, four_terms = call(
            four_terms_body, "four_terms", [VMEM] * 8, (few, shape(pair, bf16)),
            (pair_scratch, half_scratch, half_scratch),
        )(*last_stats, e_side, dp_side, other_rows, first_part)
        two_terms, ds_cross = call(
            two_terms_body, "two_terms", [VMEM] * 5, (shape(pair, bf16), half),
            (half_scratch, pair_scratch),
        )(coef, e_cross, dp_cross, other_rows, two_part)
        backs = [shifted(four_terms, -4), shifted(two_terms, -2)]
        own_terms, my_grads, other_grads = call(
            own_terms_body, "own_terms", [VMEM] * 14,
            (shape(pair, f32), shape(all_rows, f32), shape(all_rows, bf16)),
            (half_scratch,) * 4,
        )(mine_coef, coef, e_own, dp_own, e_side, dp_side, row_data, other_rows, own, two,
          ds_two, ds_cross, four, ds_first)
        taken_grads = exchanged(other_grads, "ctx", 1)
        d_queries, = call(
            add_grads_body, "add_grads", [VMEM] * 2, (shape(all_rows, bf16),),
        )(my_grads, taken_grads)
        sums, = call(sums_body, "sums", [VMEM] * 3, (shape(pair, bf16),))(own_terms, *backs)
        pieces = lax.all_to_all(sums.reshape(head_count, *slice_dims), "head", 0, 0)
        result = jnp.sum(
            pieces.reshape(groups, share, *slice_dims).astype(f32), axis=1).astype(bf16)
        return d_queries, result[..., :width], result[..., width:]

    halves = (shape(slices, bf16), shape(slices, bf16))
    part = shape(slices, f32)
    coef, two_kept, two_other, ds_cross = call(
        halved_two_terms_body, "two_terms", [VMEM] * 8, (few,) + halves + (half,),
        (half_scratch, pair_scratch),
    )(*last_stats, e_cross, dp_cross, other_rows, two_part)
    two_back = exchanged(two_kept, "ctx", 2)
    two_pair = exchanged(two_other, ("ctx", "head"), 2 * head_count + 1)
    if far:
        four_kept, four_other = call(
            far_four_terms_body, "four_terms", [VMEM] * 5, (part, halves[1]),
            (pair_scratch, half_scratch, half_scratch),
        )(coef, e_side, dp_side, other_rows, first_part)
        four_pair = exchanged(four_other, ("ctx", "head"), 4 * head_count + 1)
        own_kept, own_other, ds_own, ds_side = call(
            far_own_terms_body, "own_terms", [VMEM] * 8, (part, halves[1], half, half),
            (half_scratch, half_scratch, pair_scratch),
        )(mine_coef, coef, e_own, dp_own, e_side, dp_side, row_data, other_rows)
    else:
        ds_own = ds_first
        own_kept, own_other, ds_side = call(
            near_own_terms_body, "own_terms", [VMEM] * 5, (part, halves[1], half),
            (half_scratch, pair_scratch),
        )(coef, e_side, dp_side, other_rows, first_part)
    own_pair = exchanged(own_other, "head", 1)
    four_refs = (four, ds_first) if far else ()
    my_grads, other_grads = call(
        grads_body, "query_grads", [VMEM] * (6 + len(four_refs)),
        (shape(all_rows, f32), shape(all_rows, bf16)),
    )(own, two, ds_own, ds_two, ds_side, ds_cross, *four_refs)
    owns_four = lambda i: i < 4
    if far:
        own_kept, relayed = call(
            relay_body, "relay", [VMEM] * 4, (part, halves[0]),
        )(own_kept, four_kept, two_back, two_pair)
        four_back = exchanged(relayed, "ctx", 4)
        own_kept, = call(functools.partial(add_others_body, owns_four), "add_others", [VMEM] * 3,
                         (part,))(own_kept, own_pair, four_pair)
        final, use = four_back, owns_four
    else:
        own_kept, = call(
            near_first_sum_body, "first_sum", [VMEM] * 3, (part,),
        )(own_kept, two_back, two_pair)
        final, use = own_pair, None
    kept, sent = call(
        functools.partial(halves_sum_body, share, use), "sums", [VMEM] * 2,
        (shape(slice_dims, bf16),) * 2)(own_kept, final)
    other_grads, kept = lax.optimization_barrier((other_grads, kept))
    taken_grads = exchanged(other_grads, "ctx", 1)
    d_queries, = call(
        add_grads_body, "add_grads", [VMEM] * 2, (shape(all_rows, bf16),),
    )(my_grads, taken_grads)
    last = exchanged(sent, "head", share)
    last, d_queries = lax.optimization_barrier((last, d_queries))
    d_keys, d_values = call(
        functools.partial(last_body, share), "last", [VMEM] * 2,
        (shape((groups, tokens // head_count, width), bf16),) * 2)(kept, last)
    return d_queries, d_keys, d_values


def solution(mesh):
    placed = (
        P("head", "ctx", None),
        P(None, "ctx", None),
        P(None, "ctx", None),
        P("head", "ctx", None),
        P(),
    )
    return jax.shard_map(
        per_device,
        mesh=mesh,
        in_specs=placed,
        out_specs=(
            P("head", "ctx", None),
            P(None, ("ctx", "head"), None),
            P(None, ("ctx", "head"), None),
        ),
        check_vma=False,
    )
```
